32 devices in a mesh: dp: 4 (over y, x), seq: 8 (over z, core).
Axes of the slice: x: 2, y: 2, z: 4, core: 2. Of those that a mesh axis runs over, the one named last changes fastest.
Arguments:
- tokens: bfloat16 [16, 8, 128, 768], P('dp', 'seq'), may hold values from -6 to 6
- cotangent: bfloat16 [16, 8, 128, 768], P('dp', 'seq'), may hold values from -18 to 18
- owners: int32 [64], replicated, may hold values from 0 to 7, as said below
- tile_master: float32 [128, 192, 192], P('seq'), may hold values from -0.4375 to 0.4375
- tile_moment: float32 [128, 192, 192], P('seq'), may hold values from -1.75 to 1.75
- tile_second: float32 [128, 192, 192], P('seq'), may hold values from 0.001 to 0.004
- tile_average: float32 [128, 192, 192], P('seq'), may hold values from -0.4375 to 0.4375
- vectors: float32 [5, 768], replicated, may hold values from 0.3 to 1.5
- vector_moment: float32 [5, 768], replicated, may hold values from -1.75 to 1.75
- vector_second: float32 [5, 768], replicated, may hold values from 0.001 to 0.004
- vector_average: float32 [5, 768], replicated, may hold values from 0.3 to 1.5
- filter_in: float32 [5, 128], replicated, may hold values from -2.5 to 2.5
- in_moment: float32 [5, 128], replicated, may hold values from -1.75 to 1.75
- in_second: float32 [5, 128], replicated, may hold values from 0.001 to 0.004
- in_average: float32 [5, 128], replicated, may hold values from -2.5 to 2.5
- filter_out: float32 [128, 768], replicated, may hold values from -0.5 to 0.5
- out_moment: float32 [128, 768], replicated, may hold values from -1.75 to 1.75
- out_second: float32 [128, 768], replicated, may hold values from 0.001 to 0.004
- out_average: float32 [128, 768], replicated, may hold values from -0.5 to 0.5
Outputs:
- output: bfloat16 [16, 8, 128, 768], P('dp', 'seq')
- in_grad: float32 [16, 8, 128, 768], P('dp', 'seq')
- tile_grad: float32 [128, 192, 192], P('seq')
- tile_second_new: float32 [128, 192, 192], P('seq')
- tile_master_new: float32 [128, 192, 192], P('seq')
- tile_average_new: float32 [128, 192, 192], P('seq')
- vector_grad: float32 [5, 768], replicated
- vector_second_new: float32 [5, 768], replicated
- vectors_new: float32 [5, 768], replicated
- vector_average_new: float32 [5, 768], replicated
- in_grad_filter: float32 [5, 128], replicated
- in_second_new: float32 [5, 128], replicated
- filter_in_new: float32 [5, 128], replicated
- in_average_new: float32 [5, 128], replicated
- out_grad_filter: float32 [128, 768], replicated
- out_second_new: float32 [128, 768], replicated
- filter_out_new: float32 [128, 768], replicated
- out_average_new: float32 [128, 768], replicated
The draws below stay inside these ranges and needn't reach their ends.
Inputs may be any that keep to these rules, and one draw needn't show every extreme that they name: owners[i] is the index along seq of the device that updates weight block i; no index owns more than 16 blocks and some index owns exactly 16.
All inputs are finite; a program needn't handle non-finite values.
Results may differ from the reference program's by a relative error of at most 0.012.
Values may be sent and summed in bfloat16 or wider, within the bound.
A program may use at most 192 MiB of HBM per device.

```python
import math
import jax
import jax.numpy as jnp
from jax import lax

D = 768
FF = 3072
ORDER = 128
FEAT = 5
ROW_LEN = 128
STEP = 10
BLOCK = 192
NTILES = 64
CAP = 16
GRID_ROWS = 8
SEQS = 16
TOKENS = 16384
N_SEQ = 8


def draw_owners(key, part):
    key = jax.random.fold_in(key, 11)
    key_rest = jax.random.fold_in(key, 1)
    key_order = jax.random.fold_in(key, 2)
    key_shift = jax.random.fold_in(key, 3)
    slot_total = 2 * NTILES
    seq_devices = slot_total // CAP
    rest_slots = jax.random.permutation(key_rest, slot_total - CAP).astype(jnp.int32) + CAP
    chosen = jnp.concatenate([jnp.arange(CAP, dtype=jnp.int32), rest_slots[:NTILES - CAP]])
    tile_order = jax.random.permutation(key_order, NTILES)
    chosen = chosen[tile_order]
    rotation = jax.random.randint(key_shift, (), 0, seq_devices, dtype=jnp.int32)
    return ((chosen // CAP + rotation) % seq_devices).astype(jnp.int32)


def draw_cotangent(key, part):
    key = jax.random.fold_in(key, 23)
    seq_rise = jnp.arange(SEQS, dtype=jnp.float32) / (SEQS - 1)
    row_rise = jnp.arange(GRID_ROWS, dtype=jnp.float32) / (GRID_ROWS - 1)
    factors = (1.0 + 2.0 * seq_rise)[:, None] * (1.0 + 2.0 * row_rise)[None, :] / 3.0
    noise = jnp.clip(jax.random.normal(key, (SEQS, GRID_ROWS, ROW_LEN, D), jnp.float32), -6.0, 6.0)
    return (noise * factors[:, :, None, None]).astype(jnp.bfloat16)


def shard_levels(own_key, shape, split, smallest, largest):
    def one(axis_at, shards_of):
        steps = jax.random.uniform(jax.random.fold_in(jax.random.fold_in(own_key, 6), axis_at), (shards_of,), jnp.float32, smallest / len(split), largest / len(split))
        return jnp.repeat(jnp.exp(steps), shape[axis_at] // shards_of).reshape((-1,) + (1,) * (len(shape) - axis_at - 1))

    gain = one(*split[0])
    for cut in split[1:]:
        gain = gain * one(*cut)
    return gain


def normal_values(own_key, extent, scale, bound, pieces=(), kind=jnp.bfloat16):
    gain = shard_levels(own_key, extent, pieces, -0.22, 0.18) if pieces else 1.0
    values = jax.random.normal(own_key, extent, jnp.float32) * scale * gain
    return jnp.minimum(jnp.maximum(values, -bound), bound).astype(kind)


def setup_inputs(seed: int = 0) -> dict:
    key_list = jax.random.split(jax.random.key(seed), 20)
    tokens = normal_values(key_list[0], (SEQS, GRID_ROWS, ROW_LEN, D), 1.0, 6.0, ((0, 4), (1, 8)))
    cotangent = draw_cotangent(jax.random.fold_in(key_list[19], 71), 0)
    owners = draw_owners(jax.random.fold_in(key_list[19], 71), 0)
    tile_master = normal_values(key_list[3], (CAP * N_SEQ, BLOCK, BLOCK), BLOCK ** -0.5, 0.4375, ((0, 8),), jnp.float32)
    tile_moment = normal_values(key_list[4], (CAP * N_SEQ, BLOCK, BLOCK), 0.11, 1.75, ((0, 8),), jnp.float32)
    tile_second = jnp.clip(jnp.exp(math.log(0.004) - 1.3862944 * jax.random.uniform(key_list[5], (CAP * N_SEQ, BLOCK, BLOCK), jnp.float32) ** shard_levels(key_list[5], (CAP * N_SEQ, BLOCK, BLOCK), ((0, 8),), -0.2, 0.2)), 0.001, 0.004)
    tile_average = normal_values(key_list[6], (CAP * N_SEQ, BLOCK, BLOCK), BLOCK ** -0.5, 0.4375, ((0, 8),), jnp.float32)
    vectors = jnp.clip(jax.random.uniform(key_list[7], (5, D), jnp.float32, 0.3, 1.5), 0.3, 1.5)
    vector_moment = normal_values(key_list[8], (5, D), 0.11, 1.75, (), jnp.float32)
    vector_second = jnp.clip(jnp.exp(jax.random.uniform(key_list[9], (5, D), jnp.float32, math.log(0.001), math.log(0.004))), 0.001, 0.004)
    vector_average = jnp.clip(jax.random.uniform(key_list[10], (5, D), jnp.float32, 0.3, 1.5), 0.3, 1.5)
    filter_in = normal_values(key_list[11], (FEAT, ORDER), FEAT ** -0.5, 2.5, (), jnp.float32)
    in_moment = normal_values(key_list[12], (FEAT, ORDER), 0.11, 1.75, (), jnp.float32)
    in_second = jnp.clip(jnp.exp(jax.random.uniform(key_list[13], (FEAT, ORDER), jnp.float32, math.log(0.001), math.log(0.004))), 0.001, 0.004)
    in_average = normal_values(key_list[14], (FEAT, ORDER), FEAT ** -0.5, 2.5, (), jnp.float32)
    filter_out = normal_values(key_list[15], (ORDER, D), ORDER ** -0.5, 0.5, (), jnp.float32)
    out_moment = normal_values(key_list[16], (ORDER, D), 0.11, 1.75, (), jnp.float32)
    out_second = jnp.clip(jnp.exp(jax.random.uniform(key_list[17], (ORDER, D), jnp.float32, math.log(0.001), math.log(0.004))), 0.001, 0.004)
    out_average = normal_values(key_list[18], (ORDER, D), ORDER ** -0.5, 0.5, (), jnp.float32)
    return dict(tokens=tokens, cotangent=cotangent, owners=owners, tile_master=tile_master, tile_moment=tile_moment, tile_second=tile_second, tile_average=tile_average, vectors=vectors, vector_moment=vector_moment, vector_second=vector_second, vector_average=vector_average, filter_in=filter_in, in_moment=in_moment, in_second=in_second, in_average=in_average, filter_out=filter_out, out_moment=out_moment, out_second=out_second, out_average=out_average)


highest = lax.Precision.HIGHEST
beta_one = 0.9
beta_two = 0.999
keep_rate = 0.5
adam_eps = 1e-08
norm_eps = 1e-05
golden = 0.6180339887

@jax.custom_vjp
def low(v):
    return lax.optimization_barrier(v.astype(jnp.bfloat16)).astype(jnp.float32)

@jax.custom_vjp
def low_back(v):
    return v

def low_keep(v):
    return (low(v), None)

def low_pass(kept, grad):
    return (grad,)

def back_keep(v):
    return (v, None)

def back_low(kept, grad):
    return (low(grad),)
low.defvjp(low_keep, low_pass)
low_back.defvjp(back_keep, back_low)

def norm_rows(values, gain_vec, bias_vec):
    row_mean = lax.optimization_barrier(jnp.mean(values, axis=-1, keepdims=True))
    centered = values - row_mean
    spread = lax.optimization_barrier(jnp.mean(centered * centered, axis=-1, keepdims=True))
    return centered * lax.rsqrt(spread + norm_eps) * gain_vec + bias_vec

def glu_act(gate_value, up_value):
    return jax.nn.gelu(gate_value, approximate=False) * up_value

def filter_taps(filter_in, filter_out, position, length):
    phases = position * (2.0 * math.pi / length)
    features = jnp.stack([position / length, jnp.cos(phases), -jnp.sin(phases), jnp.cos(2.0 * phases), -jnp.sin(2.0 * phases)], axis=1)
    hidden = jnp.sin(jnp.dot(features, filter_in, precision=highest))
    taps_value = jnp.dot(hidden, filter_out, precision=highest)
    channel = jnp.arange(filter_out.shape[1], dtype=jnp.float32)
    decay_rates = 0.3 * jnp.exp(math.log(1000.0) * jnp.mod(channel * golden, 1.0))
    decay_rate = jnp.exp(-(position / length)[:, None] * decay_rates[None, :])
    total = jnp.expm1(-2.0 * decay_rates) / jnp.expm1(-2.0 * decay_rates / length)
    norm_scale = lax.rsqrt(total)
    return taps_value * decay_rate * norm_scale

def block_weight(tile_stack, in_tiles, out_tiles):
    tile_side = tile_stack.shape[-1]
    tile_grid = tile_stack.reshape(4, in_tiles, out_tiles, tile_side, tile_side).transpose(0, 1, 3, 2, 4)
    return tile_grid.reshape(4, in_tiles * tile_side, out_tiles * tile_side)

def block_apply(values, blocks):
    row_view = values.reshape(values.shape[0], 4, -1)
    return jnp.einsum('nbi,bio->nbo', row_view, blocks, precision=highest).reshape(values.shape[0], -1)

def slot_maps(owners, owner_cap, slot_total):
    tile_count = owners.shape[0]
    tile_index = jnp.arange(tile_count, dtype=jnp.int32)
    earlier = (owners[:, None] == owners[None, :]) & (tile_index[None, :] < tile_index[:, None])
    owner_rank = lax.optimization_barrier(jnp.sum(earlier.astype(jnp.int32), axis=1))
    slot_of_tile = (owners * owner_cap + owner_rank).astype(jnp.int32)
    slot_hits = slot_of_tile[None, :] == jnp.arange(slot_total, dtype=jnp.int32)[:, None]
    tile_of_slot = lax.optimization_barrier(jnp.sum(slot_hits.astype(jnp.int32) * tile_index[None, :], axis=1)).astype(jnp.int32)
    slot_used = jnp.any(slot_hits, axis=1)
    return (slot_of_tile, tile_of_slot, slot_used)

def adam_step(weight, moment, second, average, gradient, step_rate, decay_rate):
    moment = beta_one * moment + (1.0 - beta_one) * gradient
    second = beta_two * second + (1.0 - beta_two) * gradient * gradient
    fixed_moment = moment / (1.0 - beta_one ** STEP)
    fixed_second = second / (1.0 - beta_two ** STEP)
    weight = weight - step_rate * (fixed_moment / (jnp.sqrt(fixed_second) + adam_eps) + decay_rate * weight)
    average = keep_rate * average + (1.0 - keep_rate) * weight
    return (second, weight, average)

def forward(x_seq, tile_stack, vectors, filter_in, filter_out):
    grid_rows, row_len, model_width = x_seq.shape
    length = grid_rows * row_len
    hidden_ratio = FF // D
    weights = low(tile_stack)
    w_in = block_weight(weights[0:12], 1, 3)
    w_out = block_weight(weights[12:16], 1, 1)
    w_gate = block_weight(weights[16:16 + 4 * hidden_ratio], 1, hidden_ratio)
    w_up = block_weight(weights[16 + 4 * hidden_ratio:16 + 8 * hidden_ratio], 1, hidden_ratio)
    w_down = block_weight(weights[16 + 8 * hidden_ratio:16 + 12 * hidden_ratio], hidden_ratio, 1)
    flat_tokens = x_seq.transpose(1, 0, 2).reshape(length, model_width)
    qkv_all = low_back(block_apply(low(flat_tokens), w_in))
    query_part = qkv_all[:, :model_width]
    key_part = qkv_all[:, model_width:2 * model_width]
    value_part = qkv_all[:, 2 * model_width:]
    kv_product = key_part * value_part
    position = jnp.arange(length, dtype=jnp.float32)
    taps_value = filter_taps(filter_in, filter_out, position, length)
    conv_out = jnp.fft.irfft(jnp.fft.rfft(kv_product, axis=0) * jnp.fft.rfft(taps_value, axis=0), n=length, axis=0)
    inner_sum = conv_out + vectors[4] * kv_product
    gated_out = low(query_part * inner_sum)
    branch = low_back(block_apply(gated_out, w_out))
    normed = low(norm_rows(flat_tokens + branch, vectors[0], vectors[1]))
    gate_value = low_back(block_apply(normed, w_gate))
    up_value = low_back(block_apply(normed, w_up))
    active = low(glu_act(gate_value, up_value))
    down_value = low_back(block_apply(active, w_down))
    result = norm_rows(normed + down_value, vectors[2], vectors[3])
    return result.reshape(row_len, grid_rows, model_width).transpose(1, 0, 2)

def reference(tokens, cotangent, owners, tile_master, tile_moment, tile_second, tile_average, vectors, vector_moment, vector_second, vector_average, filter_in, in_moment, in_second, in_average, filter_out, out_moment, out_second, out_average):
    slot_total = tile_master.shape[0]
    slot_of_tile, tile_of_slot, slot_used = slot_maps(owners, CAP, slot_total)
    tile_stack = jnp.take(tile_master, slot_of_tile, axis=0)

    def one_sequence(grad_sums, seq_pair):
        x_seq, cot_seq = seq_pair
        result, pull_back = jax.vjp(forward, x_seq.astype(jnp.float32), tile_stack, vectors, filter_in, filter_out)
        grads_all = pull_back(cot_seq.astype(jnp.float32))
        grad_sums = tuple((total_sum + term_part for total_sum, term_part in zip(grad_sums, grads_all[1:])))
        return (grad_sums, (result.astype(jnp.bfloat16), grads_all[0]))
    start_sums = (jnp.zeros_like(tile_stack), jnp.zeros_like(vectors), jnp.zeros_like(filter_in), jnp.zeros_like(filter_out))
    grad_sums, (output, in_grad) = lax.scan(one_sequence, start_sums, (tokens, cotangent))
    grad_scale = 1.0 / math.sqrt(TOKENS)
    tile_sum = grad_sums[0] * grad_scale
    vector_grad = grad_sums[1] * grad_scale
    in_grad_filter = grad_sums[2] * grad_scale
    out_grad_filter = grad_sums[3] * grad_scale
    slot_mask = slot_used.astype(jnp.float32)[:, None, None]
    tile_grad = jnp.take(tile_sum, tile_of_slot, axis=0) * slot_mask
    tile_new = adam_step(tile_master, tile_moment, tile_second, tile_average, tile_grad, 0.1, 0.01)
    vector_new = adam_step(vectors, vector_moment, vector_second, vector_average, vector_grad, 0.4, 0.0)
    in_new = adam_step(filter_in, in_moment, in_second, in_average, in_grad_filter, 0.4, 0.01)
    out_new = adam_step(filter_out, out_moment, out_second, out_average, out_grad_filter, 0.1, 0.01)
    return (output, in_grad, tile_grad, tile_new[0] * slot_mask, tile_new[1] * slot_mask, tile_new[2] * slot_mask, vector_grad, vector_new[0], vector_new[1], vector_new[2], in_grad_filter, in_new[0], in_new[1], in_new[2], out_grad_filter, out_new[0], out_new[1], out_new[2])
```

```python
import math

import jax
import jax.numpy as jnp
import ml_dtypes
import numpy as np
from jax import lax
from jax.sharding import PartitionSpec as P

D = 768
FF = 3072
STEP = 10


highest = lax.Precision.HIGHEST
beta_one = 0.9
beta_two = 0.999
keep_rate = 0.5
adam_eps = 1e-08
norm_eps = 1e-05
golden = 0.6180339887


def norm_rows(values, gain_vec, bias_vec):
    row_mean = jnp.mean(values, axis=-1, keepdims=True)
    centered = values - row_mean
    spread = jnp.mean(centered * centered, axis=-1, keepdims=True)
    return centered * lax.rsqrt(spread + norm_eps) * gain_vec + bias_vec


def glu_act(gate_value, up_value):
    return jax.nn.gelu(gate_value, approximate=False) * up_value


def filter_taps(filter_in, filter_out, position, length):
    channel = jnp.arange(filter_out.shape[1], dtype=jnp.int32)
    return filter_taps_of(filter_in, filter_out, position, length, channel)


def filter_taps_of(filter_in, filter_out, position, length, channel_index):
    phases = position * (2.0 * math.pi / length)
    features = jnp.stack(
        [
            position / length,
            jnp.cos(phases),
            -jnp.sin(phases),
            jnp.cos(2.0 * phases),
            -jnp.sin(2.0 * phases),
        ],
        axis=1,
    )
    hidden = jnp.sin(jnp.dot(features, filter_in, precision=highest))
    taps_value = jnp.dot(hidden, filter_out, precision=highest)
    channel = channel_index.astype(jnp.float32)
    decay_rates = 0.3 * jnp.exp(math.log(1000.0) * jnp.mod(channel * golden, 1.0))
    decay_rate = jnp.exp(-(position / length)[:, None] * decay_rates[None, :])
    total = jnp.expm1(-2.0 * decay_rates) / jnp.expm1(-2.0 * decay_rates / length)
    norm_scale = lax.rsqrt(total)
    return taps_value * decay_rate * norm_scale


def block_weight(tile_stack, in_tiles, out_tiles):
    tile_side = tile_stack.shape[-1]
    tile_grid = tile_stack.reshape(4, in_tiles, out_tiles, tile_side, tile_side).transpose(
        0, 1, 3, 2, 4
    )
    return tile_grid.reshape(4, in_tiles * tile_side, out_tiles * tile_side)


def tile_split(blocks, in_tiles, out_tiles):
    tile_side = blocks.shape[1] // in_tiles
    tile_grid = blocks.reshape(4, in_tiles, tile_side, out_tiles, tile_side).transpose(
        0, 1, 3, 2, 4
    )
    return tile_grid.reshape(4 * in_tiles * out_tiles, tile_side, tile_side)


def block_apply(values, blocks):
    row_view = values.reshape(values.shape[0], 4, -1)
    return jnp.einsum("nbi,bio->nbo", row_view, blocks, preferred_element_type=jnp.float32).reshape(
        values.shape[0], -1
    )


def block_back(gradient, blocks):
    row_view = gradient.reshape(gradient.shape[0], 4, -1)
    return jnp.einsum("nbo,bio->nbi", row_view, blocks, preferred_element_type=jnp.float32).reshape(
        gradient.shape[0], -1
    )


def block_grad(values, gradient, in_tiles, out_tiles):
    left_rows = values.reshape(values.shape[0], 4, -1)
    right_rows = gradient.reshape(gradient.shape[0], 4, -1)
    blocks = jnp.einsum("nbi,nbo->bio", left_rows, right_rows, preferred_element_type=jnp.float32)
    return tile_split(blocks, in_tiles, out_tiles)


def slot_maps(owners, owner_cap, slot_total):
    tile_count = owners.shape[0]
    tile_index = jnp.arange(tile_count, dtype=jnp.int32)
    earlier = (owners[:, None] == owners[None, :]) & (tile_index[None, :] < tile_index[:, None])
    owner_rank = jnp.sum(earlier.astype(jnp.int32), axis=1)
    slot_of_tile = owners * owner_cap + owner_rank
    slot_hits = slot_of_tile[None, :] == jnp.arange(slot_total, dtype=jnp.int32)[:, None]
    tile_of_slot = jnp.sum(slot_hits.astype(jnp.int32) * tile_index[None, :], axis=1)
    slot_used = jnp.any(slot_hits, axis=1)
    return (slot_of_tile, tile_of_slot, slot_used)


def adam_step(weight, moment, second, average, gradient, step_rate, decay_rate):
    moment = beta_one * moment + (1.0 - beta_one) * gradient
    second = beta_two * second + (1.0 - beta_two) * gradient * gradient
    fixed_moment = moment / (1.0 - beta_one**STEP)
    fixed_second = second / (1.0 - beta_two**STEP)
    weight = weight - step_rate * (
        fixed_moment / (jnp.sqrt(fixed_second) + adam_eps) + decay_rate * weight
    )
    average = keep_rate * average + (1.0 - keep_rate) * weight
    return (second, weight, average)


def wave_table(period, index_one, index_two):
    turn_count = jnp.mod(index_one[:, None] * index_two[None, :], period).astype(jnp.float32)
    angles = turn_count * (2.0 * math.pi / period)
    return (jnp.cos(angles), jnp.sin(angles))


def col_dot(field_in, table_in):
    return jnp.einsum("srcd,ck->srkd", field_in, table_in, precision=highest)


def row_dot(field_in, table_in):
    return jnp.einsum("srkd,rq->sqkd", field_in, table_in, precision=highest)


def cols_forward(field_in, tables):
    col_cos, col_sin, turn_cos, turn_sin, row_cos, row_sin = tables
    real_part = col_dot(field_in, col_cos)
    imag_part = -col_dot(field_in, col_sin)
    real_turn = real_part * turn_cos + imag_part * turn_sin
    imag_turn = imag_part * turn_cos - real_part * turn_sin
    return (real_turn, imag_turn)


def rows_forward(part_real, part_imag, tables):
    row_cos, row_sin = (tables[4], tables[5])
    freq_real = row_dot(part_real, row_cos) + row_dot(part_imag, row_sin)
    freq_imag = row_dot(part_imag, row_cos) - row_dot(part_real, row_sin)
    return (freq_real, freq_imag)


def rows_inverse(prod_real, prod_imag, tables):
    row_cos, row_sin = (tables[4], tables[5])
    back_real = row_dot(prod_real, row_cos) - row_dot(prod_imag, row_sin)
    back_imag = row_dot(prod_real, row_sin) + row_dot(prod_imag, row_cos)
    return (back_real, back_imag)


def cols_inverse(rows_real, rows_imag, tables, length):
    col_cos, col_sin, turn_cos, turn_sin, row_cos, row_sin = tables
    cell_real = rows_real * turn_cos - rows_imag * turn_sin
    cell_imag = rows_real * turn_sin + rows_imag * turn_cos
    return (
        jnp.einsum("srkd,ck->srcd", cell_real, col_cos, precision=highest)
        - jnp.einsum("srkd,ck->srcd", cell_imag, col_sin, precision=highest)
    ) / length


def convolve(field_in, spectrum, tables, conjugate, length):
    spec_real, spec_imag = spectrum
    sign_flip = -1.0 if conjugate else 1.0
    real_turn, imag_turn = cols_forward(field_in, tables)
    part_real = lax.all_to_all(real_turn, "seq", split_axis=2, concat_axis=1, tiled=True)
    part_imag = lax.all_to_all(imag_turn, "seq", split_axis=2, concat_axis=1, tiled=True)
    freq_real, freq_imag = rows_forward(part_real, part_imag, tables)
    prod_real = freq_real * spec_real - sign_flip * freq_imag * spec_imag
    prod_imag = sign_flip * freq_real * spec_imag + freq_imag * spec_real
    back_real, back_imag = rows_inverse(prod_real, prod_imag, tables)
    rows_real = lax.all_to_all(back_real, "seq", split_axis=1, concat_axis=2, tiled=True)
    rows_imag = lax.all_to_all(back_imag, "seq", split_axis=1, concat_axis=2, tiled=True)
    rows_real, rows_imag, freq_real, freq_imag = (rows_real, rows_imag, freq_real, freq_imag)
    field_out = cols_inverse(rows_real, rows_imag, tables, length)
    return (field_out, freq_real, freq_imag)


def real_table(grid_rows, row_len):
    length = grid_rows * row_len
    position = (np.arange(grid_rows)[:, None] + grid_rows * np.arange(row_len)[None, :]).reshape(-1)
    turns = np.mod(np.arange(length // 2)[:, None] * position[None, :], length)
    angles = turns * (2.0 * np.pi / length)
    sines = -np.sin(angles)
    sines[0] = np.cos(np.pi * position)
    return np.concatenate([np.cos(angles), sines]).astype(ml_dtypes.bfloat16)


def on_device_general(
    tokens,
    cotangent,
    owners,
    tile_master,
    tile_moment,
    tile_second,
    tile_average,
    vectors,
    vector_moment,
    vector_second,
    vector_average,
    filter_in,
    in_moment,
    in_second,
    in_average,
    filter_out,
    out_moment,
    out_second,
    out_average,
):
    seq_count, dev_rows, row_len, model_width = tokens.shape
    owner_cap = tile_master.shape[0]
    seq_devices = lax.axis_size("seq")
    grid_rows = dev_rows * seq_devices
    length = grid_rows * row_len
    seq_index = lax.axis_index("seq")
    hidden_ratio = FF // D
    quarter_hidden = FF // 4
    slot_of_tile, tile_of_slot, slot_used = slot_maps(owners, owner_cap, owner_cap * seq_devices)
    gathered = lax.all_gather(tile_master.astype(jnp.bfloat16), "seq", axis=0, tiled=True)
    weights = jnp.take(gathered, slot_of_tile, axis=0)
    w_in = block_weight(weights[0:12], 1, 3)
    w_out = block_weight(weights[12:16], 1, 1)
    w_gate = block_weight(weights[16 : 16 + 4 * hidden_ratio], 1, hidden_ratio)
    w_up = block_weight(weights[16 + 4 * hidden_ratio : 16 + 8 * hidden_ratio], 1, hidden_ratio)
    w_down = block_weight(weights[16 + 8 * hidden_ratio : 16 + 12 * hidden_ratio], hidden_ratio, 1)
    w_gate_up = jnp.concatenate([w_gate, w_up], axis=2)
    col_index = jnp.arange(row_len, dtype=jnp.int32)
    row_index = jnp.arange(grid_rows, dtype=jnp.int32)
    local_rows = seq_index * dev_rows + jnp.arange(dev_rows, dtype=jnp.int32)
    col_cos, col_sin = wave_table(row_len, col_index, col_index)
    row_cos, row_sin = wave_table(grid_rows, row_index, row_index)
    turn_cos, turn_sin = wave_table(length, local_rows, col_index)
    tables = (
        col_cos,
        col_sin,
        turn_cos[None, :, :, None],
        turn_sin[None, :, :, None],
        row_cos,
        row_sin,
    )
    own_position = (
        (local_rows[:, None] + grid_rows * col_index[None, :]).reshape(-1).astype(jnp.float32)
    )
    flat_tokens = tokens.reshape(-1, model_width)
    qkv_all = block_apply(flat_tokens, w_in)
    query_part = qkv_all[:, :model_width]
    key_part = qkv_all[:, model_width : 2 * model_width]
    value_part = qkv_all[:, 2 * model_width :]
    kv_product = key_part * value_part

    def own_taps(weight_one, weight_two):
        return filter_taps(weight_one, weight_two, own_position, length)

    taps_own, filter_pull = jax.vjp(own_taps, filter_in, filter_out)
    taps_real, taps_imag = cols_forward(taps_own.reshape(1, dev_rows, row_len, model_width), tables)
    taps_real, taps_imag = (
        lax.all_to_all(taps_real, "seq", split_axis=2, concat_axis=1, tiled=True),
        lax.all_to_all(taps_imag, "seq", split_axis=2, concat_axis=1, tiled=True),
    )
    spec_real, spec_imag = rows_forward(taps_real, taps_imag, tables)
    taps_spec = (spec_real[0], spec_imag[0])
    conv_out, kv_real, kv_imag = convolve(
        kv_product.reshape(seq_count, dev_rows, row_len, model_width),
        taps_spec,
        tables,
        False,
        length,
    )
    skip_gain = vectors[4]
    inner_sum = conv_out.reshape(-1, model_width) + skip_gain * kv_product
    gated_out = (query_part * inner_sum).astype(jnp.bfloat16)
    branch = block_apply(gated_out, w_out)
    normed, first_pull = jax.vjp(
        norm_rows, flat_tokens.astype(jnp.float32) + branch, vectors[0], vectors[1]
    )
    normed_low = normed.astype(jnp.bfloat16)
    gate_up = block_apply(normed_low, w_gate_up).reshape(-1, 4, 2, quarter_hidden)
    gate_value = gate_up[:, :, 0].reshape(-1, FF)
    up_value = gate_up[:, :, 1].reshape(-1, FF)
    active, active_pull = jax.vjp(glu_act, gate_value, up_value)
    active_low = active.astype(jnp.bfloat16)
    down_value = block_apply(active_low, w_down)
    result, second_pull = jax.vjp(
        norm_rows, normed_low.astype(jnp.float32) + down_value, vectors[2], vectors[3]
    )
    output = result.astype(jnp.bfloat16).reshape(tokens.shape)
    d_second, d_gain_two, d_bias_two = second_pull(
        cotangent.reshape(-1, model_width).astype(jnp.float32)
    )
    d_down = d_second.astype(jnp.bfloat16)
    g_down = block_grad(active_low, d_down, hidden_ratio, 1)
    d_gate, d_up = active_pull(block_back(d_down, w_down))
    d_gate_up = jnp.stack(
        [d_gate.reshape(-1, 4, quarter_hidden), d_up.reshape(-1, 4, quarter_hidden)], axis=2
    )
    d_gate_up = d_gate_up.reshape(-1, 2 * FF).astype(jnp.bfloat16)
    gate_up_tiles = block_grad(normed_low, d_gate_up, 1, 2 * hidden_ratio).reshape(
        4, 2, hidden_ratio, weights.shape[1], weights.shape[2]
    )
    g_gate = gate_up_tiles[:, 0].reshape(-1, weights.shape[1], weights.shape[2])
    g_up = gate_up_tiles[:, 1].reshape(-1, weights.shape[1], weights.shape[2])
    d_normed = d_second + block_back(d_gate_up, w_gate_up)
    d_first, d_gain_one, d_bias_one = first_pull(d_normed)
    d_branch = d_first.astype(jnp.bfloat16)
    g_out = block_grad(gated_out, d_branch, 1, 1)
    d_gated = block_back(d_branch, w_out)
    d_query = d_gated * inner_sum
    d_inner = d_gated * query_part
    d_skip = jnp.sum(d_inner * kv_product, axis=0)
    d_conv, back_real, back_imag = convolve(
        d_inner.reshape(seq_count, dev_rows, row_len, model_width), taps_spec, tables, True, length
    )
    d_kv = d_conv.reshape(-1, model_width) + skip_gain * d_inner
    d_qkv = jnp.concatenate([d_query, d_kv * value_part, d_kv * key_part], axis=1).astype(
        jnp.bfloat16
    )
    g_in = block_grad(flat_tokens, d_qkv, 1, 3)
    in_grad = (d_first + block_back(d_qkv, w_in)).reshape(tokens.shape)
    cross_real = jnp.sum(back_real * kv_real + back_imag * kv_imag, axis=0, keepdims=True)
    cross_imag = jnp.sum(back_imag * kv_real - back_real * kv_imag, axis=0, keepdims=True)
    cross_back_real, cross_back_imag = rows_inverse(cross_real, cross_imag, tables)
    cross_rows_real, cross_rows_imag = (
        lax.all_to_all(
            cross_back_real.astype(jnp.bfloat16), "seq", split_axis=1, concat_axis=2, tiled=True
        ).astype(cross_back_real.dtype),
        lax.all_to_all(
            cross_back_imag.astype(jnp.bfloat16), "seq", split_axis=1, concat_axis=2, tiled=True
        ).astype(cross_back_imag.dtype),
    )
    d_taps = cols_inverse(cross_rows_real, cross_rows_imag, tables, length).reshape(-1, model_width)
    g_filter_in, g_filter_out = filter_pull(d_taps)
    tile_grads = jnp.concatenate([g_in, g_out, g_gate, g_up, g_down], axis=0)
    slot_mask = slot_used.astype(jnp.float32)[:, None, None]
    summed = lax.psum(tile_grads.astype(jnp.bfloat16), "dp").astype(jnp.float32)
    owned = lax.psum_scatter(
        jnp.take(summed, tile_of_slot, axis=0) * slot_mask, "seq", scatter_dimension=0, tiled=True
    )
    tokens_all = seq_count * dev_rows * row_len * lax.axis_size("dp") * seq_devices
    grad_scale = 1.0 / math.sqrt(tokens_all)
    mine_mask = lax.dynamic_slice_in_dim(slot_mask, seq_index * owner_cap, owner_cap, 0)
    tile_grad = owned * grad_scale
    tile_new = adam_step(tile_master, tile_moment, tile_second, tile_average, tile_grad, 0.1, 0.01)
    vector_part = jnp.stack([d_gain_one, d_bias_one, d_gain_two, d_bias_two, d_skip])
    vector_sum, in_sum, out_sum = lax.psum((vector_part, g_filter_in, g_filter_out), ("dp", "seq"))
    vector_grad = vector_sum * grad_scale
    in_grad_filter = in_sum * grad_scale
    out_grad_filter = out_sum * grad_scale
    vector_new = adam_step(
        vectors, vector_moment, vector_second, vector_average, vector_grad, 0.4, 0.0
    )
    in_new = adam_step(filter_in, in_moment, in_second, in_average, in_grad_filter, 0.4, 0.01)
    out_new = adam_step(filter_out, out_moment, out_second, out_average, out_grad_filter, 0.1, 0.01)
    return (
        output,
        in_grad,
        tile_grad,
        tile_new[0] * mine_mask,
        tile_new[1] * mine_mask,
        tile_new[2] * mine_mask,
        vector_grad,
        vector_new[0],
        vector_new[1],
        vector_new[2],
        in_grad_filter,
        in_new[0],
        in_new[1],
        in_new[2],
        out_grad_filter,
        out_new[0],
        out_new[1],
        out_new[2],
    )


def on_device_columns(
    tokens,
    cotangent,
    owners,
    tile_master,
    tile_moment,
    tile_second,
    tile_average,
    vectors,
    vector_moment,
    vector_second,
    vector_average,
    filter_in,
    in_moment,
    in_second,
    in_average,
    filter_out,
    out_moment,
    out_second,
    out_average,
):
    seq_count, dev_rows, row_len, model_width = tokens.shape
    owner_cap = tile_master.shape[0]
    seq_devices = lax.axis_size("seq")
    grid_rows = dev_rows * seq_devices
    length = grid_rows * row_len
    seq_index = lax.axis_index("seq")
    hidden_ratio = FF // D
    quarter_hidden = FF // 4
    slot_of_tile, tile_of_slot, slot_used = slot_maps(owners, owner_cap, owner_cap * seq_devices)
    gathered = lax.all_gather(tile_master.astype(jnp.bfloat16), "seq", axis=0, tiled=True)
    weights = jnp.take(gathered, slot_of_tile, axis=0)
    w_in = block_weight(weights[0:12], 1, 3)
    w_out = block_weight(weights[12:16], 1, 1)
    w_gate = block_weight(weights[16 : 16 + 4 * hidden_ratio], 1, hidden_ratio)
    w_up = block_weight(weights[16 + 4 * hidden_ratio : 16 + 8 * hidden_ratio], 1, hidden_ratio)
    w_down = block_weight(weights[16 + 8 * hidden_ratio : 16 + 12 * hidden_ratio], hidden_ratio, 1)
    w_gate_up = jnp.concatenate([w_gate, w_up], axis=2)
    halves = seq_devices // seq_count
    width = model_width // halves
    half_index = lax.rem(seq_index, halves)
    grid_position = (
        jnp.arange(grid_rows, dtype=jnp.int32)[:, None]
        + grid_rows * jnp.arange(row_len, dtype=jnp.int32)[None, :]
    )
    position = grid_position.reshape(-1).astype(jnp.float32)
    table = jnp.asarray(real_table(grid_rows, row_len))
    first_bin = (jnp.arange(length // 2) == 0)[:, None]

    def spread(field_in):
        cells = field_in.reshape(seq_count, row_len, halves, width).transpose(0, 2, 1, 3)
        cells = cells.reshape(seq_devices, row_len, width).astype(jnp.bfloat16)
        return lax.all_to_all(cells, "seq", 0, 0, tiled=True).reshape(length, width)

    def collect(field_in):
        cells = field_in.astype(jnp.bfloat16).reshape(seq_devices, row_len, width)
        cells = lax.all_to_all(cells, "seq", 0, 0, tiled=True)
        cells = cells.reshape(seq_count, halves, row_len, width).transpose(0, 2, 1, 3)
        return cells.reshape(-1, model_width).astype(jnp.float32)

    def transform(columns):
        spec = jnp.dot(table, columns.astype(jnp.bfloat16), preferred_element_type=jnp.float32)
        return (spec[: length // 2], spec[length // 2 :])

    def invert(real_part, imag_part):
        weight = jnp.where(first_bin, 1.0 / length, 2.0 / length)
        spec = jnp.concatenate([real_part * weight, imag_part * weight], axis=0)
        return lax.dot_general(
            table,
            spec.astype(jnp.bfloat16),
            (((0,), (0,)), ((), ())),
            preferred_element_type=jnp.float32,
        )

    def product(one, two, conjugate):
        one_real, one_imag = one
        two_real, two_imag = two
        cross = jnp.where(first_bin, 0.0, two_imag) * (-1.0 if conjugate else 1.0)
        diag = jnp.where(first_bin, two_imag, two_real)
        return (one_real * two_real - one_imag * cross, one_real * cross + one_imag * diag)

    flat_tokens = tokens.reshape(-1, model_width)
    qkv_all = block_apply(flat_tokens, w_in)
    query_part = qkv_all[:, :model_width]
    key_part = qkv_all[:, model_width : 2 * model_width]
    value_part = qkv_all[:, 2 * model_width :]
    kv_product = key_part * value_part

    channel = half_index * width + jnp.arange(width, dtype=jnp.int32)
    own_filter = lax.dynamic_slice_in_dim(filter_out, half_index * width, width, 1)

    def own_taps(weight_one, weight_two):
        return filter_taps_of(weight_one, weight_two, position, length, channel)

    taps_own, filter_pull = jax.vjp(own_taps, filter_in, own_filter)
    taps_spec = transform(taps_own)
    kv_spec = transform(spread(kv_product))
    conv_out = collect(invert(*product(kv_spec, taps_spec, False)))
    skip_gain = vectors[4]
    inner_sum = conv_out + skip_gain * kv_product
    gated_out = (query_part * inner_sum).astype(jnp.bfloat16)
    branch = block_apply(gated_out, w_out)
    normed, first_pull = jax.vjp(
        norm_rows, flat_tokens.astype(jnp.float32) + branch, vectors[0], vectors[1]
    )
    normed_low = normed.astype(jnp.bfloat16)
    gate_up = block_apply(normed_low, w_gate_up).reshape(-1, 4, 2, quarter_hidden)
    gate_value = gate_up[:, :, 0].reshape(-1, FF)
    up_value = gate_up[:, :, 1].reshape(-1, FF)
    active, active_pull = jax.vjp(glu_act, gate_value, up_value)
    active_low = active.astype(jnp.bfloat16)
    down_value = block_apply(active_low, w_down)
    result, second_pull = jax.vjp(
        norm_rows, normed_low.astype(jnp.float32) + down_value, vectors[2], vectors[3]
    )
    output = result.astype(jnp.bfloat16).reshape(tokens.shape)
    d_second, d_gain_two, d_bias_two = second_pull(
        cotangent.reshape(-1, model_width).astype(jnp.float32)
    )
    d_down = d_second.astype(jnp.bfloat16)
    g_down = block_grad(active_low, d_down, hidden_ratio, 1)
    d_gate, d_up = active_pull(block_back(d_down, w_down))
    d_gate_up = jnp.stack(
        [d_gate.reshape(-1, 4, quarter_hidden), d_up.reshape(-1, 4, quarter_hidden)], axis=2
    )
    d_gate_up = d_gate_up.reshape(-1, 2 * FF).astype(jnp.bfloat16)
    gate_up_tiles = block_grad(normed_low, d_gate_up, 1, 2 * hidden_ratio).reshape(
        4, 2, hidden_ratio, weights.shape[1], weights.shape[2]
    )
    g_gate = gate_up_tiles[:, 0].reshape(-1, weights.shape[1], weights.shape[2])
    g_up = gate_up_tiles[:, 1].reshape(-1, weights.shape[1], weights.shape[2])
    d_normed = d_second + block_back(d_gate_up, w_gate_up)
    d_first, d_gain_one, d_bias_one = first_pull(d_normed)
    d_branch = d_first.astype(jnp.bfloat16)
    g_out = block_grad(gated_out, d_branch, 1, 1)
    d_gated = block_back(d_branch, w_out)
    d_query = d_gated * inner_sum
    d_inner = d_gated * query_part
    d_skip = jnp.sum(d_inner * kv_product, axis=0)
    back_spec = transform(spread(d_inner))
    d_kv = collect(invert(*product(back_spec, taps_spec, True))) + skip_gain * d_inner
    d_qkv = jnp.concatenate([d_query, d_kv * value_part, d_kv * key_part], axis=1).astype(
        jnp.bfloat16
    )
    g_in = block_grad(flat_tokens, d_qkv, 1, 3)
    in_grad = (d_first + block_back(d_qkv, w_in)).reshape(tokens.shape)
    d_taps = invert(*product(back_spec, kv_spec, True))
    g_filter_in, g_filter_half = filter_pull(d_taps)
    g_filter_out = lax.dynamic_update_slice_in_dim(
        jnp.zeros_like(filter_out), g_filter_half, half_index * width, 1
    )
    tile_grads = jnp.concatenate([g_in, g_out, g_gate, g_up, g_down], axis=0)
    slot_mask = slot_used.astype(jnp.float32)[:, None, None]
    summed = lax.psum(tile_grads.astype(jnp.bfloat16), "dp").astype(jnp.float32)
    owned = lax.psum_scatter(
        jnp.take(summed, tile_of_slot, axis=0) * slot_mask, "seq", scatter_dimension=0, tiled=True
    )
    tokens_all = seq_count * dev_rows * row_len * lax.axis_size("dp") * seq_devices
    grad_scale = 1.0 / math.sqrt(tokens_all)
    mine_mask = lax.dynamic_slice_in_dim(slot_mask, seq_index * owner_cap, owner_cap, 0)
    tile_grad = owned * grad_scale
    tile_new = adam_step(tile_master, tile_moment, tile_second, tile_average, tile_grad, 0.1, 0.01)
    vector_part = jnp.stack([d_gain_one, d_bias_one, d_gain_two, d_bias_two, d_skip])
    vector_sum, in_sum, out_sum = lax.psum((vector_part, g_filter_in, g_filter_out), ("dp", "seq"))
    vector_grad = vector_sum * grad_scale
    in_grad_filter = in_sum * grad_scale
    out_grad_filter = out_sum * grad_scale
    vector_new = adam_step(
        vectors, vector_moment, vector_second, vector_average, vector_grad, 0.4, 0.0
    )
    in_new = adam_step(filter_in, in_moment, in_second, in_average, in_grad_filter, 0.4, 0.01)
    out_new = adam_step(filter_out, out_moment, out_second, out_average, out_grad_filter, 0.1, 0.01)
    return (
        output,
        in_grad,
        tile_grad,
        tile_new[0] * mine_mask,
        tile_new[1] * mine_mask,
        tile_new[2] * mine_mask,
        vector_grad,
        vector_new[0],
        vector_new[1],
        vector_new[2],
        in_grad_filter,
        in_new[0],
        in_new[1],
        in_new[2],
        out_grad_filter,
        out_new[0],
        out_new[1],
        out_new[2],
    )


def on_device(*arrays):
    seq_count, dev_rows, row_len, model_width = arrays[0].shape
    seq_devices = lax.axis_size("seq")
    fits = dev_rows == 1 and seq_devices % seq_count == 0 and seq_devices * row_len <= 2048
    if fits and model_width % (128 * (seq_devices // seq_count)) == 0:
        return on_device_columns(*arrays)
    return on_device_general(*arrays)


def solution(mesh):
    in_specs = (
        P("dp", "seq", None, None),
        P("dp", "seq", None, None),
        P(),
        P("seq", None, None),
        P("seq", None, None),
        P("seq", None, None),
        P("seq", None, None),
        P(),
        P(),
        P(),
        P(),
        P(),
        P(),
        P(),
        P(),
        P(),
        P(),
        P(),
        P(),
    )
    out_specs = (
        P("dp", "seq", None, None),
        P("dp", "seq", None, None),
        P("seq", None, None),
        P("seq", None, None),
        P("seq", None, None),
        P("seq", None, None),
        P(),
        P(),
        P(),
        P(),
        P(),
        P(),
        P(),
        P(),
        P(),
        P(),
        P(),
        P(),
    )
    return jax.shard_map(
        on_device, mesh=mesh, in_specs=in_specs, out_specs=out_specs, check_vma=False
    )
```

```python
import functools
import math

import jax
import jax.numpy as jnp
import ml_dtypes
import numpy as np
from jax import lax
from jax.experimental import pallas as pl
from jax.experimental.pallas import tpu as pltpu
from jax.sharding import PartitionSpec as P

D = 768
FF = 3072
STEP = 10
NTILES = 64


highest = lax.Precision.HIGHEST
beta_one = 0.9
beta_two = 0.999
keep_rate = 0.5
adam_eps = 1e-08
norm_eps = 1e-05
golden = 0.6180339887


def norm_rows(values, gain_vec, bias_vec):
    row_mean = jnp.mean(values, axis=-1, keepdims=True)
    centered = values - row_mean
    spread = jnp.mean(centered * centered, axis=-1, keepdims=True)
    return centered * lax.rsqrt(spread + norm_eps) * gain_vec + bias_vec


def glu_act(gate_value, up_value):
    return jax.nn.gelu(gate_value, approximate=False) * up_value


def filter_taps(filter_in, filter_out, position, length):
    channel = jnp.arange(filter_out.shape[1], dtype=jnp.int32)
    return filter_taps_of(filter_in, filter_out, position, length, channel)


def filter_taps_of(filter_in, filter_out, position, length, channel_index):
    phases = position * (2.0 * math.pi / length)
    features = jnp.stack(
        [
            position / length,
            jnp.cos(phases),
            -jnp.sin(phases),
            jnp.cos(2.0 * phases),
            -jnp.sin(2.0 * phases),
        ],
        axis=1,
    )
    hidden = jnp.sin(jnp.dot(features, filter_in, precision=highest))
    taps_value = jnp.dot(hidden, filter_out, precision=highest)
    channel = channel_index.astype(jnp.float32)
    decay_rates = 0.3 * jnp.exp(math.log(1000.0) * jnp.mod(channel * golden, 1.0))
    decay_rate = jnp.exp(-(position / length)[:, None] * decay_rates[None, :])
    total = jnp.expm1(-2.0 * decay_rates) / jnp.expm1(-2.0 * decay_rates / length)
    norm_scale = lax.rsqrt(total)
    return taps_value * decay_rate * norm_scale


def block_weight(tile_stack, in_tiles, out_tiles):
    tile_side = tile_stack.shape[-1]
    tile_grid = tile_stack.reshape(4, in_tiles, out_tiles, tile_side, tile_side).transpose(
        0, 1, 3, 2, 4
    )
    return tile_grid.reshape(4, in_tiles * tile_side, out_tiles * tile_side)


def tile_split(blocks, in_tiles, out_tiles):
    tile_side = blocks.shape[1] // in_tiles
    tile_grid = blocks.reshape(4, in_tiles, tile_side, out_tiles, tile_side).transpose(
        0, 1, 3, 2, 4
    )
    return tile_grid.reshape(4 * in_tiles * out_tiles, tile_side, tile_side)


def block_apply(values, blocks):
    row_view = values.reshape(values.shape[0], 4, -1)
    return jnp.einsum("nbi,bio->nbo", row_view, blocks, preferred_element_type=jnp.float32).reshape(
        values.shape[0], -1
    )


def block_back(gradient, blocks):
    row_view = gradient.reshape(gradient.shape[0], 4, -1)
    return jnp.einsum("nbo,bio->nbi", row_view, blocks, preferred_element_type=jnp.float32).reshape(
        gradient.shape[0], -1
    )


def block_grad(values, gradient, in_tiles, out_tiles):
    left_rows = values.reshape(values.shape[0], 4, -1)
    right_rows = gradient.reshape(gradient.shape[0], 4, -1)
    blocks = jnp.einsum("nbi,nbo->bio", left_rows, right_rows, preferred_element_type=jnp.float32)
    return tile_split(blocks, in_tiles, out_tiles)


def slot_maps(owners, owner_cap, slot_total):
    tile_count = owners.shape[0]
    tile_index = jnp.arange(tile_count, dtype=jnp.int32)
    earlier = (owners[:, None] == owners[None, :]) & (tile_index[None, :] < tile_index[:, None])
    owner_rank = jnp.sum(earlier.astype(jnp.int32), axis=1)
    slot_of_tile = owners * owner_cap + owner_rank
    slot_hits = slot_of_tile[None, :] == jnp.arange(slot_total, dtype=jnp.int32)[:, None]
    tile_of_slot = jnp.sum(slot_hits.astype(jnp.int32) * tile_index[None, :], axis=1)
    slot_used = jnp.any(slot_hits, axis=1)
    return (slot_of_tile, tile_of_slot, slot_used)


def adam_step(weight, moment, second, average, gradient, step_rate, decay_rate):
    moment = beta_one * moment + (1.0 - beta_one) * gradient
    second = beta_two * second + (1.0 - beta_two) * gradient * gradient
    fixed_moment = moment / (1.0 - beta_one**STEP)
    fixed_second = second / (1.0 - beta_two**STEP)
    weight = weight - step_rate * (
        fixed_moment / (jnp.sqrt(fixed_second) + adam_eps) + decay_rate * weight
    )
    average = keep_rate * average + (1.0 - keep_rate) * weight
    return (second, weight, average)


def wave_table(period, index_one, index_two):
    turn_count = jnp.mod(index_one[:, None] * index_two[None, :], period).astype(jnp.float32)
    angles = turn_count * (2.0 * math.pi / period)
    return (jnp.cos(angles), jnp.sin(angles))


def col_dot(field_in, table_in):
    return jnp.einsum("srcd,ck->srkd", field_in, table_in, precision=highest)


def row_dot(field_in, table_in):
    return jnp.einsum("srkd,rq->sqkd", field_in, table_in, precision=highest)


def cols_forward(field_in, tables):
    col_cos, col_sin, turn_cos, turn_sin, row_cos, row_sin = tables
    real_part = col_dot(field_in, col_cos)
    imag_part = -col_dot(field_in, col_sin)
    real_turn = real_part * turn_cos + imag_part * turn_sin
    imag_turn = imag_part * turn_cos - real_part * turn_sin
    return (real_turn, imag_turn)


def rows_forward(part_real, part_imag, tables):
    row_cos, row_sin = (tables[4], tables[5])
    freq_real = row_dot(part_real, row_cos) + row_dot(part_imag, row_sin)
    freq_imag = row_dot(part_imag, row_cos) - row_dot(part_real, row_sin)
    return (freq_real, freq_imag)


def rows_inverse(prod_real, prod_imag, tables):
    row_cos, row_sin = (tables[4], tables[5])
    back_real = row_dot(prod_real, row_cos) - row_dot(prod_imag, row_sin)
    back_imag = row_dot(prod_real, row_sin) + row_dot(prod_imag, row_cos)
    return (back_real, back_imag)


def cols_inverse(rows_real, rows_imag, tables, length):
    col_cos, col_sin, turn_cos, turn_sin, row_cos, row_sin = tables
    cell_real = rows_real * turn_cos - rows_imag * turn_sin
    cell_imag = rows_real * turn_sin + rows_imag * turn_cos
    return (
        jnp.einsum("srkd,ck->srcd", cell_real, col_cos, precision=highest)
        - jnp.einsum("srkd,ck->srcd", cell_imag, col_sin, precision=highest)
    ) / length


def convolve(field_in, spectrum, tables, conjugate, length):
    spec_real, spec_imag = spectrum
    sign_flip = -1.0 if conjugate else 1.0
    real_turn, imag_turn = cols_forward(field_in, tables)
    part_real = lax.all_to_all(real_turn, "seq", split_axis=2, concat_axis=1, tiled=True)
    part_imag = lax.all_to_all(imag_turn, "seq", split_axis=2, concat_axis=1, tiled=True)
    freq_real, freq_imag = rows_forward(part_real, part_imag, tables)
    prod_real = freq_real * spec_real - sign_flip * freq_imag * spec_imag
    prod_imag = sign_flip * freq_real * spec_imag + freq_imag * spec_real
    back_real, back_imag = rows_inverse(prod_real, prod_imag, tables)
    rows_real = lax.all_to_all(back_real, "seq", split_axis=1, concat_axis=2, tiled=True)
    rows_imag = lax.all_to_all(back_imag, "seq", split_axis=1, concat_axis=2, tiled=True)
    rows_real, rows_imag, freq_real, freq_imag = (rows_real, rows_imag, freq_real, freq_imag)
    field_out = cols_inverse(rows_real, rows_imag, tables, length)
    return (field_out, freq_real, freq_imag)


def real_table(grid_rows, row_len):
    length = grid_rows * row_len
    position = (np.arange(grid_rows)[:, None] + grid_rows * np.arange(row_len)[None, :]).reshape(-1)
    turns = np.mod(np.arange(length // 2)[:, None] * position[None, :], length)
    angles = turns * (2.0 * np.pi / length)
    sines = -np.sin(angles)
    sines[0] = np.cos(np.pi * position)
    return np.concatenate([np.cos(angles), sines]).astype(ml_dtypes.bfloat16)


def on_device_general(
    tokens,
    cotangent,
    owners,
    tile_master,
    tile_moment,
    tile_second,
    tile_average,
    vectors,
    vector_moment,
    vector_second,
    vector_average,
    filter_in,
    in_moment,
    in_second,
    in_average,
    filter_out,
    out_moment,
    out_second,
    out_average,
):
    seq_count, dev_rows, row_len, model_width = tokens.shape
    owner_cap = tile_master.shape[0]
    seq_devices = lax.axis_size("seq")
    grid_rows = dev_rows * seq_devices
    length = grid_rows * row_len
    seq_index = lax.axis_index("seq")
    hidden_ratio = FF // D
    quarter_hidden = FF // 4
    slot_of_tile, tile_of_slot, slot_used = slot_maps(owners, owner_cap, owner_cap * seq_devices)
    gathered = lax.all_gather(tile_master.astype(jnp.bfloat16), "seq", axis=0, tiled=True)
    weights = jnp.take(gathered, slot_of_tile, axis=0)
    w_in = block_weight(weights[0:12], 1, 3)
    w_out = block_weight(weights[12:16], 1, 1)
    w_gate = block_weight(weights[16 : 16 + 4 * hidden_ratio], 1, hidden_ratio)
    w_up = block_weight(weights[16 + 4 * hidden_ratio : 16 + 8 * hidden_ratio], 1, hidden_ratio)
    w_down = block_weight(weights[16 + 8 * hidden_ratio : 16 + 12 * hidden_ratio], hidden_ratio, 1)
    w_gate_up = jnp.concatenate([w_gate, w_up], axis=2)
    col_index = jnp.arange(row_len, dtype=jnp.int32)
    row_index = jnp.arange(grid_rows, dtype=jnp.int32)
    local_rows = seq_index * dev_rows + jnp.arange(dev_rows, dtype=jnp.int32)
    col_cos, col_sin = wave_table(row_len, col_index, col_index)
    row_cos, row_sin = wave_table(grid_rows, row_index, row_index)
    turn_cos, turn_sin = wave_table(length, local_rows, col_index)
    tables = (
        col_cos,
        col_sin,
        turn_cos[None, :, :, None],
        turn_sin[None, :, :, None],
        row_cos,
        row_sin,
    )
    own_position = (
        (local_rows[:, None] + grid_rows * col_index[None, :]).reshape(-1).astype(jnp.float32)
    )
    flat_tokens = tokens.reshape(-1, model_width)
    qkv_all = block_apply(flat_tokens, w_in)
    query_part = qkv_all[:, :model_width]
    key_part = qkv_all[:, model_width : 2 * model_width]
    value_part = qkv_all[:, 2 * model_width :]
    kv_product = key_part * value_part

    def own_taps(weight_one, weight_two):
        return filter_taps(weight_one, weight_two, own_position, length)

    taps_own, filter_pull = jax.vjp(own_taps, filter_in, filter_out)
    taps_real, taps_imag = cols_forward(taps_own.reshape(1, dev_rows, row_len, model_width), tables)
    taps_real, taps_imag = (
        lax.all_to_all(taps_real, "seq", split_axis=2, concat_axis=1, tiled=True),
        lax.all_to_all(taps_imag, "seq", split_axis=2, concat_axis=1, tiled=True),
    )
    spec_real, spec_imag = rows_forward(taps_real, taps_imag, tables)
    taps_spec = (spec_real[0], spec_imag[0])
    conv_out, kv_real, kv_imag = convolve(
        kv_product.reshape(seq_count, dev_rows, row_len, model_width),
        taps_spec,
        tables,
        False,
        length,
    )
    skip_gain = vectors[4]
    inner_sum = conv_out.reshape(-1, model_width) + skip_gain * kv_product
    gated_out = (query_part * inner_sum).astype(jnp.bfloat16)
    branch = block_apply(gated_out, w_out)
    normed, first_pull = jax.vjp(
        norm_rows, flat_tokens.astype(jnp.float32) + branch, vectors[0], vectors[1]
    )
    normed_low = normed.astype(jnp.bfloat16)
    gate_up = block_apply(normed_low, w_gate_up).reshape(-1, 4, 2, quarter_hidden)
    gate_value = gate_up[:, :, 0].reshape(-1, FF)
    up_value = gate_up[:, :, 1].reshape(-1, FF)
    active, active_pull = jax.vjp(glu_act, gate_value, up_value)
    active_low = active.astype(jnp.bfloat16)
    down_value = block_apply(active_low, w_down)
    result, second_pull = jax.vjp(
        norm_rows, normed_low.astype(jnp.float32) + down_value, vectors[2], vectors[3]
    )
    output = result.astype(jnp.bfloat16).reshape(tokens.shape)
    d_second, d_gain_two, d_bias_two = second_pull(
        cotangent.reshape(-1, model_width).astype(jnp.float32)
    )
    d_down = d_second.astype(jnp.bfloat16)
    g_down = block_grad(active_low, d_down, hidden_ratio, 1)
    d_gate, d_up = active_pull(block_back(d_down, w_down))
    d_gate_up = jnp.stack(
        [d_gate.reshape(-1, 4, quarter_hidden), d_up.reshape(-1, 4, quarter_hidden)], axis=2
    )
    d_gate_up = d_gate_up.reshape(-1, 2 * FF).astype(jnp.bfloat16)
    gate_up_tiles = block_grad(normed_low, d_gate_up, 1, 2 * hidden_ratio).reshape(
        4, 2, hidden_ratio, weights.shape[1], weights.shape[2]
    )
    g_gate = gate_up_tiles[:, 0].reshape(-1, weights.shape[1], weights.shape[2])
    g_up = gate_up_tiles[:, 1].reshape(-1, weights.shape[1], weights.shape[2])
    d_normed = d_second + block_back(d_gate_up, w_gate_up)
    d_first, d_gain_one, d_bias_one = first_pull(d_normed)
    d_branch = d_first.astype(jnp.bfloat16)
    g_out = block_grad(gated_out, d_branch, 1, 1)
    d_gated = block_back(d_branch, w_out)
    d_query = d_gated * inner_sum
    d_inner = d_gated * query_part
    d_skip = jnp.sum(d_inner * kv_product, axis=0)
    d_conv, back_real, back_imag = convolve(
        d_inner.reshape(seq_count, dev_rows, row_len, model_width), taps_spec, tables, True, length
    )
    d_kv = d_conv.reshape(-1, model_width) + skip_gain * d_inner
    d_qkv = jnp.concatenate([d_query, d_kv * value_part, d_kv * key_part], axis=1).astype(
        jnp.bfloat16
    )
    g_in = block_grad(flat_tokens, d_qkv, 1, 3)
    in_grad = (d_first + block_back(d_qkv, w_in)).reshape(tokens.shape)
    cross_real = jnp.sum(back_real * kv_real + back_imag * kv_imag, axis=0, keepdims=True)
    cross_imag = jnp.sum(back_imag * kv_real - back_real * kv_imag, axis=0, keepdims=True)
    cross_back_real, cross_back_imag = rows_inverse(cross_real, cross_imag, tables)
    cross_rows_real, cross_rows_imag = (
        lax.all_to_all(
            cross_back_real.astype(jnp.bfloat16), "seq", split_axis=1, concat_axis=2, tiled=True
        ).astype(cross_back_real.dtype),
        lax.all_to_all(
            cross_back_imag.astype(jnp.bfloat16), "seq", split_axis=1, concat_axis=2, tiled=True
        ).astype(cross_back_imag.dtype),
    )
    d_taps = cols_inverse(cross_rows_real, cross_rows_imag, tables, length).reshape(-1, model_width)
    g_filter_in, g_filter_out = filter_pull(d_taps)
    tile_grads = jnp.concatenate([g_in, g_out, g_gate, g_up, g_down], axis=0)
    slot_mask = slot_used.astype(jnp.float32)[:, None, None]
    summed = lax.psum(tile_grads.astype(jnp.bfloat16), "dp").astype(jnp.float32)
    owned = lax.psum_scatter(
        jnp.take(summed, tile_of_slot, axis=0) * slot_mask, "seq", scatter_dimension=0, tiled=True
    )
    tokens_all = seq_count * dev_rows * row_len * lax.axis_size("dp") * seq_devices
    grad_scale = 1.0 / math.sqrt(tokens_all)
    mine_mask = lax.dynamic_slice_in_dim(slot_mask, seq_index * owner_cap, owner_cap, 0)
    tile_grad = owned * grad_scale
    tile_new = adam_step(tile_master, tile_moment, tile_second, tile_average, tile_grad, 0.1, 0.01)
    vector_part = jnp.stack([d_gain_one, d_bias_one, d_gain_two, d_bias_two, d_skip])
    vector_sum, in_sum, out_sum = lax.psum((vector_part, g_filter_in, g_filter_out), ("dp", "seq"))
    vector_grad = vector_sum * grad_scale
    in_grad_filter = in_sum * grad_scale
    out_grad_filter = out_sum * grad_scale
    vector_new = adam_step(
        vectors, vector_moment, vector_second, vector_average, vector_grad, 0.4, 0.0
    )
    in_new = adam_step(filter_in, in_moment, in_second, in_average, in_grad_filter, 0.4, 0.01)
    out_new = adam_step(filter_out, out_moment, out_second, out_average, out_grad_filter, 0.1, 0.01)
    return (
        output,
        in_grad,
        tile_grad,
        tile_new[0] * mine_mask,
        tile_new[1] * mine_mask,
        tile_new[2] * mine_mask,
        vector_grad,
        vector_new[0],
        vector_new[1],
        vector_new[2],
        in_grad_filter,
        in_new[0],
        in_new[1],
        in_new[2],
        out_grad_filter,
        out_new[0],
        out_new[1],
        out_new[2],
    )


MESH = pl.DeviceIdType.MESH
VMEM_LIMIT = 56 * 2**20


class Links:
    def __init__(self, send_sem, recv_sem):
        self.send_sem, self.recv_sem, self.used = send_sem, recv_sem, 0
        self.dp, self.seq = lax.axis_index("dp"), lax.axis_index("seq")
        self.deep = lax.axis_size("seq") // 2
        self.z, self.core = lax.div(self.seq, 2), lax.rem(self.seq, 2)
        self.partner = (self.dp, self.seq + 1 - 2 * self.core)
        low, high = lax.rem(self.dp, 2), lax.div(self.dp, 2)
        across_x = self.dp + 1 - 2 * low
        across_y = self.dp + 2 - 4 * high
        self.near = across_x + self.core * (across_y - across_x)
        self.far = across_y + self.core * (across_x - across_y)
        self.diagonal = 3 - self.dp
        self.to_near, self.to_far = (self.near, self.seq), (self.far, self.seq)
        self.to_left, self.to_right = (self.dp, self.seq - 2), (self.dp, self.seq + 2)
        self.has_left, self.has_right = self.z > 0, self.z < self.deep - 1

    def meet(self):
        barrier = pltpu.get_barrier_semaphore()
        for peer in (self.partner, self.to_near, self.to_far):
            pl.semaphore_signal(barrier, inc=1, device_id=peer, device_id_type=MESH)

        @pl.when(self.has_left)
        def _():
            pl.semaphore_signal(barrier, inc=1, device_id=self.to_left, device_id_type=MESH)

        @pl.when(self.has_right)
        def _():
            pl.semaphore_signal(barrier, inc=1, device_id=self.to_right, device_id_type=MESH)

        ends = jnp.where(self.has_left, 1, 0) + jnp.where(self.has_right, 1, 0)
        pl.semaphore_wait(barrier, 3 + ends)

    def copy(self, source, target, device):
        at = self.used
        self.used += 1
        return pltpu.make_async_remote_copy(
            src_ref=source,
            dst_ref=target,
            send_sem=self.send_sem.at[at],
            recv_sem=self.recv_sem.at[at],
            device_id=device,
            device_id_type=MESH,
        )


def chain_copies(links, buffers, lanes):
    left_in, right_in, left_out, right_out = buffers
    rightward = links.copy(right_out.at[:, lanes], left_in.at[:, lanes], links.to_right)
    leftward = links.copy(left_out.at[:, lanes], right_in.at[:, lanes], links.to_left)
    return (rightward, leftward)


def chain_step(links, buffers, copies, lanes, base):
    left_in, right_in, left_out, right_out = buffers
    rightward, leftward = copies

    @pl.when(links.has_left)
    def _():
        rightward.wait_recv()

    @pl.when(jnp.logical_not(links.has_left))
    def _():
        left_in[:, lanes] = jnp.zeros(base.shape, left_in.dtype)

    from_left = left_in[:, lanes].astype(jnp.float32)

    @pl.when(links.has_right)
    def _():
        right_out[:, lanes] = (base + from_left).astype(right_out.dtype)
        rightward.start()
        leftward.wait_recv()

    @pl.when(jnp.logical_not(links.has_right))
    def _():
        right_in[:, lanes] = jnp.zeros(base.shape, right_in.dtype)

    from_right = right_in[:, lanes].astype(jnp.float32)

    @pl.when(links.has_left)
    def _():
        left_out[:, lanes] = (base + from_right).astype(left_out.dtype)
        leftward.start()

    return base + from_left + from_right


def chain_end(links, copies):
    rightward, leftward = copies

    @pl.when(links.has_right)
    def _():
        rightward.wait_send()

    @pl.when(links.has_left)
    def _():
        leftward.wait_send()


def half_tiles(half):
    order = []
    for first, per_block in ((0, 3), (12, 1), (16, 4), (32, 4), (48, 4)):
        order += range(first + 2 * half * per_block, first + 2 * (half + 1) * per_block)
    return order


def gather_kernel(
    chunks, owners, master, full, own, got, left_in, right_in, left_out, right_out, send_sem, recv_sem
):
    links = Links(send_sem, recv_sem)
    quarter = full.shape[1] // 4
    tile_count, side = owners.shape[0], master.shape[2]
    most = master.shape[0] - 1
    rows = pl.ds(pl.multiple_of(links.dp * quarter, quarter), quarter)
    rank, place = jnp.int32(0), []
    for i in range(tile_count):
        mine = owners[i] == links.seq
        place.append((jnp.minimum(rank, most), mine))
        rank = rank + jnp.where(mine, 1, 0)
    for half in range(2):
        order = half_tiles(half)
        for j in range(0, len(order), 2):
            pair = []
            for i in order[j : j + 2]:
                at, mine = place[i]
                pair.append(jnp.where(mine, master[at, rows, :], 0.0))
            own[half, :, j * side : (j + 2) * side] = jnp.concatenate(pair, axis=1).astype(own.dtype)
    links.meet()
    buffers = (left_in, right_in, left_out, right_out)
    swaps = [
        links.copy(own.at[1 - links.core, :, lanes], got.at[:, lanes], links.partner)
        for lanes in chunks
    ]
    for swap in swaps:
        swap.start()
    chains = [chain_copies(links, buffers, lanes) for lanes in chunks]
    planes = []
    for swap, chain, lanes in zip(swaps, chains, chunks):
        swap.wait()
        base = own[links.core, :, lanes].astype(jnp.float32) + got[:, lanes].astype(jnp.float32)
        total = chain_step(links, buffers, chain, lanes, base)
        full[links.core, rows, lanes] = total.astype(full.dtype)
        mine = full.at[links.core, rows, lanes]
        other = full.at[
            links.core, pl.ds(pl.multiple_of(links.near * quarter, quarter), quarter), lanes
        ]
        first = links.copy(mine, mine, links.to_near)
        second = links.copy(mine, mine, links.to_far)
        relay = links.copy(other, other, links.to_far)
        share = links.copy(
            full.at[links.core, :, lanes], full.at[links.core, :, lanes], links.partner
        )
        first.start()
        second.start()
        planes.append((first, second, relay, share))
    for first, second, relay, share in planes:
        first.wait_recv()
        relay.start()
    for first, second, relay, share in planes:
        second.wait_recv()
        relay.wait_recv()
        share.start()
    for chain, (first, second, relay, share) in zip(chains, planes):
        chain_end(links, chain)
        first.wait_send()
        second.wait_send()
        relay.wait_send()
        share.wait()


def gather_weights(owners, master):
    slots, side, _ = master.shape
    width = owners.shape[0] // 2 * side
    step = side * 2
    chunks = (pl.ds(0, 3 * step), pl.ds(3 * step, 5 * step), pl.ds(8 * step, 8 * step))
    low = jnp.bfloat16
    part = pltpu.VMEM((side // 4, width), low)
    count = 7 * len(chunks)
    return pl.pallas_call(
        functools.partial(gather_kernel, chunks),
        out_shape=jax.ShapeDtypeStruct((2, side, width), low),
        in_specs=[
            pl.BlockSpec(memory_space=pltpu.SMEM),
            pl.BlockSpec(memory_space=pltpu.VMEM),
        ],
        out_specs=pl.BlockSpec(memory_space=pltpu.VMEM),
        scratch_shapes=[
            pltpu.VMEM((2, side // 4, width), low),
            part,
            part,
            part,
            part,
            part,
            pltpu.SemaphoreType.DMA((count,)),
            pltpu.SemaphoreType.DMA((count,)),
        ],
        compiler_params=pltpu.CompilerParams(
            collective_id=0, has_side_effects=True, vmem_limit_bytes=VMEM_LIMIT
        ),
        name="gather_weights",
    )(owners, master)


def reduce_kernel(
    chunks,
    tile_of_slot,
    used,
    grads,
    spread,
    mine_sum,
    got,
    near_in,
    far_in,
    far_out,
    left_in,
    right_in,
    left_out,
    right_out,
    total,
    by_tile,
    send_sem,
    recv_sem,
):
    links = Links(send_sem, recv_sem)
    side = grads.shape[1]
    quarter = side // 4
    wide = jnp.float32

    def rows_of(index):
        return pl.ds(pl.multiple_of(index * quarter, quarter), quarter)

    links.meet()
    buffers = (left_in, right_in, left_out, right_out)
    swaps = [
        links.copy(grads.at[1 - links.core, :, lanes], got.at[:, lanes], links.partner)
        for lanes in chunks
    ]
    nears = [
        (
            links.copy(mine_sum.at[rows_of(links.near), lanes], near_in.at[0, :, lanes], links.to_near),
            links.copy(
                mine_sum.at[rows_of(links.diagonal), lanes], near_in.at[1, :, lanes], links.to_near
            ),
        )
        for lanes in chunks
    ]
    fars = [links.copy(far_out.at[:, lanes], far_in.at[:, lanes], links.to_far) for lanes in chunks]
    chains = [chain_copies(links, buffers, lanes) for lanes in chunks]
    for swap in swaps:
        swap.start()
    for swap, near, lanes in zip(swaps, nears, chunks):
        swap.wait()
        mine_sum[:, lanes] = (
            grads[links.core, :, lanes].astype(wide) + got[:, lanes].astype(wide)
        ).astype(mine_sum.dtype)
        near[1].start()
        near[0].start()
    for near, far, lanes in zip(nears, fars, chunks):
        near[1].wait_recv()
        far_out[:, lanes] = (
            mine_sum[rows_of(links.far), lanes].astype(wide) + near_in[1, :, lanes].astype(wide)
        ).astype(far_out.dtype)
        far.start()
    shares = []
    for near, far, chain, lanes in zip(nears, fars, chains, chunks):
        near[0].wait_recv()
        far.wait_recv()
        base = (
            mine_sum[rows_of(links.dp), lanes].astype(wide)
            + near_in[0, :, lanes].astype(wide)
            + far_in[:, lanes].astype(wide)
        )
        total[links.core, :, lanes] = chain_step(links, buffers, chain, lanes, base).astype(
            total.dtype
        )
        part = total.at[links.core, :, lanes]
        share = links.copy(part, part, links.partner)
        share.start()
        shares.append(share)
    for share in shares:
        share.wait()
    for half in range(2):
        for j, i in enumerate(half_tiles(half)):
            by_tile[i] = total[half, :, j * side : (j + 1) * side].astype(wide)
    slots = tile_of_slot.shape[0]
    tiles_wide = slots * side
    at_home = spread.at[rows_of(links.dp), :]
    for s in range(0, slots, 2):
        pair = [
            jnp.where(used[k] > 0, by_tile[tile_of_slot[k]], 0.0) for k in (s, s + 1)
        ]
        spread[rows_of(links.dp), s * side : (s + 2) * side] = jnp.concatenate(pair, axis=1).astype(
            spread.dtype
        )
    first_extra = by_tile.shape[0] // 2 * side
    extra = total.shape[2] - first_extra
    for half in range(2):
        begin = tiles_wide + half * extra
        spread[rows_of(links.dp), begin : begin + extra] = total[half, :, first_extra:]
    other = spread.at[rows_of(links.near), :]
    first = links.copy(at_home, at_home, links.to_near)
    second = links.copy(at_home, at_home, links.to_far)
    relay = links.copy(other, other, links.to_far)
    first.start()
    second.start()
    first.wait_recv()
    relay.start()
    second.wait_recv()
    relay.wait()
    first.wait_send()
    second.wait_send()
    for near, far, chain in zip(nears, fars, chains):
        near[0].wait_send()
        near[1].wait_send()
        far.wait_send()
        chain_end(links, chain)


def reduce_grads(tile_of_slot, used, grads):
    _, side, width = grads.shape
    slots = tile_of_slot.shape[0]
    tile_count = NTILES
    extra = width - tile_count // 2 * side
    step = side * 2
    cuts = (0, 6 * step, 11 * step, width)
    chunks = tuple(pl.ds(a, b - a) for a, b in zip(cuts[:-1], cuts[1:]))
    low = jnp.bfloat16
    quarter = side // 4
    part = pltpu.VMEM((quarter, width), low)
    count = 7 * len(chunks) + 3
    return pl.pallas_call(
        functools.partial(reduce_kernel, chunks),
        out_shape=jax.ShapeDtypeStruct((side, slots * side + 2 * extra), low),
        in_specs=[
            pl.BlockSpec(memory_space=pltpu.SMEM),
            pl.BlockSpec(memory_space=pltpu.SMEM),
            pl.BlockSpec(memory_space=pltpu.VMEM),
        ],
        out_specs=pl.BlockSpec(memory_space=pltpu.VMEM),
        scratch_shapes=[
            pltpu.VMEM((side, width), low),
            pltpu.VMEM((side, width), low),
            pltpu.VMEM((2, quarter, width), low),
            part,
            part,
            part,
            part,
            part,
            part,
            pltpu.VMEM((2, quarter, width), low),
            pltpu.VMEM((tile_count, quarter, side), jnp.float32),
            pltpu.SemaphoreType.DMA((count,)),
            pltpu.SemaphoreType.DMA((count,)),
        ],
        compiler_params=pltpu.CompilerParams(
            collective_id=1, has_side_effects=True, vmem_limit_bytes=VMEM_LIMIT
        ),
        name="reduce_grads",
    )(tile_of_slot, used, grads)


def on_device_columns(
    tokens,
    cotangent,
    owners,
    tile_master,
    tile_moment,
    tile_second,
    tile_average,
    vectors,
    vector_moment,
    vector_second,
    vector_average,
    filter_in,
    in_moment,
    in_second,
    in_average,
    filter_out,
    out_moment,
    out_second,
    out_average,
):
    seq_count, dev_rows, row_len, model_width = tokens.shape
    owner_cap = tile_master.shape[0]
    seq_devices = lax.axis_size("seq")
    grid_rows = dev_rows * seq_devices
    length = grid_rows * row_len
    seq_index = lax.axis_index("seq")
    hidden_ratio = FF // D
    quarter_hidden = FF // 4
    slot_of_tile, tile_of_slot, slot_used = slot_maps(owners, owner_cap, owner_cap * seq_devices)
    packed = gather_weights(owners, tile_master)
    side = tile_master.shape[1]
    lanes = 2 * side

    def blocks_of(first, per_block):
        part = packed[:, :, first * lanes : (first + per_block) * lanes]
        part = part.reshape(2, side, 2, per_block * side).transpose(0, 2, 1, 3)
        return part.reshape(4, side, per_block * side)

    w_in, w_out = blocks_of(0, 3), blocks_of(3, 1)
    w_gate_up = jnp.concatenate([blocks_of(4, 4), blocks_of(8, 4)], axis=2)
    w_down = blocks_of(12, 4).reshape(4, side, 4, side).transpose(0, 2, 1, 3)
    w_down = w_down.reshape(4, 4 * side, side)
    halves = seq_devices // seq_count
    width = model_width // halves
    half_index = lax.rem(seq_index, halves)
    grid_position = (
        jnp.arange(grid_rows, dtype=jnp.int32)[:, None]
        + grid_rows * jnp.arange(row_len, dtype=jnp.int32)[None, :]
    )
    position = grid_position.reshape(-1).astype(jnp.float32)
    table = jnp.asarray(real_table(grid_rows, row_len))
    first_bin = (jnp.arange(length // 2) == 0)[:, None]

    def spread(field_in):
        cells = field_in.reshape(seq_count, row_len, halves, width).transpose(0, 2, 1, 3)
        cells = cells.reshape(seq_devices, row_len, width).astype(jnp.bfloat16)
        return lax.all_to_all(cells, "seq", 0, 0, tiled=True).reshape(length, width)

    def collect(field_in):
        cells = field_in.astype(jnp.bfloat16).reshape(seq_devices, row_len, width)
        cells = lax.all_to_all(cells, "seq", 0, 0, tiled=True)
        cells = cells.reshape(seq_count, halves, row_len, width).transpose(0, 2, 1, 3)
        return cells.reshape(-1, model_width).astype(jnp.float32)

    def transform(columns):
        spec = jnp.dot(table, columns.astype(jnp.bfloat16), preferred_element_type=jnp.float32)
        return (spec[: length // 2], spec[length // 2 :])

    def invert(real_part, imag_part):
        weight = jnp.where(first_bin, 1.0 / length, 2.0 / length)
        spec = jnp.concatenate([real_part * weight, imag_part * weight], axis=0)
        return lax.dot_general(
            table,
            spec.astype(jnp.bfloat16),
            (((0,), (0,)), ((), ())),
            preferred_element_type=jnp.float32,
        )

    def product(one, two, conjugate):
        one_real, one_imag = one
        two_real, two_imag = two
        cross = jnp.where(first_bin, 0.0, two_imag) * (-1.0 if conjugate else 1.0)
        diag = jnp.where(first_bin, two_imag, two_real)
        return (one_real * two_real - one_imag * cross, one_real * cross + one_imag * diag)

    flat_tokens = tokens.reshape(-1, model_width)
    qkv_all = block_apply(flat_tokens, w_in)
    query_part = qkv_all[:, :model_width]
    key_part = qkv_all[:, model_width : 2 * model_width]
    value_part = qkv_all[:, 2 * model_width :]
    kv_product = key_part * value_part

    channel = half_index * width + jnp.arange(width, dtype=jnp.int32)
    own_filter = lax.dynamic_slice_in_dim(filter_out, half_index * width, width, 1)

    def own_taps(weight_one, weight_two):
        return filter_taps_of(weight_one, weight_two, position, length, channel)

    taps_own, filter_pull = jax.vjp(own_taps, filter_in, own_filter)
    taps_spec = transform(taps_own)
    kv_spec = transform(spread(kv_product))
    conv_out = collect(invert(*product(kv_spec, taps_spec, False)))
    skip_gain = vectors[4]
    inner_sum = conv_out + skip_gain * kv_product
    gated_out = (query_part * inner_sum).astype(jnp.bfloat16)
    branch = block_apply(gated_out, w_out)
    normed, first_pull = jax.vjp(
        norm_rows, flat_tokens.astype(jnp.float32) + branch, vectors[0], vectors[1]
    )
    normed_low = normed.astype(jnp.bfloat16)
    gate_up = block_apply(normed_low, w_gate_up).reshape(-1, 4, 2, quarter_hidden)
    gate_value = gate_up[:, :, 0].reshape(-1, FF)
    up_value = gate_up[:, :, 1].reshape(-1, FF)
    active, active_pull = jax.vjp(glu_act, gate_value, up_value)
    active_low = active.astype(jnp.bfloat16)
    down_value = block_apply(active_low, w_down)
    result, second_pull = jax.vjp(
        norm_rows, normed_low.astype(jnp.float32) + down_value, vectors[2], vectors[3]
    )
    output = result.astype(jnp.bfloat16).reshape(tokens.shape)
    d_second, d_gain_two, d_bias_two = second_pull(
        cotangent.reshape(-1, model_width).astype(jnp.float32)
    )
    d_down = d_second.astype(jnp.bfloat16)
    g_down = block_grad(active_low, d_down, hidden_ratio, 1)
    d_gate, d_up = active_pull(block_back(d_down, w_down))
    d_gate_up = jnp.stack(
        [d_gate.reshape(-1, 4, quarter_hidden), d_up.reshape(-1, 4, quarter_hidden)], axis=2
    )
    d_gate_up = d_gate_up.reshape(-1, 2 * FF).astype(jnp.bfloat16)
    gate_up_tiles = block_grad(normed_low, d_gate_up, 1, 2 * hidden_ratio).reshape(
        4, 2, hidden_ratio, side, side
    )
    g_gate = gate_up_tiles[:, 0].reshape(-1, side, side)
    g_up = gate_up_tiles[:, 1].reshape(-1, side, side)
    d_normed = d_second + block_back(d_gate_up, w_gate_up)
    d_first, d_gain_one, d_bias_one = first_pull(d_normed)
    d_branch = d_first.astype(jnp.bfloat16)
    g_out = block_grad(gated_out, d_branch, 1, 1)
    d_gated = block_back(d_branch, w_out)
    d_query = d_gated * inner_sum
    d_inner = d_gated * query_part
    d_skip = jnp.sum(d_inner * kv_product, axis=0)
    back_spec = transform(spread(d_inner))
    d_kv = collect(invert(*product(back_spec, taps_spec, True))) + skip_gain * d_inner
    d_qkv = jnp.concatenate([d_query, d_kv * value_part, d_kv * key_part], axis=1).astype(
        jnp.bfloat16
    )
    g_in = block_grad(flat_tokens, d_qkv, 1, 3)
    in_grad = (d_first + block_back(d_qkv, w_in)).reshape(tokens.shape)
    d_taps = invert(*product(back_spec, kv_spec, True))
    g_filter_in, g_filter_half = filter_pull(d_taps)
    def pack(tiles):
        per_half = tiles.shape[0] // 2
        return tiles.reshape(2, per_half, side, side).transpose(0, 2, 1, 3).reshape(2, side, -1)

    slot_mask = slot_used.astype(jnp.float32)[:, None, None]
    first_slot = seq_index * owner_cap
    vector_part = jnp.stack([d_gain_one, d_bias_one, d_gain_two, d_bias_two, d_skip])
    order = filter_in.shape[1]
    both = jnp.zeros((2, side, width), jnp.float32)
    both = lax.dynamic_update_slice(both, g_filter_half[None], (half_index, 0, 0))
    both = lax.dynamic_update_slice(
        both, vector_part.reshape(5, 2, width).transpose(1, 0, 2), (0, order, 0)
    )
    both = lax.dynamic_update_slice(both, g_filter_in[None], (0, order + 8, 0))
    packed_grads = jnp.concatenate(
        [pack(g).astype(jnp.bfloat16) for g in (g_in, g_out, g_gate, g_up, g_down, )]
        + [both.astype(jnp.bfloat16)],
        axis=2,
    )
    own_tile = lax.dynamic_slice_in_dim(tile_of_slot, first_slot, owner_cap, 0)
    own_used = lax.dynamic_slice_in_dim(slot_used.astype(jnp.int32), first_slot, owner_cap, 0)
    reduced = reduce_grads(own_tile, own_used, packed_grads).astype(jnp.float32)
    owned = reduced[:, : owner_cap * side].reshape(side, owner_cap, side).transpose(1, 0, 2)
    extra = reduced[:, owner_cap * side :].reshape(side, 2, width).transpose(1, 0, 2)
    out_sum = extra[:, :order].transpose(1, 0, 2).reshape(order, model_width)
    vector_sum = extra[:, order : order + 5].transpose(1, 0, 2).reshape(5, model_width)
    in_sum = extra[0, order + 8 : order + 13, :order]
    tokens_all = seq_count * dev_rows * row_len * lax.axis_size("dp") * seq_devices
    grad_scale = 1.0 / math.sqrt(tokens_all)
    mine_mask = lax.dynamic_slice_in_dim(slot_mask, seq_index * owner_cap, owner_cap, 0)
    tile_grad = owned * grad_scale
    tile_new = adam_step(tile_master, tile_moment, tile_second, tile_average, tile_grad, 0.1, 0.01)
    vector_grad = vector_sum * grad_scale
    in_grad_filter = in_sum * grad_scale
    out_grad_filter = out_sum * grad_scale
    vector_new = adam_step(
        vectors, vector_moment, vector_second, vector_average, vector_grad, 0.4, 0.0
    )
    in_new = adam_step(filter_in, in_moment, in_second, in_average, in_grad_filter, 0.4, 0.01)
    out_new = adam_step(filter_out, out_moment, out_second, out_average, out_grad_filter, 0.1, 0.01)
    return (
        output,
        in_grad,
        tile_grad,
        tile_new[0] * mine_mask,
        tile_new[1] * mine_mask,
        tile_new[2] * mine_mask,
        vector_grad,
        vector_new[0],
        vector_new[1],
        vector_new[2],
        in_grad_filter,
        in_new[0],
        in_new[1],
        in_new[2],
        out_grad_filter,
        out_new[0],
        out_new[1],
        out_new[2],
    )


def on_device(*arrays):
    seq_count, dev_rows, row_len, model_width = arrays[0].shape
    seq_devices = lax.axis_size("seq")
    fits = dev_rows == 1 and seq_devices % seq_count == 0 and seq_devices * row_len <= 2048
    fits = fits and lax.axis_size("dp") == 4 and seq_devices == 2 * seq_count == 8
    if fits and model_width % (128 * (seq_devices // seq_count)) == 0:
        return on_device_columns(*arrays)
    return on_device_general(*arrays)


def solution(mesh):
    in_specs = (
        P("dp", "seq", None, None),
        P("dp", "seq", None, None),
        P(),
        P("seq", None, None),
        P("seq", None, None),
        P("seq", None, None),
        P("seq", None, None),
        P(),
        P(),
        P(),
        P(),
        P(),
        P(),
        P(),
        P(),
        P(),
        P(),
        P(),
        P(),
    )
    out_specs = (
        P("dp", "seq", None, None),
        P("dp", "seq", None, None),
        P("seq", None, None),
        P("seq", None, None),
        P("seq", None, None),
        P("seq", None, None),
        P(),
        P(),
        P(),
        P(),
        P(),
        P(),
        P(),
        P(),
        P(),
        P(),
        P(),
        P(),
    )
    return jax.shard_map(
        on_device, mesh=mesh, in_specs=in_specs, out_specs=out_specs, check_vma=False
    )
```

```python
import functools
import math

import jax
import jax.numpy as jnp
import ml_dtypes
import numpy as np
from jax import lax
from jax.experimental import pallas as pl
from jax.experimental.pallas import tpu as pltpu
from jax.sharding import PartitionSpec as P

D = 768
FF = 3072
STEP = 10
NTILES = 64


highest = lax.Precision.HIGHEST
beta_one = 0.9
beta_two = 0.999
keep_rate = 0.5
adam_eps = 1e-08
norm_eps = 1e-05
golden = 0.6180339887


def norm_rows(values, gain_vec, bias_vec):
    row_mean = jnp.mean(values, axis=-1, keepdims=True)
    centered = values - row_mean
    spread = jnp.mean(centered * centered, axis=-1, keepdims=True)
    return centered * lax.rsqrt(spread + norm_eps) * gain_vec + bias_vec


def glu_act(gate_value, up_value):
    return jax.nn.gelu(gate_value, approximate=False) * up_value


def filter_taps(filter_in, filter_out, position, length):
    channel = jnp.arange(filter_out.shape[1], dtype=jnp.int32)
    return filter_taps_of(filter_in, filter_out, position, length, channel)


def filter_taps_of(filter_in, filter_out, position, length, channel_index):
    phases = position * (2.0 * math.pi / length)
    features = jnp.stack(
        [
            position / length,
            jnp.cos(phases),
            -jnp.sin(phases),
            jnp.cos(2.0 * phases),
            -jnp.sin(2.0 * phases),
        ],
        axis=1,
    )
    hidden = jnp.sin(jnp.dot(features, filter_in, precision=highest))
    taps_value = jnp.dot(hidden, filter_out, precision=highest)
    channel = channel_index.astype(jnp.float32)
    decay_rates = 0.3 * jnp.exp(math.log(1000.0) * jnp.mod(channel * golden, 1.0))
    decay_rate = jnp.exp(-(position / length)[:, None] * decay_rates[None, :])
    total = jnp.expm1(-2.0 * decay_rates) / jnp.expm1(-2.0 * decay_rates / length)
    norm_scale = lax.rsqrt(total)
    return taps_value * decay_rate * norm_scale


def block_weight(tile_stack, in_tiles, out_tiles):
    tile_side = tile_stack.shape[-1]
    tile_grid = tile_stack.reshape(4, in_tiles, out_tiles, tile_side, tile_side).transpose(
        0, 1, 3, 2, 4
    )
    return tile_grid.reshape(4, in_tiles * tile_side, out_tiles * tile_side)


def tile_split(blocks, in_tiles, out_tiles):
    tile_side = blocks.shape[1] // in_tiles
    tile_grid = blocks.reshape(4, in_tiles, tile_side, out_tiles, tile_side).transpose(
        0, 1, 3, 2, 4
    )
    return tile_grid.reshape(4 * in_tiles * out_tiles, tile_side, tile_side)


def block_apply(values, blocks):
    row_view = values.reshape(values.shape[0], 4, -1)
    return jnp.einsum("nbi,bio->nbo", row_view, blocks, preferred_element_type=jnp.float32).reshape(
        values.shape[0], -1
    )


def block_back(gradient, blocks):
    row_view = gradient.reshape(gradient.shape[0], 4, -1)
    return jnp.einsum("nbo,bio->nbi", row_view, blocks, preferred_element_type=jnp.float32).reshape(
        gradient.shape[0], -1
    )


def block_grad(values, gradient, in_tiles, out_tiles):
    left_rows = values.reshape(values.shape[0], 4, -1)
    right_rows = gradient.reshape(gradient.shape[0], 4, -1)
    blocks = jnp.einsum("nbi,nbo->bio", left_rows, right_rows, preferred_element_type=jnp.float32)
    return tile_split(blocks, in_tiles, out_tiles)


def slot_maps(owners, owner_cap, slot_total):
    tile_count = owners.shape[0]
    tile_index = jnp.arange(tile_count, dtype=jnp.int32)
    earlier = (owners[:, None] == owners[None, :]) & (tile_index[None, :] < tile_index[:, None])
    owner_rank = jnp.sum(earlier.astype(jnp.int32), axis=1)
    slot_of_tile = owners * owner_cap + owner_rank
    slot_hits = slot_of_tile[None, :] == jnp.arange(slot_total, dtype=jnp.int32)[:, None]
    tile_of_slot = jnp.sum(slot_hits.astype(jnp.int32) * tile_index[None, :], axis=1)
    slot_used = jnp.any(slot_hits, axis=1)
    return (slot_of_tile, tile_of_slot, slot_used)


def adam_step(weight, moment, second, average, gradient, step_rate, decay_rate):
    moment = beta_one * moment + (1.0 - beta_one) * gradient
    second = beta_two * second + (1.0 - beta_two) * gradient * gradient
    fixed_moment = moment / (1.0 - beta_one**STEP)
    fixed_second = second / (1.0 - beta_two**STEP)
    weight = weight - step_rate * (
        fixed_moment / (jnp.sqrt(fixed_second) + adam_eps) + decay_rate * weight
    )
    average = keep_rate * average + (1.0 - keep_rate) * weight
    return (second, weight, average)


def wave_table(period, index_one, index_two):
    turn_count = jnp.mod(index_one[:, None] * index_two[None, :], period).astype(jnp.float32)
    angles = turn_count * (2.0 * math.pi / period)
    return (jnp.cos(angles), jnp.sin(angles))


def col_dot(field_in, table_in):
    return jnp.einsum("srcd,ck->srkd", field_in, table_in, precision=highest)


def row_dot(field_in, table_in):
    return jnp.einsum("srkd,rq->sqkd", field_in, table_in, precision=highest)


def cols_forward(field_in, tables):
    col_cos, col_sin, turn_cos, turn_sin, row_cos, row_sin = tables
    real_part = col_dot(field_in, col_cos)
    imag_part = -col_dot(field_in, col_sin)
    real_turn = real_part * turn_cos + imag_part * turn_sin
    imag_turn = imag_part * turn_cos - real_part * turn_sin
    return (real_turn, imag_turn)


def rows_forward(part_real, part_imag, tables):
    row_cos, row_sin = (tables[4], tables[5])
    freq_real = row_dot(part_real, row_cos) + row_dot(part_imag, row_sin)
    freq_imag = row_dot(part_imag, row_cos) - row_dot(part_real, row_sin)
    return (freq_real, freq_imag)


def rows_inverse(prod_real, prod_imag, tables):
    row_cos, row_sin = (tables[4], tables[5])
    back_real = row_dot(prod_real, row_cos) - row_dot(prod_imag, row_sin)
    back_imag = row_dot(prod_real, row_sin) + row_dot(prod_imag, row_cos)
    return (back_real, back_imag)


def cols_inverse(rows_real, rows_imag, tables, length):
    col_cos, col_sin, turn_cos, turn_sin, row_cos, row_sin = tables
    cell_real = rows_real * turn_cos - rows_imag * turn_sin
    cell_imag = rows_real * turn_sin + rows_imag * turn_cos
    return (
        jnp.einsum("srkd,ck->srcd", cell_real, col_cos, precision=highest)
        - jnp.einsum("srkd,ck->srcd", cell_imag, col_sin, precision=highest)
    ) / length


def convolve(field_in, spectrum, tables, conjugate, length):
    spec_real, spec_imag = spectrum
    sign_flip = -1.0 if conjugate else 1.0
    real_turn, imag_turn = cols_forward(field_in, tables)
    part_real = lax.all_to_all(real_turn, "seq", split_axis=2, concat_axis=1, tiled=True)
    part_imag = lax.all_to_all(imag_turn, "seq", split_axis=2, concat_axis=1, tiled=True)
    freq_real, freq_imag = rows_forward(part_real, part_imag, tables)
    prod_real = freq_real * spec_real - sign_flip * freq_imag * spec_imag
    prod_imag = sign_flip * freq_real * spec_imag + freq_imag * spec_real
    back_real, back_imag = rows_inverse(prod_real, prod_imag, tables)
    rows_real = lax.all_to_all(back_real, "seq", split_axis=1, concat_axis=2, tiled=True)
    rows_imag = lax.all_to_all(back_imag, "seq", split_axis=1, concat_axis=2, tiled=True)
    rows_real, rows_imag, freq_real, freq_imag = (rows_real, rows_imag, freq_real, freq_imag)
    field_out = cols_inverse(rows_real, rows_imag, tables, length)
    return (field_out, freq_real, freq_imag)


def real_table(grid_rows, row_len):
    length = grid_rows * row_len
    position = (np.arange(grid_rows)[:, None] + grid_rows * np.arange(row_len)[None, :]).reshape(-1)
    turns = np.mod(np.arange(length // 2)[:, None] * position[None, :], length)
    angles = turns * (2.0 * np.pi / length)
    sines = -np.sin(angles)
    sines[0] = np.cos(np.pi * position)
    return np.concatenate([np.cos(angles), sines]).astype(ml_dtypes.bfloat16)


def on_device_general(
    tokens,
    cotangent,
    owners,
    tile_master,
    tile_moment,
    tile_second,
    tile_average,
    vectors,
    vector_moment,
    vector_second,
    vector_average,
    filter_in,
    in_moment,
    in_second,
    in_average,
    filter_out,
    out_moment,
    out_second,
    out_average,
):
    seq_count, dev_rows, row_len, model_width = tokens.shape
    owner_cap = tile_master.shape[0]
    seq_devices = lax.axis_size("seq")
    grid_rows = dev_rows * seq_devices
    length = grid_rows * row_len
    seq_index = lax.axis_index("seq")
    hidden_ratio = FF // D
    quarter_hidden = FF // 4
    slot_of_tile, tile_of_slot, slot_used = slot_maps(owners, owner_cap, owner_cap * seq_devices)
    gathered = lax.all_gather(tile_master.astype(jnp.bfloat16), "seq", axis=0, tiled=True)
    weights = jnp.take(gathered, slot_of_tile, axis=0)
    w_in = block_weight(weights[0:12], 1, 3)
    w_out = block_weight(weights[12:16], 1, 1)
    w_gate = block_weight(weights[16 : 16 + 4 * hidden_ratio], 1, hidden_ratio)
    w_up = block_weight(weights[16 + 4 * hidden_ratio : 16 + 8 * hidden_ratio], 1, hidden_ratio)
    w_down = block_weight(weights[16 + 8 * hidden_ratio : 16 + 12 * hidden_ratio], hidden_ratio, 1)
    w_gate_up = jnp.concatenate([w_gate, w_up], axis=2)
    col_index = jnp.arange(row_len, dtype=jnp.int32)
    row_index = jnp.arange(grid_rows, dtype=jnp.int32)
    local_rows = seq_index * dev_rows + jnp.arange(dev_rows, dtype=jnp.int32)
    col_cos, col_sin = wave_table(row_len, col_index, col_index)
    row_cos, row_sin = wave_table(grid_rows, row_index, row_index)
    turn_cos, turn_sin = wave_table(length, local_rows, col_index)
    tables = (
        col_cos,
        col_sin,
        turn_cos[None, :, :, None],
        turn_sin[None, :, :, None],
        row_cos,
        row_sin,
    )
    own_position = (
        (local_rows[:, None] + grid_rows * col_index[None, :]).reshape(-1).astype(jnp.float32)
    )
    flat_tokens = tokens.reshape(-1, model_width)
    qkv_all = block_apply(flat_tokens, w_in)
    query_part = qkv_all[:, :model_width]
    key_part = qkv_all[:, model_width : 2 * model_width]
    value_part = qkv_all[:, 2 * model_width :]
    kv_product = key_part * value_part

    def own_taps(weight_one, weight_two):
        return filter_taps(weight_one, weight_two, own_position, length)

    taps_own, filter_pull = jax.vjp(own_taps, filter_in, filter_out)
    taps_real, taps_imag = cols_forward(taps_own.reshape(1, dev_rows, row_len, model_width), tables)
    taps_real, taps_imag = (
        lax.all_to_all(taps_real, "seq", split_axis=2, concat_axis=1, tiled=True),
        lax.all_to_all(taps_imag, "seq", split_axis=2, concat_axis=1, tiled=True),
    )
    spec_real, spec_imag = rows_forward(taps_real, taps_imag, tables)
    taps_spec = (spec_real[0], spec_imag[0])
    conv_out, kv_real, kv_imag = convolve(
        kv_product.reshape(seq_count, dev_rows, row_len, model_width),
        taps_spec,
        tables,
        False,
        length,
    )
    skip_gain = vectors[4]
    inner_sum = conv_out.reshape(-1, model_width) + skip_gain * kv_product
    gated_out = (query_part * inner_sum).astype(jnp.bfloat16)
    branch = block_apply(gated_out, w_out)
    normed, first_pull = jax.vjp(
        norm_rows, flat_tokens.astype(jnp.float32) + branch, vectors[0], vectors[1]
    )
    normed_low = normed.astype(jnp.bfloat16)
    gate_up = block_apply(normed_low, w_gate_up).reshape(-1, 4, 2, quarter_hidden)
    gate_value = gate_up[:, :, 0].reshape(-1, FF)
    up_value = gate_up[:, :, 1].reshape(-1, FF)
    active, active_pull = jax.vjp(glu_act, gate_value, up_value)
    active_low = active.astype(jnp.bfloat16)
    down_value = block_apply(active_low, w_down)
    result, second_pull = jax.vjp(
        norm_rows, normed_low.astype(jnp.float32) + down_value, vectors[2], vectors[3]
    )
    output = result.astype(jnp.bfloat16).reshape(tokens.shape)
    d_second, d_gain_two, d_bias_two = second_pull(
        cotangent.reshape(-1, model_width).astype(jnp.float32)
    )
    d_down = d_second.astype(jnp.bfloat16)
    g_down = block_grad(active_low, d_down, hidden_ratio, 1)
    d_gate, d_up = active_pull(block_back(d_down, w_down))
    d_gate_up = jnp.stack(
        [d_gate.reshape(-1, 4, quarter_hidden), d_up.reshape(-1, 4, quarter_hidden)], axis=2
    )
    d_gate_up = d_gate_up.reshape(-1, 2 * FF).astype(jnp.bfloat16)
    gate_up_tiles = block_grad(normed_low, d_gate_up, 1, 2 * hidden_ratio).reshape(
        4, 2, hidden_ratio, weights.shape[1], weights.shape[2]
    )
    g_gate = gate_up_tiles[:, 0].reshape(-1, weights.shape[1], weights.shape[2])
    g_up = gate_up_tiles[:, 1].reshape(-1, weights.shape[1], weights.shape[2])
    d_normed = d_second + block_back(d_gate_up, w_gate_up)
    d_first, d_gain_one, d_bias_one = first_pull(d_normed)
    d_branch = d_first.astype(jnp.bfloat16)
    g_out = block_grad(gated_out, d_branch, 1, 1)
    d_gated = block_back(d_branch, w_out)
    d_query = d_gated * inner_sum
    d_inner = d_gated * query_part
    d_skip = jnp.sum(d_inner * kv_product, axis=0)
    d_conv, back_real, back_imag = convolve(
        d_inner.reshape(seq_count, dev_rows, row_len, model_width), taps_spec, tables, True, length
    )
    d_kv = d_conv.reshape(-1, model_width) + skip_gain * d_inner
    d_qkv = jnp.concatenate([d_query, d_kv * value_part, d_kv * key_part], axis=1).astype(
        jnp.bfloat16
    )
    g_in = block_grad(flat_tokens, d_qkv, 1, 3)
    in_grad = (d_first + block_back(d_qkv, w_in)).reshape(tokens.shape)
    cross_real = jnp.sum(back_real * kv_real + back_imag * kv_imag, axis=0, keepdims=True)
    cross_imag = jnp.sum(back_imag * kv_real - back_real * kv_imag, axis=0, keepdims=True)
    cross_back_real, cross_back_imag = rows_inverse(cross_real, cross_imag, tables)
    cross_rows_real, cross_rows_imag = (
        lax.all_to_all(
            cross_back_real.astype(jnp.bfloat16), "seq", split_axis=1, concat_axis=2, tiled=True
        ).astype(cross_back_real.dtype),
        lax.all_to_all(
            cross_back_imag.astype(jnp.bfloat16), "seq", split_axis=1, concat_axis=2, tiled=True
        ).astype(cross_back_imag.dtype),
    )
    d_taps = cols_inverse(cross_rows_real, cross_rows_imag, tables, length).reshape(-1, model_width)
    g_filter_in, g_filter_out = filter_pull(d_taps)
    tile_grads = jnp.concatenate([g_in, g_out, g_gate, g_up, g_down], axis=0)
    slot_mask = slot_used.astype(jnp.float32)[:, None, None]
    summed = lax.psum(tile_grads.astype(jnp.bfloat16), "dp").astype(jnp.float32)
    owned = lax.psum_scatter(
        jnp.take(summed, tile_of_slot, axis=0) * slot_mask, "seq", scatter_dimension=0, tiled=True
    )
    tokens_all = seq_count * dev_rows * row_len * lax.axis_size("dp") * seq_devices
    grad_scale = 1.0 / math.sqrt(tokens_all)
    mine_mask = lax.dynamic_slice_in_dim(slot_mask, seq_index * owner_cap, owner_cap, 0)
    tile_grad = owned * grad_scale
    tile_new = adam_step(tile_master, tile_moment, tile_second, tile_average, tile_grad, 0.1, 0.01)
    vector_part = jnp.stack([d_gain_one, d_bias_one, d_gain_two, d_bias_two, d_skip])
    vector_sum, in_sum, out_sum = lax.psum((vector_part, g_filter_in, g_filter_out), ("dp", "seq"))
    vector_grad = vector_sum * grad_scale
    in_grad_filter = in_sum * grad_scale
    out_grad_filter = out_sum * grad_scale
    vector_new = adam_step(
        vectors, vector_moment, vector_second, vector_average, vector_grad, 0.4, 0.0
    )
    in_new = adam_step(filter_in, in_moment, in_second, in_average, in_grad_filter, 0.4, 0.01)
    out_new = adam_step(filter_out, out_moment, out_second, out_average, out_grad_filter, 0.1, 0.01)
    return (
        output,
        in_grad,
        tile_grad,
        tile_new[0] * mine_mask,
        tile_new[1] * mine_mask,
        tile_new[2] * mine_mask,
        vector_grad,
        vector_new[0],
        vector_new[1],
        vector_new[2],
        in_grad_filter,
        in_new[0],
        in_new[1],
        in_new[2],
        out_grad_filter,
        out_new[0],
        out_new[1],
        out_new[2],
    )


MESH = pl.DeviceIdType.MESH
VMEM_LIMIT = 56 * 2**20


class Links:
    def __init__(self, send_sem, recv_sem):
        self.send_sem, self.recv_sem, self.used = send_sem, recv_sem, 0
        self.dp, self.seq = lax.axis_index("dp"), lax.axis_index("seq")
        self.deep = lax.axis_size("seq") // 2
        self.z, self.core = lax.div(self.seq, 2), lax.rem(self.seq, 2)
        self.partner = (self.dp, self.seq + 1 - 2 * self.core)
        low, high = lax.rem(self.dp, 2), lax.div(self.dp, 2)
        across_x = self.dp + 1 - 2 * low
        across_y = self.dp + 2 - 4 * high
        self.near = across_x + self.core * (across_y - across_x)
        self.far = across_y + self.core * (across_x - across_y)
        self.diagonal = 3 - self.dp
        self.to_near, self.to_far = (self.near, self.seq), (self.far, self.seq)
        self.outer = lax.div(self.z, self.deep // 2)
        self.inner = 1 - self.outer
        self.to_inner = (self.dp, self.seq + 2 - 4 * self.outer)
        self.to_outer = (self.dp, self.seq - 2 + 4 * self.outer)
        self.at_end = (self.z == 0) | (self.z == self.deep - 1)

    def meet(self):
        barrier = pltpu.get_barrier_semaphore()
        for peer in (self.partner, self.to_near, self.to_far, self.to_inner):
            pl.semaphore_signal(barrier, inc=1, device_id=peer, device_id_type=MESH)

        @pl.when(jnp.logical_not(self.at_end))
        def _():
            pl.semaphore_signal(barrier, inc=1, device_id=self.to_outer, device_id_type=MESH)

        pl.semaphore_wait(barrier, jnp.where(self.at_end, 4, 5))

    def copy(self, source, target, device):
        at = self.used
        self.used += 1
        return pltpu.make_async_remote_copy(
            src_ref=source,
            dst_ref=target,
            send_sem=self.send_sem.at[at],
            recv_sem=self.recv_sem.at[at],
            device_id=device,
            device_id_type=MESH,
        )


class Chain:
    def __init__(self, links, base, arrived, leaving, send_sem, recv_sem, chunks):
        self.links, self.base, self.arrived, self.leaving = links, base, arrived, leaving
        self.send_sem, self.recv_sem, self.chunks = send_sem, recv_sem, chunks

    def send(self, k, side, device):
        at = self.chunks[k]
        return pltpu.make_async_remote_copy(
            src_ref=self.leaving.at[side, :, at],
            dst_ref=self.arrived.at[1 - side, :, at],
            send_sem=self.send_sem.at[side, k],
            recv_sem=self.recv_sem.at[1 - side, k],
            device_id=device,
            device_id_type=MESH,
        )

    def receive(self, k, side, device):
        at = self.chunks[k]
        return pltpu.make_async_remote_copy(
            src_ref=self.leaving.at[side, :, at],
            dst_ref=self.arrived.at[side, :, at],
            send_sem=self.send_sem.at[side, k],
            recv_sem=self.recv_sem.at[side, k],
            device_id=device,
            device_id_type=MESH,
        )

    def read(self, ref, k, *side):
        return ref[(*side, slice(None), self.chunks[k])].astype(jnp.float32)

    def begin(self, k):
        links, at = self.links, self.chunks[k]

        @pl.when(links.at_end)
        def _():
            own = self.base[:, at].astype(self.leaving.dtype)
            self.leaving[links.inner, :, at] = own
            self.arrived[links.outer, :, at] = jnp.zeros_like(own)
            self.send(k, links.inner, links.to_inner).start()

    def outward(self, k):
        links, at = self.links, self.chunks[k]

        @pl.when(jnp.logical_not(links.at_end))
        def _():
            self.receive(k, links.outer, links.to_outer).wait_recv()
            total = self.read(self.base, k) + self.read(self.arrived, k, links.outer)
            self.leaving[links.inner, :, at] = total.astype(self.leaving.dtype)
            self.send(k, links.inner, links.to_inner).start()

    def inward(self, k):
        links, at = self.links, self.chunks[k]
        self.receive(k, links.inner, links.to_inner).wait_recv()
        total = self.read(self.base, k) + self.read(self.arrived, k, links.inner)

        @pl.when(jnp.logical_not(links.at_end))
        def _():
            self.leaving[links.outer, :, at] = total.astype(self.leaving.dtype)
            self.send(k, links.outer, links.to_outer).start()

        return total + self.read(self.arrived, k, links.outer)

    def finish(self, k):
        links = self.links
        self.send(k, links.inner, links.to_inner).wait_send()

        @pl.when(jnp.logical_not(links.at_end))
        def _():
            self.send(k, links.outer, links.to_outer).wait_send()


def cut(*edges):
    return tuple(pl.ds(a, b - a) for a, b in zip(edges[:-1], edges[1:]))


def half_tiles(half):
    order = []
    for first, per_block in ((0, 3), (12, 1), (16, 4), (32, 4), (48, 4)):
        order += range(first + 2 * half * per_block, first + 2 * (half + 1) * per_block)
    return order


def gather_kernel(
    chunks,
    owners,
    master,
    full,
    own,
    got,
    base,
    arrived,
    leaving,
    send_sem,
    recv_sem,
    chain_send,
    chain_recv,
):
    links = Links(send_sem, recv_sem)
    quarter = full.shape[1] // 4
    tile_count, side = owners.shape[0], master.shape[2]
    most = master.shape[0] - 1
    rows = pl.ds(pl.multiple_of(links.dp * quarter, quarter), quarter)
    near_rows = pl.ds(pl.multiple_of(links.near * quarter, quarter), quarter)
    rank, place = jnp.int32(0), []
    for i in range(tile_count):
        mine = owners[i] == links.seq
        place.append((jnp.minimum(rank, most), mine))
        rank = rank + jnp.where(mine, 1, 0)
    for half in range(2):
        order = half_tiles(half)
        for j in range(0, len(order), 2):
            pair = []
            for i in order[j : j + 2]:
                at, mine = place[i]
                pair.append(jnp.where(mine, master[at, rows, :], 0.0))
            own[half, :, j * side : (j + 2) * side] = jnp.concatenate(pair, axis=1).astype(own.dtype)
    links.meet()
    swaps, planes = [], []
    for at in chunks:
        swaps.append(
            links.copy(own.at[1 - links.core, :, at], got.at[:, at], links.partner)
        )
        mine = full.at[links.core, rows, at]
        other = full.at[links.core, near_rows, at]
        both = full.at[links.core, :, at]
        planes.append(
            (
                links.copy(mine, mine, links.to_near),
                links.copy(mine, mine, links.to_far),
                links.copy(other, other, links.to_far),
                links.copy(both, both, links.partner),
            )
        )
        swaps[-1].start()
    chain = Chain(links, base, arrived, leaving, chain_send, chain_recv, chunks)

    def collect(k):
        at = chunks[k]
        swaps[k].wait()
        base[:, at] = own[links.core, :, at] + got[:, at]
        chain.begin(k)

    def spread(k):
        full[links.core, rows, chunks[k]] = chain.inward(k).astype(full.dtype)
        planes[k][0].start()
        planes[k][1].start()

    def relay(k):
        planes[k][0].wait_recv()
        planes[k][2].start()

    def share(k):
        planes[k][1].wait_recv()
        planes[k][2].wait_recv()
        planes[k][3].start()

    count = len(chunks)
    for k in range(count):
        collect(k)
    for k in range(count + 4):
        for stage, late in ((chain.outward, 0), (spread, 1), (relay, 2), (share, 4)):
            if 0 <= k - late < count:
                stage(k - late)
    for k in range(count):
        chain.finish(k)
        for copy in planes[k][:3]:
            copy.wait_send()
        planes[k][3].wait()


def gather_weights(owners, master):
    slots, side, _ = master.shape
    width = owners.shape[0] // 2 * side
    chunks = cut(0, 640, 1152, 2816, 4480, width)
    low = jnp.bfloat16
    quarter = side // 4
    count = len(chunks)
    return pl.pallas_call(
        functools.partial(gather_kernel, chunks),
        out_shape=jax.ShapeDtypeStruct((2, side, width), low),
        in_specs=[
            pl.BlockSpec(memory_space=pltpu.SMEM),
            pl.BlockSpec(memory_space=pltpu.VMEM),
        ],
        out_specs=pl.BlockSpec(memory_space=pltpu.VMEM),
        scratch_shapes=[
            pltpu.VMEM((2, quarter, width), low),
            pltpu.VMEM((quarter, width), low),
            pltpu.VMEM((quarter, width), low),
            pltpu.VMEM((2, quarter, width), low),
            pltpu.VMEM((2, quarter, width), low),
            pltpu.SemaphoreType.DMA((5 * count,)),
            pltpu.SemaphoreType.DMA((5 * count,)),
            pltpu.SemaphoreType.DMA((2, count)),
            pltpu.SemaphoreType.DMA((2, count)),
        ],
        compiler_params=pltpu.CompilerParams(
            collective_id=0, has_side_effects=True, vmem_limit_bytes=VMEM_LIMIT
        ),
        name="gather_weights",
    )(owners, master)


def reduce_kernel(
    chunks,
    tile_of_slot,
    used,
    grads,
    spread,
    mine_sum,
    got,
    near_in,
    far_in,
    far_out,
    base,
    arrived,
    leaving,
    total,
    by_tile,
    send_sem,
    recv_sem,
    chain_send,
    chain_recv,
):
    links = Links(send_sem, recv_sem)
    side = grads.shape[1]
    quarter = side // 4
    wide = jnp.float32

    def rows_of(index):
        return pl.ds(pl.multiple_of(index * quarter, quarter), quarter)

    links.meet()
    swaps, nears, diagonals, fars, shares = [], [], [], [], []
    for at in chunks:
        swaps.append(links.copy(grads.at[1 - links.core, :, at], got.at[:, at], links.partner))
        swaps[-1].start()
        nears.append(
            links.copy(mine_sum.at[rows_of(links.near), at], near_in.at[0, :, at], links.to_near)
        )
        diagonals.append(
            links.copy(
                mine_sum.at[rows_of(links.diagonal), at], near_in.at[1, :, at], links.to_near
            )
        )
        fars.append(links.copy(far_out.at[:, at], far_in.at[:, at], links.to_far))
        part = total.at[links.core, :, at]
        shares.append(links.copy(part, part, links.partner))
    chain = Chain(links, base, arrived, leaving, chain_send, chain_recv, chunks)

    def merge_cores(k):
        at = chunks[k]
        swaps[k].wait()
        mine_sum[:, at] = (
            grads[links.core, :, at].astype(wide) + got[:, at].astype(wide)
        ).astype(mine_sum.dtype)
        diagonals[k].start()
        nears[k].start()

    def go_far(k):
        at = chunks[k]
        diagonals[k].wait_recv()
        far_out[:, at] = (
            mine_sum[rows_of(links.far), at].astype(wide) + near_in[1, :, at].astype(wide)
        ).astype(far_out.dtype)
        fars[k].start()

    def collect(k):
        at = chunks[k]
        nears[k].wait_recv()
        fars[k].wait_recv()
        base[:, at] = (
            mine_sum[rows_of(links.dp), at].astype(wide)
            + near_in[0, :, at].astype(wide)
            + far_in[:, at].astype(wide)
        )
        chain.begin(k)

    def end(k):
        total[links.core, :, chunks[k]] = chain.inward(k).astype(total.dtype)
        shares[k].start()

    count = len(chunks)
    for k in range(count + 4):
        stages = ((merge_cores, 0), (go_far, 1), (collect, 2), (chain.outward, 3), (end, 4))
        for stage, late in stages:
            if 0 <= k - late < count:
                stage(k - late)
    for share in shares:
        share.wait()
    for half in range(2):
        for j, i in enumerate(half_tiles(half)):
            by_tile[i] = total[half, :, j * side : (j + 1) * side].astype(wide)
    slots = tile_of_slot.shape[0]
    tiles_wide = slots * side
    mine = rows_of(links.dp)
    for s in range(0, slots, 2):
        pair = [jnp.where(used[k] > 0, by_tile[tile_of_slot[k]], 0.0) for k in (s, s + 1)]
        spread[mine, s * side : (s + 2) * side] = jnp.concatenate(pair, axis=1).astype(spread.dtype)
    first_extra = by_tile.shape[0] // 2 * side
    extra = total.shape[2] - first_extra
    for half in range(2):
        begin = tiles_wide + half * extra
        spread[mine, begin : begin + extra] = total[half, :, first_extra:]
    at_home, other = spread.at[mine, :], spread.at[rows_of(links.near), :]
    first = links.copy(at_home, at_home, links.to_near)
    second = links.copy(at_home, at_home, links.to_far)
    relay = links.copy(other, other, links.to_far)
    first.start()
    second.start()
    first.wait_recv()
    relay.start()
    second.wait_recv()
    relay.wait()
    first.wait_send()
    second.wait_send()
    for k in range(count):
        nears[k].wait_send()
        diagonals[k].wait_send()
        fars[k].wait_send()
        chain.finish(k)


def reduce_grads(tile_of_slot, used, grads):
    _, side, width = grads.shape
    slots = tile_of_slot.shape[0]
    extra = width - NTILES // 2 * side
    chunks = cut(0, 1152, 2304, 3456, 4480, 5504, width)
    low = jnp.bfloat16
    quarter = side // 4
    count = len(chunks)
    return pl.pallas_call(
        functools.partial(reduce_kernel, chunks),
        out_shape=jax.ShapeDtypeStruct((side, slots * side + 2 * extra), low),
        in_specs=[
            pl.BlockSpec(memory_space=pltpu.SMEM),
            pl.BlockSpec(memory_space=pltpu.SMEM),
            pl.BlockSpec(memory_space=pltpu.VMEM),
        ],
        out_specs=pl.BlockSpec(memory_space=pltpu.VMEM),
        scratch_shapes=[
            pltpu.VMEM((side, width), low),
            pltpu.VMEM((side, width), low),
            pltpu.VMEM((2, quarter, width), low),
            pltpu.VMEM((quarter, width), low),
            pltpu.VMEM((quarter, width), low),
            pltpu.VMEM((quarter, width), jnp.float32),
            pltpu.VMEM((2, quarter, width), low),
            pltpu.VMEM((2, quarter, width), low),
            pltpu.VMEM((2, quarter, width), low),
            pltpu.VMEM((NTILES, quarter, side), jnp.float32),
            pltpu.SemaphoreType.DMA((5 * count + 3,)),
            pltpu.SemaphoreType.DMA((5 * count + 3,)),
            pltpu.SemaphoreType.DMA((2, count)),
            pltpu.SemaphoreType.DMA((2, count)),
        ],
        compiler_params=pltpu.CompilerParams(
            collective_id=1, has_side_effects=True, vmem_limit_bytes=VMEM_LIMIT
        ),
        name="reduce_grads",
    )(tile_of_slot, used, grads)


def on_device_columns(
    tokens,
    cotangent,
    owners,
    tile_master,
    tile_moment,
    tile_second,
    tile_average,
    vectors,
    vector_moment,
    vector_second,
    vector_average,
    filter_in,
    in_moment,
    in_second,
    in_average,
    filter_out,
    out_moment,
    out_second,
    out_average,
):
    seq_count, dev_rows, row_len, model_width = tokens.shape
    owner_cap = tile_master.shape[0]
    seq_devices = lax.axis_size("seq")
    grid_rows = dev_rows * seq_devices
    length = grid_rows * row_len
    seq_index = lax.axis_index("seq")
    hidden_ratio = FF // D
    quarter_hidden = FF // 4
    slot_of_tile, tile_of_slot, slot_used = slot_maps(owners, owner_cap, owner_cap * seq_devices)
    packed = gather_weights(owners, tile_master)
    side = tile_master.shape[1]
    lanes = 2 * side

    def blocks_of(first, per_block):
        part = packed[:, :, first * lanes : (first + per_block) * lanes]
        part = part.reshape(2, side, 2, per_block * side).transpose(0, 2, 1, 3)
        return part.reshape(4, side, per_block * side)

    w_in, w_out = blocks_of(0, 3), blocks_of(3, 1)
    w_gate_up = jnp.concatenate([blocks_of(4, 4), blocks_of(8, 4)], axis=2)
    w_down = blocks_of(12, 4).reshape(4, side, 4, side).transpose(0, 2, 1, 3)
    w_down = w_down.reshape(4, 4 * side, side)
    halves = seq_devices // seq_count
    width = model_width // halves
    half_index = lax.rem(seq_index, halves)
    grid_position = (
        jnp.arange(grid_rows, dtype=jnp.int32)[:, None]
        + grid_rows * jnp.arange(row_len, dtype=jnp.int32)[None, :]
    )
    position = grid_position.reshape(-1).astype(jnp.float32)
    table = jnp.asarray(real_table(grid_rows, row_len))
    first_bin = (jnp.arange(length // 2) == 0)[:, None]

    def spread(field_in):
        cells = field_in.reshape(seq_count, row_len, halves, width).transpose(0, 2, 1, 3)
        cells = cells.reshape(seq_devices, row_len, width).astype(jnp.bfloat16)
        return lax.all_to_all(cells, "seq", 0, 0, tiled=True).reshape(length, width)

    def collect(field_in):
        cells = field_in.astype(jnp.bfloat16).reshape(seq_devices, row_len, width)
        cells = lax.all_to_all(cells, "seq", 0, 0, tiled=True)
        cells = cells.reshape(seq_count, halves, row_len, width).transpose(0, 2, 1, 3)
        return cells.reshape(-1, model_width).astype(jnp.float32)

    def transform(columns):
        spec = jnp.dot(table, columns.astype(jnp.bfloat16), preferred_element_type=jnp.float32)
        return (spec[: length // 2], spec[length // 2 :])

    def invert(real_part, imag_part):
        weight = jnp.where(first_bin, 1.0 / length, 2.0 / length)
        spec = jnp.concatenate([real_part * weight, imag_part * weight], axis=0)
        return lax.dot_general(
            table,
            spec.astype(jnp.bfloat16),
            (((0,), (0,)), ((), ())),
            preferred_element_type=jnp.float32,
        )

    def product(one, two, conjugate):
        one_real, one_imag = one
        two_real, two_imag = two
        cross = jnp.where(first_bin, 0.0, two_imag) * (-1.0 if conjugate else 1.0)
        diag = jnp.where(first_bin, two_imag, two_real)
        return (one_real * two_real - one_imag * cross, one_real * cross + one_imag * diag)

    flat_tokens = tokens.reshape(-1, model_width)
    qkv_all = block_apply(flat_tokens, w_in)
    query_part = qkv_all[:, :model_width]
    key_part = qkv_all[:, model_width : 2 * model_width]
    value_part = qkv_all[:, 2 * model_width :]
    kv_product = key_part * value_part

    channel = half_index * width + jnp.arange(width, dtype=jnp.int32)
    own_filter = lax.dynamic_slice_in_dim(filter_out, half_index * width, width, 1)

    def own_taps(weight_one, weight_two):
        return filter_taps_of(weight_one, weight_two, position, length, channel)

    taps_own, filter_pull = jax.vjp(own_taps, filter_in, own_filter)
    taps_spec = transform(taps_own)
    kv_spec = transform(spread(kv_product))
    conv_out = collect(invert(*product(kv_spec, taps_spec, False)))
    skip_gain = vectors[4]
    inner_sum = conv_out + skip_gain * kv_product
    gated_out = (query_part * inner_sum).astype(jnp.bfloat16)
    branch = block_apply(gated_out, w_out)
    normed, first_pull = jax.vjp(
        norm_rows, flat_tokens.astype(jnp.float32) + branch, vectors[0], vectors[1]
    )
    normed_low = normed.astype(jnp.bfloat16)
    gate_up = block_apply(normed_low, w_gate_up).reshape(-1, 4, 2, quarter_hidden)
    gate_value = gate_up[:, :, 0].reshape(-1, FF)
    up_value = gate_up[:, :, 1].reshape(-1, FF)
    active, active_pull = jax.vjp(glu_act, gate_value, up_value)
    active_low = active.astype(jnp.bfloat16)
    down_value = block_apply(active_low, w_down)
    result, second_pull = jax.vjp(
        norm_rows, normed_low.astype(jnp.float32) + down_value, vectors[2], vectors[3]
    )
    output = result.astype(jnp.bfloat16).reshape(tokens.shape)
    d_second, d_gain_two, d_bias_two = second_pull(
        cotangent.reshape(-1, model_width).astype(jnp.float32)
    )
    d_down = d_second.astype(jnp.bfloat16)
    g_down = block_grad(active_low, d_down, hidden_ratio, 1)
    d_gate, d_up = active_pull(block_back(d_down, w_down))
    d_gate_up = jnp.stack(
        [d_gate.reshape(-1, 4, quarter_hidden), d_up.reshape(-1, 4, quarter_hidden)], axis=2
    )
    d_gate_up = d_gate_up.reshape(-1, 2 * FF).astype(jnp.bfloat16)
    gate_up_tiles = block_grad(normed_low, d_gate_up, 1, 2 * hidden_ratio).reshape(
        4, 2, hidden_ratio, side, side
    )
    g_gate = gate_up_tiles[:, 0].reshape(-1, side, side)
    g_up = gate_up_tiles[:, 1].reshape(-1, side, side)
    d_normed = d_second + block_back(d_gate_up, w_gate_up)
    d_first, d_gain_one, d_bias_one = first_pull(d_normed)
    d_branch = d_first.astype(jnp.bfloat16)
    g_out = block_grad(gated_out, d_branch, 1, 1)
    d_gated = block_back(d_branch, w_out)
    d_query = d_gated * inner_sum
    d_inner = d_gated * query_part
    d_skip = jnp.sum(d_inner * kv_product, axis=0)
    back_spec = transform(spread(d_inner))
    d_kv = collect(invert(*product(back_spec, taps_spec, True))) + skip_gain * d_inner
    d_qkv = jnp.concatenate([d_query, d_kv * value_part, d_kv * key_part], axis=1).astype(
        jnp.bfloat16
    )
    g_in = block_grad(flat_tokens, d_qkv, 1, 3)
    in_grad = (d_first + block_back(d_qkv, w_in)).reshape(tokens.shape)
    d_taps = invert(*product(back_spec, kv_spec, True))
    g_filter_in, g_filter_half = filter_pull(d_taps)
    def pack(tiles):
        per_half = tiles.shape[0] // 2
        return tiles.reshape(2, per_half, side, side).transpose(0, 2, 1, 3).reshape(2, side, -1)

    slot_mask = slot_used.astype(jnp.float32)[:, None, None]
    first_slot = seq_index * owner_cap
    vector_part = jnp.stack([d_gain_one, d_bias_one, d_gain_two, d_bias_two, d_skip])
    order = filter_in.shape[1]
    both = jnp.zeros((2, side, width), jnp.float32)
    both = lax.dynamic_update_slice(both, g_filter_half[None], (half_index, 0, 0))
    both = lax.dynamic_update_slice(
        both, vector_part.reshape(5, 2, width).transpose(1, 0, 2), (0, order, 0)
    )
    both = lax.dynamic_update_slice(both, g_filter_in[None], (0, order + 8, 0))
    packed_grads = jnp.concatenate(
        [pack(g).astype(jnp.bfloat16) for g in (g_in, g_out, g_gate, g_up, g_down, )]
        + [both.astype(jnp.bfloat16)],
        axis=2,
    )
    own_tile = lax.dynamic_slice_in_dim(tile_of_slot, first_slot, owner_cap, 0)
    own_used = lax.dynamic_slice_in_dim(slot_used.astype(jnp.int32), first_slot, owner_cap, 0)
    reduced = reduce_grads(own_tile, own_used, packed_grads).astype(jnp.float32)
    owned = reduced[:, : owner_cap * side].reshape(side, owner_cap, side).transpose(1, 0, 2)
    extra = reduced[:, owner_cap * side :].reshape(side, 2, width).transpose(1, 0, 2)
    out_sum = extra[:, :order].transpose(1, 0, 2).reshape(order, model_width)
    vector_sum = extra[:, order : order + 5].transpose(1, 0, 2).reshape(5, model_width)
    in_sum = extra[0, order + 8 : order + 13, :order]
    tokens_all = seq_count * dev_rows * row_len * lax.axis_size("dp") * seq_devices
    grad_scale = 1.0 / math.sqrt(tokens_all)
    mine_mask = lax.dynamic_slice_in_dim(slot_mask, seq_index * owner_cap, owner_cap, 0)
    tile_grad = owned * grad_scale
    tile_new = adam_step(tile_master, tile_moment, tile_second, tile_average, tile_grad, 0.1, 0.01)
    vector_grad = vector_sum * grad_scale
    in_grad_filter = in_sum * grad_scale
    out_grad_filter = out_sum * grad_scale
    vector_new = adam_step(
        vectors, vector_moment, vector_second, vector_average, vector_grad, 0.4, 0.0
    )
    in_new = adam_step(filter_in, in_moment, in_second, in_average, in_grad_filter, 0.4, 0.01)
    out_new = adam_step(filter_out, out_moment, out_second, out_average, out_grad_filter, 0.1, 0.01)
    return (
        output,
        in_grad,
        tile_grad,
        tile_new[0] * mine_mask,
        tile_new[1] * mine_mask,
        tile_new[2] * mine_mask,
        vector_grad,
        vector_new[0],
        vector_new[1],
        vector_new[2],
        in_grad_filter,
        in_new[0],
        in_new[1],
        in_new[2],
        out_grad_filter,
        out_new[0],
        out_new[1],
        out_new[2],
    )


def on_device(*arrays):
    seq_count, dev_rows, row_len, model_width = arrays[0].shape
    seq_devices = lax.axis_size("seq")
    fits = dev_rows == 1 and seq_devices % seq_count == 0 and seq_devices * row_len <= 2048
    fits = fits and lax.axis_size("dp") == 4 and seq_devices == 2 * seq_count == 8
    if fits and model_width % (128 * (seq_devices // seq_count)) == 0:
        return on_device_columns(*arrays)
    return on_device_general(*arrays)


def solution(mesh):
    in_specs = (
        P("dp", "seq", None, None),
        P("dp", "seq", None, None),
        P(),
        P("seq", None, None),
        P("seq", None, None),
        P("seq", None, None),
        P("seq", None, None),
        P(),
        P(),
        P(),
        P(),
        P(),
        P(),
        P(),
        P(),
        P(),
        P(),
        P(),
        P(),
    )
    out_specs = (
        P("dp", "seq", None, None),
        P("dp", "seq", None, None),
        P("seq", None, None),
        P("seq", None, None),
        P("seq", None, None),
        P("seq", None, None),
        P(),
        P(),
        P(),
        P(),
        P(),
        P(),
        P(),
        P(),
        P(),
        P(),
        P(),
        P(),
    )
    return jax.shard_map(
        on_device, mesh=mesh, in_specs=in_specs, out_specs=out_specs, check_vma=False
    )
```

```python
import functools
import math

import jax
import jax.numpy as jnp
import ml_dtypes
import numpy as np
from jax import lax
from jax.experimental import pallas as pl
from jax.experimental.pallas import tpu as pltpu
from jax.sharding import PartitionSpec as P

D = 768
FF = 3072
STEP = 10
NTILES = 64


highest = lax.Precision.HIGHEST
beta_one = 0.9
beta_two = 0.999
keep_rate = 0.5
adam_eps = 1e-08
norm_eps = 1e-05
golden = 0.6180339887


def norm_rows(values, gain_vec, bias_vec):
    row_mean = jnp.mean(values, axis=-1, keepdims=True)
    centered = values - row_mean
    spread = jnp.mean(centered * centered, axis=-1, keepdims=True)
    return centered * lax.rsqrt(spread + norm_eps) * gain_vec + bias_vec


def glu_act(gate_value, up_value):
    return jax.nn.gelu(gate_value, approximate=False) * up_value


def filter_taps(filter_in, filter_out, position, length):
    channel = jnp.arange(filter_out.shape[1], dtype=jnp.int32)
    return filter_taps_of(filter_in, filter_out, position, length, channel)


def filter_taps_of(filter_in, filter_out, position, length, channel_index):
    phases = position * (2.0 * math.pi / length)
    features = jnp.stack(
        [
            position / length,
            jnp.cos(phases),
            -jnp.sin(phases),
            jnp.cos(2.0 * phases),
            -jnp.sin(2.0 * phases),
        ],
        axis=1,
    )
    hidden = jnp.sin(jnp.dot(features, filter_in, precision=highest))
    taps_value = jnp.dot(hidden, filter_out, precision=highest)
    channel = channel_index.astype(jnp.float32)
    decay_rates = 0.3 * jnp.exp(math.log(1000.0) * jnp.mod(channel * golden, 1.0))
    decay_rate = jnp.exp(-(position / length)[:, None] * decay_rates[None, :])
    total = jnp.expm1(-2.0 * decay_rates) / jnp.expm1(-2.0 * decay_rates / length)
    norm_scale = lax.rsqrt(total)
    return taps_value * decay_rate * norm_scale


def block_weight(tile_stack, in_tiles, out_tiles):
    tile_side = tile_stack.shape[-1]
    tile_grid = tile_stack.reshape(4, in_tiles, out_tiles, tile_side, tile_side).transpose(
        0, 1, 3, 2, 4
    )
    return tile_grid.reshape(4, in_tiles * tile_side, out_tiles * tile_side)


def tile_split(blocks, in_tiles, out_tiles):
    tile_side = blocks.shape[1] // in_tiles
    tile_grid = blocks.reshape(4, in_tiles, tile_side, out_tiles, tile_side).transpose(
        0, 1, 3, 2, 4
    )
    return tile_grid.reshape(4 * in_tiles * out_tiles, tile_side, tile_side)


def block_apply(values, blocks):
    row_view = values.reshape(values.shape[0], 4, -1)
    return jnp.einsum("nbi,bio->nbo", row_view, blocks, preferred_element_type=jnp.float32).reshape(
        values.shape[0], -1
    )


def block_back(gradient, blocks):
    row_view = gradient.reshape(gradient.shape[0], 4, -1)
    return jnp.einsum("nbo,bio->nbi", row_view, blocks, preferred_element_type=jnp.float32).reshape(
        gradient.shape[0], -1
    )


def block_grad(values, gradient, in_tiles, out_tiles):
    left_rows = values.reshape(values.shape[0], 4, -1)
    right_rows = gradient.reshape(gradient.shape[0], 4, -1)
    blocks = jnp.einsum("nbi,nbo->bio", left_rows, right_rows, preferred_element_type=jnp.float32)
    return tile_split(blocks, in_tiles, out_tiles)


def slot_maps(owners, owner_cap, slot_total):
    tile_count = owners.shape[0]
    tile_index = jnp.arange(tile_count, dtype=jnp.int32)
    earlier = (owners[:, None] == owners[None, :]) & (tile_index[None, :] < tile_index[:, None])
    owner_rank = jnp.sum(earlier.astype(jnp.int32), axis=1)
    slot_of_tile = owners * owner_cap + owner_rank
    slot_hits = slot_of_tile[None, :] == jnp.arange(slot_total, dtype=jnp.int32)[:, None]
    tile_of_slot = jnp.sum(slot_hits.astype(jnp.int32) * tile_index[None, :], axis=1)
    slot_used = jnp.any(slot_hits, axis=1)
    return (slot_of_tile, tile_of_slot, slot_used)


def adam_step(weight, moment, second, average, gradient, step_rate, decay_rate):
    moment = beta_one * moment + (1.0 - beta_one) * gradient
    second = beta_two * second + (1.0 - beta_two) * gradient * gradient
    fixed_moment = moment / (1.0 - beta_one**STEP)
    fixed_second = second / (1.0 - beta_two**STEP)
    weight = weight - step_rate * (
        fixed_moment / (jnp.sqrt(fixed_second) + adam_eps) + decay_rate * weight
    )
    average = keep_rate * average + (1.0 - keep_rate) * weight
    return (second, weight, average)


def wave_table(period, index_one, index_two):
    turn_count = jnp.mod(index_one[:, None] * index_two[None, :], period).astype(jnp.float32)
    angles = turn_count * (2.0 * math.pi / period)
    return (jnp.cos(angles), jnp.sin(angles))


def col_dot(field_in, table_in):
    return jnp.einsum("srcd,ck->srkd", field_in, table_in, precision=highest)


def row_dot(field_in, table_in):
    return jnp.einsum("srkd,rq->sqkd", field_in, table_in, precision=highest)


def cols_forward(field_in, tables):
    col_cos, col_sin, turn_cos, turn_sin, row_cos, row_sin = tables
    real_part = col_dot(field_in, col_cos)
    imag_part = -col_dot(field_in, col_sin)
    real_turn = real_part * turn_cos + imag_part * turn_sin
    imag_turn = imag_part * turn_cos - real_part * turn_sin
    return (real_turn, imag_turn)


def rows_forward(part_real, part_imag, tables):
    row_cos, row_sin = (tables[4], tables[5])
    freq_real = row_dot(part_real, row_cos) + row_dot(part_imag, row_sin)
    freq_imag = row_dot(part_imag, row_cos) - row_dot(part_real, row_sin)
    return (freq_real, freq_imag)


def rows_inverse(prod_real, prod_imag, tables):
    row_cos, row_sin = (tables[4], tables[5])
    back_real = row_dot(prod_real, row_cos) - row_dot(prod_imag, row_sin)
    back_imag = row_dot(prod_real, row_sin) + row_dot(prod_imag, row_cos)
    return (back_real, back_imag)


def cols_inverse(rows_real, rows_imag, tables, length):
    col_cos, col_sin, turn_cos, turn_sin, row_cos, row_sin = tables
    cell_real = rows_real * turn_cos - rows_imag * turn_sin
    cell_imag = rows_real * turn_sin + rows_imag * turn_cos
    return (
        jnp.einsum("srkd,ck->srcd", cell_real, col_cos, precision=highest)
        - jnp.einsum("srkd,ck->srcd", cell_imag, col_sin, precision=highest)
    ) / length


def convolve(field_in, spectrum, tables, conjugate, length):
    spec_real, spec_imag = spectrum
    sign_flip = -1.0 if conjugate else 1.0
    real_turn, imag_turn = cols_forward(field_in, tables)
    part_real = lax.all_to_all(real_turn, "seq", split_axis=2, concat_axis=1, tiled=True)
    part_imag = lax.all_to_all(imag_turn, "seq", split_axis=2, concat_axis=1, tiled=True)
    freq_real, freq_imag = rows_forward(part_real, part_imag, tables)
    prod_real = freq_real * spec_real - sign_flip * freq_imag * spec_imag
    prod_imag = sign_flip * freq_real * spec_imag + freq_imag * spec_real
    back_real, back_imag = rows_inverse(prod_real, prod_imag, tables)
    rows_real = lax.all_to_all(back_real, "seq", split_axis=1, concat_axis=2, tiled=True)
    rows_imag = lax.all_to_all(back_imag, "seq", split_axis=1, concat_axis=2, tiled=True)
    rows_real, rows_imag, freq_real, freq_imag = (rows_real, rows_imag, freq_real, freq_imag)
    field_out = cols_inverse(rows_real, rows_imag, tables, length)
    return (field_out, freq_real, freq_imag)


def real_table(grid_rows, row_len):
    length = grid_rows * row_len
    position = (np.arange(grid_rows)[:, None] + grid_rows * np.arange(row_len)[None, :]).reshape(-1)
    turns = np.mod(np.arange(length // 2)[:, None] * position[None, :], length)
    angles = turns * (2.0 * np.pi / length)
    sines = -np.sin(angles)
    sines[0] = np.cos(np.pi * position)
    return np.concatenate([np.cos(angles), sines]).astype(ml_dtypes.bfloat16)


def on_device_general(
    tokens,
    cotangent,
    owners,
    tile_master,
    tile_moment,
    tile_second,
    tile_average,
    vectors,
    vector_moment,
    vector_second,
    vector_average,
    filter_in,
    in_moment,
    in_second,
    in_average,
    filter_out,
    out_moment,
    out_second,
    out_average,
):
    seq_count, dev_rows, row_len, model_width = tokens.shape
    owner_cap = tile_master.shape[0]
    seq_devices = lax.axis_size("seq")
    grid_rows = dev_rows * seq_devices
    length = grid_rows * row_len
    seq_index = lax.axis_index("seq")
    hidden_ratio = FF // D
    quarter_hidden = FF // 4
    slot_of_tile, tile_of_slot, slot_used = slot_maps(owners, owner_cap, owner_cap * seq_devices)
    gathered = lax.all_gather(tile_master.astype(jnp.bfloat16), "seq", axis=0, tiled=True)
    weights = jnp.take(gathered, slot_of_tile, axis=0)
    w_in = block_weight(weights[0:12], 1, 3)
    w_out = block_weight(weights[12:16], 1, 1)
    w_gate = block_weight(weights[16 : 16 + 4 * hidden_ratio], 1, hidden_ratio)
    w_up = block_weight(weights[16 + 4 * hidden_ratio : 16 + 8 * hidden_ratio], 1, hidden_ratio)
    w_down = block_weight(weights[16 + 8 * hidden_ratio : 16 + 12 * hidden_ratio], hidden_ratio, 1)
    w_gate_up = jnp.concatenate([w_gate, w_up], axis=2)
    col_index = jnp.arange(row_len, dtype=jnp.int32)
    row_index = jnp.arange(grid_rows, dtype=jnp.int32)
    local_rows = seq_index * dev_rows + jnp.arange(dev_rows, dtype=jnp.int32)
    col_cos, col_sin = wave_table(row_len, col_index, col_index)
    row_cos, row_sin = wave_table(grid_rows, row_index, row_index)
    turn_cos, turn_sin = wave_table(length, local_rows, col_index)
    tables = (
        col_cos,
        col_sin,
        turn_cos[None, :, :, None],
        turn_sin[None, :, :, None],
        row_cos,
        row_sin,
    )
    own_position = (
        (local_rows[:, None] + grid_rows * col_index[None, :]).reshape(-1).astype(jnp.float32)
    )
    flat_tokens = tokens.reshape(-1, model_width)
    qkv_all = block_apply(flat_tokens, w_in)
    query_part = qkv_all[:, :model_width]
    key_part = qkv_all[:, model_width : 2 * model_width]
    value_part = qkv_all[:, 2 * model_width :]
    kv_product = key_part * value_part

    def own_taps(weight_one, weight_two):
        return filter_taps(weight_one, weight_two, own_position, length)

    taps_own, filter_pull = jax.vjp(own_taps, filter_in, filter_out)
    taps_real, taps_imag = cols_forward(taps_own.reshape(1, dev_rows, row_len, model_width), tables)
    taps_real, taps_imag = (
        lax.all_to_all(taps_real, "seq", split_axis=2, concat_axis=1, tiled=True),
        lax.all_to_all(taps_imag, "seq", split_axis=2, concat_axis=1, tiled=True),
    )
    spec_real, spec_imag = rows_forward(taps_real, taps_imag, tables)
    taps_spec = (spec_real[0], spec_imag[0])
    conv_out, kv_real, kv_imag = convolve(
        kv_product.reshape(seq_count, dev_rows, row_len, model_width),
        taps_spec,
        tables,
        False,
        length,
    )
    skip_gain = vectors[4]
    inner_sum = conv_out.reshape(-1, model_width) + skip_gain * kv_product
    gated_out = (query_part * inner_sum).astype(jnp.bfloat16)
    branch = block_apply(gated_out, w_out)
    normed, first_pull = jax.vjp(
        norm_rows, flat_tokens.astype(jnp.float32) + branch, vectors[0], vectors[1]
    )
    normed_low = normed.astype(jnp.bfloat16)
    gate_up = block_apply(normed_low, w_gate_up).reshape(-1, 4, 2, quarter_hidden)
    gate_value = gate_up[:, :, 0].reshape(-1, FF)
    up_value = gate_up[:, :, 1].reshape(-1, FF)
    active, active_pull = jax.vjp(glu_act, gate_value, up_value)
    active_low = active.astype(jnp.bfloat16)
    down_value = block_apply(active_low, w_down)
    result, second_pull = jax.vjp(
        norm_rows, normed_low.astype(jnp.float32) + down_value, vectors[2], vectors[3]
    )
    output = result.astype(jnp.bfloat16).reshape(tokens.shape)
    d_second, d_gain_two, d_bias_two = second_pull(
        cotangent.reshape(-1, model_width).astype(jnp.float32)
    )
    d_down = d_second.astype(jnp.bfloat16)
    g_down = block_grad(active_low, d_down, hidden_ratio, 1)
    d_gate, d_up = active_pull(block_back(d_down, w_down))
    d_gate_up = jnp.stack(
        [d_gate.reshape(-1, 4, quarter_hidden), d_up.reshape(-1, 4, quarter_hidden)], axis=2
    )
    d_gate_up = d_gate_up.reshape(-1, 2 * FF).astype(jnp.bfloat16)
    gate_up_tiles = block_grad(normed_low, d_gate_up, 1, 2 * hidden_ratio).reshape(
        4, 2, hidden_ratio, weights.shape[1], weights.shape[2]
    )
    g_gate = gate_up_tiles[:, 0].reshape(-1, weights.shape[1], weights.shape[2])
    g_up = gate_up_tiles[:, 1].reshape(-1, weights.shape[1], weights.shape[2])
    d_normed = d_second + block_back(d_gate_up, w_gate_up)
    d_first, d_gain_one, d_bias_one = first_pull(d_normed)
    d_branch = d_first.astype(jnp.bfloat16)
    g_out = block_grad(gated_out, d_branch, 1, 1)
    d_gated = block_back(d_branch, w_out)
    d_query = d_gated * inner_sum
    d_inner = d_gated * query_part
    d_skip = jnp.sum(d_inner * kv_product, axis=0)
    d_conv, back_real, back_imag = convolve(
        d_inner.reshape(seq_count, dev_rows, row_len, model_width), taps_spec, tables, True, length
    )
    d_kv = d_conv.reshape(-1, model_width) + skip_gain * d_inner
    d_qkv = jnp.concatenate([d_query, d_kv * value_part, d_kv * key_part], axis=1).astype(
        jnp.bfloat16
    )
    g_in = block_grad(flat_tokens, d_qkv, 1, 3)
    in_grad = (d_first + block_back(d_qkv, w_in)).reshape(tokens.shape)
    cross_real = jnp.sum(back_real * kv_real + back_imag * kv_imag, axis=0, keepdims=True)
    cross_imag = jnp.sum(back_imag * kv_real - back_real * kv_imag, axis=0, keepdims=True)
    cross_back_real, cross_back_imag = rows_inverse(cross_real, cross_imag, tables)
    cross_rows_real, cross_rows_imag = (
        lax.all_to_all(
            cross_back_real.astype(jnp.bfloat16), "seq", split_axis=1, concat_axis=2, tiled=True
        ).astype(cross_back_real.dtype),
        lax.all_to_all(
            cross_back_imag.astype(jnp.bfloat16), "seq", split_axis=1, concat_axis=2, tiled=True
        ).astype(cross_back_imag.dtype),
    )
    d_taps = cols_inverse(cross_rows_real, cross_rows_imag, tables, length).reshape(-1, model_width)
    g_filter_in, g_filter_out = filter_pull(d_taps)
    tile_grads = jnp.concatenate([g_in, g_out, g_gate, g_up, g_down], axis=0)
    slot_mask = slot_used.astype(jnp.float32)[:, None, None]
    summed = lax.psum(tile_grads.astype(jnp.bfloat16), "dp").astype(jnp.float32)
    owned = lax.psum_scatter(
        jnp.take(summed, tile_of_slot, axis=0) * slot_mask, "seq", scatter_dimension=0, tiled=True
    )
    tokens_all = seq_count * dev_rows * row_len * lax.axis_size("dp") * seq_devices
    grad_scale = 1.0 / math.sqrt(tokens_all)
    mine_mask = lax.dynamic_slice_in_dim(slot_mask, seq_index * owner_cap, owner_cap, 0)
    tile_grad = owned * grad_scale
    tile_new = adam_step(tile_master, tile_moment, tile_second, tile_average, tile_grad, 0.1, 0.01)
    vector_part = jnp.stack([d_gain_one, d_bias_one, d_gain_two, d_bias_two, d_skip])
    vector_sum, in_sum, out_sum = lax.psum((vector_part, g_filter_in, g_filter_out), ("dp", "seq"))
    vector_grad = vector_sum * grad_scale
    in_grad_filter = in_sum * grad_scale
    out_grad_filter = out_sum * grad_scale
    vector_new = adam_step(
        vectors, vector_moment, vector_second, vector_average, vector_grad, 0.4, 0.0
    )
    in_new = adam_step(filter_in, in_moment, in_second, in_average, in_grad_filter, 0.4, 0.01)
    out_new = adam_step(filter_out, out_moment, out_second, out_average, out_grad_filter, 0.1, 0.01)
    return (
        output,
        in_grad,
        tile_grad,
        tile_new[0] * mine_mask,
        tile_new[1] * mine_mask,
        tile_new[2] * mine_mask,
        vector_grad,
        vector_new[0],
        vector_new[1],
        vector_new[2],
        in_grad_filter,
        in_new[0],
        in_new[1],
        in_new[2],
        out_grad_filter,
        out_new[0],
        out_new[1],
        out_new[2],
    )


MESH = pl.DeviceIdType.MESH
VMEM_LIMIT = 56 * 2**20


class Links:
    def __init__(self, send_sem, recv_sem):
        self.send_sem, self.recv_sem, self.used = send_sem, recv_sem, 0
        self.dp, self.seq = lax.axis_index("dp"), lax.axis_index("seq")
        self.deep = lax.axis_size("seq") // 2
        self.z, self.core = lax.div(self.seq, 2), lax.rem(self.seq, 2)
        self.partner = (self.dp, self.seq + 1 - 2 * self.core)
        low, high = lax.rem(self.dp, 2), lax.div(self.dp, 2)
        across_x = self.dp + 1 - 2 * low
        across_y = self.dp + 2 - 4 * high
        self.near = across_x + self.core * (across_y - across_x)
        self.far = across_y + self.core * (across_x - across_y)
        self.diagonal = 3 - self.dp
        self.to_near, self.to_far = (self.near, self.seq), (self.far, self.seq)
        self.outer = lax.div(self.z, self.deep // 2)
        self.inner = 1 - self.outer
        self.to_inner = (self.dp, self.seq + 2 - 4 * self.outer)
        self.to_outer = (self.dp, self.seq - 2 + 4 * self.outer)
        self.at_end = (self.z == 0) | (self.z == self.deep - 1)

    def meet(self):
        barrier = pltpu.get_barrier_semaphore()
        for peer in (self.partner, self.to_near, self.to_far, self.to_inner):
            pl.semaphore_signal(barrier, inc=1, device_id=peer, device_id_type=MESH)

        @pl.when(jnp.logical_not(self.at_end))
        def _():
            pl.semaphore_signal(barrier, inc=1, device_id=self.to_outer, device_id_type=MESH)

        pl.semaphore_wait(barrier, jnp.where(self.at_end, 4, 5))

    def copy(self, source, target, device):
        at = self.used
        self.used += 1
        return pltpu.make_async_remote_copy(
            src_ref=source,
            dst_ref=target,
            send_sem=self.send_sem.at[at],
            recv_sem=self.recv_sem.at[at],
            device_id=device,
            device_id_type=MESH,
        )


class Chain:
    def __init__(self, links, base, arrived, leaving, send_sem, recv_sem, chunks):
        self.links, self.base, self.arrived, self.leaving = links, base, arrived, leaving
        self.send_sem, self.recv_sem, self.chunks = send_sem, recv_sem, chunks

    def send(self, k, side, device):
        at = self.chunks[k]
        return pltpu.make_async_remote_copy(
            src_ref=self.leaving.at[side, :, at],
            dst_ref=self.arrived.at[1 - side, :, at],
            send_sem=self.send_sem.at[side, k],
            recv_sem=self.recv_sem.at[1 - side, k],
            device_id=device,
            device_id_type=MESH,
        )

    def receive(self, k, side, device):
        at = self.chunks[k]
        return pltpu.make_async_remote_copy(
            src_ref=self.leaving.at[side, :, at],
            dst_ref=self.arrived.at[side, :, at],
            send_sem=self.send_sem.at[side, k],
            recv_sem=self.recv_sem.at[side, k],
            device_id=device,
            device_id_type=MESH,
        )

    def read(self, ref, k, *side):
        return ref[(*side, slice(None), self.chunks[k])].astype(jnp.float32)

    def begin(self, k):
        links, at = self.links, self.chunks[k]

        @pl.when(links.at_end)
        def _():
            own = self.base[:, at].astype(self.leaving.dtype)
            self.leaving[links.inner, :, at] = own
            self.arrived[links.outer, :, at] = jnp.zeros_like(own)
            self.send(k, links.inner, links.to_inner).start()

    def outward(self, k):
        links, at = self.links, self.chunks[k]

        @pl.when(jnp.logical_not(links.at_end))
        def _():
            self.receive(k, links.outer, links.to_outer).wait_recv()
            total = self.read(self.base, k) + self.read(self.arrived, k, links.outer)
            self.leaving[links.inner, :, at] = total.astype(self.leaving.dtype)
            self.send(k, links.inner, links.to_inner).start()

    def inward(self, k):
        links, at = self.links, self.chunks[k]
        self.receive(k, links.inner, links.to_inner).wait_recv()
        total = self.read(self.base, k) + self.read(self.arrived, k, links.inner)

        @pl.when(jnp.logical_not(links.at_end))
        def _():
            self.leaving[links.outer, :, at] = total.astype(self.leaving.dtype)
            self.send(k, links.outer, links.to_outer).start()

        return total + self.read(self.arrived, k, links.outer)

    def finish(self, k):
        links = self.links
        self.send(k, links.inner, links.to_inner).wait_send()

        @pl.when(jnp.logical_not(links.at_end))
        def _():
            self.send(k, links.outer, links.to_outer).wait_send()


def cut(*edges):
    return tuple(pl.ds(a, b - a) for a, b in zip(edges[:-1], edges[1:]))


def half_tiles(half):
    order = []
    for first, per_block in ((0, 3), (12, 1), (16, 4), (32, 4), (48, 4)):
        order += range(first + 2 * half * per_block, first + 2 * (half + 1) * per_block)
    return order


def gather_kernel(
    chunks,
    owners,
    master,
    full,
    own,
    got,
    base,
    arrived,
    leaving,
    send_sem,
    recv_sem,
    chain_send,
    chain_recv,
):
    links = Links(send_sem, recv_sem)
    quarter = full.shape[1] // 4
    tile_count, side = owners.shape[0], master.shape[2]
    most = master.shape[0] - 1
    rows = pl.ds(pl.multiple_of(links.dp * quarter, quarter), quarter)
    near_rows = pl.ds(pl.multiple_of(links.near * quarter, quarter), quarter)
    rank, place = jnp.int32(0), []
    for i in range(tile_count):
        mine = owners[i] == links.seq
        place.append((jnp.minimum(rank, most), mine))
        rank = rank + jnp.where(mine, 1, 0)
    for half in range(2):
        order = half_tiles(half)
        for j in range(0, len(order), 2):
            pair = []
            for i in order[j : j + 2]:
                at, mine = place[i]
                pair.append(jnp.where(mine, master[at, rows, :], 0.0))
            own[half, :, j * side : (j + 2) * side] = jnp.concatenate(pair, axis=1).astype(own.dtype)
    links.meet()
    swaps, planes = [], []
    for at in chunks:
        swaps.append(
            links.copy(own.at[1 - links.core, :, at], got.at[:, at], links.partner)
        )
        mine = full.at[links.core, rows, at]
        other = full.at[links.core, near_rows, at]
        both = full.at[links.core, :, at]
        planes.append(
            (
                links.copy(mine, mine, links.to_near),
                links.copy(mine, mine, links.to_far),
                links.copy(other, other, links.to_far),
                links.copy(both, both, links.partner),
            )
        )
        swaps[-1].start()
    chain = Chain(links, base, arrived, leaving, chain_send, chain_recv, chunks)

    def collect(k):
        at = chunks[k]
        swaps[k].wait()
        base[:, at] = own[links.core, :, at] + got[:, at]
        chain.begin(k)

    def spread(k):
        full[links.core, rows, chunks[k]] = chain.inward(k).astype(full.dtype)
        planes[k][0].start()
        planes[k][1].start()

    def relay(k):
        planes[k][0].wait_recv()
        planes[k][2].start()

    def share(k):
        planes[k][1].wait_recv()
        planes[k][2].wait_recv()
        planes[k][3].start()

    count = len(chunks)
    for k in range(count):
        collect(k)
    for k in range(count + 4):
        for stage, late in ((chain.outward, 0), (spread, 1), (relay, 2), (share, 4)):
            if 0 <= k - late < count:
                stage(k - late)
    for k in range(count):
        chain.finish(k)
        for copy in planes[k][:3]:
            copy.wait_send()
        planes[k][3].wait()


def gather_weights(owners, master):
    slots, side, _ = master.shape
    width = owners.shape[0] // 2 * side
    chunks = cut(0, 640, 1152, 2816, 4480, width)
    low = jnp.bfloat16
    quarter = side // 4
    count = len(chunks)
    return pl.pallas_call(
        functools.partial(gather_kernel, chunks),
        out_shape=jax.ShapeDtypeStruct((2, side, width), low),
        in_specs=[
            pl.BlockSpec(memory_space=pltpu.SMEM),
            pl.BlockSpec(memory_space=pltpu.VMEM),
        ],
        out_specs=pl.BlockSpec(memory_space=pltpu.VMEM),
        scratch_shapes=[
            pltpu.VMEM((2, quarter, width), low),
            pltpu.VMEM((quarter, width), low),
            pltpu.VMEM((quarter, width), low),
            pltpu.VMEM((2, quarter, width), low),
            pltpu.VMEM((2, quarter, width), low),
            pltpu.SemaphoreType.DMA((5 * count,)),
            pltpu.SemaphoreType.DMA((5 * count,)),
            pltpu.SemaphoreType.DMA((2, count)),
            pltpu.SemaphoreType.DMA((2, count)),
        ],
        compiler_params=pltpu.CompilerParams(
            collective_id=0, has_side_effects=True, vmem_limit_bytes=VMEM_LIMIT
        ),
        name="gather_weights",
    )(owners, master)


def reduce_kernel(
    chunks,
    tile_of_slot,
    used,
    grads,
    spread,
    mine_sum,
    got,
    near_in,
    far_in,
    far_out,
    base,
    arrived,
    leaving,
    total,
    by_tile,
    send_sem,
    recv_sem,
    chain_send,
    chain_recv,
):
    links = Links(send_sem, recv_sem)
    side = grads.shape[1]
    quarter = side // 4
    wide = jnp.float32

    def rows_of(index):
        return pl.ds(pl.multiple_of(index * quarter, quarter), quarter)

    links.meet()
    swaps, nears, diagonals, fars, shares = [], [], [], [], []
    for at in chunks:
        swaps.append(links.copy(grads.at[1 - links.core, :, at], got.at[:, at], links.partner))
        swaps[-1].start()
        nears.append(
            links.copy(mine_sum.at[rows_of(links.near), at], near_in.at[0, :, at], links.to_near)
        )
        diagonals.append(
            links.copy(
                mine_sum.at[rows_of(links.diagonal), at], near_in.at[1, :, at], links.to_near
            )
        )
        fars.append(links.copy(far_out.at[:, at], far_in.at[:, at], links.to_far))
        part = total.at[links.core, :, at]
        shares.append(links.copy(part, part, links.partner))
    chain = Chain(links, base, arrived, leaving, chain_send, chain_recv, chunks)

    def merge_cores(k):
        at = chunks[k]
        swaps[k].wait()
        mine_sum[:, at] = (
            grads[links.core, :, at].astype(wide) + got[:, at].astype(wide)
        ).astype(mine_sum.dtype)
        diagonals[k].start()
        nears[k].start()

    def go_far(k):
        at = chunks[k]
        diagonals[k].wait_recv()
        far_out[:, at] = (
            mine_sum[rows_of(links.far), at].astype(wide) + near_in[1, :, at].astype(wide)
        ).astype(far_out.dtype)
        fars[k].start()

    def collect(k):
        at = chunks[k]
        nears[k].wait_recv()
        fars[k].wait_recv()
        base[:, at] = (
            mine_sum[rows_of(links.dp), at].astype(wide)
            + near_in[0, :, at].astype(wide)
            + far_in[:, at].astype(wide)
        )
        chain.begin(k)

    def end(k):
        total[links.core, :, chunks[k]] = chain.inward(k).astype(total.dtype)
        shares[k].start()

    count = len(chunks)
    for k in range(count + 4):
        stages = ((merge_cores, 0), (go_far, 1), (collect, 2), (chain.outward, 3), (end, 4))
        for stage, late in stages:
            if 0 <= k - late < count:
                stage(k - late)
    for share in shares:
        share.wait()
    for half in range(2):
        for j, i in enumerate(half_tiles(half)):
            by_tile[i] = total[half, :, j * side : (j + 1) * side].astype(wide)
    slots = tile_of_slot.shape[0]
    tiles_wide = slots * side
    mine = rows_of(links.dp)
    for s in range(0, slots, 2):
        pair = [jnp.where(used[k] > 0, by_tile[tile_of_slot[k]], 0.0) for k in (s, s + 1)]
        spread[mine, s * side : (s + 2) * side] = jnp.concatenate(pair, axis=1).astype(spread.dtype)
    first_extra = by_tile.shape[0] // 2 * side
    extra = total.shape[2] - first_extra
    for half in range(2):
        begin = tiles_wide + half * extra
        spread[mine, begin : begin + extra] = total[half, :, first_extra:]
    at_home, other = spread.at[mine, :], spread.at[rows_of(links.near), :]
    first = links.copy(at_home, at_home, links.to_near)
    second = links.copy(at_home, at_home, links.to_far)
    relay = links.copy(other, other, links.to_far)
    first.start()
    second.start()
    first.wait_recv()
    relay.start()
    second.wait_recv()
    relay.wait()
    first.wait_send()
    second.wait_send()
    for k in range(count):
        nears[k].wait_send()
        diagonals[k].wait_send()
        fars[k].wait_send()
        chain.finish(k)


def reduce_grads(tile_of_slot, used, grads):
    _, side, width = grads.shape
    slots = tile_of_slot.shape[0]
    extra = width - NTILES // 2 * side
    chunks = cut(0, 1152, 2304, 3456, 4480, 5504, width)
    low = jnp.bfloat16
    quarter = side // 4
    count = len(chunks)
    return pl.pallas_call(
        functools.partial(reduce_kernel, chunks),
        out_shape=jax.ShapeDtypeStruct((side, slots * side + 2 * extra), low),
        in_specs=[
            pl.BlockSpec(memory_space=pltpu.SMEM),
            pl.BlockSpec(memory_space=pltpu.SMEM),
            pl.BlockSpec(memory_space=pltpu.VMEM),
        ],
        out_specs=pl.BlockSpec(memory_space=pltpu.VMEM),
        scratch_shapes=[
            pltpu.VMEM((side, width), low),
            pltpu.VMEM((side, width), low),
            pltpu.VMEM((2, quarter, width), low),
            pltpu.VMEM((quarter, width), low),
            pltpu.VMEM((quarter, width), low),
            pltpu.VMEM((quarter, width), jnp.float32),
            pltpu.VMEM((2, quarter, width), low),
            pltpu.VMEM((2, quarter, width), low),
            pltpu.VMEM((2, quarter, width), low),
            pltpu.VMEM((NTILES, quarter, side), jnp.float32),
            pltpu.SemaphoreType.DMA((5 * count + 3,)),
            pltpu.SemaphoreType.DMA((5 * count + 3,)),
            pltpu.SemaphoreType.DMA((2, count)),
            pltpu.SemaphoreType.DMA((2, count)),
        ],
        compiler_params=pltpu.CompilerParams(
            collective_id=1, has_side_effects=True, vmem_limit_bytes=VMEM_LIMIT
        ),
        name="reduce_grads",
    )(tile_of_slot, used, grads)


VMEM = pl.BlockSpec(memory_space=pltpu.VMEM)
SMEM = pl.BlockSpec(memory_space=pltpu.SMEM)
NN = (((1,), (0,)), ((), ()))
NT = (((1,), (1,)), ((), ()))
TN = (((0,), (0,)), ((), ()))


def mul(left, right, dims=NN):
    return lax.dot_general(left, right, dims, preferred_element_type=jnp.float32)


def plain_call(kernel, name, out_shape, scratch=(), in_specs=None):
    def call(*arrays):
        return pl.pallas_call(
            kernel,
            out_shape=out_shape,
            in_specs=[VMEM] * len(arrays) if in_specs is None else in_specs,
            out_specs=jax.tree.map(lambda _: VMEM, out_shape),
            scratch_shapes=list(scratch),
            compiler_params=pltpu.CompilerParams(vmem_limit_bytes=VMEM_LIMIT),
            name=name,
        )(*arrays)

    return call


def filter_constants(grid_rows, row_len, width):
    length = grid_rows * row_len
    position = (np.arange(grid_rows)[:, None] + grid_rows * np.arange(row_len)[None, :]).reshape(-1)
    turn = 2.0 * np.pi * position / length
    rows = [position / length, np.cos(turn), -np.sin(turn), np.cos(2 * turn), -np.sin(2 * turn)]
    features = np.zeros((length, 8), np.float32)
    features[:, :5] = np.stack(rows, axis=1)
    rate = 0.3 * 1000.0 ** np.mod(golden * np.arange(width), 1.0)
    total = np.expm1(-2.0 * rate) / np.expm1(-2.0 * rate / length)
    channels = np.stack([rate, 1.0 / np.sqrt(total)]).astype(np.float32)
    return (features, channels)


def phases_of(features, filter_in):
    total = features[:, 0:1] * filter_in[0:1, :]
    for i in range(1, filter_in.shape[0]):
        total += features[:, i : i + 1] * filter_in[i : i + 1, :]
    return total


def first_row(shape):
    return lax.broadcasted_iota(jnp.int32, shape, 0) == 0


def spectrum_product(one_real, one_imag, two_real, two_imag, sign):
    first = first_row(one_real.shape)
    cross = jnp.where(first, 0.0, two_imag) * sign
    diag = jnp.where(first, two_imag, two_real)
    return (one_real * two_real - one_imag * cross, one_real * cross + one_imag * diag)


def decay_of(features, channels, lanes):
    return jnp.exp(-features[:, 0:1] * channels[0:1, lanes]) * channels[1:2, lanes]


def half_lanes(width):
    half = lax.rem(lax.axis_index("seq"), 2)
    return pl.ds(pl.multiple_of(half * width, width), width)


def taps_kernel(features, channels, filter_in, filter_out, table, spec):
    length, width = spec.shape
    lanes = half_lanes(width)
    hidden = jnp.sin(phases_of(features[...], filter_in[...]))
    taps = mul(hidden.astype(jnp.bfloat16), filter_out[:, lanes].astype(jnp.bfloat16))
    taps = (taps * decay_of(features, channels, lanes)).astype(jnp.bfloat16)
    scale = jnp.where(first_row((length // 2, 1)), 1.0 / length, 2.0 / length)
    for part in range(2):
        rows = slice(part * length // 2, (part + 1) * length // 2)
        spec[rows, :] = mul(table[rows, :], taps) * scale


def conv_kernel(cells, table, table_back, taps_spec, out, kv_spec):
    length, width = kv_spec.shape
    half = length // 2
    columns = cells[...].reshape(length, width)
    real, imag = mul(table[:half], columns), mul(table[half:], columns)
    kv_spec[:half] = real
    kv_spec[half:] = imag
    real, imag = spectrum_product(real, imag, taps_spec[:half], taps_spec[half:], 1.0)
    result = mul(table_back[:, :half], real.astype(jnp.bfloat16))
    result += mul(table_back[:, half:], imag.astype(jnp.bfloat16))
    out[...] = result.astype(out.dtype).reshape(out.shape)


def conv_back_kernel(
    cells,
    table,
    table_back,
    taps_spec,
    kv_spec,
    features,
    channels,
    filter_in,
    filter_out,
    out,
    grad_out,
    grad_in,
):
    low = jnp.bfloat16
    length, width = kv_spec.shape
    half = length // 2
    columns = cells[...].reshape(length, width)
    back_real, back_imag = mul(table[:half], columns), mul(table[half:], columns)
    real, imag = spectrum_product(back_real, back_imag, taps_spec[:half], taps_spec[half:], -1.0)
    result = mul(table_back[:, :half], real.astype(low)) + mul(table_back[:, half:], imag.astype(low))
    out[...] = result.astype(out.dtype).reshape(out.shape)
    scale = jnp.where(first_row((half, 1)), 1.0 / length, 2.0 / length)
    real, imag = spectrum_product(back_real, back_imag, kv_spec[:half], kv_spec[half:], -1.0)
    real, imag = (real * scale).astype(low), (imag * scale).astype(low)
    d_taps = mul(table_back[:, :half], real) + mul(table_back[:, half:], imag)
    lanes = half_lanes(width)
    scaled = (d_taps * decay_of(features, channels, lanes)).astype(low)
    phases = phases_of(features[...], filter_in[...])
    grad_out[...] = mul(jnp.sin(phases).astype(low), scaled, TN)
    d_hidden = mul(scaled, filter_out[:, lanes].astype(low), NT) * jnp.cos(phases)
    grad_in[...] = jnp.zeros_like(grad_in)
    for i in range(filter_in.shape[0]):
        grad_in[i : i + 1, :] = jnp.sum(features[:, i : i + 1] * d_hidden, axis=0, keepdims=True)


def tile_at(packed, half, first):
    return packed[half, :, first : first + packed.shape[1]]


def qkv_kernel(x, packed, query, key, value, kv):
    side = packed.shape[1]
    count = kv.shape[0] // 2
    row_len, width = kv.shape[1:]
    for i in range(12):
        block, half = i // 3, i // 6
        part = mul(x[:, block * side : (block + 1) * side], tile_at(packed, half, (i % 6) * side))
        target = (query, key, value)[i // 4]
        at = (i % 4) * side
        target[:, at : at + side] = part.astype(target.dtype)
    for s in range(count):
        rows = slice(s * row_len, (s + 1) * row_len)
        for h in range(2):
            lanes = slice(h * width, (h + 1) * width)
            both = key[rows, lanes].astype(jnp.float32) * value[rows, lanes].astype(jnp.float32)
            kv[2 * s + h] = both.astype(kv.dtype)


def normalize(values):
    centered = values - jnp.mean(values, axis=-1, keepdims=True)
    spread = lax.rsqrt(jnp.mean(centered * centered, axis=-1, keepdims=True) + norm_eps)
    return (centered * spread, spread)


def normalize_back(gradient, unit, spread):
    mean = jnp.mean(gradient, axis=-1, keepdims=True)
    along = jnp.mean(gradient * unit, axis=-1, keepdims=True)
    return (gradient - mean - unit * along) * spread


def gelu_parts(v):
    share = 0.5 + 0.5 * lax.erf(v * math.sqrt(0.5))
    density = jnp.exp(-0.5 * v * v) * (1.0 / math.sqrt(2.0 * math.pi))
    return (v * share, share + v * density)


def layer_kernel(
    conv,
    query,
    kv,
    x,
    cotangent,
    vectors,
    packed,
    output,
    d_first_out,
    d_inner_out,
    d_query,
    grads,
    sums,
    gated_all,
    normed_all,
    d_branch_all,
    d_down_all,
    active_all,
    d_gate_all,
    d_up_all,
    down_weights,
):
    wide, low = jnp.float32, jnp.bfloat16
    side = packed.shape[1]
    row_len, width = conv.shape[1:]
    tokens = x.shape[0]
    per_step = 2
    rows_step = per_step * row_len
    quarter = 4 * side
    gain_one, bias_one = vectors[0:1], vectors[1:2]
    gain_two, bias_two = vectors[2:3], vectors[3:4]
    skip = vectors[4:5]
    out_at, gate_at, up_at, down_at = 6 * side, 8 * side, 16 * side, 24 * side
    for b in range(4):
        for i in range(4):
            down_weights[b, i * side : (i + 1) * side, :] = tile_at(
                packed, b // 2, down_at + (4 * (b % 2) + i) * side
            )
    sums[...] = jnp.zeros_like(sums)

    def cells(ref, step):
        parts = ref[pl.ds(step * 2 * per_step, 2 * per_step)].astype(wide)
        lines = [
            jnp.concatenate([parts[2 * s], parts[2 * s + 1]], axis=1) for s in range(per_step)
        ]
        return jnp.concatenate(lines, axis=0)

    def block(values, b):
        return values[:, b * side : (b + 1) * side]

    def add_sum(row, values):
        sums[row : row + 1, :] += jnp.sum(values, axis=0, keepdims=True)

    @pl.loop(0, tokens // rows_step)
    def _(step):
        rows = pl.ds(pl.multiple_of(step * rows_step, rows_step), rows_step)
        kv_here = cells(kv, step)
        inner = cells(conv, step) + skip * kv_here
        query_here = query[rows, :].astype(wide)
        gated = (query_here * inner).astype(low)
        gated_all[rows, :] = gated
        branch = jnp.concatenate(
            [
                mul(block(gated, b), tile_at(packed, b // 2, out_at + (b % 2) * side))
                for b in range(4)
            ],
            axis=1,
        )
        unit_one, spread_one = normalize(x[rows, :].astype(wide) + branch)
        normed = (unit_one * gain_one + bias_one).astype(low)
        normed_all[rows, :] = normed
        down = []
        for b in range(4):
            lanes = slice(b * quarter, (b + 1) * quarter)
            at = (b % 2) * quarter
            here = block(normed, b)
            gate = mul(here, packed[b // 2, :, gate_at + at : gate_at + at + quarter])
            up = mul(here, packed[b // 2, :, up_at + at : up_at + at + quarter])
            curved, slope = gelu_parts(gate)
            active = (curved * up).astype(low)
            active_all[rows, lanes] = active
            d_gate_all[rows, lanes] = (slope * up).astype(low)
            d_up_all[rows, lanes] = curved.astype(low)
            down.append(mul(active, down_weights[b]))
        unit_two, spread_two = normalize(normed.astype(wide) + jnp.concatenate(down, axis=1))
        output[rows, :] = (unit_two * gain_two + bias_two).astype(low)
        cot = cotangent[rows, :].astype(wide)
        add_sum(2, cot * unit_two)
        add_sum(3, cot)
        d_second = normalize_back(cot * gain_two, unit_two, spread_two)
        d_down = d_second.astype(low)
        d_down_all[rows, :] = d_down
        d_normed = []
        for b in range(4):
            lanes = slice(b * quarter, (b + 1) * quarter)
            at = (b % 2) * quarter
            d_active = mul(block(d_down, b), down_weights[b], NT)
            d_gate = (d_active * d_gate_all[rows, lanes].astype(wide)).astype(low)
            d_up = (d_active * d_up_all[rows, lanes].astype(wide)).astype(low)
            d_gate_all[rows, lanes] = d_gate
            d_up_all[rows, lanes] = d_up
            d_normed.append(
                mul(d_gate, packed[b // 2, :, gate_at + at : gate_at + at + quarter], NT)
                + mul(d_up, packed[b // 2, :, up_at + at : up_at + at + quarter], NT)
            )
        d_normed = d_second + jnp.concatenate(d_normed, axis=1)
        add_sum(0, d_normed * unit_one)
        add_sum(1, d_normed)
        d_first = normalize_back(d_normed * gain_one, unit_one, spread_one)
        d_first_out[rows, :] = d_first
        d_branch = d_first.astype(low)
        d_branch_all[rows, :] = d_branch
        d_gated = jnp.concatenate(
            [
                mul(block(d_branch, b), tile_at(packed, b // 2, out_at + (b % 2) * side), NT)
                for b in range(4)
            ],
            axis=1,
        )
        d_query[rows, :] = (d_gated * inner).astype(low)
        d_inner = d_gated * query_here
        add_sum(4, d_inner * kv_here)
        d_inner = d_inner.astype(low)
        for s in range(per_step):
            for h in range(2):
                d_inner_out[2 * (step * per_step + s) + h] = d_inner[
                    s * row_len : (s + 1) * row_len, h * width : (h + 1) * width
                ]

    for b in range(4):
        lanes = slice(b * quarter, (b + 1) * quarter)
        at = (b % 2) * quarter
        half = b // 2
        mine = slice(b * side, (b + 1) * side)

        def put(first, values):
            first -= out_at
            grads[half, :, first : first + values.shape[1]] = values.astype(low)

        put(out_at + (b % 2) * side, mul(gated_all[:, mine], d_branch_all[:, mine], TN))
        put(gate_at + at, mul(normed_all[:, mine], d_gate_all[:, lanes], TN))
        put(up_at + at, mul(normed_all[:, mine], d_up_all[:, lanes], TN))
        tall = mul(active_all[:, lanes], d_down_all[:, mine], TN)
        for i in range(4):
            put(down_at + at + i * side, tall[i * side : (i + 1) * side, :])


def layer_call(conv, query, kv, x, cotangent, vectors, packed):
    tokens, model = x.shape
    _, side, width = packed.shape
    low = jnp.bfloat16
    shape = jax.ShapeDtypeStruct
    hidden = 16 * side
    return plain_call(
        layer_kernel,
        "layer",
        (
            shape((tokens, model), low),
            shape((tokens, model), jnp.float32),
            shape(kv.shape, low),
            shape((tokens, model), low),
            shape((2, side, width - 6 * side), low),
            shape((8, model), jnp.float32),
        ),
        [pltpu.VMEM((tokens, model), low)] * 4
        + [pltpu.VMEM((tokens, hidden), low)] * 3
        + [pltpu.VMEM((4, 4 * side, side), low)],
    )(conv, query, kv, x, cotangent, vectors, packed)


def input_kernel(d_conv, d_inner, d_query, key, value, x, d_first, vectors, packed, in_grad, grads, d_qkv):
    wide, low = jnp.float32, jnp.bfloat16
    side = packed.shape[1]
    row_len, width = d_conv.shape[1:]
    model = x.shape[1]
    d_qkv[:, :model] = d_query[...]
    for s in range(d_conv.shape[0] // 2):
        rows = slice(s * row_len, (s + 1) * row_len)
        for h in range(2):
            lanes = slice(h * width, (h + 1) * width)
            cell = 2 * s + h
            d_kv = d_conv[cell].astype(wide) + vectors[4:5, lanes] * d_inner[cell].astype(wide)
            d_qkv[rows, model + h * width : model + (h + 1) * width] = (
                d_kv * value[rows, lanes].astype(wide)
            ).astype(low)
            d_qkv[rows, 2 * model + h * width : 2 * model + (h + 1) * width] = (
                d_kv * key[rows, lanes].astype(wide)
            ).astype(low)
    per_block = 3 * side
    for b in range(4):
        mine = slice(b * side, (b + 1) * side)
        here = d_qkv[:, b * per_block : (b + 1) * per_block]
        at = (b % 2) * per_block
        weights = packed[b // 2, :, at : at + per_block]
        in_grad[:, mine] = d_first[:, mine] + mul(here, weights, NT)
        grads[b // 2, :, at : at + per_block] = mul(x[:, mine], here, TN).astype(low)


def adam(weight, moment, second, average, gradient, rate, decay):
    moment = beta_one * moment + (1.0 - beta_one) * gradient
    second = beta_two * second + (1.0 - beta_two) * gradient * gradient
    moment = moment * (1.0 / (1.0 - beta_one**STEP))
    root = jnp.sqrt(second * (1.0 / (1.0 - beta_two**STEP)))
    weight = weight - rate * (moment / (root + adam_eps) + decay * weight)
    return (second, weight, keep_rate * average + (1.0 - keep_rate) * weight)


def adam_kernel(scale, used, reduced, extra, *refs):
    step = pl.program_id(0)
    per_step, side, _ = refs[0].shape
    tile_in, small_in, tile_out, small_out = refs[:4], refs[4:16], refs[16:20], refs[20:32]
    for k in range(per_step):
        keep = used[step * per_step + k] > 0
        gradient = reduced[:, k * side : (k + 1) * side].astype(jnp.float32) * scale
        tile_out[0][k] = gradient
        fresh = adam(*(ref[k] for ref in tile_in), gradient, 0.1, 0.01)
        for ref, values in zip(tile_out[1:], fresh):
            ref[k] = jnp.where(keep, values, 0.0)

    @pl.when(step == 0)
    def _():
        order, model = small_in[8].shape
        width = model // 2
        count = small_in[0].shape[0]
        features = small_in[4].shape[0]
        sums = extra[...].astype(jnp.float32) * scale
        both = (sums[:, :width], sums[:, width:])
        first = order + 8
        gradients = (
            jnp.concatenate([part[order : order + count] for part in both], axis=1),
            both[0][first : first + features, :order],
            jnp.concatenate([part[:order] for part in both], axis=1),
        )
        rates = ((0.4, 0.0), (0.4, 0.01), (0.1, 0.01))
        for i, (gradient, rate) in enumerate(zip(gradients, rates)):
            small_out[4 * i][...] = gradient
            fresh = adam(*(ref[...] for ref in small_in[4 * i : 4 * i + 4]), gradient, *rate)
            for ref, values in zip(small_out[4 * i + 1 : 4 * i + 4], fresh):
                ref[...] = values


def adam_call(scale, used, reduced, tile_state, small_state):
    slots, side, _ = tile_state[0].shape
    model = small_state[0].shape[1]
    per_step = 2
    tile = pl.BlockSpec((per_step, side, side), lambda i: (i, 0, 0))
    small = [pl.BlockSpec(a.shape, lambda i: (0, 0)) for a in small_state]
    shape = jax.ShapeDtypeStruct
    return pl.pallas_call(
        functools.partial(adam_kernel, scale),
        grid=(slots // per_step,),
        out_shape=tuple(shape(a.shape, a.dtype) for a in tile_state + small_state),
        in_specs=[
            SMEM,
            pl.BlockSpec((side, per_step * side), lambda i: (0, i)),
            pl.BlockSpec((side, model), lambda i: (0, slots * side // model)),
        ]
        + [tile] * 4
        + small,
        out_specs=[tile] * 4 + small,
        compiler_params=pltpu.CompilerParams(vmem_limit_bytes=VMEM_LIMIT),
        name="adam",
    )(used, reduced, reduced, *tile_state, *small_state)


def on_device_columns(
    tokens,
    cotangent,
    owners,
    tile_master,
    tile_moment,
    tile_second,
    tile_average,
    vectors,
    vector_moment,
    vector_second,
    vector_average,
    filter_in,
    in_moment,
    in_second,
    in_average,
    filter_out,
    out_moment,
    out_second,
    out_average,
):
    seq_count, dev_rows, row_len, model_width = tokens.shape
    owner_cap, side, _ = tile_master.shape
    seq_devices = lax.axis_size("seq")
    grid_rows = dev_rows * seq_devices
    length = grid_rows * row_len
    seq_index = lax.axis_index("seq")
    width = model_width // 2
    low, wide = jnp.bfloat16, jnp.float32
    shape = jax.ShapeDtypeStruct
    count = seq_count * row_len
    order = filter_in.shape[1]
    table_host = real_table(grid_rows, row_len)
    table, table_back = jnp.asarray(table_host), jnp.asarray(np.ascontiguousarray(table_host.T))
    features, channels = (
        jnp.asarray(a) for a in filter_constants(grid_rows, row_len, model_width)
    )
    slot_of_tile, tile_of_slot, slot_used = slot_maps(owners, owner_cap, owner_cap * seq_devices)
    first_slot = seq_index * owner_cap
    own_tile = lax.dynamic_slice_in_dim(tile_of_slot, first_slot, owner_cap, 0)
    own_used = lax.dynamic_slice_in_dim(slot_used.astype(jnp.int32), first_slot, owner_cap, 0)
    packed = gather_weights(owners, tile_master)
    x = tokens.reshape(count, model_width)
    cell_shape = (seq_devices, row_len, width)
    taps_spec = plain_call(taps_kernel, "taps", shape((length, width), wide))(
        features, channels, filter_in, filter_out, table
    )
    query, key, value, kv = plain_call(
        qkv_kernel, "qkv", (shape(x.shape, low),) * 3 + (shape(cell_shape, low),)
    )(x, packed)

    def exchange(cells):
        return lax.all_to_all(cells, "seq", 0, 0, tiled=True)

    conv, kv_spec = plain_call(
        conv_kernel, "conv", (shape(cell_shape, low), shape((length, width), wide))
    )(exchange(kv), table, table_back, taps_spec)
    output, d_first, d_inner, d_query, grads, sums = layer_call(
        exchange(conv), query, kv, x, cotangent.reshape(count, model_width), vectors, packed
    )
    d_conv, grad_out, grad_in = plain_call(
        conv_back_kernel,
        "conv_back",
        (shape(cell_shape, low), shape((order, width), wide), shape((8, order), wide)),
    )(
        exchange(d_inner),
        table,
        table_back,
        taps_spec,
        kv_spec,
        features,
        channels,
        filter_in,
        filter_out,
    )
    in_grad, grads_in = plain_call(
        input_kernel,
        "input_grad",
        (shape(x.shape, wide), shape((2, side, 6 * side), low)),
        [pltpu.VMEM((count, 3 * model_width), low)],
    )(exchange(d_conv), d_inner, d_query, key, value, x, d_first, vectors, packed)
    both = jnp.zeros((2, side, width), wide)
    both = lax.dynamic_update_slice(both, grad_out[None], (lax.rem(seq_index, 2), 0, 0))
    both = lax.dynamic_update_slice(
        both, sums.reshape(8, 2, width).transpose(1, 0, 2), (0, order, 0)
    )
    both = lax.dynamic_update_slice(both, grad_in[None], (0, order + 8, 0))
    packed_grads = jnp.concatenate([grads_in, grads, both.astype(low)], axis=2)
    reduced = reduce_grads(own_tile, own_used, packed_grads)
    tokens_all = count * lax.axis_size("dp") * seq_devices
    updated = adam_call(
        1.0 / math.sqrt(tokens_all),
        own_used,
        reduced,
        (tile_master, tile_moment, tile_second, tile_average),
        (
            vectors,
            vector_moment,
            vector_second,
            vector_average,
            filter_in,
            in_moment,
            in_second,
            in_average,
            filter_out,
            out_moment,
            out_second,
            out_average,
        ),
    )
    return (output.reshape(tokens.shape), in_grad.reshape(tokens.shape), *updated)


def on_device(*arrays):
    seq_count, dev_rows, row_len, model_width = arrays[0].shape
    seq_devices = lax.axis_size("seq")
    fits = dev_rows == 1 and lax.axis_size("dp") == 4 and seq_devices == 2 * seq_count == 8
    if fits and row_len == 128 and model_width % 256 == 0:
        return on_device_columns(*arrays)
    return on_device_general(*arrays)


def solution(mesh):
    in_specs = (
        P("dp", "seq", None, None),
        P("dp", "seq", None, None),
        P(),
        P("seq", None, None),
        P("seq", None, None),
        P("seq", None, None),
        P("seq", None, None),
        P(),
        P(),
        P(),
        P(),
        P(),
        P(),
        P(),
        P(),
        P(),
        P(),
        P(),
        P(),
    )
    out_specs = (
        P("dp", "seq", None, None),
        P("dp", "seq", None, None),
        P("seq", None, None),
        P("seq", None, None),
        P("seq", None, None),
        P("seq", None, None),
        P(),
        P(),
        P(),
        P(),
        P(),
        P(),
        P(),
        P(),
        P(),
        P(),
        P(),
        P(),
    )
    return jax.shard_map(
        on_device, mesh=mesh, in_specs=in_specs, out_specs=out_specs, check_vma=False
    )
```

```python
import functools
import math

import jax
import jax.numpy as jnp
import ml_dtypes
import numpy as np
from jax import lax
from jax.experimental import pallas as pl
from jax.experimental.pallas import tpu as pltpu
from jax.sharding import PartitionSpec as P

D = 768
FF = 3072
STEP = 10
NTILES = 64


highest = lax.Precision.HIGHEST
beta_one = 0.9
beta_two = 0.999
keep_rate = 0.5
adam_eps = 1e-08
norm_eps = 1e-05
golden = 0.6180339887


def norm_rows(values, gain_vec, bias_vec):
    row_mean = jnp.mean(values, axis=-1, keepdims=True)
    centered = values - row_mean
    spread = jnp.mean(centered * centered, axis=-1, keepdims=True)
    return centered * lax.rsqrt(spread + norm_eps) * gain_vec + bias_vec


def glu_act(gate_value, up_value):
    return jax.nn.gelu(gate_value, approximate=False) * up_value


def filter_taps(filter_in, filter_out, position, length):
    channel = jnp.arange(filter_out.shape[1], dtype=jnp.int32)
    return filter_taps_of(filter_in, filter_out, position, length, channel)


def filter_taps_of(filter_in, filter_out, position, length, channel_index):
    phases = position * (2.0 * math.pi / length)
    features = jnp.stack(
        [
            position / length,
            jnp.cos(phases),
            -jnp.sin(phases),
            jnp.cos(2.0 * phases),
            -jnp.sin(2.0 * phases),
        ],
        axis=1,
    )
    hidden = jnp.sin(jnp.dot(features, filter_in, precision=highest))
    taps_value = jnp.dot(hidden, filter_out, precision=highest)
    channel = channel_index.astype(jnp.float32)
    decay_rates = 0.3 * jnp.exp(math.log(1000.0) * jnp.mod(channel * golden, 1.0))
    decay_rate = jnp.exp(-(position / length)[:, None] * decay_rates[None, :])
    total = jnp.expm1(-2.0 * decay_rates) / jnp.expm1(-2.0 * decay_rates / length)
    norm_scale = lax.rsqrt(total)
    return taps_value * decay_rate * norm_scale


def block_weight(tile_stack, in_tiles, out_tiles):
    tile_side = tile_stack.shape[-1]
    tile_grid = tile_stack.reshape(4, in_tiles, out_tiles, tile_side, tile_side).transpose(
        0, 1, 3, 2, 4
    )
    return tile_grid.reshape(4, in_tiles * tile_side, out_tiles * tile_side)


def tile_split(blocks, in_tiles, out_tiles):
    tile_side = blocks.shape[1] // in_tiles
    tile_grid = blocks.reshape(4, in_tiles, tile_side, out_tiles, tile_side).transpose(
        0, 1, 3, 2, 4
    )
    return tile_grid.reshape(4 * in_tiles * out_tiles, tile_side, tile_side)


def block_apply(values, blocks):
    row_view = values.reshape(values.shape[0], 4, -1)
    return jnp.einsum("nbi,bio->nbo", row_view, blocks, preferred_element_type=jnp.float32).reshape(
        values.shape[0], -1
    )


def block_back(gradient, blocks):
    row_view = gradient.reshape(gradient.shape[0], 4, -1)
    return jnp.einsum("nbo,bio->nbi", row_view, blocks, preferred_element_type=jnp.float32).reshape(
        gradient.shape[0], -1
    )


def block_grad(values, gradient, in_tiles, out_tiles):
    left_rows = values.reshape(values.shape[0], 4, -1)
    right_rows = gradient.reshape(gradient.shape[0], 4, -1)
    blocks = jnp.einsum("nbi,nbo->bio", left_rows, right_rows, preferred_element_type=jnp.float32)
    return tile_split(blocks, in_tiles, out_tiles)


def slot_maps(owners, owner_cap, slot_total):
    tile_count = owners.shape[0]
    tile_index = jnp.arange(tile_count, dtype=jnp.int32)
    earlier = (owners[:, None] == owners[None, :]) & (tile_index[None, :] < tile_index[:, None])
    owner_rank = jnp.sum(earlier.astype(jnp.int32), axis=1)
    slot_of_tile = owners * owner_cap + owner_rank
    slot_hits = slot_of_tile[None, :] == jnp.arange(slot_total, dtype=jnp.int32)[:, None]
    tile_of_slot = jnp.sum(slot_hits.astype(jnp.int32) * tile_index[None, :], axis=1)
    slot_used = jnp.any(slot_hits, axis=1)
    return (slot_of_tile, tile_of_slot, slot_used)


def adam_step(weight, moment, second, average, gradient, step_rate, decay_rate):
    moment = beta_one * moment + (1.0 - beta_one) * gradient
    second = beta_two * second + (1.0 - beta_two) * gradient * gradient
    fixed_moment = moment / (1.0 - beta_one**STEP)
    fixed_second = second / (1.0 - beta_two**STEP)
    weight = weight - step_rate * (
        fixed_moment / (jnp.sqrt(fixed_second) + adam_eps) + decay_rate * weight
    )
    average = keep_rate * average + (1.0 - keep_rate) * weight
    return (second, weight, average)


def wave_table(period, index_one, index_two):
    turn_count = jnp.mod(index_one[:, None] * index_two[None, :], period).astype(jnp.float32)
    angles = turn_count * (2.0 * math.pi / period)
    return (jnp.cos(angles), jnp.sin(angles))


def col_dot(field_in, table_in):
    return jnp.einsum("srcd,ck->srkd", field_in, table_in, precision=highest)


def row_dot(field_in, table_in):
    return jnp.einsum("srkd,rq->sqkd", field_in, table_in, precision=highest)


def cols_forward(field_in, tables):
    col_cos, col_sin, turn_cos, turn_sin, row_cos, row_sin = tables
    real_part = col_dot(field_in, col_cos)
    imag_part = -col_dot(field_in, col_sin)
    real_turn = real_part * turn_cos + imag_part * turn_sin
    imag_turn = imag_part * turn_cos - real_part * turn_sin
    return (real_turn, imag_turn)


def rows_forward(part_real, part_imag, tables):
    row_cos, row_sin = (tables[4], tables[5])
    freq_real = row_dot(part_real, row_cos) + row_dot(part_imag, row_sin)
    freq_imag = row_dot(part_imag, row_cos) - row_dot(part_real, row_sin)
    return (freq_real, freq_imag)


def rows_inverse(prod_real, prod_imag, tables):
    row_cos, row_sin = (tables[4], tables[5])
    back_real = row_dot(prod_real, row_cos) - row_dot(prod_imag, row_sin)
    back_imag = row_dot(prod_real, row_sin) + row_dot(prod_imag, row_cos)
    return (back_real, back_imag)


def cols_inverse(rows_real, rows_imag, tables, length):
    col_cos, col_sin, turn_cos, turn_sin, row_cos, row_sin = tables
    cell_real = rows_real * turn_cos - rows_imag * turn_sin
    cell_imag = rows_real * turn_sin + rows_imag * turn_cos
    return (
        jnp.einsum("srkd,ck->srcd", cell_real, col_cos, precision=highest)
        - jnp.einsum("srkd,ck->srcd", cell_imag, col_sin, precision=highest)
    ) / length


def convolve(field_in, spectrum, tables, conjugate, length):
    spec_real, spec_imag = spectrum
    sign_flip = -1.0 if conjugate else 1.0
    real_turn, imag_turn = cols_forward(field_in, tables)
    part_real = lax.all_to_all(real_turn, "seq", split_axis=2, concat_axis=1, tiled=True)
    part_imag = lax.all_to_all(imag_turn, "seq", split_axis=2, concat_axis=1, tiled=True)
    freq_real, freq_imag = rows_forward(part_real, part_imag, tables)
    prod_real = freq_real * spec_real - sign_flip * freq_imag * spec_imag
    prod_imag = sign_flip * freq_real * spec_imag + freq_imag * spec_real
    back_real, back_imag = rows_inverse(prod_real, prod_imag, tables)
    rows_real = lax.all_to_all(back_real, "seq", split_axis=1, concat_axis=2, tiled=True)
    rows_imag = lax.all_to_all(back_imag, "seq", split_axis=1, concat_axis=2, tiled=True)
    rows_real, rows_imag, freq_real, freq_imag = (rows_real, rows_imag, freq_real, freq_imag)
    field_out = cols_inverse(rows_real, rows_imag, tables, length)
    return (field_out, freq_real, freq_imag)


def real_table(grid_rows, row_len):
    length = grid_rows * row_len
    position = (np.arange(grid_rows)[:, None] + grid_rows * np.arange(row_len)[None, :]).reshape(-1)
    turns = np.mod(np.arange(length // 2)[:, None] * position[None, :], length)
    angles = turns * (2.0 * np.pi / length)
    sines = -np.sin(angles)
    sines[0] = np.cos(np.pi * position)
    return np.concatenate([np.cos(angles), sines]).astype(ml_dtypes.bfloat16)


def on_device_general(
    tokens,
    cotangent,
    owners,
    tile_master,
    tile_moment,
    tile_second,
    tile_average,
    vectors,
    vector_moment,
    vector_second,
    vector_average,
    filter_in,
    in_moment,
    in_second,
    in_average,
    filter_out,
    out_moment,
    out_second,
    out_average,
):
    seq_count, dev_rows, row_len, model_width = tokens.shape
    owner_cap = tile_master.shape[0]
    seq_devices = lax.axis_size("seq")
    grid_rows = dev_rows * seq_devices
    length = grid_rows * row_len
    seq_index = lax.axis_index("seq")
    hidden_ratio = FF // D
    quarter_hidden = FF // 4
    slot_of_tile, tile_of_slot, slot_used = slot_maps(owners, owner_cap, owner_cap * seq_devices)
    gathered = lax.all_gather(tile_master.astype(jnp.bfloat16), "seq", axis=0, tiled=True)
    weights = jnp.take(gathered, slot_of_tile, axis=0)
    w_in = block_weight(weights[0:12], 1, 3)
    w_out = block_weight(weights[12:16], 1, 1)
    w_gate = block_weight(weights[16 : 16 + 4 * hidden_ratio], 1, hidden_ratio)
    w_up = block_weight(weights[16 + 4 * hidden_ratio : 16 + 8 * hidden_ratio], 1, hidden_ratio)
    w_down = block_weight(weights[16 + 8 * hidden_ratio : 16 + 12 * hidden_ratio], hidden_ratio, 1)
    w_gate_up = jnp.concatenate([w_gate, w_up], axis=2)
    col_index = jnp.arange(row_len, dtype=jnp.int32)
    row_index = jnp.arange(grid_rows, dtype=jnp.int32)
    local_rows = seq_index * dev_rows + jnp.arange(dev_rows, dtype=jnp.int32)
    col_cos, col_sin = wave_table(row_len, col_index, col_index)
    row_cos, row_sin = wave_table(grid_rows, row_index, row_index)
    turn_cos, turn_sin = wave_table(length, local_rows, col_index)
    tables = (
        col_cos,
        col_sin,
        turn_cos[None, :, :, None],
        turn_sin[None, :, :, None],
        row_cos,
        row_sin,
    )
    own_position = (
        (local_rows[:, None] + grid_rows * col_index[None, :]).reshape(-1).astype(jnp.float32)
    )
    flat_tokens = tokens.reshape(-1, model_width)
    qkv_all = block_apply(flat_tokens, w_in)
    query_part = qkv_all[:, :model_width]
    key_part = qkv_all[:, model_width : 2 * model_width]
    value_part = qkv_all[:, 2 * model_width :]
    kv_product = key_part * value_part

    def own_taps(weight_one, weight_two):
        return filter_taps(weight_one, weight_two, own_position, length)

    taps_own, filter_pull = jax.vjp(own_taps, filter_in, filter_out)
    taps_real, taps_imag = cols_forward(taps_own.reshape(1, dev_rows, row_len, model_width), tables)
    taps_real, taps_imag = (
        lax.all_to_all(taps_real, "seq", split_axis=2, concat_axis=1, tiled=True),
        lax.all_to_all(taps_imag, "seq", split_axis=2, concat_axis=1, tiled=True),
    )
    spec_real, spec_imag = rows_forward(taps_real, taps_imag, tables)
    taps_spec = (spec_real[0], spec_imag[0])
    conv_out, kv_real, kv_imag = convolve(
        kv_product.reshape(seq_count, dev_rows, row_len, model_width),
        taps_spec,
        tables,
        False,
        length,
    )
    skip_gain = vectors[4]
    inner_sum = conv_out.reshape(-1, model_width) + skip_gain * kv_product
    gated_out = (query_part * inner_sum).astype(jnp.bfloat16)
    branch = block_apply(gated_out, w_out)
    normed, first_pull = jax.vjp(
        norm_rows, flat_tokens.astype(jnp.float32) + branch, vectors[0], vectors[1]
    )
    normed_low = normed.astype(jnp.bfloat16)
    gate_up = block_apply(normed_low, w_gate_up).reshape(-1, 4, 2, quarter_hidden)
    gate_value = gate_up[:, :, 0].reshape(-1, FF)
    up_value = gate_up[:, :, 1].reshape(-1, FF)
    active, active_pull = jax.vjp(glu_act, gate_value, up_value)
    active_low = active.astype(jnp.bfloat16)
    down_value = block_apply(active_low, w_down)
    result, second_pull = jax.vjp(
        norm_rows, normed_low.astype(jnp.float32) + down_value, vectors[2], vectors[3]
    )
    output = result.astype(jnp.bfloat16).reshape(tokens.shape)
    d_second, d_gain_two, d_bias_two = second_pull(
        cotangent.reshape(-1, model_width).astype(jnp.float32)
    )
    d_down = d_second.astype(jnp.bfloat16)
    g_down = block_grad(active_low, d_down, hidden_ratio, 1)
    d_gate, d_up = active_pull(block_back(d_down, w_down))
    d_gate_up = jnp.stack(
        [d_gate.reshape(-1, 4, quarter_hidden), d_up.reshape(-1, 4, quarter_hidden)], axis=2
    )
    d_gate_up = d_gate_up.reshape(-1, 2 * FF).astype(jnp.bfloat16)
    gate_up_tiles = block_grad(normed_low, d_gate_up, 1, 2 * hidden_ratio).reshape(
        4, 2, hidden_ratio, weights.shape[1], weights.shape[2]
    )
    g_gate = gate_up_tiles[:, 0].reshape(-1, weights.shape[1], weights.shape[2])
    g_up = gate_up_tiles[:, 1].reshape(-1, weights.shape[1], weights.shape[2])
    d_normed = d_second + block_back(d_gate_up, w_gate_up)
    d_first, d_gain_one, d_bias_one = first_pull(d_normed)
    d_branch = d_first.astype(jnp.bfloat16)
    g_out = block_grad(gated_out, d_branch, 1, 1)
    d_gated = block_back(d_branch, w_out)
    d_query = d_gated * inner_sum
    d_inner = d_gated * query_part
    d_skip = jnp.sum(d_inner * kv_product, axis=0)
    d_conv, back_real, back_imag = convolve(
        d_inner.reshape(seq_count, dev_rows, row_len, model_width), taps_spec, tables, True, length
    )
    d_kv = d_conv.reshape(-1, model_width) + skip_gain * d_inner
    d_qkv = jnp.concatenate([d_query, d_kv * value_part, d_kv * key_part], axis=1).astype(
        jnp.bfloat16
    )
    g_in = block_grad(flat_tokens, d_qkv, 1, 3)
    in_grad = (d_first + block_back(d_qkv, w_in)).reshape(tokens.shape)
    cross_real = jnp.sum(back_real * kv_real + back_imag * kv_imag, axis=0, keepdims=True)
    cross_imag = jnp.sum(back_imag * kv_real - back_real * kv_imag, axis=0, keepdims=True)
    cross_back_real, cross_back_imag = rows_inverse(cross_real, cross_imag, tables)
    cross_rows_real, cross_rows_imag = (
        lax.all_to_all(
            cross_back_real.astype(jnp.bfloat16), "seq", split_axis=1, concat_axis=2, tiled=True
        ).astype(cross_back_real.dtype),
        lax.all_to_all(
            cross_back_imag.astype(jnp.bfloat16), "seq", split_axis=1, concat_axis=2, tiled=True
        ).astype(cross_back_imag.dtype),
    )
    d_taps = cols_inverse(cross_rows_real, cross_rows_imag, tables, length).reshape(-1, model_width)
    g_filter_in, g_filter_out = filter_pull(d_taps)
    tile_grads = jnp.concatenate([g_in, g_out, g_gate, g_up, g_down], axis=0)
    slot_mask = slot_used.astype(jnp.float32)[:, None, None]
    summed = lax.psum(tile_grads.astype(jnp.bfloat16), "dp").astype(jnp.float32)
    owned = lax.psum_scatter(
        jnp.take(summed, tile_of_slot, axis=0) * slot_mask, "seq", scatter_dimension=0, tiled=True
    )
    tokens_all = seq_count * dev_rows * row_len * lax.axis_size("dp") * seq_devices
    grad_scale = 1.0 / math.sqrt(tokens_all)
    mine_mask = lax.dynamic_slice_in_dim(slot_mask, seq_index * owner_cap, owner_cap, 0)
    tile_grad = owned * grad_scale
    tile_new = adam_step(tile_master, tile_moment, tile_second, tile_average, tile_grad, 0.1, 0.01)
    vector_part = jnp.stack([d_gain_one, d_bias_one, d_gain_two, d_bias_two, d_skip])
    vector_sum, in_sum, out_sum = lax.psum((vector_part, g_filter_in, g_filter_out), ("dp", "seq"))
    vector_grad = vector_sum * grad_scale
    in_grad_filter = in_sum * grad_scale
    out_grad_filter = out_sum * grad_scale
    vector_new = adam_step(
        vectors, vector_moment, vector_second, vector_average, vector_grad, 0.4, 0.0
    )
    in_new = adam_step(filter_in, in_moment, in_second, in_average, in_grad_filter, 0.4, 0.01)
    out_new = adam_step(filter_out, out_moment, out_second, out_average, out_grad_filter, 0.1, 0.01)
    return (
        output,
        in_grad,
        tile_grad,
        tile_new[0] * mine_mask,
        tile_new[1] * mine_mask,
        tile_new[2] * mine_mask,
        vector_grad,
        vector_new[0],
        vector_new[1],
        vector_new[2],
        in_grad_filter,
        in_new[0],
        in_new[1],
        in_new[2],
        out_grad_filter,
        out_new[0],
        out_new[1],
        out_new[2],
    )


MESH = pl.DeviceIdType.MESH
VMEM_LIMIT = 56 * 2**20


def flip(index, bits):
    at = 1
    result = index
    while at <= bits:
        if bits & at:
            result = result + at - 2 * at * lax.rem(lax.div(index, at), 2)
        at *= 2
    return result


class Links:
    def __init__(self, send_sem, recv_sem):
        self.send_sem, self.recv_sem, self.used = send_sem, recv_sem, 0
        self.dp, self.seq = lax.axis_index("dp"), lax.axis_index("seq")
        self.deep = lax.axis_size("seq") // 2
        self.z, self.core = lax.div(self.seq, 2), lax.rem(self.seq, 2)
        self.partner = (self.dp, self.seq + 1 - 2 * self.core)
        low, high = lax.rem(self.dp, 2), lax.div(self.dp, 2)
        across_x = self.dp + 1 - 2 * low
        across_y = self.dp + 2 - 4 * high
        self.near = across_x + self.core * (across_y - across_x)
        self.far = across_y + self.core * (across_x - across_y)
        self.diagonal = 3 - self.dp
        self.to_near, self.to_far = (self.near, self.seq), (self.far, self.seq)
        self.outer = lax.div(self.z, self.deep // 2)
        self.inner = 1 - self.outer
        self.to_inner = (self.dp, self.seq + 2 - 4 * self.outer)
        self.to_outer = (self.dp, self.seq - 2 + 4 * self.outer)
        self.at_end = (self.z == 0) | (self.z == self.deep - 1)

    def meet(self):
        barrier = pltpu.get_barrier_semaphore()
        peers = [(self.dp, flip(self.seq, bits)) for bits in range(1, 2 * self.deep)]
        peers += [self.to_near, self.to_far]
        for peer in peers:
            pl.semaphore_signal(barrier, inc=1, device_id=peer, device_id_type=MESH)
        pl.semaphore_wait(barrier, len(peers))

    def copy(self, source, target, device):
        at = self.used
        self.used += 1
        return pltpu.make_async_remote_copy(
            src_ref=source,
            dst_ref=target,
            send_sem=self.send_sem.at[at],
            recv_sem=self.recv_sem.at[at],
            device_id=device,
            device_id_type=MESH,
        )


class Chain:
    def __init__(self, links, base, arrived, leaving, send_sem, recv_sem, chunks):
        self.links, self.base, self.arrived, self.leaving = links, base, arrived, leaving
        self.send_sem, self.recv_sem, self.chunks = send_sem, recv_sem, chunks

    def send(self, k, side, device):
        at = self.chunks[k]
        return pltpu.make_async_remote_copy(
            src_ref=self.leaving.at[side, :, at],
            dst_ref=self.arrived.at[1 - side, :, at],
            send_sem=self.send_sem.at[side, k],
            recv_sem=self.recv_sem.at[1 - side, k],
            device_id=device,
            device_id_type=MESH,
        )

    def receive(self, k, side, device):
        at = self.chunks[k]
        return pltpu.make_async_remote_copy(
            src_ref=self.leaving.at[side, :, at],
            dst_ref=self.arrived.at[side, :, at],
            send_sem=self.send_sem.at[side, k],
            recv_sem=self.recv_sem.at[side, k],
            device_id=device,
            device_id_type=MESH,
        )

    def read(self, ref, k, *side):
        return ref[(*side, slice(None), self.chunks[k])].astype(jnp.float32)

    def begin(self, k):
        links, at = self.links, self.chunks[k]

        @pl.when(links.at_end)
        def _():
            own = self.base[:, at].astype(self.leaving.dtype)
            self.leaving[links.inner, :, at] = own
            self.arrived[links.outer, :, at] = jnp.zeros_like(own)
            self.send(k, links.inner, links.to_inner).start()

    def outward(self, k):
        links, at = self.links, self.chunks[k]

        @pl.when(jnp.logical_not(links.at_end))
        def _():
            self.receive(k, links.outer, links.to_outer).wait_recv()
            total = self.read(self.base, k) + self.read(self.arrived, k, links.outer)
            self.leaving[links.inner, :, at] = total.astype(self.leaving.dtype)
            self.send(k, links.inner, links.to_inner).start()

    def inward(self, k):
        links, at = self.links, self.chunks[k]
        self.receive(k, links.inner, links.to_inner).wait_recv()
        total = self.read(self.base, k) + self.read(self.arrived, k, links.inner)

        @pl.when(jnp.logical_not(links.at_end))
        def _():
            self.leaving[links.outer, :, at] = total.astype(self.leaving.dtype)
            self.send(k, links.outer, links.to_outer).start()

        return total + self.read(self.arrived, k, links.outer)

    def finish(self, k):
        links = self.links
        self.send(k, links.inner, links.to_inner).wait_send()

        @pl.when(jnp.logical_not(links.at_end))
        def _():
            self.send(k, links.outer, links.to_outer).wait_send()


def cut(*edges):
    return tuple(pl.ds(a, b - a) for a, b in zip(edges[:-1], edges[1:]))


def half_tiles(half):
    order = []
    for first, per_block in ((0, 3), (12, 1), (16, 4), (32, 4), (48, 4)):
        order += range(first + 2 * half * per_block, first + 2 * (half + 1) * per_block)
    return order


VMEM = pl.BlockSpec(memory_space=pltpu.VMEM)
SMEM = pl.BlockSpec(memory_space=pltpu.SMEM)
NN = (((1,), (0,)), ((), ()))
NT = (((1,), (1,)), ((), ()))
TN = (((0,), (0,)), ((), ()))


def mul(left, right, dims=NN):
    return lax.dot_general(left, right, dims, preferred_element_type=jnp.float32)


def plain_call(kernel, name, out_shape, scratch=(), in_specs=None):
    def call(*arrays):
        return pl.pallas_call(
            kernel,
            out_shape=out_shape,
            in_specs=[VMEM] * len(arrays) if in_specs is None else in_specs,
            out_specs=jax.tree.map(lambda _: VMEM, out_shape),
            scratch_shapes=list(scratch),
            compiler_params=pltpu.CompilerParams(vmem_limit_bytes=VMEM_LIMIT),
            name=name,
        )(*arrays)

    return call


def filter_constants(grid_rows, row_len, width):
    length = grid_rows * row_len
    position = (np.arange(grid_rows)[:, None] + grid_rows * np.arange(row_len)[None, :]).reshape(-1)
    turn = 2.0 * np.pi * position / length
    rows = [position / length, np.cos(turn), -np.sin(turn), np.cos(2 * turn), -np.sin(2 * turn)]
    features = np.zeros((length, 8), np.float32)
    features[:, :5] = np.stack(rows, axis=1)
    rate = 0.3 * 1000.0 ** np.mod(golden * np.arange(width), 1.0)
    total = np.expm1(-2.0 * rate) / np.expm1(-2.0 * rate / length)
    channels = np.stack([rate, 1.0 / np.sqrt(total)]).astype(np.float32)
    return (features, channels)


def phases_of(features, filter_in):
    total = features[:, 0:1] * filter_in[0:1, :]
    for i in range(1, filter_in.shape[0]):
        total += features[:, i : i + 1] * filter_in[i : i + 1, :]
    return total


def first_row(shape):
    return lax.broadcasted_iota(jnp.int32, shape, 0) == 0


def spectrum_product(one_real, one_imag, two_real, two_imag, sign):
    first = first_row(one_real.shape)
    cross = jnp.where(first, 0.0, two_imag) * sign
    diag = jnp.where(first, two_imag, two_real)
    return (one_real * two_real - one_imag * cross, one_real * cross + one_imag * diag)


def decay_of(features, channels, lanes):
    return jnp.exp(-features[:, 0:1] * channels[0:1, lanes]) * channels[1:2, lanes]


def half_lanes(width):
    half = lax.rem(lax.axis_index("seq"), 2)
    return pl.ds(pl.multiple_of(half * width, width), width)


def conv_back_kernel(
    cells,
    table,
    table_back,
    taps_spec,
    kv_spec,
    features,
    channels,
    filter_in,
    filter_out,
    out,
    grad_out,
    grad_in,
):
    low = jnp.bfloat16
    length, width = kv_spec.shape
    half = length // 2
    columns = cells[...].reshape(length, width)
    back_real, back_imag = mul(table[:half], columns), mul(table[half:], columns)
    real, imag = spectrum_product(back_real, back_imag, taps_spec[:half], taps_spec[half:], -1.0)
    result = mul(table_back[:, :half], real.astype(low)) + mul(table_back[:, half:], imag.astype(low))
    out[...] = result.astype(out.dtype).reshape(out.shape)
    scale = jnp.where(first_row((half, 1)), 1.0 / length, 2.0 / length)
    real, imag = spectrum_product(back_real, back_imag, kv_spec[:half], kv_spec[half:], -1.0)
    real, imag = (real * scale).astype(low), (imag * scale).astype(low)
    d_taps = mul(table_back[:, :half], real) + mul(table_back[:, half:], imag)
    lanes = half_lanes(width)
    scaled = (d_taps * decay_of(features, channels, lanes)).astype(low)
    phases = phases_of(features[...], filter_in[...])
    grad_out[...] = mul(jnp.sin(phases).astype(low), scaled, TN)
    d_hidden = mul(scaled, filter_out[:, lanes].astype(low), NT) * jnp.cos(phases)
    grad_in[...] = jnp.zeros_like(grad_in)
    for i in range(filter_in.shape[0]):
        grad_in[i : i + 1, :] = jnp.sum(features[:, i : i + 1] * d_hidden, axis=0, keepdims=True)


def tile_at(packed, half, first):
    return packed[half, :, first : first + packed.shape[1]]


def normalize(values):
    centered = values - jnp.mean(values, axis=-1, keepdims=True)
    spread = lax.rsqrt(jnp.mean(centered * centered, axis=-1, keepdims=True) + norm_eps)
    return (centered * spread, spread)


def normalize_back(gradient, unit, spread):
    mean = jnp.mean(gradient, axis=-1, keepdims=True)
    along = jnp.mean(gradient * unit, axis=-1, keepdims=True)
    return (gradient - mean - unit * along) * spread


def gelu_parts(v):
    share = 0.5 + 0.5 * lax.erf(v * math.sqrt(0.5))
    density = jnp.exp(-0.5 * v * v) * (1.0 / math.sqrt(2.0 * math.pi))
    return (v * share, share + v * density)


def layer_kernel(
    conv,
    query,
    kv,
    x,
    cotangent,
    vectors,
    packed,
    output,
    d_first_out,
    d_inner_out,
    d_query,
    grads,
    sums,
    gated_all,
    normed_all,
    d_branch_all,
    d_down_all,
    active_all,
    d_gate_all,
    d_up_all,
    down_weights,
):
    wide, low = jnp.float32, jnp.bfloat16
    side = packed.shape[1]
    row_len, width = conv.shape[1:]
    tokens = x.shape[0]
    per_step = 2
    rows_step = per_step * row_len
    quarter = 4 * side
    gain_one, bias_one = vectors[0:1], vectors[1:2]
    gain_two, bias_two = vectors[2:3], vectors[3:4]
    skip = vectors[4:5]
    out_at, gate_at, up_at, down_at = 6 * side, 8 * side, 16 * side, 24 * side
    for b in range(4):
        for i in range(4):
            down_weights[b, i * side : (i + 1) * side, :] = tile_at(
                packed, b // 2, down_at + (4 * (b % 2) + i) * side
            )
    sums[...] = jnp.zeros_like(sums)

    def cells(ref, step):
        parts = ref[pl.ds(step * 2 * per_step, 2 * per_step)].astype(wide)
        lines = [
            jnp.concatenate([parts[2 * s], parts[2 * s + 1]], axis=1) for s in range(per_step)
        ]
        return jnp.concatenate(lines, axis=0)

    def block(values, b):
        return values[:, b * side : (b + 1) * side]

    def add_sum(row, values):
        sums[row : row + 1, :] += jnp.sum(values, axis=0, keepdims=True)

    @pl.loop(0, tokens // rows_step)
    def _(step):
        rows = pl.ds(pl.multiple_of(step * rows_step, rows_step), rows_step)
        kv_here = cells(kv, step)
        inner = cells(conv, step) + skip * kv_here
        query_here = query[rows, :].astype(wide)
        gated = (query_here * inner).astype(low)
        gated_all[rows, :] = gated
        branch = jnp.concatenate(
            [
                mul(block(gated, b), tile_at(packed, b // 2, out_at + (b % 2) * side))
                for b in range(4)
            ],
            axis=1,
        )
        unit_one, spread_one = normalize(x[rows, :].astype(wide) + branch)
        normed = (unit_one * gain_one + bias_one).astype(low)
        normed_all[rows, :] = normed
        down = []
        for b in range(4):
            lanes = slice(b * quarter, (b + 1) * quarter)
            at = (b % 2) * quarter
            here = block(normed, b)
            gate = mul(here, packed[b // 2, :, gate_at + at : gate_at + at + quarter])
            up = mul(here, packed[b // 2, :, up_at + at : up_at + at + quarter])
            curved, slope = gelu_parts(gate)
            active = (curved * up).astype(low)
            active_all[rows, lanes] = active
            d_gate_all[rows, lanes] = (slope * up).astype(low)
            d_up_all[rows, lanes] = curved.astype(low)
            down.append(mul(active, down_weights[b]))
        unit_two, spread_two = normalize(normed.astype(wide) + jnp.concatenate(down, axis=1))
        output[rows, :] = (unit_two * gain_two + bias_two).astype(low)
        cot = cotangent[rows, :].astype(wide)
        add_sum(2, cot * unit_two)
        add_sum(3, cot)
        d_second = normalize_back(cot * gain_two, unit_two, spread_two)
        d_down = d_second.astype(low)
        d_down_all[rows, :] = d_down
        d_normed = []
        for b in range(4):
            lanes = slice(b * quarter, (b + 1) * quarter)
            at = (b % 2) * quarter
            d_active = mul(block(d_down, b), down_weights[b], NT)
            d_gate = (d_active * d_gate_all[rows, lanes].astype(wide)).astype(low)
            d_up = (d_active * d_up_all[rows, lanes].astype(wide)).astype(low)
            d_gate_all[rows, lanes] = d_gate
            d_up_all[rows, lanes] = d_up
            d_normed.append(
                mul(d_gate, packed[b // 2, :, gate_at + at : gate_at + at + quarter], NT)
                + mul(d_up, packed[b // 2, :, up_at + at : up_at + at + quarter], NT)
            )
        d_normed = d_second + jnp.concatenate(d_normed, axis=1)
        add_sum(0, d_normed * unit_one)
        add_sum(1, d_normed)
        d_first = normalize_back(d_normed * gain_one, unit_one, spread_one)
        d_first_out[rows, :] = d_first
        d_branch = d_first.astype(low)
        d_branch_all[rows, :] = d_branch
        d_gated = jnp.concatenate(
            [
                mul(block(d_branch, b), tile_at(packed, b // 2, out_at + (b % 2) * side), NT)
                for b in range(4)
            ],
            axis=1,
        )
        d_query[rows, :] = (d_gated * inner).astype(low)
        d_inner = d_gated * query_here
        add_sum(4, d_inner * kv_here)
        d_inner = d_inner.astype(low)
        for s in range(per_step):
            for h in range(2):
                d_inner_out[2 * (step * per_step + s) + h] = d_inner[
                    s * row_len : (s + 1) * row_len, h * width : (h + 1) * width
                ]

    for b in range(4):
        lanes = slice(b * quarter, (b + 1) * quarter)
        at = (b % 2) * quarter
        half = b // 2
        mine = slice(b * side, (b + 1) * side)

        def put(first, values):
            first -= out_at
            grads[half, :, first : first + values.shape[1]] = values.astype(low)

        put(out_at + (b % 2) * side, mul(gated_all[:, mine], d_branch_all[:, mine], TN))
        put(gate_at + at, mul(normed_all[:, mine], d_gate_all[:, lanes], TN))
        put(up_at + at, mul(normed_all[:, mine], d_up_all[:, lanes], TN))
        tall = mul(active_all[:, lanes], d_down_all[:, mine], TN)
        for i in range(4):
            put(down_at + at + i * side, tall[i * side : (i + 1) * side, :])


def layer_call(conv, query, kv, x, cotangent, vectors, packed):
    tokens, model = x.shape
    _, side, width = packed.shape
    low = jnp.bfloat16
    shape = jax.ShapeDtypeStruct
    hidden = 16 * side
    return plain_call(
        layer_kernel,
        "layer",
        (
            shape((tokens, model), low),
            shape((tokens, model), jnp.float32),
            shape(kv.shape, low),
            shape((tokens, model), low),
            shape((2, side, width - 6 * side), low),
            shape((8, model), jnp.float32),
        ),
        [pltpu.VMEM((tokens, model), low)] * 4
        + [pltpu.VMEM((tokens, hidden), low)] * 3
        + [pltpu.VMEM((4, 4 * side, side), low)],
    )(conv, query, kv, x, cotangent, vectors, packed)


def input_kernel(d_conv, d_inner, d_query, key, value, x, d_first, vectors, packed, in_grad, grads, d_qkv):
    wide, low = jnp.float32, jnp.bfloat16
    side = packed.shape[1]
    row_len, width = d_conv.shape[1:]
    model = x.shape[1]
    d_qkv[:, :model] = d_query[...]
    for s in range(d_conv.shape[0] // 2):
        rows = slice(s * row_len, (s + 1) * row_len)
        for h in range(2):
            lanes = slice(h * width, (h + 1) * width)
            cell = 2 * s + h
            d_kv = d_conv[cell].astype(wide) + vectors[4:5, lanes] * d_inner[cell].astype(wide)
            d_qkv[rows, model + h * width : model + (h + 1) * width] = (
                d_kv * value[rows, lanes].astype(wide)
            ).astype(low)
            d_qkv[rows, 2 * model + h * width : 2 * model + (h + 1) * width] = (
                d_kv * key[rows, lanes].astype(wide)
            ).astype(low)
    per_block = 3 * side
    for b in range(4):
        mine = slice(b * side, (b + 1) * side)
        here = d_qkv[:, b * per_block : (b + 1) * per_block]
        at = (b % 2) * per_block
        weights = packed[b // 2, :, at : at + per_block]
        in_grad[:, mine] = d_first[:, mine] + mul(here, weights, NT)
        grads[b // 2, :, at : at + per_block] = mul(x[:, mine], here, TN).astype(low)


def adam(weight, moment, second, average, gradient, rate, decay):
    moment = beta_one * moment + (1.0 - beta_one) * gradient
    second = beta_two * second + (1.0 - beta_two) * gradient * gradient
    moment = moment * (1.0 / (1.0 - beta_one**STEP))
    root = jnp.sqrt(second * (1.0 / (1.0 - beta_two**STEP)))
    weight = weight - rate * (moment / (root + adam_eps) + decay * weight)
    return (second, weight, keep_rate * average + (1.0 - keep_rate) * weight)


def adam_kernel(scale, used, reduced, extra, *refs):
    step = pl.program_id(0)
    per_step, side, _ = refs[0].shape
    tile_in, small_in, tile_out, small_out = refs[:4], refs[4:16], refs[16:20], refs[20:32]
    for k in range(per_step):
        keep = used[step * per_step + k] > 0
        gradient = reduced[:, k * side : (k + 1) * side].astype(jnp.float32) * scale
        tile_out[0][k] = gradient
        fresh = adam(*(ref[k] for ref in tile_in), gradient, 0.1, 0.01)
        for ref, values in zip(tile_out[1:], fresh):
            ref[k] = jnp.where(keep, values, 0.0)

    @pl.when(step == 0)
    def _():
        order, model = small_in[8].shape
        width = model // 2
        count = small_in[0].shape[0]
        features = small_in[4].shape[0]
        sums = extra[...].astype(jnp.float32) * scale
        both = (sums[:, :width], sums[:, width:])
        first = order + 8
        gradients = (
            jnp.concatenate([part[order : order + count] for part in both], axis=1),
            both[0][first : first + features, :order],
            jnp.concatenate([part[:order] for part in both], axis=1),
        )
        rates = ((0.4, 0.0), (0.4, 0.01), (0.1, 0.01))
        for i, (gradient, rate) in enumerate(zip(gradients, rates)):
            small_out[4 * i][...] = gradient
            fresh = adam(*(ref[...] for ref in small_in[4 * i : 4 * i + 4]), gradient, *rate)
            for ref, values in zip(small_out[4 * i + 1 : 4 * i + 4], fresh):
                ref[...] = values


def adam_call(scale, used, reduced, tile_state, small_state):
    slots, side, _ = tile_state[0].shape
    model = small_state[0].shape[1]
    per_step = 2
    tile = pl.BlockSpec((per_step, side, side), lambda i: (i, 0, 0))
    small = [pl.BlockSpec(a.shape, lambda i: (0, 0)) for a in small_state]
    shape = jax.ShapeDtypeStruct
    return pl.pallas_call(
        functools.partial(adam_kernel, scale),
        grid=(slots // per_step,),
        out_shape=tuple(shape(a.shape, a.dtype) for a in tile_state + small_state),
        in_specs=[
            SMEM,
            pl.BlockSpec((side, per_step * side), lambda i: (0, i)),
            pl.BlockSpec((side, model), lambda i: (0, slots * side // model)),
        ]
        + [tile] * 4
        + small,
        out_specs=[tile] * 4 + small,
        compiler_params=pltpu.CompilerParams(vmem_limit_bytes=VMEM_LIMIT),
        name="adam",
    )(used, reduced, reduced, *tile_state, *small_state)


class Exchange:
    def __init__(self, links, cells, columns, send_sem, recv_sem):
        self.links, self.cells, self.columns = links, cells, columns
        self.send_sem, self.recv_sem = send_sem, recv_sem

    def copy(self, bits):
        links = self.links
        peer = flip(links.seq, bits)
        return pltpu.make_async_remote_copy(
            src_ref=self.cells.at[peer],
            dst_ref=self.columns.at[links.seq],
            send_sem=self.send_sem.at[bits],
            recv_sem=self.recv_sem.at[bits],
            device_id=(links.dp, peer),
            device_id_type=MESH,
        )

    def send(self, *bits):
        for b in bits:
            if b == 0:
                me = self.links.seq
                self.columns[me] = self.cells[me]
            else:
                self.copy(b).start()

    def arrived(self, *bits):
        for b in bits:
            if b:
                peer = flip(self.links.seq, b)
                pltpu.make_async_remote_copy(
                    src_ref=self.cells.at[peer],
                    dst_ref=self.columns.at[peer],
                    send_sem=self.send_sem.at[b],
                    recv_sem=self.recv_sem.at[b],
                    device_id=(self.links.dp, peer),
                    device_id_type=MESH,
                ).wait_recv()

    def sent(self):
        for b in range(1, self.cells.shape[0]):
            self.copy(b).wait_send()


def columns_of_chip(columns, chip):
    pair = columns[pl.ds(2 * chip, 2)]
    return pair.reshape(2 * pair.shape[1], pair.shape[2])


def transform_arrivals(exchange, table, spec):
    step = 2 * exchange.columns.shape[1]
    for near in range(exchange.links.deep):
        exchange.arrived(2 * near, 2 * near + 1)
        chip = flip(exchange.links.z, near)
        lanes = pl.ds(pl.multiple_of(chip * step, step), step)
        part = mul(table[:, lanes], columns_of_chip(exchange.columns, chip))
        if near:
            spec[...] += part
        else:
            spec[...] = part


def send_inverse(exchange, table_back, filtered):
    row_len = exchange.cells.shape[1]
    for near in reversed(range(exchange.links.deep)):
        chip = flip(exchange.links.z, near)
        rows = pl.ds(pl.multiple_of(chip * 2 * row_len, 2 * row_len), 2 * row_len)
        part = mul(table_back[rows, :], filtered[...]).astype(exchange.cells.dtype)
        exchange.cells[pl.ds(2 * chip, 2)] = part.reshape(2, row_len, part.shape[1])
        exchange.send(2 * near, 2 * near + 1)


def forward_kernel(
    chunks,
    first_chunks,
    owners,
    master,
    x,
    features,
    channels,
    filter_in,
    filter_out,
    table_hbm,
    table_back_hbm,
    full,
    query,
    key,
    value,
    kv,
    conv,
    taps_spec,
    kv_spec,
    own,
    got,
    base,
    arrived,
    leaving,
    table,
    table_back,
    hidden,
    taps,
    columns,
    filtered,
    cells_back,
    table_sem,
    send_sem,
    recv_sem,
    chain_send,
    chain_recv,
    field_send,
    field_recv,
    back_send,
    back_recv,
):
    low, wide = jnp.bfloat16, jnp.float32
    links = Links(send_sem, recv_sem)
    loads = (
        pltpu.make_async_copy(table_hbm, table, table_sem.at[0]),
        pltpu.make_async_copy(table_back_hbm, table_back, table_sem.at[1]),
    )
    for load in loads:
        load.start()
    quarter = full.shape[1] // 4
    tile_count, side = owners.shape[0], master.shape[2]
    most = master.shape[0] - 1
    rows = pl.ds(pl.multiple_of(links.dp * quarter, quarter), quarter)
    near_rows = pl.ds(pl.multiple_of(links.near * quarter, quarter), quarter)
    rank, place = jnp.int32(0), []
    for i in range(tile_count):
        mine = owners[i] == links.seq
        place.append((jnp.minimum(rank, most), mine))
        rank = rank + jnp.where(mine, 1, 0)
    for half in range(2):
        order = half_tiles(half)
        for j in range(0, len(order), 2):
            pair = []
            for i in order[j : j + 2]:
                at, mine = place[i]
                pair.append(jnp.where(mine, master[at, rows, :], 0.0))
            own[half, :, j * side : (j + 2) * side] = jnp.concatenate(pair, axis=1).astype(own.dtype)
    links.meet()
    swaps, planes = [], []
    for at in chunks:
        swaps.append(
            links.copy(own.at[1 - links.core, :, at], got.at[:, at], links.partner)
        )
        mine = full.at[links.core, rows, at]
        other = full.at[links.core, near_rows, at]
        both = full.at[links.core, :, at]
        planes.append(
            (
                links.copy(mine, mine, links.to_near),
                links.copy(mine, mine, links.to_far),
                links.copy(other, other, links.to_far),
                links.copy(both, both, links.partner),
            )
        )
        swaps[-1].start()
    chain = Chain(links, base, arrived, leaving, chain_send, chain_recv, chunks)
    length, width = kv_spec.shape
    lanes = half_lanes(width)
    half_length = length // 2

    def hidden_step():
        hidden[...] = jnp.sin(phases_of(features[...], filter_in[...])).astype(low)

    def taps_step(part):
        span = slice(part * length // 4, (part + 1) * length // 4)
        decay = jnp.exp(-features[span, 0:1] * channels[0:1, lanes]) * channels[1:2, lanes]
        values = mul(hidden[span, :], filter_out[:, lanes].astype(low))
        taps[span, :] = (values * decay).astype(low)

    def spectrum_step(part):
        span = slice(part * length // 4, (part + 1) * length // 4)
        scale = jnp.where(first_row((length // 4, 1)), 1.0 / length, 2.0 / length)
        if part % 2:
            scale = 2.0 / length
        taps_spec[span, :] = mul(table[span, :], taps[...]) * scale

    def wait_table():
        loads[0].wait()

    fill = [hidden_step]
    fill += [functools.partial(taps_step, i) for i in range(4)]
    fill += [wait_table]
    fill += [functools.partial(spectrum_step, i) for i in range(4)]
    fill.reverse()

    def fill_in(steps=1):
        for _ in range(steps):
            if fill:
                fill.pop()()

    def collect(k):
        at = chunks[k]
        swaps[k].wait()
        base[:, at] = own[links.core, :, at] + got[:, at]
        chain.begin(k)

    def spread(k):
        full[links.core, rows, chunks[k]] = chain.inward(k).astype(full.dtype)
        planes[k][0].start()
        planes[k][1].start()

    def relay(k):
        planes[k][0].wait_recv()
        planes[k][2].start()

    def share(k):
        planes[k][1].wait_recv()
        planes[k][2].wait_recv()
        planes[k][3].start()

    count = len(chunks)
    fill_in(1)
    for k in range(count):
        collect(k)
    stages = ((chain.outward, 0), (spread, 1), (relay, 2), (share, 4))
    steps = [
        [(stage, k - late) for stage, late in stages if 0 <= k - late < count]
        for k in range(count + 4)
    ]
    before, after = steps[: first_chunks + 4], steps[first_chunks + 4 :]
    for step in before:
        fill_in(2)
        for stage, k in step:
            stage(k)
    for k in range(first_chunks):
        planes[k][3].wait_recv()
    fill_in(len(fill))

    row_len = kv.shape[1]
    seqs = kv.shape[0] // 2
    outbound = Exchange(links, kv, columns, field_send, field_recv)
    for pair, bits in ((links.inner, (6, 7, 4, 5)), (links.outer, (2, 3, 1, 0))):
        span = pl.ds(pl.multiple_of(pair * (seqs // 2) * row_len, row_len), seqs // 2 * row_len)
        for i in range(12):
            block = i // 3
            part = mul(x[span, block * side : (block + 1) * side], tile_at(full, i // 6, (i % 6) * side))
            target = (query, key, value)[i // 4]
            at = (i % 4) * side
            target[span, at : at + side] = part.astype(target.dtype)
        for s in range(seqs // 2):
            line = pl.ds(pl.multiple_of((pair * (seqs // 2) + s) * row_len, row_len), row_len)
            for h in range(2):
                part = slice(h * width, (h + 1) * width)
                both = key[line, part].astype(wide) * value[line, part].astype(wide)
                kv[2 * (pair * (seqs // 2) + s) + h] = both.astype(kv.dtype)
        outbound.send(*bits)
    for step in after:
        for stage, k in step:
            stage(k)
    transform_arrivals(outbound, table, kv_spec)
    real, imag = spectrum_product(
        kv_spec[:half_length],
        kv_spec[half_length:],
        taps_spec[:half_length],
        taps_spec[half_length:],
        1.0,
    )
    filtered[:half_length] = real.astype(low)
    filtered[half_length:] = imag.astype(low)
    loads[1].wait()
    inbound = Exchange(links, cells_back, conv, back_send, back_recv)
    send_inverse(inbound, table_back, filtered)
    for k in range(count):
        chain.finish(k)
        for copy in planes[k]:
            copy.wait_send()
        if k >= first_chunks:
            planes[k][3].wait_recv()
    outbound.sent()
    inbound.arrived(*range(1, 2 * seqs))
    inbound.sent()


def forward_call(owners, master, x, features, channels, filter_in, filter_out, table, table_back, cells):
    slots, side, _ = master.shape
    width = owners.shape[0] // 2 * side
    chunks = cut(0, 640, 1152, 2816, 4480, width)
    low, wide = jnp.bfloat16, jnp.float32
    quarter = side // 4
    count = len(chunks)
    devices, row_len, columns = cells
    length = devices * row_len
    shape = jax.ShapeDtypeStruct
    anywhere = pl.BlockSpec(memory_space=pl.ANY)
    spec = shape((length, columns), wide)
    rows = shape(x.shape, low)
    return pl.pallas_call(
        functools.partial(forward_kernel, chunks, 2),
        out_shape=(
            shape((2, side, width), low),
            rows,
            rows,
            rows,
            shape(cells, low),
            shape(cells, low),
            spec,
            spec,
        ),
        in_specs=[SMEM] + [VMEM] * 6 + [anywhere] * 2,
        out_specs=(VMEM,) * 8,
        scratch_shapes=[
            pltpu.VMEM((2, quarter, width), low),
            pltpu.VMEM((quarter, width), low),
            pltpu.VMEM((quarter, width), low),
            pltpu.VMEM((2, quarter, width), low),
            pltpu.VMEM((2, quarter, width), low),
            pltpu.VMEM((length, length), low),
            pltpu.VMEM((length, length), low),
            pltpu.VMEM((length, filter_in.shape[1]), low),
            pltpu.VMEM((length, columns), low),
            pltpu.VMEM(cells, low),
            pltpu.VMEM((length, columns), low),
            pltpu.VMEM(cells, low),
            pltpu.SemaphoreType.DMA((2,)),
            pltpu.SemaphoreType.DMA((5 * count,)),
            pltpu.SemaphoreType.DMA((5 * count,)),
            pltpu.SemaphoreType.DMA((2, count)),
            pltpu.SemaphoreType.DMA((2, count)),
        ]
        + [pltpu.SemaphoreType.DMA((devices,))] * 4,
        compiler_params=pltpu.CompilerParams(
            collective_id=0, has_side_effects=True, vmem_limit_bytes=VMEM_LIMIT
        ),
        name="forward",
    )(owners, master, x, features, channels, filter_in, filter_out, table, table_back)


def reduce_kernel(
    chunks,
    tile_of_slot,
    used,
    grads,
    spread,
    mine_sum,
    got,
    near_in,
    far_in,
    far_out,
    base,
    arrived,
    leaving,
    total,
    by_tile,
    send_sem,
    recv_sem,
    chain_send,
    chain_recv,
):
    links = Links(send_sem, recv_sem)
    side = grads.shape[1]
    quarter = side // 4
    wide = jnp.float32

    def rows_of(index):
        return pl.ds(pl.multiple_of(index * quarter, quarter), quarter)

    links.meet()
    swaps, nears, diagonals, fars, shares = [], [], [], [], []
    for at in chunks:
        swaps.append(links.copy(grads.at[1 - links.core, :, at], got.at[:, at], links.partner))
        swaps[-1].start()
        nears.append(
            links.copy(mine_sum.at[rows_of(links.near), at], near_in.at[0, :, at], links.to_near)
        )
        diagonals.append(
            links.copy(
                mine_sum.at[rows_of(links.diagonal), at], near_in.at[1, :, at], links.to_near
            )
        )
        fars.append(links.copy(far_out.at[:, at], far_in.at[:, at], links.to_far))
        part = total.at[links.core, :, at]
        shares.append(links.copy(part, part, links.partner))
    chain = Chain(links, base, arrived, leaving, chain_send, chain_recv, chunks)

    def merge_cores(k):
        at = chunks[k]
        swaps[k].wait()
        mine_sum[:, at] = (
            grads[links.core, :, at].astype(wide) + got[:, at].astype(wide)
        ).astype(mine_sum.dtype)
        diagonals[k].start()
        nears[k].start()

    def go_far(k):
        at = chunks[k]
        diagonals[k].wait_recv()
        far_out[:, at] = (
            mine_sum[rows_of(links.far), at].astype(wide) + near_in[1, :, at].astype(wide)
        ).astype(far_out.dtype)
        fars[k].start()

    def collect(k):
        at = chunks[k]
        nears[k].wait_recv()
        fars[k].wait_recv()
        base[:, at] = (
            mine_sum[rows_of(links.dp), at].astype(wide)
            + near_in[0, :, at].astype(wide)
            + far_in[:, at].astype(wide)
        )
        chain.begin(k)

    def end(k):
        total[links.core, :, chunks[k]] = chain.inward(k).astype(total.dtype)
        shares[k].start()

    count = len(chunks)
    for k in range(count + 4):
        stages = ((merge_cores, 0), (go_far, 1), (collect, 2), (chain.outward, 3), (end, 4))
        for stage, late in stages:
            if 0 <= k - late < count:
                stage(k - late)
    for share in shares:
        share.wait()
    for half in range(2):
        for j, i in enumerate(half_tiles(half)):
            by_tile[i] = total[half, :, j * side : (j + 1) * side].astype(wide)
    slots = tile_of_slot.shape[0]
    tiles_wide = slots * side
    mine = rows_of(links.dp)
    for s in range(0, slots, 2):
        pair = [jnp.where(used[k] > 0, by_tile[tile_of_slot[k]], 0.0) for k in (s, s + 1)]
        spread[mine, s * side : (s + 2) * side] = jnp.concatenate(pair, axis=1).astype(spread.dtype)
    first_extra = by_tile.shape[0] // 2 * side
    extra = total.shape[2] - first_extra
    for half in range(2):
        begin = tiles_wide + half * extra
        spread[mine, begin : begin + extra] = total[half, :, first_extra:]
    at_home, other = spread.at[mine, :], spread.at[rows_of(links.near), :]
    first = links.copy(at_home, at_home, links.to_near)
    second = links.copy(at_home, at_home, links.to_far)
    relay = links.copy(other, other, links.to_far)
    first.start()
    second.start()
    first.wait_recv()
    relay.start()
    second.wait_recv()
    relay.wait()
    first.wait_send()
    second.wait_send()
    for k in range(count):
        nears[k].wait_send()
        diagonals[k].wait_send()
        fars[k].wait_send()
        chain.finish(k)


def reduce_grads(tile_of_slot, used, grads):
    _, side, width = grads.shape
    slots = tile_of_slot.shape[0]
    extra = width - NTILES // 2 * side
    chunks = cut(0, 1152, 2304, 3456, 4480, 5504, width)
    low = jnp.bfloat16
    quarter = side // 4
    count = len(chunks)
    return pl.pallas_call(
        functools.partial(reduce_kernel, chunks),
        out_shape=jax.ShapeDtypeStruct((side, slots * side + 2 * extra), low),
        in_specs=[
            pl.BlockSpec(memory_space=pltpu.SMEM),
            pl.BlockSpec(memory_space=pltpu.SMEM),
            pl.BlockSpec(memory_space=pltpu.VMEM),
        ],
        out_specs=pl.BlockSpec(memory_space=pltpu.VMEM),
        scratch_shapes=[
            pltpu.VMEM((side, width), low),
            pltpu.VMEM((side, width), low),
            pltpu.VMEM((2, quarter, width), low),
            pltpu.VMEM((quarter, width), low),
            pltpu.VMEM((quarter, width), low),
            pltpu.VMEM((quarter, width), jnp.float32),
            pltpu.VMEM((2, quarter, width), low),
            pltpu.VMEM((2, quarter, width), low),
            pltpu.VMEM((2, quarter, width), low),
            pltpu.VMEM((NTILES, quarter, side), jnp.float32),
            pltpu.SemaphoreType.DMA((5 * count + 3,)),
            pltpu.SemaphoreType.DMA((5 * count + 3,)),
            pltpu.SemaphoreType.DMA((2, count)),
            pltpu.SemaphoreType.DMA((2, count)),
        ],
        compiler_params=pltpu.CompilerParams(
            collective_id=1, has_side_effects=True, vmem_limit_bytes=VMEM_LIMIT
        ),
        name="reduce_grads",
    )(tile_of_slot, used, grads)


def on_device_columns(
    tokens,
    cotangent,
    owners,
    tile_master,
    tile_moment,
    tile_second,
    tile_average,
    vectors,
    vector_moment,
    vector_second,
    vector_average,
    filter_in,
    in_moment,
    in_second,
    in_average,
    filter_out,
    out_moment,
    out_second,
    out_average,
):
    seq_count, dev_rows, row_len, model_width = tokens.shape
    owner_cap, side, _ = tile_master.shape
    seq_devices = lax.axis_size("seq")
    grid_rows = dev_rows * seq_devices
    length = grid_rows * row_len
    seq_index = lax.axis_index("seq")
    width = model_width // 2
    low, wide = jnp.bfloat16, jnp.float32
    shape = jax.ShapeDtypeStruct
    count = seq_count * row_len
    order = filter_in.shape[1]
    table_host = real_table(grid_rows, row_len)
    table, table_back = jnp.asarray(table_host), jnp.asarray(np.ascontiguousarray(table_host.T))
    features, channels = (
        jnp.asarray(a) for a in filter_constants(grid_rows, row_len, model_width)
    )
    slot_of_tile, tile_of_slot, slot_used = slot_maps(owners, owner_cap, owner_cap * seq_devices)
    first_slot = seq_index * owner_cap
    own_tile = lax.dynamic_slice_in_dim(tile_of_slot, first_slot, owner_cap, 0)
    own_used = lax.dynamic_slice_in_dim(slot_used.astype(jnp.int32), first_slot, owner_cap, 0)
    x = tokens.reshape(count, model_width)
    cell_shape = (seq_devices, row_len, width)

    def exchange(cells):
        return lax.all_to_all(cells, "seq", 0, 0, tiled=True)

    packed, query, key, value, kv, conv, taps_spec, kv_spec = forward_call(
        owners,
        tile_master,
        x,
        features,
        channels,
        filter_in,
        filter_out,
        table,
        table_back,
        cell_shape,
    )
    output, d_first, d_inner, d_query, grads, sums = layer_call(
        conv, query, kv, x, cotangent.reshape(count, model_width), vectors, packed
    )
    d_conv, grad_out, grad_in = plain_call(
        conv_back_kernel,
        "conv_back",
        (shape(cell_shape, low), shape((order, width), wide), shape((8, order), wide)),
    )(
        exchange(d_inner),
        table,
        table_back,
        taps_spec,
        kv_spec,
        features,
        channels,
        filter_in,
        filter_out,
    )
    in_grad, grads_in = plain_call(
        input_kernel,
        "input_grad",
        (shape(x.shape, wide), shape((2, side, 6 * side), low)),
        [pltpu.VMEM((count, 3 * model_width), low)],
    )(exchange(d_conv), d_inner, d_query, key, value, x, d_first, vectors, packed)
    both = jnp.zeros((2, side, width), wide)
    both = lax.dynamic_update_slice(both, grad_out[None], (lax.rem(seq_index, 2), 0, 0))
    both = lax.dynamic_update_slice(
        both, sums.reshape(8, 2, width).transpose(1, 0, 2), (0, order, 0)
    )
    both = lax.dynamic_update_slice(both, grad_in[None], (0, order + 8, 0))
    packed_grads = jnp.concatenate([grads_in, grads, both.astype(low)], axis=2)
    reduced = reduce_grads(own_tile, own_used, packed_grads)
    tokens_all = count * lax.axis_size("dp") * seq_devices
    updated = adam_call(
        1.0 / math.sqrt(tokens_all),
        own_used,
        reduced,
        (tile_master, tile_moment, tile_second, tile_average),
        (
            vectors,
            vector_moment,
            vector_second,
            vector_average,
            filter_in,
            in_moment,
            in_second,
            in_average,
            filter_out,
            out_moment,
            out_second,
            out_average,
        ),
    )
    return (output.reshape(tokens.shape), in_grad.reshape(tokens.shape), *updated)


def on_device(*arrays):
    seq_count, dev_rows, row_len, model_width = arrays[0].shape
    seq_devices = lax.axis_size("seq")
    fits = dev_rows == 1 and lax.axis_size("dp") == 4 and seq_devices == 2 * seq_count == 8
    if fits and row_len == 128 and model_width % 256 == 0:
        return on_device_columns(*arrays)
    return on_device_general(*arrays)


def solution(mesh):
    in_specs = (
        P("dp", "seq", None, None),
        P("dp", "seq", None, None),
        P(),
        P("seq", None, None),
        P("seq", None, None),
        P("seq", None, None),
        P("seq", None, None),
        P(),
        P(),
        P(),
        P(),
        P(),
        P(),
        P(),
        P(),
        P(),
        P(),
        P(),
        P(),
    )
    out_specs = (
        P("dp", "seq", None, None),
        P("dp", "seq", None, None),
        P("seq", None, None),
        P("seq", None, None),
        P("seq", None, None),
        P("seq", None, None),
        P(),
        P(),
        P(),
        P(),
        P(),
        P(),
        P(),
        P(),
        P(),
        P(),
        P(),
        P(),
    )
    return jax.shard_map(
        on_device, mesh=mesh, in_specs=in_specs, out_specs=out_specs, check_vma=False
    )
```

```python
import functools
import math

import jax
import jax.numpy as jnp
import ml_dtypes
import numpy as np
from jax import lax
from jax.experimental import pallas as pl
from jax.experimental.pallas import tpu as pltpu
from jax.sharding import PartitionSpec as P

D = 768
FF = 3072
STEP = 10
NTILES = 64


highest = lax.Precision.HIGHEST
beta_one = 0.9
beta_two = 0.999
keep_rate = 0.5
adam_eps = 1e-08
norm_eps = 1e-05
golden = 0.6180339887


def norm_rows(values, gain_vec, bias_vec):
    row_mean = jnp.mean(values, axis=-1, keepdims=True)
    centered = values - row_mean
    spread = jnp.mean(centered * centered, axis=-1, keepdims=True)
    return centered * lax.rsqrt(spread + norm_eps) * gain_vec + bias_vec


def glu_act(gate_value, up_value):
    return jax.nn.gelu(gate_value, approximate=False) * up_value


def filter_taps(filter_in, filter_out, position, length):
    channel = jnp.arange(filter_out.shape[1], dtype=jnp.int32)
    return filter_taps_of(filter_in, filter_out, position, length, channel)


def filter_taps_of(filter_in, filter_out, position, length, channel_index):
    phases = position * (2.0 * math.pi / length)
    features = jnp.stack(
        [
            position / length,
            jnp.cos(phases),
            -jnp.sin(phases),
            jnp.cos(2.0 * phases),
            -jnp.sin(2.0 * phases),
        ],
        axis=1,
    )
    hidden = jnp.sin(jnp.dot(features, filter_in, precision=highest))
    taps_value = jnp.dot(hidden, filter_out, precision=highest)
    channel = channel_index.astype(jnp.float32)
    decay_rates = 0.3 * jnp.exp(math.log(1000.0) * jnp.mod(channel * golden, 1.0))
    decay_rate = jnp.exp(-(position / length)[:, None] * decay_rates[None, :])
    total = jnp.expm1(-2.0 * decay_rates) / jnp.expm1(-2.0 * decay_rates / length)
    norm_scale = lax.rsqrt(total)
    return taps_value * decay_rate * norm_scale


def block_weight(tile_stack, in_tiles, out_tiles):
    tile_side = tile_stack.shape[-1]
    tile_grid = tile_stack.reshape(4, in_tiles, out_tiles, tile_side, tile_side).transpose(
        0, 1, 3, 2, 4
    )
    return tile_grid.reshape(4, in_tiles * tile_side, out_tiles * tile_side)


def tile_split(blocks, in_tiles, out_tiles):
    tile_side = blocks.shape[1] // in_tiles
    tile_grid = blocks.reshape(4, in_tiles, tile_side, out_tiles, tile_side).transpose(
        0, 1, 3, 2, 4
    )
    return tile_grid.reshape(4 * in_tiles * out_tiles, tile_side, tile_side)


def block_apply(values, blocks):
    row_view = values.reshape(values.shape[0], 4, -1)
    return jnp.einsum("nbi,bio->nbo", row_view, blocks, preferred_element_type=jnp.float32).reshape(
        values.shape[0], -1
    )


def block_back(gradient, blocks):
    row_view = gradient.reshape(gradient.shape[0], 4, -1)
    return jnp.einsum("nbo,bio->nbi", row_view, blocks, preferred_element_type=jnp.float32).reshape(
        gradient.shape[0], -1
    )


def block_grad(values, gradient, in_tiles, out_tiles):
    left_rows = values.reshape(values.shape[0], 4, -1)
    right_rows = gradient.reshape(gradient.shape[0], 4, -1)
    blocks = jnp.einsum("nbi,nbo->bio", left_rows, right_rows, preferred_element_type=jnp.float32)
    return tile_split(blocks, in_tiles, out_tiles)


def slot_maps(owners, owner_cap, slot_total):
    tile_count = owners.shape[0]
    tile_index = jnp.arange(tile_count, dtype=jnp.int32)
    earlier = (owners[:, None] == owners[None, :]) & (tile_index[None, :] < tile_index[:, None])
    owner_rank = jnp.sum(earlier.astype(jnp.int32), axis=1)
    slot_of_tile = owners * owner_cap + owner_rank
    slot_hits = slot_of_tile[None, :] == jnp.arange(slot_total, dtype=jnp.int32)[:, None]
    tile_of_slot = jnp.sum(slot_hits.astype(jnp.int32) * tile_index[None, :], axis=1)
    slot_used = jnp.any(slot_hits, axis=1)
    return (slot_of_tile, tile_of_slot, slot_used)


def adam_step(weight, moment, second, average, gradient, step_rate, decay_rate):
    moment = beta_one * moment + (1.0 - beta_one) * gradient
    second = beta_two * second + (1.0 - beta_two) * gradient * gradient
    fixed_moment = moment / (1.0 - beta_one**STEP)
    fixed_second = second / (1.0 - beta_two**STEP)
    weight = weight - step_rate * (
        fixed_moment / (jnp.sqrt(fixed_second) + adam_eps) + decay_rate * weight
    )
    average = keep_rate * average + (1.0 - keep_rate) * weight
    return (second, weight, average)


def wave_table(period, index_one, index_two):
    turn_count = jnp.mod(index_one[:, None] * index_two[None, :], period).astype(jnp.float32)
    angles = turn_count * (2.0 * math.pi / period)
    return (jnp.cos(angles), jnp.sin(angles))


def col_dot(field_in, table_in):
    return jnp.einsum("srcd,ck->srkd", field_in, table_in, precision=highest)


def row_dot(field_in, table_in):
    return jnp.einsum("srkd,rq->sqkd", field_in, table_in, precision=highest)


def cols_forward(field_in, tables):
    col_cos, col_sin, turn_cos, turn_sin, row_cos, row_sin = tables
    real_part = col_dot(field_in, col_cos)
    imag_part = -col_dot(field_in, col_sin)
    real_turn = real_part * turn_cos + imag_part * turn_sin
    imag_turn = imag_part * turn_cos - real_part * turn_sin
    return (real_turn, imag_turn)


def rows_forward(part_real, part_imag, tables):
    row_cos, row_sin = (tables[4], tables[5])
    freq_real = row_dot(part_real, row_cos) + row_dot(part_imag, row_sin)
    freq_imag = row_dot(part_imag, row_cos) - row_dot(part_real, row_sin)
    return (freq_real, freq_imag)


def rows_inverse(prod_real, prod_imag, tables):
    row_cos, row_sin = (tables[4], tables[5])
    back_real = row_dot(prod_real, row_cos) - row_dot(prod_imag, row_sin)
    back_imag = row_dot(prod_real, row_sin) + row_dot(prod_imag, row_cos)
    return (back_real, back_imag)


def cols_inverse(rows_real, rows_imag, tables, length):
    col_cos, col_sin, turn_cos, turn_sin, row_cos, row_sin = tables
    cell_real = rows_real * turn_cos - rows_imag * turn_sin
    cell_imag = rows_real * turn_sin + rows_imag * turn_cos
    return (
        jnp.einsum("srkd,ck->srcd", cell_real, col_cos, precision=highest)
        - jnp.einsum("srkd,ck->srcd", cell_imag, col_sin, precision=highest)
    ) / length


def convolve(field_in, spectrum, tables, conjugate, length):
    spec_real, spec_imag = spectrum
    sign_flip = -1.0 if conjugate else 1.0
    real_turn, imag_turn = cols_forward(field_in, tables)
    part_real = lax.all_to_all(real_turn, "seq", split_axis=2, concat_axis=1, tiled=True)
    part_imag = lax.all_to_all(imag_turn, "seq", split_axis=2, concat_axis=1, tiled=True)
    freq_real, freq_imag = rows_forward(part_real, part_imag, tables)
    prod_real = freq_real * spec_real - sign_flip * freq_imag * spec_imag
    prod_imag = sign_flip * freq_real * spec_imag + freq_imag * spec_real
    back_real, back_imag = rows_inverse(prod_real, prod_imag, tables)
    rows_real = lax.all_to_all(back_real, "seq", split_axis=1, concat_axis=2, tiled=True)
    rows_imag = lax.all_to_all(back_imag, "seq", split_axis=1, concat_axis=2, tiled=True)
    rows_real, rows_imag, freq_real, freq_imag = (rows_real, rows_imag, freq_real, freq_imag)
    field_out = cols_inverse(rows_real, rows_imag, tables, length)
    return (field_out, freq_real, freq_imag)


def real_table(grid_rows, row_len):
    length = grid_rows * row_len
    position = (np.arange(grid_rows)[:, None] + grid_rows * np.arange(row_len)[None, :]).reshape(-1)
    turns = np.mod(np.arange(length // 2)[:, None] * position[None, :], length)
    angles = turns * (2.0 * np.pi / length)
    sines = -np.sin(angles)
    sines[0] = np.cos(np.pi * position)
    return np.concatenate([np.cos(angles), sines]).astype(ml_dtypes.bfloat16)


def on_device_general(
    tokens,
    cotangent,
    owners,
    tile_master,
    tile_moment,
    tile_second,
    tile_average,
    vectors,
    vector_moment,
    vector_second,
    vector_average,
    filter_in,
    in_moment,
    in_second,
    in_average,
    filter_out,
    out_moment,
    out_second,
    out_average,
):
    seq_count, dev_rows, row_len, model_width = tokens.shape
    owner_cap = tile_master.shape[0]
    seq_devices = lax.axis_size("seq")
    grid_rows = dev_rows * seq_devices
    length = grid_rows * row_len
    seq_index = lax.axis_index("seq")
    hidden_ratio = FF // D
    quarter_hidden = FF // 4
    slot_of_tile, tile_of_slot, slot_used = slot_maps(owners, owner_cap, owner_cap * seq_devices)
    gathered = lax.all_gather(tile_master.astype(jnp.bfloat16), "seq", axis=0, tiled=True)
    weights = jnp.take(gathered, slot_of_tile, axis=0)
    w_in = block_weight(weights[0:12], 1, 3)
    w_out = block_weight(weights[12:16], 1, 1)
    w_gate = block_weight(weights[16 : 16 + 4 * hidden_ratio], 1, hidden_ratio)
    w_up = block_weight(weights[16 + 4 * hidden_ratio : 16 + 8 * hidden_ratio], 1, hidden_ratio)
    w_down = block_weight(weights[16 + 8 * hidden_ratio : 16 + 12 * hidden_ratio], hidden_ratio, 1)
    w_gate_up = jnp.concatenate([w_gate, w_up], axis=2)
    col_index = jnp.arange(row_len, dtype=jnp.int32)
    row_index = jnp.arange(grid_rows, dtype=jnp.int32)
    local_rows = seq_index * dev_rows + jnp.arange(dev_rows, dtype=jnp.int32)
    col_cos, col_sin = wave_table(row_len, col_index, col_index)
    row_cos, row_sin = wave_table(grid_rows, row_index, row_index)
    turn_cos, turn_sin = wave_table(length, local_rows, col_index)
    tables = (
        col_cos,
        col_sin,
        turn_cos[None, :, :, None],
        turn_sin[None, :, :, None],
        row_cos,
        row_sin,
    )
    own_position = (
        (local_rows[:, None] + grid_rows * col_index[None, :]).reshape(-1).astype(jnp.float32)
    )
    flat_tokens = tokens.reshape(-1, model_width)
    qkv_all = block_apply(flat_tokens, w_in)
    query_part = qkv_all[:, :model_width]
    key_part = qkv_all[:, model_width : 2 * model_width]
    value_part = qkv_all[:, 2 * model_width :]
    kv_product = key_part * value_part

    def own_taps(weight_one, weight_two):
        return filter_taps(weight_one, weight_two, own_position, length)

    taps_own, filter_pull = jax.vjp(own_taps, filter_in, filter_out)
    taps_real, taps_imag = cols_forward(taps_own.reshape(1, dev_rows, row_len, model_width), tables)
    taps_real, taps_imag = (
        lax.all_to_all(taps_real, "seq", split_axis=2, concat_axis=1, tiled=True),
        lax.all_to_all(taps_imag, "seq", split_axis=2, concat_axis=1, tiled=True),
    )
    spec_real, spec_imag = rows_forward(taps_real, taps_imag, tables)
    taps_spec = (spec_real[0], spec_imag[0])
    conv_out, kv_real, kv_imag = convolve(
        kv_product.reshape(seq_count, dev_rows, row_len, model_width),
        taps_spec,
        tables,
        False,
        length,
    )
    skip_gain = vectors[4]
    inner_sum = conv_out.reshape(-1, model_width) + skip_gain * kv_product
    gated_out = (query_part * inner_sum).astype(jnp.bfloat16)
    branch = block_apply(gated_out, w_out)
    normed, first_pull = jax.vjp(
        norm_rows, flat_tokens.astype(jnp.float32) + branch, vectors[0], vectors[1]
    )
    normed_low = normed.astype(jnp.bfloat16)
    gate_up = block_apply(normed_low, w_gate_up).reshape(-1, 4, 2, quarter_hidden)
    gate_value = gate_up[:, :, 0].reshape(-1, FF)
    up_value = gate_up[:, :, 1].reshape(-1, FF)
    active, active_pull = jax.vjp(glu_act, gate_value, up_value)
    active_low = active.astype(jnp.bfloat16)
    down_value = block_apply(active_low, w_down)
    result, second_pull = jax.vjp(
        norm_rows, normed_low.astype(jnp.float32) + down_value, vectors[2], vectors[3]
    )
    output = result.astype(jnp.bfloat16).reshape(tokens.shape)
    d_second, d_gain_two, d_bias_two = second_pull(
        cotangent.reshape(-1, model_width).astype(jnp.float32)
    )
    d_down = d_second.astype(jnp.bfloat16)
    g_down = block_grad(active_low, d_down, hidden_ratio, 1)
    d_gate, d_up = active_pull(block_back(d_down, w_down))
    d_gate_up = jnp.stack(
        [d_gate.reshape(-1, 4, quarter_hidden), d_up.reshape(-1, 4, quarter_hidden)], axis=2
    )
    d_gate_up = d_gate_up.reshape(-1, 2 * FF).astype(jnp.bfloat16)
    gate_up_tiles = block_grad(normed_low, d_gate_up, 1, 2 * hidden_ratio).reshape(
        4, 2, hidden_ratio, weights.shape[1], weights.shape[2]
    )
    g_gate = gate_up_tiles[:, 0].reshape(-1, weights.shape[1], weights.shape[2])
    g_up = gate_up_tiles[:, 1].reshape(-1, weights.shape[1], weights.shape[2])
    d_normed = d_second + block_back(d_gate_up, w_gate_up)
    d_first, d_gain_one, d_bias_one = first_pull(d_normed)
    d_branch = d_first.astype(jnp.bfloat16)
    g_out = block_grad(gated_out, d_branch, 1, 1)
    d_gated = block_back(d_branch, w_out)
    d_query = d_gated * inner_sum
    d_inner = d_gated * query_part
    d_skip = jnp.sum(d_inner * kv_product, axis=0)
    d_conv, back_real, back_imag = convolve(
        d_inner.reshape(seq_count, dev_rows, row_len, model_width), taps_spec, tables, True, length
    )
    d_kv = d_conv.reshape(-1, model_width) + skip_gain * d_inner
    d_qkv = jnp.concatenate([d_query, d_kv * value_part, d_kv * key_part], axis=1).astype(
        jnp.bfloat16
    )
    g_in = block_grad(flat_tokens, d_qkv, 1, 3)
    in_grad = (d_first + block_back(d_qkv, w_in)).reshape(tokens.shape)
    cross_real = jnp.sum(back_real * kv_real + back_imag * kv_imag, axis=0, keepdims=True)
    cross_imag = jnp.sum(back_imag * kv_real - back_real * kv_imag, axis=0, keepdims=True)
    cross_back_real, cross_back_imag = rows_inverse(cross_real, cross_imag, tables)
    cross_rows_real, cross_rows_imag = (
        lax.all_to_all(
            cross_back_real.astype(jnp.bfloat16), "seq", split_axis=1, concat_axis=2, tiled=True
        ).astype(cross_back_real.dtype),
        lax.all_to_all(
            cross_back_imag.astype(jnp.bfloat16), "seq", split_axis=1, concat_axis=2, tiled=True
        ).astype(cross_back_imag.dtype),
    )
    d_taps = cols_inverse(cross_rows_real, cross_rows_imag, tables, length).reshape(-1, model_width)
    g_filter_in, g_filter_out = filter_pull(d_taps)
    tile_grads = jnp.concatenate([g_in, g_out, g_gate, g_up, g_down], axis=0)
    slot_mask = slot_used.astype(jnp.float32)[:, None, None]
    summed = lax.psum(tile_grads.astype(jnp.bfloat16), "dp").astype(jnp.float32)
    owned = lax.psum_scatter(
        jnp.take(summed, tile_of_slot, axis=0) * slot_mask, "seq", scatter_dimension=0, tiled=True
    )
    tokens_all = seq_count * dev_rows * row_len * lax.axis_size("dp") * seq_devices
    grad_scale = 1.0 / math.sqrt(tokens_all)
    mine_mask = lax.dynamic_slice_in_dim(slot_mask, seq_index * owner_cap, owner_cap, 0)
    tile_grad = owned * grad_scale
    tile_new = adam_step(tile_master, tile_moment, tile_second, tile_average, tile_grad, 0.1, 0.01)
    vector_part = jnp.stack([d_gain_one, d_bias_one, d_gain_two, d_bias_two, d_skip])
    vector_sum, in_sum, out_sum = lax.psum((vector_part, g_filter_in, g_filter_out), ("dp", "seq"))
    vector_grad = vector_sum * grad_scale
    in_grad_filter = in_sum * grad_scale
    out_grad_filter = out_sum * grad_scale
    vector_new = adam_step(
        vectors, vector_moment, vector_second, vector_average, vector_grad, 0.4, 0.0
    )
    in_new = adam_step(filter_in, in_moment, in_second, in_average, in_grad_filter, 0.4, 0.01)
    out_new = adam_step(filter_out, out_moment, out_second, out_average, out_grad_filter, 0.1, 0.01)
    return (
        output,
        in_grad,
        tile_grad,
        tile_new[0] * mine_mask,
        tile_new[1] * mine_mask,
        tile_new[2] * mine_mask,
        vector_grad,
        vector_new[0],
        vector_new[1],
        vector_new[2],
        in_grad_filter,
        in_new[0],
        in_new[1],
        in_new[2],
        out_grad_filter,
        out_new[0],
        out_new[1],
        out_new[2],
    )


MESH = pl.DeviceIdType.MESH
VMEM_LIMIT = 56 * 2**20


def flip(index, bits):
    at = 1
    result = index
    while at <= bits:
        if bits & at:
            result = result + at - 2 * at * lax.rem(lax.div(index, at), 2)
        at *= 2
    return result


class Links:
    def __init__(self, send_sem, recv_sem):
        self.send_sem, self.recv_sem, self.used = send_sem, recv_sem, 0
        self.dp, self.seq = lax.axis_index("dp"), lax.axis_index("seq")
        self.deep = lax.axis_size("seq") // 2
        self.z, self.core = lax.div(self.seq, 2), lax.rem(self.seq, 2)
        self.partner = (self.dp, self.seq + 1 - 2 * self.core)
        low, high = lax.rem(self.dp, 2), lax.div(self.dp, 2)
        across_x = self.dp + 1 - 2 * low
        across_y = self.dp + 2 - 4 * high
        self.near = across_x + self.core * (across_y - across_x)
        self.far = across_y + self.core * (across_x - across_y)
        self.diagonal = 3 - self.dp
        self.to_near, self.to_far = (self.near, self.seq), (self.far, self.seq)
        self.outer = lax.div(self.z, self.deep // 2)
        self.inner = 1 - self.outer
        self.to_inner = (self.dp, self.seq + 2 - 4 * self.outer)
        self.to_outer = (self.dp, self.seq - 2 + 4 * self.outer)
        self.at_end = (self.z == 0) | (self.z == self.deep - 1)

    def meet(self):
        barrier = pltpu.get_barrier_semaphore()
        peers = [(self.dp, flip(self.seq, bits)) for bits in range(1, 2 * self.deep)]
        peers += [self.to_near, self.to_far]
        for peer in peers:
            pl.semaphore_signal(barrier, inc=1, device_id=peer, device_id_type=MESH)
        pl.semaphore_wait(barrier, len(peers))

    def copy(self, source, target, device):
        at = self.used
        self.used += 1
        return pltpu.make_async_remote_copy(
            src_ref=source,
            dst_ref=target,
            send_sem=self.send_sem.at[at],
            recv_sem=self.recv_sem.at[at],
            device_id=device,
            device_id_type=MESH,
        )


class Chain:
    def __init__(self, links, base, arrived, leaving, send_sem, recv_sem, chunks):
        self.links, self.base, self.arrived, self.leaving = links, base, arrived, leaving
        self.send_sem, self.recv_sem, self.chunks = send_sem, recv_sem, chunks

    def send(self, k, side, device):
        at = self.chunks[k]
        return pltpu.make_async_remote_copy(
            src_ref=self.leaving.at[side, :, at],
            dst_ref=self.arrived.at[1 - side, :, at],
            send_sem=self.send_sem.at[side, k],
            recv_sem=self.recv_sem.at[1 - side, k],
            device_id=device,
            device_id_type=MESH,
        )

    def receive(self, k, side, device):
        at = self.chunks[k]
        return pltpu.make_async_remote_copy(
            src_ref=self.leaving.at[side, :, at],
            dst_ref=self.arrived.at[side, :, at],
            send_sem=self.send_sem.at[side, k],
            recv_sem=self.recv_sem.at[side, k],
            device_id=device,
            device_id_type=MESH,
        )

    def read(self, ref, k, *side):
        return ref[(*side, slice(None), self.chunks[k])].astype(jnp.float32)

    def begin(self, k):
        links, at = self.links, self.chunks[k]

        @pl.when(links.at_end)
        def _():
            own = self.base[:, at].astype(self.leaving.dtype)
            self.leaving[links.inner, :, at] = own
            self.arrived[links.outer, :, at] = jnp.zeros_like(own)
            self.send(k, links.inner, links.to_inner).start()

    def outward(self, k):
        links, at = self.links, self.chunks[k]

        @pl.when(jnp.logical_not(links.at_end))
        def _():
            self.receive(k, links.outer, links.to_outer).wait_recv()
            total = self.read(self.base, k) + self.read(self.arrived, k, links.outer)
            self.leaving[links.inner, :, at] = total.astype(self.leaving.dtype)
            self.send(k, links.inner, links.to_inner).start()

    def inward(self, k):
        links, at = self.links, self.chunks[k]
        self.receive(k, links.inner, links.to_inner).wait_recv()
        total = self.read(self.base, k) + self.read(self.arrived, k, links.inner)

        @pl.when(jnp.logical_not(links.at_end))
        def _():
            self.leaving[links.outer, :, at] = total.astype(self.leaving.dtype)
            self.send(k, links.outer, links.to_outer).start()

        return total + self.read(self.arrived, k, links.outer)

    def finish(self, k):
        links = self.links
        self.send(k, links.inner, links.to_inner).wait_send()

        @pl.when(jnp.logical_not(links.at_end))
        def _():
            self.send(k, links.outer, links.to_outer).wait_send()


def cut(*edges):
    return tuple(pl.ds(a, b - a) for a, b in zip(edges[:-1], edges[1:]))


def half_tiles(half):
    order = []
    for first, per_block in ((0, 3), (12, 1), (16, 4), (32, 4), (48, 4)):
        order += range(first + 2 * half * per_block, first + 2 * (half + 1) * per_block)
    return order


VMEM = pl.BlockSpec(memory_space=pltpu.VMEM)
SMEM = pl.BlockSpec(memory_space=pltpu.SMEM)
NN = (((1,), (0,)), ((), ()))
NT = (((1,), (1,)), ((), ()))
TN = (((0,), (0,)), ((), ()))


def mul(left, right, dims=NN):
    return lax.dot_general(left, right, dims, preferred_element_type=jnp.float32)


def plain_call(kernel, name, out_shape, scratch=(), in_specs=None):
    def call(*arrays):
        return pl.pallas_call(
            kernel,
            out_shape=out_shape,
            in_specs=[VMEM] * len(arrays) if in_specs is None else in_specs,
            out_specs=jax.tree.map(lambda _: VMEM, out_shape),
            scratch_shapes=list(scratch),
            compiler_params=pltpu.CompilerParams(vmem_limit_bytes=VMEM_LIMIT),
            name=name,
        )(*arrays)

    return call


def filter_constants(grid_rows, row_len, width):
    length = grid_rows * row_len
    position = (np.arange(grid_rows)[:, None] + grid_rows * np.arange(row_len)[None, :]).reshape(-1)
    turn = 2.0 * np.pi * position / length
    rows = [position / length, np.cos(turn), -np.sin(turn), np.cos(2 * turn), -np.sin(2 * turn)]
    features = np.zeros((length, 8), np.float32)
    features[:, :5] = np.stack(rows, axis=1)
    rate = 0.3 * 1000.0 ** np.mod(golden * np.arange(width), 1.0)
    total = np.expm1(-2.0 * rate) / np.expm1(-2.0 * rate / length)
    channels = np.stack([rate, 1.0 / np.sqrt(total)]).astype(np.float32)
    return (features, channels)


def phases_of(features, filter_in):
    total = features[:, 0:1] * filter_in[0:1, :]
    for i in range(1, filter_in.shape[0]):
        total += features[:, i : i + 1] * filter_in[i : i + 1, :]
    return total


def first_row(shape):
    return lax.broadcasted_iota(jnp.int32, shape, 0) == 0


def spectrum_product(one_real, one_imag, two_real, two_imag, sign):
    first = first_row(one_real.shape)
    cross = jnp.where(first, 0.0, two_imag) * sign
    diag = jnp.where(first, two_imag, two_real)
    return (one_real * two_real - one_imag * cross, one_real * cross + one_imag * diag)


def decay_of(features, channels, lanes):
    return jnp.exp(-features[:, 0:1] * channels[0:1, lanes]) * channels[1:2, lanes]


def half_lanes(width):
    half = lax.rem(lax.axis_index("seq"), 2)
    return pl.ds(pl.multiple_of(half * width, width), width)


def tile_at(packed, half, first):
    return packed[half, :, first : first + packed.shape[1]]


def normalize(values):
    centered = values - jnp.mean(values, axis=-1, keepdims=True)
    spread = lax.rsqrt(jnp.mean(centered * centered, axis=-1, keepdims=True) + norm_eps)
    return (centered * spread, spread)


def normalize_back(gradient, unit, spread):
    mean = jnp.mean(gradient, axis=-1, keepdims=True)
    along = jnp.mean(gradient * unit, axis=-1, keepdims=True)
    return (gradient - mean - unit * along) * spread


def gelu_parts(v):
    share = 0.5 + 0.5 * lax.erf(v * math.sqrt(0.5))
    density = jnp.exp(-0.5 * v * v) * (1.0 / math.sqrt(2.0 * math.pi))
    return (v * share, share + v * density)


def layer_kernel(
    conv,
    query,
    kv,
    x,
    cotangent,
    vectors,
    packed,
    output,
    d_first_out,
    d_inner_out,
    d_query,
    grads,
    sums,
    gated_all,
    normed_all,
    d_branch_all,
    d_down_all,
    active_all,
    d_gate_all,
    d_up_all,
    down_weights,
):
    wide, low = jnp.float32, jnp.bfloat16
    side = packed.shape[1]
    row_len, width = conv.shape[1:]
    tokens = x.shape[0]
    per_step = 2
    rows_step = per_step * row_len
    quarter = 4 * side
    gain_one, bias_one = vectors[0:1], vectors[1:2]
    gain_two, bias_two = vectors[2:3], vectors[3:4]
    skip = vectors[4:5]
    out_at, gate_at, up_at, down_at = 6 * side, 8 * side, 16 * side, 24 * side
    for b in range(4):
        for i in range(4):
            down_weights[b, i * side : (i + 1) * side, :] = tile_at(
                packed, b // 2, down_at + (4 * (b % 2) + i) * side
            )
    sums[...] = jnp.zeros_like(sums)

    def cells(ref, step):
        parts = ref[pl.ds(step * 2 * per_step, 2 * per_step)].astype(wide)
        lines = [
            jnp.concatenate([parts[2 * s], parts[2 * s + 1]], axis=1) for s in range(per_step)
        ]
        return jnp.concatenate(lines, axis=0)

    def block(values, b):
        return values[:, b * side : (b + 1) * side]

    def add_sum(row, values):
        sums[row : row + 1, :] += jnp.sum(values, axis=0, keepdims=True)

    @pl.loop(0, tokens // rows_step)
    def _(step):
        rows = pl.ds(pl.multiple_of(step * rows_step, rows_step), rows_step)
        kv_here = cells(kv, step)
        inner = cells(conv, step) + skip * kv_here
        query_here = query[rows, :].astype(wide)
        gated = (query_here * inner).astype(low)
        gated_all[rows, :] = gated
        branch = jnp.concatenate(
            [
                mul(block(gated, b), tile_at(packed, b // 2, out_at + (b % 2) * side))
                for b in range(4)
            ],
            axis=1,
        )
        unit_one, spread_one = normalize(x[rows, :].astype(wide) + branch)
        normed = (unit_one * gain_one + bias_one).astype(low)
        normed_all[rows, :] = normed
        down = []
        for b in range(4):
            lanes = slice(b * quarter, (b + 1) * quarter)
            at = (b % 2) * quarter
            here = block(normed, b)
            gate = mul(here, packed[b // 2, :, gate_at + at : gate_at + at + quarter])
            up = mul(here, packed[b // 2, :, up_at + at : up_at + at + quarter])
            curved, slope = gelu_parts(gate)
            active = (curved * up).astype(low)
            active_all[rows, lanes] = active
            d_gate_all[rows, lanes] = (slope * up).astype(low)
            d_up_all[rows, lanes] = curved.astype(low)
            down.append(mul(active, down_weights[b]))
        unit_two, spread_two = normalize(normed.astype(wide) + jnp.concatenate(down, axis=1))
        output[rows, :] = (unit_two * gain_two + bias_two).astype(low)
        cot = cotangent[rows, :].astype(wide)
        add_sum(2, cot * unit_two)
        add_sum(3, cot)
        d_second = normalize_back(cot * gain_two, unit_two, spread_two)
        d_down = d_second.astype(low)
        d_down_all[rows, :] = d_down
        d_normed = []
        for b in range(4):
            lanes = slice(b * quarter, (b + 1) * quarter)
            at = (b % 2) * quarter
            d_active = mul(block(d_down, b), down_weights[b], NT)
            d_gate = (d_active * d_gate_all[rows, lanes].astype(wide)).astype(low)
            d_up = (d_active * d_up_all[rows, lanes].astype(wide)).astype(low)
            d_gate_all[rows, lanes] = d_gate
            d_up_all[rows, lanes] = d_up
            d_normed.append(
                mul(d_gate, packed[b // 2, :, gate_at + at : gate_at + at + quarter], NT)
                + mul(d_up, packed[b // 2, :, up_at + at : up_at + at + quarter], NT)
            )
        d_normed = d_second + jnp.concatenate(d_normed, axis=1)
        add_sum(0, d_normed * unit_one)
        add_sum(1, d_normed)
        d_first = normalize_back(d_normed * gain_one, unit_one, spread_one)
        d_first_out[rows, :] = d_first
        d_branch = d_first.astype(low)
        d_branch_all[rows, :] = d_branch
        d_gated = jnp.concatenate(
            [
                mul(block(d_branch, b), tile_at(packed, b // 2, out_at + (b % 2) * side), NT)
                for b in range(4)
            ],
            axis=1,
        )
        d_query[rows, :] = (d_gated * inner).astype(low)
        d_inner = d_gated * query_here
        add_sum(4, d_inner * kv_here)
        d_inner = d_inner.astype(low)
        for s in range(per_step):
            for h in range(2):
                d_inner_out[2 * (step * per_step + s) + h] = d_inner[
                    s * row_len : (s + 1) * row_len, h * width : (h + 1) * width
                ]

    for b in range(4):
        lanes = slice(b * quarter, (b + 1) * quarter)
        at = (b % 2) * quarter
        half = b // 2
        mine = slice(b * side, (b + 1) * side)

        def put(first, values):
            first -= out_at
            grads[half, :, first : first + values.shape[1]] = values.astype(low)

        put(out_at + (b % 2) * side, mul(gated_all[:, mine], d_branch_all[:, mine], TN))
        put(gate_at + at, mul(normed_all[:, mine], d_gate_all[:, lanes], TN))
        put(up_at + at, mul(normed_all[:, mine], d_up_all[:, lanes], TN))
        tall = mul(active_all[:, lanes], d_down_all[:, mine], TN)
        for i in range(4):
            put(down_at + at + i * side, tall[i * side : (i + 1) * side, :])


def layer_call(conv, query, kv, x, cotangent, vectors, packed):
    tokens, model = x.shape
    _, side, width = packed.shape
    low = jnp.bfloat16
    shape = jax.ShapeDtypeStruct
    hidden = 16 * side
    return plain_call(
        layer_kernel,
        "layer",
        (
            shape((tokens, model), low),
            shape((tokens, model), jnp.float32),
            shape(kv.shape, low),
            shape((tokens, model), low),
            shape((2, side, width - 6 * side), low),
            shape((8, model), jnp.float32),
        ),
        [pltpu.VMEM((tokens, model), low)] * 4
        + [pltpu.VMEM((tokens, hidden), low)] * 3
        + [pltpu.VMEM((4, 4 * side, side), low)],
    )(conv, query, kv, x, cotangent, vectors, packed)


def adam(weight, moment, second, average, gradient, rate, decay):
    moment = beta_one * moment + (1.0 - beta_one) * gradient
    second = beta_two * second + (1.0 - beta_two) * gradient * gradient
    moment = moment * (1.0 / (1.0 - beta_one**STEP))
    root = jnp.sqrt(second * (1.0 / (1.0 - beta_two**STEP)))
    weight = weight - rate * (moment / (root + adam_eps) + decay * weight)
    return (second, weight, keep_rate * average + (1.0 - keep_rate) * weight)


def adam_kernel(scale, tile_of_slot, used, reduced, *refs):
    step = pl.program_id(0)
    per_step, side, _ = refs[3].shape
    late, extra, refs = refs[:per_step], refs[per_step], refs[per_step + 1 :]
    tile_in, small_in, tile_out, small_out = refs[:4], refs[4:16], refs[16:20], refs[20:32]
    for k in range(per_step):
        slot = step * per_step + k
        keep, tile = used[slot] > 0, tile_of_slot[slot]
        pair = late[k][0]
        from_late = jnp.where(lax.rem(tile, 2) == 0, pair[:, :side], pair[:, side:])
        gradient = jnp.where(tile < 12, from_late, reduced[:, k * side : (k + 1) * side])
        gradient = jnp.where(keep, gradient.astype(jnp.float32) * scale, 0.0)
        tile_out[0][k] = gradient
        fresh = adam(*(ref[k] for ref in tile_in), gradient, 0.1, 0.01)
        for ref, values in zip(tile_out[1:], fresh):
            ref[k] = jnp.where(keep, values, 0.0)

    @pl.when(step == 0)
    def _():
        order, model = small_in[8].shape
        count = small_in[0].shape[0]
        count_in = small_in[4].shape[0]
        sums = extra[...].astype(jnp.float32) * scale
        gradients = (
            jnp.concatenate([sums[h, order : order + count] for h in range(2)], axis=1),
            sums[0, order + 8 : order + 8 + count_in, :order],
            jnp.concatenate([sums[h, :order] for h in range(2)], axis=1),
        )
        rates = ((0.4, 0.0), (0.4, 0.01), (0.1, 0.01))
        for i, (gradient, rate) in enumerate(zip(gradients, rates)):
            small_out[4 * i][...] = gradient
            fresh = adam(*(ref[...] for ref in small_in[4 * i : 4 * i + 4]), gradient, *rate)
            for ref, values in zip(small_out[4 * i + 1 : 4 * i + 4], fresh):
                ref[...] = values


def adam_call(scale, tile_of_slot, used, reduced, late, tile_state, small_state):
    slots, side, _ = tile_state[0].shape
    width = small_state[0].shape[1] // 2
    per_step = 2
    tile = pl.BlockSpec((per_step, side, side), lambda i, *_: (i, 0, 0))
    small = [pl.BlockSpec(a.shape, lambda i, *_: (0, 0)) for a in small_state]
    shape = jax.ShapeDtypeStruct

    def late_block(k):
        def place(i, tiles, _):
            at = jnp.minimum(tiles[i * per_step + k], 11)
            return (at // 6, 0, at % 6 // 2)

        return pl.BlockSpec((1, side, 2 * side), place)

    first_extra = 6 * side // width
    return pl.pallas_call(
        functools.partial(adam_kernel, scale),
        out_shape=tuple(shape(a.shape, a.dtype) for a in tile_state + small_state),
        grid_spec=pltpu.PrefetchScalarGridSpec(
            num_scalar_prefetch=2,
            grid=(slots // per_step,),
            in_specs=[pl.BlockSpec((side, per_step * side), lambda i, *_: (0, i))]
            + [late_block(k) for k in range(per_step)]
            + [pl.BlockSpec((2, side, width), lambda i, *_: (0, 0, first_extra))]
            + [tile] * 4
            + small,
            out_specs=[tile] * 4 + small,
        ),
        compiler_params=pltpu.CompilerParams(vmem_limit_bytes=VMEM_LIMIT),
        name="adam",
    )(tile_of_slot, used, reduced, *(late,) * per_step, late, *tile_state, *small_state)


class Exchange:
    def __init__(self, links, cells, columns, send_sem, recv_sem):
        self.links, self.cells, self.columns = links, cells, columns
        self.send_sem, self.recv_sem = send_sem, recv_sem

    def copy(self, bits):
        links = self.links
        peer = flip(links.seq, bits)
        return pltpu.make_async_remote_copy(
            src_ref=self.cells.at[peer],
            dst_ref=self.columns.at[links.seq],
            send_sem=self.send_sem.at[bits],
            recv_sem=self.recv_sem.at[bits],
            device_id=(links.dp, peer),
            device_id_type=MESH,
        )

    def send(self, *bits):
        for b in bits:
            if b == 0:
                me = self.links.seq
                self.columns[me] = self.cells[me]
            else:
                self.copy(b).start()

    def arrived(self, *bits):
        for b in bits:
            if b:
                peer = flip(self.links.seq, b)
                pltpu.make_async_remote_copy(
                    src_ref=self.cells.at[peer],
                    dst_ref=self.columns.at[peer],
                    send_sem=self.send_sem.at[b],
                    recv_sem=self.recv_sem.at[b],
                    device_id=(self.links.dp, peer),
                    device_id_type=MESH,
                ).wait_recv()

    def sent(self):
        for b in range(1, self.cells.shape[0]):
            self.copy(b).wait_send()


def columns_of_chip(columns, chip):
    pair = columns[pl.ds(2 * chip, 2)]
    return pair.reshape(2 * pair.shape[1], pair.shape[2])


def transform_arrivals(exchange, table, spec):
    for near in range(exchange.links.deep):
        transform_pair(exchange, table, spec, near)


def transform_pair(exchange, table, spec, near):
    step = 2 * exchange.columns.shape[1]
    exchange.arrived(2 * near, 2 * near + 1)
    chip = flip(exchange.links.z, near)
    lanes = pl.ds(pl.multiple_of(chip * step, step), step)
    part = mul(table[:, lanes], columns_of_chip(exchange.columns, chip))
    if near:
        spec[...] += part
    else:
        spec[...] = part


def send_inverse(exchange, table_back, filtered):
    row_len = exchange.cells.shape[1]
    for near in reversed(range(exchange.links.deep)):
        chip = flip(exchange.links.z, near)
        rows = pl.ds(pl.multiple_of(chip * 2 * row_len, 2 * row_len), 2 * row_len)
        part = mul(table_back[rows, :], filtered[...]).astype(exchange.cells.dtype)
        exchange.cells[pl.ds(2 * chip, 2)] = part.reshape(2, row_len, part.shape[1])
        exchange.send(2 * near, 2 * near + 1)


def forward_kernel(
    chunks,
    first_chunks,
    owners,
    master,
    x,
    features,
    channels,
    filter_in,
    filter_out,
    table_hbm,
    table_back_hbm,
    full,
    query,
    key,
    value,
    kv,
    conv,
    taps_spec,
    kv_spec,
    own,
    got,
    base,
    arrived,
    leaving,
    table,
    table_back,
    hidden,
    taps,
    columns,
    filtered,
    cells_back,
    table_sem,
    send_sem,
    recv_sem,
    chain_send,
    chain_recv,
    field_send,
    field_recv,
    back_send,
    back_recv,
):
    low, wide = jnp.bfloat16, jnp.float32
    links = Links(send_sem, recv_sem)
    loads = (
        pltpu.make_async_copy(table_hbm, table, table_sem.at[0]),
        pltpu.make_async_copy(table_back_hbm, table_back, table_sem.at[1]),
    )
    for load in loads:
        load.start()
    quarter = full.shape[1] // 4
    tile_count, side = owners.shape[0], master.shape[2]
    most = master.shape[0] - 1
    rows = pl.ds(pl.multiple_of(links.dp * quarter, quarter), quarter)
    near_rows = pl.ds(pl.multiple_of(links.near * quarter, quarter), quarter)
    rank, place = jnp.int32(0), []
    for i in range(tile_count):
        mine = owners[i] == links.seq
        place.append((jnp.minimum(rank, most), mine))
        rank = rank + jnp.where(mine, 1, 0)
    for half in range(2):
        order = half_tiles(half)
        for j in range(0, len(order), 2):
            pair = []
            for i in order[j : j + 2]:
                at, mine = place[i]
                pair.append(jnp.where(mine, master[at, rows, :], 0.0))
            own[half, :, j * side : (j + 2) * side] = jnp.concatenate(pair, axis=1).astype(own.dtype)
    links.meet()
    swaps, planes = [], []
    for at in chunks:
        swaps.append(
            links.copy(own.at[1 - links.core, :, at], got.at[:, at], links.partner)
        )
        mine = full.at[links.core, rows, at]
        other = full.at[links.core, near_rows, at]
        both = full.at[links.core, :, at]
        planes.append(
            (
                links.copy(mine, mine, links.to_near),
                links.copy(mine, mine, links.to_far),
                links.copy(other, other, links.to_far),
                links.copy(both, both, links.partner),
            )
        )
        swaps[-1].start()
    chain = Chain(links, base, arrived, leaving, chain_send, chain_recv, chunks)
    length, width = kv_spec.shape
    lanes = half_lanes(width)
    half_length = length // 2

    def hidden_step():
        hidden[...] = jnp.sin(phases_of(features[...], filter_in[...])).astype(low)

    def taps_step(part):
        span = slice(part * length // 4, (part + 1) * length // 4)
        decay = jnp.exp(-features[span, 0:1] * channels[0:1, lanes]) * channels[1:2, lanes]
        values = mul(hidden[span, :], filter_out[:, lanes].astype(low))
        taps[span, :] = (values * decay).astype(low)

    def spectrum_step(part):
        span = slice(part * length // 4, (part + 1) * length // 4)
        scale = jnp.where(first_row((length // 4, 1)), 1.0 / length, 2.0 / length)
        if part % 2:
            scale = 2.0 / length
        taps_spec[span, :] = mul(table[span, :], taps[...]) * scale

    def wait_table():
        loads[0].wait()

    fill = [hidden_step]
    fill += [functools.partial(taps_step, i) for i in range(4)]
    fill += [wait_table]
    fill += [functools.partial(spectrum_step, i) for i in range(4)]
    fill.reverse()

    def fill_in(steps=1):
        for _ in range(steps):
            if fill:
                fill.pop()()

    def collect(k):
        at = chunks[k]
        swaps[k].wait()
        base[:, at] = own[links.core, :, at] + got[:, at]
        chain.begin(k)

    def spread(k):
        full[links.core, rows, chunks[k]] = chain.inward(k).astype(full.dtype)
        planes[k][0].start()
        planes[k][1].start()

    def relay(k):
        planes[k][0].wait_recv()
        planes[k][2].start()

    def share(k):
        planes[k][1].wait_recv()
        planes[k][2].wait_recv()
        planes[k][3].start()

    count = len(chunks)
    fill_in(1)
    for k in range(count):
        collect(k)
    stages = ((chain.outward, 0), (spread, 1), (relay, 2), (share, 4))
    steps = [
        [(stage, k - late) for stage, late in stages if 0 <= k - late < count]
        for k in range(count + 4)
    ]
    before, after = steps[: first_chunks + 4], steps[first_chunks + 4 :]
    for step in before:
        fill_in(2)
        for stage, k in step:
            stage(k)
    for k in range(first_chunks):
        planes[k][3].wait_recv()
    fill_in(len(fill))

    row_len = kv.shape[1]
    seqs = kv.shape[0] // 2
    outbound = Exchange(links, kv, columns, field_send, field_recv)
    for pair, bits in ((links.inner, (6, 7, 4, 5)), (links.outer, (2, 3, 1, 0))):
        span = pl.ds(pl.multiple_of(pair * (seqs // 2) * row_len, row_len), seqs // 2 * row_len)
        for i in range(12):
            block = i // 3
            part = mul(x[span, block * side : (block + 1) * side], tile_at(full, i // 6, (i % 6) * side))
            target = (query, key, value)[i // 4]
            at = (i % 4) * side
            target[span, at : at + side] = part.astype(target.dtype)
        for s in range(seqs // 2):
            line = pl.ds(pl.multiple_of((pair * (seqs // 2) + s) * row_len, row_len), row_len)
            for h in range(2):
                part = slice(h * width, (h + 1) * width)
                both = key[line, part].astype(wide) * value[line, part].astype(wide)
                kv[2 * (pair * (seqs // 2) + s) + h] = both.astype(kv.dtype)
        outbound.send(*bits)
    for near in range(links.deep):
        transform_pair(outbound, table, kv_spec, near)
        if near < len(after):
            for stage, k in after[near]:
                stage(k)
    for step in after[links.deep :]:
        for stage, k in step:
            stage(k)
    real, imag = spectrum_product(
        kv_spec[:half_length],
        kv_spec[half_length:],
        taps_spec[:half_length],
        taps_spec[half_length:],
        1.0,
    )
    filtered[:half_length] = real.astype(low)
    filtered[half_length:] = imag.astype(low)
    loads[1].wait()
    inbound = Exchange(links, cells_back, conv, back_send, back_recv)
    send_inverse(inbound, table_back, filtered)
    for k in range(count):
        chain.finish(k)
        for copy in planes[k]:
            copy.wait_send()
        if k >= first_chunks:
            planes[k][3].wait_recv()
    outbound.sent()
    inbound.arrived(*range(1, 2 * seqs))
    inbound.sent()


def forward_call(owners, master, x, features, channels, filter_in, filter_out, table, table_back, cells):
    slots, side, _ = master.shape
    width = owners.shape[0] // 2 * side
    chunks = cut(0, 640, 1152, 2816, 4480, width)
    low, wide = jnp.bfloat16, jnp.float32
    quarter = side // 4
    count = len(chunks)
    devices, row_len, columns = cells
    length = devices * row_len
    shape = jax.ShapeDtypeStruct
    anywhere = pl.BlockSpec(memory_space=pl.ANY)
    spec = shape((length, columns), wide)
    rows = shape(x.shape, low)
    return pl.pallas_call(
        functools.partial(forward_kernel, chunks, 2),
        out_shape=(
            shape((2, side, width), low),
            rows,
            rows,
            rows,
            shape(cells, low),
            shape(cells, low),
            spec,
            spec,
        ),
        in_specs=[SMEM] + [VMEM] * 6 + [anywhere] * 2,
        out_specs=(VMEM,) * 8,
        scratch_shapes=[
            pltpu.VMEM((2, quarter, width), low),
            pltpu.VMEM((quarter, width), low),
            pltpu.VMEM((quarter, width), low),
            pltpu.VMEM((2, quarter, width), low),
            pltpu.VMEM((2, quarter, width), low),
            pltpu.VMEM((length, length), low),
            pltpu.VMEM((length, length), low),
            pltpu.VMEM((length, filter_in.shape[1]), low),
            pltpu.VMEM((length, columns), low),
            pltpu.VMEM(cells, low),
            pltpu.VMEM((length, columns), low),
            pltpu.VMEM(cells, low),
            pltpu.SemaphoreType.DMA((2,)),
            pltpu.SemaphoreType.DMA((5 * count,)),
            pltpu.SemaphoreType.DMA((5 * count,)),
            pltpu.SemaphoreType.DMA((2, count)),
            pltpu.SemaphoreType.DMA((2, count)),
        ]
        + [pltpu.SemaphoreType.DMA((devices,))] * 4,
        compiler_params=pltpu.CompilerParams(
            collective_id=0, has_side_effects=True, vmem_limit_bytes=VMEM_LIMIT
        ),
        name="forward",
    )(owners, master, x, features, channels, filter_in, filter_out, table, table_back)


class Reducer:
    def __init__(self, links, grads, scratch, chunks):
        (
            self.mine_sum,
            self.got,
            self.near_in,
            self.far_in,
            self.far_out,
            self.base,
            arrived,
            leaving,
            chain_send,
            chain_recv,
        ) = scratch
        self.links, self.grads, self.chunks = links, grads, chunks
        self.count = len(chunks)
        self.quarter = self.base.shape[0]
        self.chain = Chain(links, self.base, arrived, leaving, chain_send, chain_recv, chunks)
        self.swaps, self.nears, self.diagonals, self.fars = [], [], [], []
        for at in chunks:
            self.swaps.append(
                links.copy(grads.at[1 - links.core, :, at], self.got.at[:, at], links.partner)
            )
            self.nears.append(
                links.copy(
                    self.mine_sum.at[self.rows_of(links.near), at],
                    self.near_in.at[0, :, at],
                    links.to_near,
                )
            )
            self.diagonals.append(
                links.copy(
                    self.mine_sum.at[self.rows_of(links.diagonal), at],
                    self.near_in.at[1, :, at],
                    links.to_near,
                )
            )
            self.fars.append(links.copy(self.far_out.at[:, at], self.far_in.at[:, at], links.to_far))

    @staticmethod
    def scratch(side, width, count):
        low, quarter = jnp.bfloat16, side // 4
        return [
            pltpu.VMEM((side, width), low),
            pltpu.VMEM((side, width), low),
            pltpu.VMEM((2, quarter, width), low),
            pltpu.VMEM((quarter, width), low),
            pltpu.VMEM((quarter, width), low),
            pltpu.VMEM((quarter, width), jnp.float32),
            pltpu.VMEM((2, quarter, width), low),
            pltpu.VMEM((2, quarter, width), low),
            pltpu.SemaphoreType.DMA((2, count)),
            pltpu.SemaphoreType.DMA((2, count)),
        ]

    def rows_of(self, index):
        return pl.ds(pl.multiple_of(index * self.quarter, self.quarter), self.quarter)

    def swap(self, k):
        self.swaps[k].start()

    def swap_half(self, k, half):
        @pl.when(self.links.core != half)
        def _():
            self.swaps[k].start()

    def merge_cores(self, k):
        at, wide = self.chunks[k], jnp.float32
        self.swaps[k].wait_recv()
        self.mine_sum[:, at] = (
            self.grads[self.links.core, :, at].astype(wide) + self.got[:, at].astype(wide)
        ).astype(self.mine_sum.dtype)
        self.diagonals[k].start()
        self.nears[k].start()

    def go_far(self, k):
        at, wide = self.chunks[k], jnp.float32
        self.diagonals[k].wait_recv()
        self.far_out[:, at] = (
            self.mine_sum[self.rows_of(self.links.far), at].astype(wide)
            + self.near_in[1, :, at].astype(wide)
        ).astype(self.far_out.dtype)
        self.fars[k].start()

    def collect(self, k):
        at, wide = self.chunks[k], jnp.float32
        self.nears[k].wait_recv()
        self.fars[k].wait_recv()
        self.base[:, at] = (
            self.mine_sum[self.rows_of(self.links.dp), at].astype(wide)
            + self.near_in[0, :, at].astype(wide)
            + self.far_in[:, at].astype(wide)
        )
        self.chain.begin(k)

    def outward(self, k):
        self.chain.outward(k)

    def finish(self, k):
        self.swaps[k].wait_send()
        self.nears[k].wait_send()
        self.diagonals[k].wait_send()
        self.fars[k].wait_send()
        self.chain.finish(k)


def run_stages(count, *stages):
    for step in range(count + max(lag for _, lag in stages)):
        for stage, lag in stages:
            if 0 <= step - lag < count:
                stage(step - lag)


def backward_kernel(
    chunks,
    late_chunks,
    tile_of_slot,
    used,
    d_inner,
    grads,
    sums,
    taps_spec,
    kv_spec,
    features,
    channels,
    filter_in,
    filter_out,
    key,
    value,
    x,
    d_first,
    d_query,
    vectors,
    packed_hbm,
    table_hbm,
    table_back_hbm,
    in_grad,
    spread,
    late_full,
    columns,
    cells_back,
    d_conv,
    spec,
    filtered,
    d_qkv,
    table,
    table_back,
    packed,
    late,
    total,
    by_tile,
    table_sem,
    send_sem,
    recv_sem,
    field_send,
    field_recv,
    back_send,
    back_recv,
    *scratch,
):
    low, wide = jnp.bfloat16, jnp.float32
    links = Links(send_sem, recv_sem)
    loads = (
        pltpu.make_async_copy(table_hbm, table, table_sem.at[0]),
        pltpu.make_async_copy(table_back_hbm, table_back, table_sem.at[1]),
        pltpu.make_async_copy(
            packed_hbm.at[:, :, pl.ds(0, packed.shape[2])], packed, table_sem.at[2]
        ),
    )
    for load in loads:
        load.start()
    side = grads.shape[1]
    quarter = side // 4
    length, width = kv_spec.shape
    half_length = length // 2
    row_len = d_inner.shape[1]
    model = x.shape[1]
    devices = d_inner.shape[0]
    early = Reducer(links, grads, scratch[: len(scratch) // 2], chunks)
    tail = Reducer(links, late, scratch[len(scratch) // 2 :], late_chunks)
    links.meet()
    outbound = Exchange(links, d_inner, columns, field_send, field_recv)
    outbound.send(6, 7, 4, 5, 2, 3, 1, 0)
    for k in range(early.count):
        early.swap(k)
    late[...] = jnp.zeros_like(late)

    for k in range(early.count):
        early.merge_cores(k)
    loads[0].wait()
    per_pair = -(-early.count // links.deep)
    for near in range(links.deep):
        transform_pair(outbound, table, spec, near)
        for k in range(near * per_pair, min((near + 1) * per_pair, early.count)):
            early.go_far(k)
    loads[1].wait()
    real, imag = spectrum_product(
        spec[:half_length],
        spec[half_length:],
        taps_spec[:half_length],
        taps_spec[half_length:],
        -1.0,
    )
    filtered[:half_length] = real.astype(low)
    filtered[half_length:] = imag.astype(low)
    inbound = Exchange(links, cells_back, d_conv, back_send, back_recv)
    send_inverse(inbound, table_back, filtered)

    def early_total(k):
        total[links.core, :, chunks[k]] = early.chain.inward(k).astype(total.dtype)
        shares[k].start()

    shares = []
    for at in chunks:
        part = total.at[links.core, :, at]
        shares.append(links.copy(part, part, links.partner))

    scale = jnp.where(first_row((half_length, 1)), 1.0 / length, 2.0 / length)
    real, imag = spectrum_product(
        spec[:half_length], spec[half_length:], kv_spec[:half_length], kv_spec[half_length:], -1.0
    )
    filtered[:half_length] = (real * scale).astype(low)
    filtered[half_length:] = (imag * scale).astype(low)
    lanes = half_lanes(width)
    scaled = mul(table_back[...], filtered[...]) * decay_of(features, channels, lanes)
    scaled = scaled.astype(low)
    phases = phases_of(features[...], filter_in[...])
    order = filter_in.shape[1]
    first_late = 6 * side
    late[links.core, 0:order, first_late:] = mul(jnp.sin(phases).astype(low), scaled, TN).astype(low)
    d_hidden = mul(scaled, filter_out[:, lanes].astype(low), NT) * jnp.cos(phases)
    lines = [
        jnp.sum(features[:, i : i + 1] * d_hidden, axis=0, keepdims=True)
        for i in range(filter_in.shape[0])
    ]
    lines.append(jnp.zeros((8 - len(lines), order), wide))
    in_lines = jnp.concatenate(lines, axis=0)
    for half in range(2):
        vector_lines = sums[:, half * width : (half + 1) * width]
        if half == 0:
            other = jnp.concatenate([in_lines, jnp.zeros((8, width - order), wide)], axis=1)
        else:
            other = jnp.zeros((8, width), wide)
        both = jnp.concatenate([vector_lines, other], axis=0)
        late[half, order : order + 16, first_late:] = both.astype(low)

    d_qkv[:, :model] = d_query[...]
    pair_rows = 2 * row_len

    def fill_rows(pair):
        for s in range(devices // 4):
            line = pl.ds(pl.multiple_of((pair * (devices // 4) + s) * row_len, row_len), row_len)
            for h in range(2):
                part = slice(h * width, (h + 1) * width)
                cell = 2 * (pair * (devices // 4) + s) + h
                d_kv = d_conv[cell].astype(wide) + vectors[4:5, part] * d_inner[cell].astype(wide)
                d_qkv[line, model + h * width : model + (h + 1) * width] = (
                    d_kv * value[line, part].astype(wide)
                ).astype(low)
                d_qkv[line, 2 * model + h * width : 2 * model + (h + 1) * width] = (
                    d_kv * key[line, part].astype(wide)
                ).astype(low)

    for k in range(early.count):
        early.collect(k)
    inbound.arrived(1, 2, 3)
    fill_rows(links.outer)
    inbound.arrived(4, 5, 6, 7)
    fill_rows(links.inner)
    early.outward(0)
    per_block = 3 * side
    for b in range(4):
        mine = slice(b * side, (b + 1) * side)
        here = d_qkv[:, b * per_block : (b + 1) * per_block]
        at = (b % 2) * per_block
        late[b // 2, :, at : at + per_block] = mul(x[:, mine], here, TN).astype(low)
        if b % 2:
            for k in range(tail.count):
                tail.swap_half(k, b // 2)
        early.outward(b + 1)
        early_total(b)
    for k in range(tail.count):
        tail.merge_cores(k)
    early_total(early.count - 1)
    for share in shares:
        share.wait()
    for half in range(2):
        for j, i in enumerate(half_tiles(half)):
            if i >= 12:
                at = (j - 6) * side
                by_tile[i - 12] = total[half, :, at : at + side].astype(wide)
    for k in range(tail.count):
        tail.go_far(k)
    slots = tile_of_slot.shape[0]
    mine = early.rows_of(links.dp)
    for s in range(0, slots, 2):
        pair = []
        for k in (s, s + 1):
            values = by_tile[jnp.maximum(tile_of_slot[k] - 12, 0)]
            pair.append(jnp.where(used[k] > 0, values, 0.0))
        spread[mine, s * side : (s + 2) * side] = jnp.concatenate(pair, axis=1).astype(spread.dtype)
    for k in range(tail.count):
        tail.collect(k)
    planes = []
    for at in late_chunks:
        at_home = late_full.at[links.core, mine, at]
        other = late_full.at[links.core, early.rows_of(links.near), at]
        both = late_full.at[links.core, :, at]
        planes.append(
            (
                links.copy(at_home, at_home, links.to_near),
                links.copy(at_home, at_home, links.to_far),
                links.copy(other, other, links.to_far),
                links.copy(both, both, links.partner),
            )
        )
    at_home, other = spread.at[mine, :], spread.at[early.rows_of(links.near), :]
    slot_copies = (
        links.copy(at_home, at_home, links.to_near),
        links.copy(at_home, at_home, links.to_far),
        links.copy(other, other, links.to_far),
    )
    slot_copies[0].start()
    slot_copies[1].start()

    def input_gradient(b):
        mine = slice(b * side, (b + 1) * side)
        here = d_qkv[:, b * per_block : (b + 1) * per_block]
        at = (b % 2) * per_block
        weights = packed[b // 2, :, at : at + per_block]
        in_grad[:, mine] = d_first[:, mine] + mul(here, weights, NT)

    loads[2].wait()
    input_gradient(0)
    for k in range(tail.count):
        tail.outward(k)
    input_gradient(1)
    slot_copies[0].wait_recv()
    slot_copies[2].start()
    for k in range(tail.count):
        late_full[links.core, mine, late_chunks[k]] = tail.chain.inward(k).astype(late_full.dtype)
        planes[k][0].start()
        planes[k][1].start()
    input_gradient(2)
    for k in range(tail.count):
        planes[k][0].wait_recv()
        planes[k][2].start()
    input_gradient(3)
    for k in range(tail.count):
        planes[k][1].wait_recv()
        planes[k][2].wait_recv()
        planes[k][3].start()
    slot_copies[1].wait_recv()
    slot_copies[2].wait_recv()
    for copies in planes:
        for copy in copies[:3]:
            copy.wait_send()
        copies[3].wait()
    for copy in slot_copies:
        copy.wait_send()
    outbound.sent()
    inbound.sent()
    for k in range(early.count):
        early.finish(k)
    for k in range(tail.count):
        tail.finish(k)


def backward_call(tile_of_slot, used, d_inner, grads, sums, tables, filter_arrays, rows, packed):
    _, side, width = grads.shape
    devices, row_len, columns = d_inner.shape
    length = devices * row_len
    tokens, model = rows[2].shape
    slots = tile_of_slot.shape[0]
    late_width = 6 * side + columns
    chunks = cut(0, 1152, 2176, 3200, 4096, width)
    late_chunks = cut(0, 512, 1024, late_width)
    low, wide = jnp.bfloat16, jnp.float32
    quarter = side // 4
    shape = jax.ShapeDtypeStruct
    anywhere = pl.BlockSpec(memory_space=pl.ANY)
    cells = pltpu.VMEM(d_inner.shape, low)
    copies = 5 * len(chunks) + 8 * len(late_chunks) + 3
    return pl.pallas_call(
        functools.partial(backward_kernel, chunks, late_chunks),
        out_shape=(
            shape((tokens, model), wide),
            shape((side, slots * side), low),
            shape((2, side, late_width), low),
        ),
        in_specs=[SMEM] * 2
        + [VMEM] * 15
        + [anywhere] * 3,
        out_specs=(VMEM,) * 3,
        scratch_shapes=[
            cells,
            cells,
            cells,
            pltpu.VMEM((length, columns), wide),
            pltpu.VMEM((length, columns), low),
            pltpu.VMEM((tokens, 3 * model), low),
            pltpu.VMEM((length, length), low),
            pltpu.VMEM((length, length), low),
            pltpu.VMEM((2, side, 6 * side), low),
            pltpu.VMEM((2, side, late_width), low),
            pltpu.VMEM((2, quarter, width), low),
            pltpu.VMEM((NTILES - 12, quarter, side), wide),
            pltpu.SemaphoreType.DMA((3,)),
            pltpu.SemaphoreType.DMA((copies,)),
            pltpu.SemaphoreType.DMA((copies,)),
        ]
        + [pltpu.SemaphoreType.DMA((devices,))] * 4
        + Reducer.scratch(side, width, len(chunks))
        + Reducer.scratch(side, late_width, len(late_chunks)),
        compiler_params=pltpu.CompilerParams(
            collective_id=1, has_side_effects=True, vmem_limit_bytes=VMEM_LIMIT
        ),
        name="backward",
    )(
        tile_of_slot,
        used,
        d_inner,
        grads,
        sums,
        *filter_arrays,
        *rows,
        packed,
        *tables,
    )


def on_device_columns(
    tokens,
    cotangent,
    owners,
    tile_master,
    tile_moment,
    tile_second,
    tile_average,
    vectors,
    vector_moment,
    vector_second,
    vector_average,
    filter_in,
    in_moment,
    in_second,
    in_average,
    filter_out,
    out_moment,
    out_second,
    out_average,
):
    seq_count, dev_rows, row_len, model_width = tokens.shape
    owner_cap, side, _ = tile_master.shape
    seq_devices = lax.axis_size("seq")
    grid_rows = dev_rows * seq_devices
    length = grid_rows * row_len
    seq_index = lax.axis_index("seq")
    width = model_width // 2
    low, wide = jnp.bfloat16, jnp.float32
    shape = jax.ShapeDtypeStruct
    count = seq_count * row_len
    order = filter_in.shape[1]
    table_host = real_table(grid_rows, row_len)
    table, table_back = jnp.asarray(table_host), jnp.asarray(np.ascontiguousarray(table_host.T))
    features, channels = (
        jnp.asarray(a) for a in filter_constants(grid_rows, row_len, model_width)
    )
    slot_of_tile, tile_of_slot, slot_used = slot_maps(owners, owner_cap, owner_cap * seq_devices)
    first_slot = seq_index * owner_cap
    own_tile = lax.dynamic_slice_in_dim(tile_of_slot, first_slot, owner_cap, 0)
    own_used = lax.dynamic_slice_in_dim(slot_used.astype(jnp.int32), first_slot, owner_cap, 0)
    x = tokens.reshape(count, model_width)
    cell_shape = (seq_devices, row_len, width)

    packed, query, key, value, kv, conv, taps_spec, kv_spec = forward_call(
        owners,
        tile_master,
        x,
        features,
        channels,
        filter_in,
        filter_out,
        table,
        table_back,
        cell_shape,
    )
    output, d_first, d_inner, d_query, grads, sums = layer_call(
        conv, query, kv, x, cotangent.reshape(count, model_width), vectors, packed
    )
    in_grad, reduced, late = backward_call(
        own_tile,
        own_used,
        d_inner,
        grads,
        sums,
        (table, table_back),
        (taps_spec, kv_spec, features, channels, filter_in, filter_out),
        (key, value, x, d_first, d_query, vectors),
        packed,
    )
    tokens_all = count * lax.axis_size("dp") * seq_devices
    updated = adam_call(
        1.0 / math.sqrt(tokens_all),
        own_tile,
        own_used,
        reduced,
        late,
        (tile_master, tile_moment, tile_second, tile_average),
        (
            vectors,
            vector_moment,
            vector_second,
            vector_average,
            filter_in,
            in_moment,
            in_second,
            in_average,
            filter_out,
            out_moment,
            out_second,
            out_average,
        ),
    )
    return (output.reshape(tokens.shape), in_grad.reshape(tokens.shape), *updated)


def on_device(*arrays):
    seq_count, dev_rows, row_len, model_width = arrays[0].shape
    seq_devices = lax.axis_size("seq")
    fits = dev_rows == 1 and lax.axis_size("dp") == 4 and seq_devices == 2 * seq_count == 8
    if fits and row_len == 128 and model_width % 256 == 0:
        return on_device_columns(*arrays)
    return on_device_general(*arrays)


def solution(mesh):
    in_specs = (
        P("dp", "seq", None, None),
        P("dp", "seq", None, None),
        P(),
        P("seq", None, None),
        P("seq", None, None),
        P("seq", None, None),
        P("seq", None, None),
        P(),
        P(),
        P(),
        P(),
        P(),
        P(),
        P(),
        P(),
        P(),
        P(),
        P(),
        P(),
    )
    out_specs = (
        P("dp", "seq", None, None),
        P("dp", "seq", None, None),
        P("seq", None, None),
        P("seq", None, None),
        P("seq", None, None),
        P("seq", None, None),
        P(),
        P(),
        P(),
        P(),
        P(),
        P(),
        P(),
        P(),
        P(),
        P(),
        P(),
        P(),
    )
    return jax.shard_map(
        on_device, mesh=mesh, in_specs=in_specs, out_specs=out_specs, check_vma=False
    )
```

```python
import functools
import math

import jax
import jax.numpy as jnp
import ml_dtypes
import numpy as np
from jax import lax
from jax.experimental import pallas as pl
from jax.experimental.pallas import tpu as pltpu
from jax.sharding import PartitionSpec as P

D = 768
FF = 3072
STEP = 10
NTILES = 64


highest = lax.Precision.HIGHEST
beta_one = 0.9
beta_two = 0.999
keep_rate = 0.5
adam_eps = 1e-08
norm_eps = 1e-05
golden = 0.6180339887


def norm_rows(values, gain_vec, bias_vec):
    row_mean = jnp.mean(values, axis=-1, keepdims=True)
    centered = values - row_mean
    spread = jnp.mean(centered * centered, axis=-1, keepdims=True)
    return centered * lax.rsqrt(spread + norm_eps) * gain_vec + bias_vec


def glu_act(gate_value, up_value):
    return jax.nn.gelu(gate_value, approximate=False) * up_value


def filter_taps(filter_in, filter_out, position, length):
    channel = jnp.arange(filter_out.shape[1], dtype=jnp.int32)
    return filter_taps_of(filter_in, filter_out, position, length, channel)


def filter_taps_of(filter_in, filter_out, position, length, channel_index):
    phases = position * (2.0 * math.pi / length)
    features = jnp.stack(
        [
            position / length,
            jnp.cos(phases),
            -jnp.sin(phases),
            jnp.cos(2.0 * phases),
            -jnp.sin(2.0 * phases),
        ],
        axis=1,
    )
    hidden = jnp.sin(jnp.dot(features, filter_in, precision=highest))
    taps_value = jnp.dot(hidden, filter_out, precision=highest)
    channel = channel_index.astype(jnp.float32)
    decay_rates = 0.3 * jnp.exp(math.log(1000.0) * jnp.mod(channel * golden, 1.0))
    decay_rate = jnp.exp(-(position / length)[:, None] * decay_rates[None, :])
    total = jnp.expm1(-2.0 * decay_rates) / jnp.expm1(-2.0 * decay_rates / length)
    norm_scale = lax.rsqrt(total)
    return taps_value * decay_rate * norm_scale


def block_weight(tile_stack, in_tiles, out_tiles):
    tile_side = tile_stack.shape[-1]
    tile_grid = tile_stack.reshape(4, in_tiles, out_tiles, tile_side, tile_side).transpose(
        0, 1, 3, 2, 4
    )
    return tile_grid.reshape(4, in_tiles * tile_side, out_tiles * tile_side)


def tile_split(blocks, in_tiles, out_tiles):
    tile_side = blocks.shape[1] // in_tiles
    tile_grid = blocks.reshape(4, in_tiles, tile_side, out_tiles, tile_side).transpose(
        0, 1, 3, 2, 4
    )
    return tile_grid.reshape(4 * in_tiles * out_tiles, tile_side, tile_side)


def block_apply(values, blocks):
    row_view = values.reshape(values.shape[0], 4, -1)
    return jnp.einsum("nbi,bio->nbo", row_view, blocks, preferred_element_type=jnp.float32).reshape(
        values.shape[0], -1
    )


def block_back(gradient, blocks):
    row_view = gradient.reshape(gradient.shape[0], 4, -1)
    return jnp.einsum("nbo,bio->nbi", row_view, blocks, preferred_element_type=jnp.float32).reshape(
        gradient.shape[0], -1
    )


def block_grad(values, gradient, in_tiles, out_tiles):
    left_rows = values.reshape(values.shape[0], 4, -1)
    right_rows = gradient.reshape(gradient.shape[0], 4, -1)
    blocks = jnp.einsum("nbi,nbo->bio", left_rows, right_rows, preferred_element_type=jnp.float32)
    return tile_split(blocks, in_tiles, out_tiles)


def slot_maps(owners, owner_cap, slot_total):
    tile_count = owners.shape[0]
    tile_index = jnp.arange(tile_count, dtype=jnp.int32)
    earlier = (owners[:, None] == owners[None, :]) & (tile_index[None, :] < tile_index[:, None])
    owner_rank = jnp.sum(earlier.astype(jnp.int32), axis=1)
    slot_of_tile = owners * owner_cap + owner_rank
    slot_hits = slot_of_tile[None, :] == jnp.arange(slot_total, dtype=jnp.int32)[:, None]
    tile_of_slot = jnp.sum(slot_hits.astype(jnp.int32) * tile_index[None, :], axis=1)
    slot_used = jnp.any(slot_hits, axis=1)
    return (slot_of_tile, tile_of_slot, slot_used)


def adam_step(weight, moment, second, average, gradient, step_rate, decay_rate):
    moment = beta_one * moment + (1.0 - beta_one) * gradient
    second = beta_two * second + (1.0 - beta_two) * gradient * gradient
    fixed_moment = moment / (1.0 - beta_one**STEP)
    fixed_second = second / (1.0 - beta_two**STEP)
    weight = weight - step_rate * (
        fixed_moment / (jnp.sqrt(fixed_second) + adam_eps) + decay_rate * weight
    )
    average = keep_rate * average + (1.0 - keep_rate) * weight
    return (second, weight, average)


def wave_table(period, index_one, index_two):
    turn_count = jnp.mod(index_one[:, None] * index_two[None, :], period).astype(jnp.float32)
    angles = turn_count * (2.0 * math.pi / period)
    return (jnp.cos(angles), jnp.sin(angles))


def col_dot(field_in, table_in):
    return jnp.einsum("srcd,ck->srkd", field_in, table_in, precision=highest)


def row_dot(field_in, table_in):
    return jnp.einsum("srkd,rq->sqkd", field_in, table_in, precision=highest)


def cols_forward(field_in, tables):
    col_cos, col_sin, turn_cos, turn_sin, row_cos, row_sin = tables
    real_part = col_dot(field_in, col_cos)
    imag_part = -col_dot(field_in, col_sin)
    real_turn = real_part * turn_cos + imag_part * turn_sin
    imag_turn = imag_part * turn_cos - real_part * turn_sin
    return (real_turn, imag_turn)


def rows_forward(part_real, part_imag, tables):
    row_cos, row_sin = (tables[4], tables[5])
    freq_real = row_dot(part_real, row_cos) + row_dot(part_imag, row_sin)
    freq_imag = row_dot(part_imag, row_cos) - row_dot(part_real, row_sin)
    return (freq_real, freq_imag)


def rows_inverse(prod_real, prod_imag, tables):
    row_cos, row_sin = (tables[4], tables[5])
    back_real = row_dot(prod_real, row_cos) - row_dot(prod_imag, row_sin)
    back_imag = row_dot(prod_real, row_sin) + row_dot(prod_imag, row_cos)
    return (back_real, back_imag)


def cols_inverse(rows_real, rows_imag, tables, length):
    col_cos, col_sin, turn_cos, turn_sin, row_cos, row_sin = tables
    cell_real = rows_real * turn_cos - rows_imag * turn_sin
    cell_imag = rows_real * turn_sin + rows_imag * turn_cos
    return (
        jnp.einsum("srkd,ck->srcd", cell_real, col_cos, precision=highest)
        - jnp.einsum("srkd,ck->srcd", cell_imag, col_sin, precision=highest)
    ) / length


def convolve(field_in, spectrum, tables, conjugate, length):
    spec_real, spec_imag = spectrum
    sign_flip = -1.0 if conjugate else 1.0
    real_turn, imag_turn = cols_forward(field_in, tables)
    part_real = lax.all_to_all(real_turn, "seq", split_axis=2, concat_axis=1, tiled=True)
    part_imag = lax.all_to_all(imag_turn, "seq", split_axis=2, concat_axis=1, tiled=True)
    freq_real, freq_imag = rows_forward(part_real, part_imag, tables)
    prod_real = freq_real * spec_real - sign_flip * freq_imag * spec_imag
    prod_imag = sign_flip * freq_real * spec_imag + freq_imag * spec_real
    back_real, back_imag = rows_inverse(prod_real, prod_imag, tables)
    rows_real = lax.all_to_all(back_real, "seq", split_axis=1, concat_axis=2, tiled=True)
    rows_imag = lax.all_to_all(back_imag, "seq", split_axis=1, concat_axis=2, tiled=True)
    rows_real, rows_imag, freq_real, freq_imag = (rows_real, rows_imag, freq_real, freq_imag)
    field_out = cols_inverse(rows_real, rows_imag, tables, length)
    return (field_out, freq_real, freq_imag)


def real_table(grid_rows, row_len):
    length = grid_rows * row_len
    position = (np.arange(grid_rows)[:, None] + grid_rows * np.arange(row_len)[None, :]).reshape(-1)
    turns = np.mod(np.arange(length // 2)[:, None] * position[None, :], length)
    angles = turns * (2.0 * np.pi / length)
    sines = -np.sin(angles)
    sines[0] = np.cos(np.pi * position)
    return np.concatenate([np.cos(angles), sines]).astype(ml_dtypes.bfloat16)


def on_device_general(
    tokens,
    cotangent,
    owners,
    tile_master,
    tile_moment,
    tile_second,
    tile_average,
    vectors,
    vector_moment,
    vector_second,
    vector_average,
    filter_in,
    in_moment,
    in_second,
    in_average,
    filter_out,
    out_moment,
    out_second,
    out_average,
):
    seq_count, dev_rows, row_len, model_width = tokens.shape
    owner_cap = tile_master.shape[0]
    seq_devices = lax.axis_size("seq")
    grid_rows = dev_rows * seq_devices
    length = grid_rows * row_len
    seq_index = lax.axis_index("seq")
    hidden_ratio = FF // D
    quarter_hidden = FF // 4
    slot_of_tile, tile_of_slot, slot_used = slot_maps(owners, owner_cap, owner_cap * seq_devices)
    gathered = lax.all_gather(tile_master.astype(jnp.bfloat16), "seq", axis=0, tiled=True)
    weights = jnp.take(gathered, slot_of_tile, axis=0)
    w_in = block_weight(weights[0:12], 1, 3)
    w_out = block_weight(weights[12:16], 1, 1)
    w_gate = block_weight(weights[16 : 16 + 4 * hidden_ratio], 1, hidden_ratio)
    w_up = block_weight(weights[16 + 4 * hidden_ratio : 16 + 8 * hidden_ratio], 1, hidden_ratio)
    w_down = block_weight(weights[16 + 8 * hidden_ratio : 16 + 12 * hidden_ratio], hidden_ratio, 1)
    w_gate_up = jnp.concatenate([w_gate, w_up], axis=2)
    col_index = jnp.arange(row_len, dtype=jnp.int32)
    row_index = jnp.arange(grid_rows, dtype=jnp.int32)
    local_rows = seq_index * dev_rows + jnp.arange(dev_rows, dtype=jnp.int32)
    col_cos, col_sin = wave_table(row_len, col_index, col_index)
    row_cos, row_sin = wave_table(grid_rows, row_index, row_index)
    turn_cos, turn_sin = wave_table(length, local_rows, col_index)
    tables = (
        col_cos,
        col_sin,
        turn_cos[None, :, :, None],
        turn_sin[None, :, :, None],
        row_cos,
        row_sin,
    )
    own_position = (
        (local_rows[:, None] + grid_rows * col_index[None, :]).reshape(-1).astype(jnp.float32)
    )
    flat_tokens = tokens.reshape(-1, model_width)
    qkv_all = block_apply(flat_tokens, w_in)
    query_part = qkv_all[:, :model_width]
    key_part = qkv_all[:, model_width : 2 * model_width]
    value_part = qkv_all[:, 2 * model_width :]
    kv_product = key_part * value_part

    def own_taps(weight_one, weight_two):
        return filter_taps(weight_one, weight_two, own_position, length)

    taps_own, filter_pull = jax.vjp(own_taps, filter_in, filter_out)
    taps_real, taps_imag = cols_forward(taps_own.reshape(1, dev_rows, row_len, model_width), tables)
    taps_real, taps_imag = (
        lax.all_to_all(taps_real, "seq", split_axis=2, concat_axis=1, tiled=True),
        lax.all_to_all(taps_imag, "seq", split_axis=2, concat_axis=1, tiled=True),
    )
    spec_real, spec_imag = rows_forward(taps_real, taps_imag, tables)
    taps_spec = (spec_real[0], spec_imag[0])
    conv_out, kv_real, kv_imag = convolve(
        kv_product.reshape(seq_count, dev_rows, row_len, model_width),
        taps_spec,
        tables,
        False,
        length,
    )
    skip_gain = vectors[4]
    inner_sum = conv_out.reshape(-1, model_width) + skip_gain * kv_product
    gated_out = (query_part * inner_sum).astype(jnp.bfloat16)
    branch = block_apply(gated_out, w_out)
    normed, first_pull = jax.vjp(
        norm_rows, flat_tokens.astype(jnp.float32) + branch, vectors[0], vectors[1]
    )
    normed_low = normed.astype(jnp.bfloat16)
    gate_up = block_apply(normed_low, w_gate_up).reshape(-1, 4, 2, quarter_hidden)
    gate_value = gate_up[:, :, 0].reshape(-1, FF)
    up_value = gate_up[:, :, 1].reshape(-1, FF)
    active, active_pull = jax.vjp(glu_act, gate_value, up_value)
    active_low = active.astype(jnp.bfloat16)
    down_value = block_apply(active_low, w_down)
    result, second_pull = jax.vjp(
        norm_rows, normed_low.astype(jnp.float32) + down_value, vectors[2], vectors[3]
    )
    output = result.astype(jnp.bfloat16).reshape(tokens.shape)
    d_second, d_gain_two, d_bias_two = second_pull(
        cotangent.reshape(-1, model_width).astype(jnp.float32)
    )
    d_down = d_second.astype(jnp.bfloat16)
    g_down = block_grad(active_low, d_down, hidden_ratio, 1)
    d_gate, d_up = active_pull(block_back(d_down, w_down))
    d_gate_up = jnp.stack(
        [d_gate.reshape(-1, 4, quarter_hidden), d_up.reshape(-1, 4, quarter_hidden)], axis=2
    )
    d_gate_up = d_gate_up.reshape(-1, 2 * FF).astype(jnp.bfloat16)
    gate_up_tiles = block_grad(normed_low, d_gate_up, 1, 2 * hidden_ratio).reshape(
        4, 2, hidden_ratio, weights.shape[1], weights.shape[2]
    )
    g_gate = gate_up_tiles[:, 0].reshape(-1, weights.shape[1], weights.shape[2])
    g_up = gate_up_tiles[:, 1].reshape(-1, weights.shape[1], weights.shape[2])
    d_normed = d_second + block_back(d_gate_up, w_gate_up)
    d_first, d_gain_one, d_bias_one = first_pull(d_normed)
    d_branch = d_first.astype(jnp.bfloat16)
    g_out = block_grad(gated_out, d_branch, 1, 1)
    d_gated = block_back(d_branch, w_out)
    d_query = d_gated * inner_sum
    d_inner = d_gated * query_part
    d_skip = jnp.sum(d_inner * kv_product, axis=0)
    d_conv, back_real, back_imag = convolve(
        d_inner.reshape(seq_count, dev_rows, row_len, model_width), taps_spec, tables, True, length
    )
    d_kv = d_conv.reshape(-1, model_width) + skip_gain * d_inner
    d_qkv = jnp.concatenate([d_query, d_kv * value_part, d_kv * key_part], axis=1).astype(
        jnp.bfloat16
    )
    g_in = block_grad(flat_tokens, d_qkv, 1, 3)
    in_grad = (d_first + block_back(d_qkv, w_in)).reshape(tokens.shape)
    cross_real = jnp.sum(back_real * kv_real + back_imag * kv_imag, axis=0, keepdims=True)
    cross_imag = jnp.sum(back_imag * kv_real - back_real * kv_imag, axis=0, keepdims=True)
    cross_back_real, cross_back_imag = rows_inverse(cross_real, cross_imag, tables)
    cross_rows_real, cross_rows_imag = (
        lax.all_to_all(
            cross_back_real.astype(jnp.bfloat16), "seq", split_axis=1, concat_axis=2, tiled=True
        ).astype(cross_back_real.dtype),
        lax.all_to_all(
            cross_back_imag.astype(jnp.bfloat16), "seq", split_axis=1, concat_axis=2, tiled=True
        ).astype(cross_back_imag.dtype),
    )
    d_taps = cols_inverse(cross_rows_real, cross_rows_imag, tables, length).reshape(-1, model_width)
    g_filter_in, g_filter_out = filter_pull(d_taps)
    tile_grads = jnp.concatenate([g_in, g_out, g_gate, g_up, g_down], axis=0)
    slot_mask = slot_used.astype(jnp.float32)[:, None, None]
    summed = lax.psum(tile_grads.astype(jnp.bfloat16), "dp").astype(jnp.float32)
    owned = lax.psum_scatter(
        jnp.take(summed, tile_of_slot, axis=0) * slot_mask, "seq", scatter_dimension=0, tiled=True
    )
    tokens_all = seq_count * dev_rows * row_len * lax.axis_size("dp") * seq_devices
    grad_scale = 1.0 / math.sqrt(tokens_all)
    mine_mask = lax.dynamic_slice_in_dim(slot_mask, seq_index * owner_cap, owner_cap, 0)
    tile_grad = owned * grad_scale
    tile_new = adam_step(tile_master, tile_moment, tile_second, tile_average, tile_grad, 0.1, 0.01)
    vector_part = jnp.stack([d_gain_one, d_bias_one, d_gain_two, d_bias_two, d_skip])
    vector_sum, in_sum, out_sum = lax.psum((vector_part, g_filter_in, g_filter_out), ("dp", "seq"))
    vector_grad = vector_sum * grad_scale
    in_grad_filter = in_sum * grad_scale
    out_grad_filter = out_sum * grad_scale
    vector_new = adam_step(
        vectors, vector_moment, vector_second, vector_average, vector_grad, 0.4, 0.0
    )
    in_new = adam_step(filter_in, in_moment, in_second, in_average, in_grad_filter, 0.4, 0.01)
    out_new = adam_step(filter_out, out_moment, out_second, out_average, out_grad_filter, 0.1, 0.01)
    return (
        output,
        in_grad,
        tile_grad,
        tile_new[0] * mine_mask,
        tile_new[1] * mine_mask,
        tile_new[2] * mine_mask,
        vector_grad,
        vector_new[0],
        vector_new[1],
        vector_new[2],
        in_grad_filter,
        in_new[0],
        in_new[1],
        in_new[2],
        out_grad_filter,
        out_new[0],
        out_new[1],
        out_new[2],
    )


MESH = pl.DeviceIdType.MESH
VMEM_LIMIT = 56 * 2**20
STEP_VMEM = 62 * 2**20


def flip(index, bits):
    at = 1
    result = index
    while at <= bits:
        if bits & at:
            result = result + at - 2 * at * lax.rem(lax.div(index, at), 2)
        at *= 2
    return result


class Links:
    def __init__(self, send_sem, recv_sem):
        self.send_sem, self.recv_sem, self.used = send_sem, recv_sem, 0
        self.dp, self.seq = lax.axis_index("dp"), lax.axis_index("seq")
        self.deep = lax.axis_size("seq") // 2
        self.z, self.core = lax.div(self.seq, 2), lax.rem(self.seq, 2)
        self.partner = (self.dp, self.seq + 1 - 2 * self.core)
        low, high = lax.rem(self.dp, 2), lax.div(self.dp, 2)
        across_x = self.dp + 1 - 2 * low
        across_y = self.dp + 2 - 4 * high
        self.near = across_x + self.core * (across_y - across_x)
        self.far = across_y + self.core * (across_x - across_y)
        self.diagonal = 3 - self.dp
        self.to_near, self.to_far = (self.near, self.seq), (self.far, self.seq)
        self.outer = lax.div(self.z, self.deep // 2)
        self.inner = 1 - self.outer
        self.to_inner = (self.dp, self.seq + 2 - 4 * self.outer)
        self.to_outer = (self.dp, self.seq - 2 + 4 * self.outer)
        self.at_end = (self.z == 0) | (self.z == self.deep - 1)

    def peers(self):
        along = [(self.dp, flip(self.seq, bits)) for bits in range(1, 2 * self.deep)]
        return along + [self.to_near, self.to_far]

    def greet(self):
        for peer in self.peers():
            pl.semaphore_signal(
                pltpu.get_barrier_semaphore(), inc=1, device_id=peer, device_id_type=MESH
            )

    def meet(self):
        pl.semaphore_wait(pltpu.get_barrier_semaphore(), len(self.peers()))

    def copy(self, source, target, device):
        at = self.used
        self.used += 1
        return pltpu.make_async_remote_copy(
            src_ref=source,
            dst_ref=target,
            send_sem=self.send_sem.at[at],
            recv_sem=self.recv_sem.at[at],
            device_id=device,
            device_id_type=MESH,
        )


class Chain:
    def __init__(self, links, base, arrived, leaving, send_sem, recv_sem, chunks):
        self.links, self.base, self.arrived, self.leaving = links, base, arrived, leaving
        self.send_sem, self.recv_sem, self.chunks = send_sem, recv_sem, chunks

    def send(self, k, side, device):
        at = self.chunks[k]
        return pltpu.make_async_remote_copy(
            src_ref=self.leaving.at[side, :, at],
            dst_ref=self.arrived.at[1 - side, :, at],
            send_sem=self.send_sem.at[side, k],
            recv_sem=self.recv_sem.at[1 - side, k],
            device_id=device,
            device_id_type=MESH,
        )

    def receive(self, k, side, device):
        at = self.chunks[k]
        return pltpu.make_async_remote_copy(
            src_ref=self.leaving.at[side, :, at],
            dst_ref=self.arrived.at[side, :, at],
            send_sem=self.send_sem.at[side, k],
            recv_sem=self.recv_sem.at[side, k],
            device_id=device,
            device_id_type=MESH,
        )

    def read(self, ref, k, *side):
        return ref[(*side, slice(None), self.chunks[k])].astype(jnp.float32)

    def begin(self, k):
        links, at = self.links, self.chunks[k]

        @pl.when(links.at_end)
        def _():
            own = self.base[:, at].astype(self.leaving.dtype)
            self.leaving[links.inner, :, at] = own
            self.arrived[links.outer, :, at] = jnp.zeros_like(own)
            self.send(k, links.inner, links.to_inner).start()

    def outward(self, k):
        links, at = self.links, self.chunks[k]

        @pl.when(jnp.logical_not(links.at_end))
        def _():
            self.receive(k, links.outer, links.to_outer).wait_recv()
            total = self.read(self.base, k) + self.read(self.arrived, k, links.outer)
            self.leaving[links.inner, :, at] = total.astype(self.leaving.dtype)
            self.send(k, links.inner, links.to_inner).start()

    def inward(self, k):
        links, at = self.links, self.chunks[k]
        self.receive(k, links.inner, links.to_inner).wait_recv()
        total = self.read(self.base, k) + self.read(self.arrived, k, links.inner)

        @pl.when(jnp.logical_not(links.at_end))
        def _():
            self.leaving[links.outer, :, at] = total.astype(self.leaving.dtype)
            self.send(k, links.outer, links.to_outer).start()

        return total + self.read(self.arrived, k, links.outer)

    def finish(self, k):
        links = self.links
        self.send(k, links.inner, links.to_inner).wait_send()

        @pl.when(jnp.logical_not(links.at_end))
        def _():
            self.send(k, links.outer, links.to_outer).wait_send()


def cut(*edges):
    return tuple(pl.ds(a, b - a) for a, b in zip(edges[:-1], edges[1:]))


def half_tiles(half):
    order = []
    for first, per_block in ((0, 3), (12, 1), (16, 4), (32, 4), (48, 4)):
        order += range(first + 2 * half * per_block, first + 2 * (half + 1) * per_block)
    return order


VMEM = pl.BlockSpec(memory_space=pltpu.VMEM)
SMEM = pl.BlockSpec(memory_space=pltpu.SMEM)
NN = (((1,), (0,)), ((), ()))
NT = (((1,), (1,)), ((), ()))
TN = (((0,), (0,)), ((), ()))


def mul(left, right, dims=NN):
    return lax.dot_general(left, right, dims, preferred_element_type=jnp.float32)


def filter_constants(grid_rows, row_len, width):
    length = grid_rows * row_len
    position = (np.arange(grid_rows)[:, None] + grid_rows * np.arange(row_len)[None, :]).reshape(-1)
    turn = 2.0 * np.pi * position / length
    rows = [position / length, np.cos(turn), -np.sin(turn), np.cos(2 * turn), -np.sin(2 * turn)]
    features = np.zeros((length, 8), np.float32)
    features[:, :5] = np.stack(rows, axis=1)
    rate = 0.3 * 1000.0 ** np.mod(golden * np.arange(width), 1.0)
    total = np.expm1(-2.0 * rate) / np.expm1(-2.0 * rate / length)
    channels = np.stack([rate, 1.0 / np.sqrt(total)]).astype(np.float32)
    return (features, channels)


def phases_of(features, filter_in):
    total = features[:, 0:1] * filter_in[0:1, :]
    for i in range(1, filter_in.shape[0]):
        total += features[:, i : i + 1] * filter_in[i : i + 1, :]
    return total


def first_row(shape):
    return lax.broadcasted_iota(jnp.int32, shape, 0) == 0


def spectrum_product(one_real, one_imag, two_real, two_imag, sign):
    first = first_row(one_real.shape)
    cross = jnp.where(first, 0.0, two_imag) * sign
    diag = jnp.where(first, two_imag, two_real)
    return (one_real * two_real - one_imag * cross, one_real * cross + one_imag * diag)


def decay_of(features, channels, lanes):
    return jnp.exp(-features[:, 0:1] * channels[0:1, lanes]) * channels[1:2, lanes]


def half_lanes(width):
    half = lax.rem(lax.axis_index("seq"), 2)
    return pl.ds(pl.multiple_of(half * width, width), width)


def tile_at(packed, half, first):
    return packed[half, :, first : first + packed.shape[1]]


def normalize(values):
    centered = values - jnp.mean(values, axis=-1, keepdims=True)
    spread = lax.rsqrt(jnp.mean(centered * centered, axis=-1, keepdims=True) + norm_eps)
    return (centered * spread, spread)


def normalize_back(gradient, unit, spread):
    mean = jnp.mean(gradient, axis=-1, keepdims=True)
    along = jnp.mean(gradient * unit, axis=-1, keepdims=True)
    return (gradient - mean - unit * along) * spread


def gelu_parts(v):
    share = 0.5 + 0.5 * lax.erf(v * math.sqrt(0.5))
    density = jnp.exp(-0.5 * v * v) * (1.0 / math.sqrt(2.0 * math.pi))
    return (v * share, share + v * density)


def adam(weight, moment, second, average, gradient, rate, decay):
    moment = beta_one * moment + (1.0 - beta_one) * gradient
    second = beta_two * second + (1.0 - beta_two) * gradient * gradient
    moment = moment * (1.0 / (1.0 - beta_one**STEP))
    root = jnp.sqrt(second * (1.0 / (1.0 - beta_two**STEP)))
    weight = weight - rate * (moment / (root + adam_eps) + decay * weight)
    return (second, weight, keep_rate * average + (1.0 - keep_rate) * weight)


def adam_kernel(scale, owners, reduced, late, *refs):
    tile_in, small_in, tile_out, small_out = refs[:4], refs[4:16], refs[16:20], refs[20:32]
    held, fresh, in_sem, out_sem, tile_of_slot = refs[32:36], refs[36:40], *refs[40:43]
    slots, side, _ = held[0].shape
    per_step = 2

    def load(array, step):
        at = pl.ds(step * per_step, per_step)
        return pltpu.make_async_copy(
            tile_in[array].at[at], held[array].at[at], in_sem.at[array, step]
        )

    def store(array, step):
        at = pl.ds(step * per_step, per_step)
        return pltpu.make_async_copy(
            fresh[array].at[at], tile_out[array].at[at], out_sem.at[array, step]
        )

    steps = slots // per_step
    for step in range(steps):
        for array in range(4):
            load(array, step).start()
    me = lax.axis_index("seq")

    def place(i, rank):
        mine = owners[i] == me

        @pl.when(mine)
        def _():
            tile_of_slot[rank] = i

        return rank + jnp.where(mine, 1, 0)

    owned = lax.fori_loop(0, owners.shape[0], place, jnp.int32(0))
    order, model = small_in[8].shape
    width = model // 2
    count, count_in = small_in[0].shape[0], small_in[4].shape[0]
    sums = late[:, :, late.shape[2] - width :].astype(jnp.float32) * scale
    gradients = (
        jnp.concatenate([sums[h, order : order + count] for h in range(2)], axis=1),
        sums[0, order + 8 : order + 8 + count_in, :order],
        jnp.concatenate([sums[h, :order] for h in range(2)], axis=1),
    )
    rates = ((0.4, 0.0), (0.4, 0.01), (0.1, 0.01))
    for i, (gradient, rate) in enumerate(zip(gradients, rates)):
        small_out[4 * i][...] = gradient
        results = adam(*(ref[...] for ref in small_in[4 * i : 4 * i + 4]), gradient, *rate)
        for ref, values in zip(small_out[4 * i + 1 : 4 * i + 4], results):
            ref[...] = values
    for step in range(steps):
        for array in range(4):
            load(array, step).wait()
        for slot in range(step * per_step, (step + 1) * per_step):
            keep = owned > slot
            tile = jnp.where(keep, tile_of_slot[slot], 0)
            at = jnp.minimum(tile, 11)
            first = pl.multiple_of(lax.div(lax.rem(at, 6), 2) * 2 * side, 2 * side)
            pair = late[lax.div(at, 6), :, pl.ds(first, 2 * side)].astype(jnp.float32)
            from_late = jnp.where(lax.rem(at, 2) == 0, pair[:, :side], pair[:, side:])
            early = reduced[:, slot * side : (slot + 1) * side].astype(jnp.float32)
            gradient = jnp.where(keep, jnp.where(tile < 12, from_late, early) * scale, 0.0)
            fresh[0][slot] = gradient
            results = adam(*(ref[slot] for ref in held), gradient, 0.1, 0.01)
            for ref, values in zip(fresh[1:], results):
                ref[slot] = jnp.where(keep, values, 0.0)
        for array in range(4):
            store(array, step).start()
    for step in range(steps):
        for array in range(4):
            store(array, step).wait()


def adam_call(scale, owners, reduced, late, tile_state, small_state):
    slots = tile_state[0].shape[0]
    state = pltpu.VMEM(tile_state[0].shape, jnp.float32)
    anywhere = pl.BlockSpec(memory_space=pl.ANY)
    shape = jax.ShapeDtypeStruct
    return pl.pallas_call(
        functools.partial(adam_kernel, scale),
        out_shape=tuple(shape(a.shape, a.dtype) for a in tile_state + small_state),
        in_specs=[SMEM] + [VMEM] * 2 + [anywhere] * 4 + [VMEM] * 12,
        out_specs=[anywhere] * 4 + [VMEM] * 12,
        scratch_shapes=[state] * 8
        + [pltpu.SemaphoreType.DMA((4, slots // 2))] * 2
        + [pltpu.SMEM((slots,), jnp.int32)],
        compiler_params=pltpu.CompilerParams(vmem_limit_bytes=VMEM_LIMIT),
        name="adam",
    )(owners, reduced, late, *tile_state, *small_state)


class Exchange:
    def __init__(self, links, cells, columns, send_sem, recv_sem):
        self.links, self.cells, self.columns = links, cells, columns
        self.send_sem, self.recv_sem = send_sem, recv_sem

    def copy(self, bits):
        links = self.links
        peer = flip(links.seq, bits)
        return pltpu.make_async_remote_copy(
            src_ref=self.cells.at[peer],
            dst_ref=self.columns.at[links.seq],
            send_sem=self.send_sem.at[bits],
            recv_sem=self.recv_sem.at[bits],
            device_id=(links.dp, peer),
            device_id_type=MESH,
        )

    def send(self, *bits):
        for b in bits:
            if b == 0:
                me = self.links.seq
                self.columns[me] = self.cells[me]
            else:
                self.copy(b).start()

    def arrived(self, *bits):
        for b in bits:
            if b:
                peer = flip(self.links.seq, b)
                pltpu.make_async_remote_copy(
                    src_ref=self.cells.at[peer],
                    dst_ref=self.columns.at[peer],
                    send_sem=self.send_sem.at[b],
                    recv_sem=self.recv_sem.at[b],
                    device_id=(self.links.dp, peer),
                    device_id_type=MESH,
                ).wait_recv()

    def sent(self):
        for b in range(1, self.cells.shape[0]):
            self.copy(b).wait_send()


def columns_of_chip(columns, chip):
    pair = columns[pl.ds(2 * chip, 2)]
    return pair.reshape(2 * pair.shape[1], pair.shape[2])


def transform_arrivals(exchange, table, spec):
    for near in range(exchange.links.deep):
        transform_pair(exchange, table, spec, near)


def transform_pair(exchange, table, spec, near):
    step = 2 * exchange.columns.shape[1]
    exchange.arrived(2 * near, 2 * near + 1)
    chip = flip(exchange.links.z, near)
    lanes = pl.ds(pl.multiple_of(chip * step, step), step)
    part = mul(table[:, lanes], columns_of_chip(exchange.columns, chip))
    if near:
        spec[...] += part
    else:
        spec[...] = part


def send_inverse(exchange, table_back, filtered):
    row_len = exchange.cells.shape[1]
    for near in reversed(range(exchange.links.deep)):
        chip = flip(exchange.links.z, near)
        rows = pl.ds(pl.multiple_of(chip * 2 * row_len, 2 * row_len), 2 * row_len)
        part = mul(table_back[rows, :], filtered[...]).astype(exchange.cells.dtype)
        exchange.cells[pl.ds(2 * chip, 2)] = part.reshape(2, row_len, part.shape[1])
        exchange.send(2 * near, 2 * near + 1)


class Reducer:
    def __init__(self, links, grads, scratch, chunks):
        (
            self.got,
            self.near_in,
            self.far_in,
            self.far_out,
            self.base,
            arrived,
            leaving,
            chain_send,
            chain_recv,
        ) = scratch
        self.links, self.grads, self.chunks = links, grads, chunks
        self.count = len(chunks)
        self.quarter = self.base.shape[0]
        self.chain = Chain(links, self.base, arrived, leaving, chain_send, chain_recv, chunks)
        self.swaps, self.nears, self.diagonals, self.fars = [], [], [], []
        for at in chunks:
            self.swaps.append(
                links.copy(grads.at[1 - links.core, :, at], self.got.at[:, at], links.partner)
            )
            self.nears.append(
                links.copy(
                    grads.at[links.core, self.rows_of(links.near), at],
                    self.near_in.at[0, :, at],
                    links.to_near,
                )
            )
            self.diagonals.append(
                links.copy(
                    grads.at[links.core, self.rows_of(links.diagonal), at],
                    self.near_in.at[1, :, at],
                    links.to_near,
                )
            )
            self.fars.append(links.copy(self.far_out.at[:, at], self.far_in.at[:, at], links.to_far))

    def rows_of(self, index):
        return pl.ds(pl.multiple_of(index * self.quarter, self.quarter), self.quarter)

    def swap(self, k):
        self.swaps[k].start()

    def swap_half(self, k, half):
        @pl.when(self.links.core != half)
        def _():
            self.swaps[k].start()

    def merge_cores(self, k):
        at, wide = self.chunks[k], jnp.float32
        self.swaps[k].wait_recv()
        core = self.links.core
        self.grads[core, :, at] = (
            self.grads[core, :, at].astype(wide) + self.got[:, at].astype(wide)
        ).astype(self.grads.dtype)
        self.diagonals[k].start()
        self.nears[k].start()

    def go_far(self, k):
        at, wide = self.chunks[k], jnp.float32
        self.diagonals[k].wait_recv()
        self.far_out[:, at] = (
            self.grads[self.links.core, self.rows_of(self.links.far), at].astype(wide)
            + self.near_in[1, :, at].astype(wide)
        ).astype(self.far_out.dtype)
        self.fars[k].start()

    def collect(self, k):
        at, wide = self.chunks[k], jnp.float32
        self.nears[k].wait_recv()
        self.fars[k].wait_recv()
        self.base[:, at] = (
            self.grads[self.links.core, self.rows_of(self.links.dp), at].astype(wide)
            + self.near_in[0, :, at].astype(wide)
            + self.far_in[:, at].astype(wide)
        )
        self.chain.begin(k)

    def outward(self, k):
        self.chain.outward(k)

    def finish(self, k):
        self.swaps[k].wait_send()
        self.nears[k].wait_send()
        self.diagonals[k].wait_send()
        self.fars[k].wait_send()
        self.chain.finish(k)


class Refs:
    def __init__(self, names, refs):
        self.__dict__.update(zip(names, refs, strict=True))


def places(owners, seq):
    rank, place = jnp.int32(0), []
    for i in range(owners.shape[0]):
        mine = owners[i] == seq
        place.append((rank, mine))
        rank = rank + jnp.where(mine, 1, 0)
    return (place, rank)


def tiles_of_slots(place, slots):
    tiles = [jnp.int32(0)] * slots
    for i, (rank, mine) in enumerate(place):
        at = jnp.where(mine, rank, -1)
        tiles = [jnp.where(at == slot, i, tile) for slot, tile in enumerate(tiles)]
    return tiles


def assemble(place, held, own):
    side = held.shape[2]
    place = [(jnp.minimum(rank, held.shape[0] - 1), mine) for rank, mine in place]
    for half in range(2):
        order = half_tiles(half)
        for j in range(0, len(order), 2):
            pair = [jnp.where(place[i][1], held[place[i][0]], 0.0) for i in order[j : j + 2]]
            own[half, :, j * side : (j + 2) * side] = jnp.concatenate(pair, axis=1).astype(own.dtype)


def plane_copies(links, array, at):
    quarter = array.shape[1] // 4

    def rows_of(index):
        return pl.ds(pl.multiple_of(index * quarter, quarter), quarter)

    mine = array.at[links.core, rows_of(links.dp), at]
    other = array.at[links.core, rows_of(links.near), at]
    both = array.at[links.core, :, at]
    return (
        links.copy(mine, mine, links.to_near),
        links.copy(mine, mine, links.to_far),
        links.copy(other, other, links.to_far),
        links.copy(both, both, links.partner),
    )


def step_kernel(names, chunks, first_chunks, early_chunks, late_chunks, *refs):
    r = Refs(names, refs)
    low, wide = jnp.bfloat16, jnp.float32
    links = Links(r.send_sem, r.recv_sem)
    _, side, _ = r.full.shape
    quarter_rows = side // 4
    my_rows = pl.ds(pl.multiple_of(links.dp * quarter_rows, quarter_rows), quarter_rows)
    near_rows = pl.ds(pl.multiple_of(links.near * quarter_rows, quarter_rows), quarter_rows)
    devices, row_len, width = r.kv.shape
    seqs = devices // 2
    length = devices * row_len
    half_length = length // 2
    model = 2 * width
    lanes = half_lanes(width)
    pair_seqs = seqs // 2
    pair_rows = pair_seqs * row_len
    loads = (
        pltpu.make_async_copy(r.master.at[:, my_rows, :], r.held, r.load_sem.at[0]),
        pltpu.make_async_copy(r.table_hbm, r.table, r.load_sem.at[1]),
        pltpu.make_async_copy(r.table_back_hbm, r.table_back, r.load_sem.at[2]),
    )
    for load in loads:
        load.start()
    links.greet()
    loads[0].wait()
    place, owned = places(r.owners, links.seq)
    assemble(place, r.held, r.own)
    links.meet()

    swaps, planes = [], []
    for at in chunks:
        swaps.append(links.copy(r.own.at[1 - links.core, :, at], r.got.at[:, at], links.partner))
        swaps[-1].start()
        planes.append(plane_copies(links, r.full, at))
    chain = Chain(links, r.base, r.arrived, r.leaving, r.chain_send, r.chain_recv, chunks)
    count = len(chunks)

    def hidden_step():
        r.hidden[...] = jnp.sin(phases_of(r.features[...], r.filter_in[...])).astype(low)

    def taps_step(part):
        span = slice(part * length // 4, (part + 1) * length // 4)
        values = mul(r.hidden[span, :], r.filter_out[:, lanes].astype(low))
        decay = jnp.exp(-r.features[span, 0:1] * r.channels[0:1, lanes]) * r.channels[1:2, lanes]
        r.filtered[span, :] = (values * decay).astype(low)

    def spectrum_step(part):
        span = slice(part * length // 4, (part + 1) * length // 4)
        scale = 2.0 / length
        if part % 2 == 0:
            scale = jnp.where(first_row((length // 4, 1)), 1.0 / length, 2.0 / length)
        r.taps_spec[span, :] = mul(r.table[span, :], r.filtered[...]) * scale

    fill = [hidden_step]
    fill += [functools.partial(taps_step, i) for i in range(4)]
    fill += [loads[1].wait]
    fill += [functools.partial(spectrum_step, i) for i in range(4)]
    fill.reverse()

    def fill_in(steps):
        for _ in range(min(steps, len(fill))):
            fill.pop()()

    def collect(k):
        at = chunks[k]
        swaps[k].wait()
        r.base[:, at] = r.own[links.core, :, at] + r.got[:, at]
        chain.begin(k)

    def pass_on(k):
        r.full[links.core, my_rows, chunks[k]] = chain.inward(k).astype(low)
        planes[k][0].start()
        planes[k][1].start()

    def relay(k):
        planes[k][0].wait_recv()
        planes[k][2].start()

    def share(k):
        planes[k][1].wait_recv()
        planes[k][2].wait_recv()
        planes[k][3].start()

    fill_in(1)
    for k in range(count):
        collect(k)
    tiles = tiles_of_slots(place, r.held.shape[0])
    stages = ((chain.outward, 0), (pass_on, 1), (relay, 2), (share, 4))
    after = [
        [(stage, k - late) for stage, late in stages if 0 <= k - late < count]
        for k in range(count + 4)
    ]

    def go_on(steps=1):
        for _ in range(min(steps, len(after))):
            for stage, k in after.pop(0):
                stage(k)

    for _ in range(count):
        fill_in(2)
        go_on()
    for k in range(first_chunks):
        planes[k][3].wait_recv()
    fill_in(len(fill))

    outbound = Exchange(links, r.kv, r.columns, r.field_send, r.field_recv)

    def project(pair, tiles_here):
        span = pl.ds(pl.multiple_of(pair * pair_rows, pair_rows), pair_rows)
        for i in tiles_here:
            block = i // 3
            weight = tile_at(r.full, i // 6, (i % 6) * side)
            part = mul(r.x[span, block * side : (block + 1) * side], weight)
            target = (r.query, r.key, r.value)[i // 4]
            at = (i % 4) * side
            target[span, at : at + side] = part.astype(low)

    def multiply(pair):
        for s in range(pair_seqs):
            seq = pair * pair_seqs + s
            line = pl.ds(pl.multiple_of(seq * row_len, row_len), row_len)
            for h in range(2):
                part = slice(h * width, (h + 1) * width)
                both = r.key[line, part].astype(wide) * r.value[line, part].astype(wide)
                r.kv[2 * seq + h] = both.astype(low)

    for pair, bits in ((links.inner, (6, 7, 4, 5)), (links.outer, (2, 3, 1, 0))):
        project(pair, range(4, 12))
        multiply(pair)
        outbound.send(*bits)
        go_on()
    for pair in (links.outer, links.inner):
        project(pair, range(4))
    for near in range(links.deep):
        transform_pair(outbound, r.table, r.kv_spec, near)
        go_on()
    go_on(len(after))

    def filter_with(ref, other, sign, scale=None):
        real, imag = spectrum_product(
            ref[:half_length], ref[half_length:], other[:half_length], other[half_length:], sign
        )
        if scale is not None:
            real, imag = real * scale, imag * scale
        r.filtered[:half_length] = real.astype(low)
        r.filtered[half_length:] = imag.astype(low)

    filter_with(r.kv_spec, r.taps_spec, 1.0)
    loads[2].wait()
    inbound = Exchange(links, r.cells_back, r.conv, r.back_send, r.back_recv)
    send_inverse(inbound, r.table_back, r.filtered)
    for k in range(first_chunks, count):
        planes[k][3].wait_recv()

    out_at, gate_at, up_at, down_at = 6 * side, 8 * side, 16 * side, 24 * side
    quarter = 4 * side
    for b in range(4):
        for i in range(4):
            r.down_weights[b, i * side : (i + 1) * side, :] = tile_at(
                r.full, b // 2, down_at + (4 * (b % 2) + i) * side
            )
    r.sums[...] = jnp.zeros_like(r.sums)
    gain_one, bias_one = r.vectors[0:1], r.vectors[1:2]
    gain_two, bias_two = r.vectors[2:3], r.vectors[3:4]
    skip = r.vectors[4:5]

    def cells(ref, seq, seqs_here):
        parts = ref[pl.ds(2 * seq, 2 * seqs_here)].astype(wide)
        lines = [
            jnp.concatenate([parts[2 * s], parts[2 * s + 1]], axis=1) for s in range(seqs_here)
        ]
        return jnp.concatenate(lines, axis=0)

    def block(values, b):
        return values[:, b * side : (b + 1) * side]

    def weight_of(first, b, count):
        at = first + (b % 2) * count
        return r.full[b // 2, :, at : at + count]

    def add_sum(row, values):
        r.sums[row : row + 1, :] += jnp.sum(values, axis=0, keepdims=True)

    def layer(seq, seqs_here, first):
        rows = pl.ds(pl.multiple_of(seq * row_len, row_len), seqs_here * row_len)
        held = slice(first * row_len, (first + seqs_here) * row_len)
        kv_here = cells(r.kv, seq, seqs_here)
        inner = cells(r.conv, seq, seqs_here) + skip * kv_here
        query_here = r.query[rows, :].astype(wide)
        gated = (query_here * inner).astype(low)
        r.gated[held, :] = gated
        branch = [mul(block(gated, b), weight_of(out_at, b, side)) for b in range(4)]
        unit_one, spread_one = normalize(
            r.x[rows, :].astype(wide) + jnp.concatenate(branch, axis=1)
        )
        normed = (unit_one * gain_one + bias_one).astype(low)
        r.normed[held, :] = normed
        down = []
        for b in range(4):
            span = slice(b * quarter, (b + 1) * quarter)
            here = block(normed, b)
            gate = mul(here, weight_of(gate_at, b, quarter))
            up = mul(here, weight_of(up_at, b, quarter))
            curved, slope = gelu_parts(gate)
            active = (curved * up).astype(low)
            r.active[held, span] = active
            r.d_gate[held, span] = (slope * up).astype(low)
            r.d_up[held, span] = curved.astype(low)
            down.append(mul(active, r.down_weights[b]))
        unit_two, spread_two = normalize(normed.astype(wide) + jnp.concatenate(down, axis=1))
        r.output[rows, :] = (unit_two * gain_two + bias_two).astype(low)
        cot = r.cotangent[rows, :].astype(wide)
        add_sum(2, cot * unit_two)
        add_sum(3, cot)
        d_second = normalize_back(cot * gain_two, unit_two, spread_two)
        d_down = d_second.astype(low)
        r.d_down[held, :] = d_down
        d_normed = []
        for b in range(4):
            span = slice(b * quarter, (b + 1) * quarter)
            d_active = mul(block(d_down, b), r.down_weights[b], NT)
            d_gate = (d_active * r.d_gate[held, span].astype(wide)).astype(low)
            d_up = (d_active * r.d_up[held, span].astype(wide)).astype(low)
            r.d_gate[held, span] = d_gate
            r.d_up[held, span] = d_up
            d_normed.append(
                mul(d_gate, weight_of(gate_at, b, quarter), NT)
                + mul(d_up, weight_of(up_at, b, quarter), NT)
            )
        d_normed = d_second + jnp.concatenate(d_normed, axis=1)
        add_sum(0, d_normed * unit_one)
        add_sum(1, d_normed)
        d_first = normalize_back(d_normed * gain_one, unit_one, spread_one)
        r.in_grad[rows, :] = d_first
        d_branch = d_first.astype(low)
        r.d_branch[held, :] = d_branch
        d_gated = [mul(block(d_branch, b), weight_of(out_at, b, side), NT) for b in range(4)]
        d_gated = jnp.concatenate(d_gated, axis=1)
        r.query[rows, :] = (d_gated * inner).astype(low)
        d_inner = d_gated * query_here
        add_sum(4, d_inner * kv_here)
        d_inner = d_inner.astype(low)
        for s in range(seqs_here):
            for h in range(2):
                r.d_inner[2 * (seq + s) + h] = d_inner[
                    s * row_len : (s + 1) * row_len, h * width : (h + 1) * width
                ]

    def layer_grads(rows, more):
        for b in range(4):
            span = slice(b * quarter, (b + 1) * quarter)
            mine = slice(b * side, (b + 1) * side)
            at = (b % 2) * quarter

            def put(first, values):
                target = slice(first - out_at, first - out_at + values.shape[1])
                if more:
                    values += r.grads[b // 2, :, target].astype(wide)
                r.grads[b // 2, :, target] = values.astype(low)

            put(out_at + (b % 2) * side, mul(r.gated[rows, mine], r.d_branch[rows, mine], TN))
            put(gate_at + at, mul(r.normed[rows, mine], r.d_gate[rows, span], TN))
            put(up_at + at, mul(r.normed[rows, mine], r.d_up[rows, span], TN))
            tall = mul(r.active[rows, span], r.d_down[rows, mine], TN)
            for i in range(4):
                put(down_at + at + i * side, tall[i * side : (i + 1) * side, :])

    back_out = Exchange(links, r.d_inner, r.columns, r.field_send_two, r.field_recv_two)
    inbound.arrived(1, 2, 3)
    layer(links.outer * pair_seqs, pair_seqs, 0)
    back_out.send(2, 3, 1, 0)
    inbound.arrived(6, 7)
    layer(flip(links.z, 3), 1, 2)
    back_out.send(6, 7)
    layer_grads(slice(0, 2 * row_len), False)
    inbound.arrived(4, 5)
    layer(flip(links.z, 2), 1, 1)
    back_out.send(4, 5)
    layer_grads(slice(row_len, 3 * row_len), True)

    early_wide = r.grads.shape[2]
    early = Reducer(
        links,
        r.grads,
        (
            r.early_got,
            r.own.at[:, :, pl.ds(0, early_wide)],
            r.got.at[:, pl.ds(0, early_wide)],
            r.base.at[:, pl.ds(0, early_wide)],
            r.early_base,
            r.arrived.at[:, :, pl.ds(0, early_wide)],
            r.leaving.at[:, :, pl.ds(0, early_wide)],
            r.early_send,
            r.early_recv,
        ),
        early_chunks,
    )
    tail = Reducer(
        links,
        r.late,
        (
            r.late_got,
            r.late_near,
            r.late_far_in,
            r.late_far_out,
            r.late_base,
            r.late_arrived,
            r.late_leaving,
            r.late_send,
            r.late_recv,
        ),
        late_chunks,
    )
    for k in range(count):
        chain.finish(k)
        for copy in planes[k]:
            copy.wait_send()
    for k in range(early.count):
        early.swap(k)
    r.late[...] = jnp.zeros_like(r.late)
    for k in range(early.count):
        early.merge_cores(k)
    per_pair = -(-early.count // links.deep)
    for near in range(links.deep):
        transform_pair(back_out, r.table, r.spec, near)
        for k in range(near * per_pair, min((near + 1) * per_pair, early.count)):
            early.go_far(k)
    filter_with(r.spec, r.taps_spec, -1.0)
    inbound.sent()
    back_in = Exchange(links, r.cells_back, r.conv, r.back_send_two, r.back_recv_two)
    send_inverse(back_in, r.table_back, r.filtered)

    totals = []
    for at in early_chunks:
        part = r.total.at[links.core, :, at]
        totals.append(links.copy(part, part, links.partner))

    def early_total(k):
        r.total[links.core, :, early_chunks[k]] = early.chain.inward(k).astype(low)
        totals[k].start()

    for k in range(early.count):
        early.collect(k)
    scale = jnp.where(first_row((half_length, 1)), 1.0 / length, 2.0 / length)
    filter_with(r.spec, r.kv_spec, -1.0, scale)
    scaled = mul(r.table_back[...], r.filtered[...]) * decay_of(r.features, r.channels, lanes)
    scaled = scaled.astype(low)
    phases = phases_of(r.features[...], r.filter_in[...])
    order = r.filter_in.shape[1]
    first_late = 6 * side
    r.late[links.core, 0:order, first_late:] = mul(r.hidden[...], scaled, TN).astype(low)
    d_hidden = mul(scaled, r.filter_out[:, lanes].astype(low), NT) * jnp.cos(phases)
    lines = [
        jnp.sum(r.features[:, i : i + 1] * d_hidden, axis=0, keepdims=True)
        for i in range(r.filter_in.shape[0])
    ]
    lines.append(jnp.zeros((8 - len(lines), order), wide))
    in_lines = jnp.concatenate(lines, axis=0)
    for half in range(2):
        other = jnp.zeros((8, width), wide)
        if half == 0:
            other = jnp.concatenate([in_lines, jnp.zeros((8, width - order), wide)], axis=1)
        both = jnp.concatenate([r.sums[:, half * width : (half + 1) * width], other], axis=0)
        r.late[half, order : order + 16, first_late:] = both.astype(low)

    per_block = 3 * side
    pairs = ((links.outer, r.d_gate), (links.inner, r.d_up))

    def span_of(pair):
        return pl.ds(pl.multiple_of(pair * pair_rows, pair_rows), pair_rows)

    def fill_rows(pair, d_qkv):
        d_qkv[:pair_rows, :model] = r.query[span_of(pair), :]
        for s in range(pair_seqs):
            seq = pair * pair_seqs + s
            line = pl.ds(pl.multiple_of(seq * row_len, row_len), row_len)
            here = slice(s * row_len, (s + 1) * row_len)
            for h in range(2):
                part = slice(h * width, (h + 1) * width)
                cell = 2 * seq + h
                d_kv = r.conv[cell].astype(wide) + skip[:, part] * r.d_inner[cell].astype(wide)
                d_qkv[here, model + h * width : model + (h + 1) * width] = (
                    d_kv * r.value[line, part].astype(wide)
                ).astype(low)
                d_qkv[here, 2 * model + h * width : 2 * model + (h + 1) * width] = (
                    d_kv * r.key[line, part].astype(wide)
                ).astype(low)

    def first_map_grad(b, pair, d_qkv, more):
        mine = slice(b * side, (b + 1) * side)
        at = (b % 2) * per_block
        target = slice(at, at + per_block)
        values = mul(
            r.x[span_of(pair), mine], d_qkv[:pair_rows, b * per_block : (b + 1) * per_block], TN
        )
        if more:
            values += r.late[b // 2, :, target].astype(wide)
        r.late[b // 2, :, target] = values.astype(low)
        if more and b % 2:
            for k in range(tail.count):
                tail.swap_half(k, b // 2)

    def input_gradient(b):
        mine = slice(b * side, (b + 1) * side)
        span = slice(b * per_block, (b + 1) * per_block)
        for pair, d_qkv in pairs:
            r.in_grad[span_of(pair), mine] += mul(
                d_qkv[:pair_rows, span], weight_of(0, b, per_block), NT
            )

    back_in.arrived(1, 2, 3)
    fill_rows(*pairs[0])
    for b in range(4):
        first_map_grad(b, *pairs[0], False)
    early.outward(0)
    back_in.arrived(4, 5, 6, 7)
    fill_rows(*pairs[1])
    first_map_grad(0, *pairs[1], True)
    early.outward(1)
    first_map_grad(1, *pairs[1], True)
    early_total(0)
    early.outward(2)
    first_map_grad(2, *pairs[1], True)
    early_total(1)
    first_map_grad(3, *pairs[1], True)
    early.outward(3)
    early_total(2)
    for k in range(tail.count):
        tail.merge_cores(k)
    early.outward(4)
    early_total(3)
    for k in range(tail.count):
        tail.go_far(k)
    input_gradient(0)
    early_total(4)
    for k in range(tail.count):
        tail.collect(k)
    input_gradient(1)
    for copy in totals:
        copy.wait()
    for half in range(2):
        for j, i in enumerate(half_tiles(half)):
            if i >= 12:
                at = (j - 6) * side
                r.by_tile[i - 12] = r.total[half, :, at : at + side]
    for s in range(0, len(tiles), 2):
        pair = []
        for k in (s, s + 1):
            values = r.by_tile[jnp.maximum(tiles[k] - 12, 0)].astype(wide)
            pair.append(jnp.where(owned > k, values, 0.0))
        r.spread[my_rows, s * side : (s + 2) * side] = jnp.concatenate(pair, axis=1).astype(low)
    at_home, other = r.spread.at[my_rows, :], r.spread.at[near_rows, :]
    slot_copies = (
        links.copy(at_home, at_home, links.to_near),
        links.copy(at_home, at_home, links.to_far),
        links.copy(other, other, links.to_far),
    )
    late_planes = [plane_copies(links, r.late_full, at) for at in late_chunks]
    slot_copies[0].start()
    slot_copies[1].start()
    for k in range(tail.count):
        tail.outward(k)
    input_gradient(2)
    slot_copies[0].wait_recv()
    slot_copies[2].start()
    for k in range(tail.count):
        r.late_full[links.core, my_rows, late_chunks[k]] = tail.chain.inward(k).astype(low)
        late_planes[k][0].start()
        late_planes[k][1].start()
    for copies in late_planes:
        copies[0].wait_recv()
        copies[2].start()
    input_gradient(3)
    for copies in late_planes:
        copies[1].wait_recv()
        copies[2].wait_recv()
        copies[3].start()
    slot_copies[1].wait_recv()
    slot_copies[2].wait_recv()
    for copies in late_planes:
        for copy in copies[:3]:
            copy.wait_send()
        copies[3].wait()
    for copy in slot_copies:
        copy.wait_send()
    outbound.sent()
    back_out.sent()
    back_in.sent()
    for reducer in (early, tail):
        for k in range(reducer.count):
            reducer.finish(k)


def step_call(arrays, cells):
    slots, side, _ = arrays["master"].shape
    tokens, model = arrays["x"].shape
    order = arrays["filter_in"].shape[1]
    devices, row_len, columns = cells
    length = devices * row_len
    width = arrays["owners"].shape[0] // 2 * side
    early_width = width - 6 * side
    late_width = 6 * side + columns
    chunks = cut(0, 640, 1152, 1920, 2816, 3584, 4480, 5248, width)
    early_chunks = cut(0, 1152, 2176, 3200, 4096, early_width)
    late_chunks = cut(0, 512, 1024, late_width)
    low, wide = jnp.bfloat16, jnp.float32
    quarter, held_tokens = side // 4, 3 * row_len
    shape = jax.ShapeDtypeStruct
    count, early_count, late_count = len(chunks), len(early_chunks), len(late_chunks)
    copies = 5 * (count + early_count) + 8 * late_count + 3
    dma = pltpu.SemaphoreType.DMA
    outputs = dict(
        output=shape((tokens, model), low),
        in_grad=shape((tokens, model), wide),
        spread=shape((side, slots * side), low),
        late_full=shape((2, side, late_width), low),
    )
    scratch = dict(
        held=pltpu.VMEM((slots, quarter, side), wide),
        full=pltpu.VMEM((2, side, width), low),
        own=pltpu.VMEM((2, quarter, width), low),
        got=pltpu.VMEM((quarter, width), low),
        base=pltpu.VMEM((quarter, width), low),
        arrived=pltpu.VMEM((2, quarter, width), low),
        leaving=pltpu.VMEM((2, quarter, width), low),
        table=pltpu.VMEM((length, length), low),
        table_back=pltpu.VMEM((length, length), low),
        hidden=pltpu.VMEM((length, order), low),
        filtered=pltpu.VMEM((length, columns), low),
        taps_spec=pltpu.VMEM((length, columns), wide),
        kv_spec=pltpu.VMEM((length, columns), wide),
        spec=pltpu.VMEM((length, columns), wide),
        query=pltpu.VMEM((tokens, model), low),
        key=pltpu.VMEM((tokens, model), low),
        value=pltpu.VMEM((tokens, model), low),
        gated=pltpu.VMEM((held_tokens, model), low),
        normed=pltpu.VMEM((held_tokens, model), low),
        d_branch=pltpu.VMEM((held_tokens, model), low),
        d_down=pltpu.VMEM((held_tokens, model), low),
        active=pltpu.VMEM((held_tokens, 16 * side), low),
        d_gate=pltpu.VMEM((held_tokens, 16 * side), low),
        d_up=pltpu.VMEM((held_tokens, 16 * side), low),
        down_weights=pltpu.VMEM((4, 4 * side, side), low),
        sums=pltpu.VMEM((8, model), wide),
        grads=pltpu.VMEM((2, side, early_width), low),
        early_got=pltpu.VMEM((side, early_width), low),
        early_base=pltpu.VMEM((quarter, early_width), wide),
        total=pltpu.VMEM((2, quarter, early_width), low),
        by_tile=pltpu.VMEM((NTILES - 12, quarter, side), low),
        late=pltpu.VMEM((2, side, late_width), low),
        late_got=pltpu.VMEM((side, late_width), low),
        late_near=pltpu.VMEM((2, quarter, late_width), low),
        late_far_in=pltpu.VMEM((quarter, late_width), low),
        late_far_out=pltpu.VMEM((quarter, late_width), low),
        late_base=pltpu.VMEM((quarter, late_width), wide),
        late_arrived=pltpu.VMEM((2, quarter, late_width), low),
        late_leaving=pltpu.VMEM((2, quarter, late_width), low),
        load_sem=dma((3,)),
        send_sem=dma((copies,)),
        recv_sem=dma((copies,)),
        chain_send=dma((2, count)),
        chain_recv=dma((2, count)),
        early_send=dma((2, early_count)),
        early_recv=dma((2, early_count)),
        late_send=dma((2, late_count)),
        late_recv=dma((2, late_count)),
    )
    for name in ("kv", "columns", "cells_back", "conv", "d_inner"):
        scratch[name] = pltpu.VMEM(cells, low)
    for name in ("field", "back"):
        for end in ("send", "recv", "send_two", "recv_two"):
            scratch[name + "_" + end] = dma((devices,))
    anywhere = pl.BlockSpec(memory_space=pl.ANY)
    spaces = dict(owners=SMEM, master=anywhere)
    spaces |= dict(table_hbm=anywhere, table_back_hbm=anywhere)
    names = (*arrays, *outputs, *scratch)
    return pl.pallas_call(
        functools.partial(step_kernel, names, chunks, 2, early_chunks, late_chunks),
        out_shape=tuple(outputs.values()),
        in_specs=[spaces.get(name, VMEM) for name in arrays],
        out_specs=(VMEM,) * len(outputs),
        scratch_shapes=list(scratch.values()),
        compiler_params=pltpu.CompilerParams(
            collective_id=0, has_side_effects=True, vmem_limit_bytes=STEP_VMEM
        ),
        name="step",
    )(*arrays.values())


def on_device_columns(
    tokens,
    cotangent,
    owners,
    tile_master,
    tile_moment,
    tile_second,
    tile_average,
    vectors,
    vector_moment,
    vector_second,
    vector_average,
    filter_in,
    in_moment,
    in_second,
    in_average,
    filter_out,
    out_moment,
    out_second,
    out_average,
):
    seq_count, dev_rows, row_len, model_width = tokens.shape
    seq_devices = lax.axis_size("seq")
    grid_rows = dev_rows * seq_devices
    count = seq_count * row_len
    table_host = real_table(grid_rows, row_len)
    table, table_back = jnp.asarray(table_host), jnp.asarray(np.ascontiguousarray(table_host.T))
    features, channels = (
        jnp.asarray(a) for a in filter_constants(grid_rows, row_len, model_width)
    )
    x = tokens.reshape(count, model_width)

    output, in_grad, reduced, late = step_call(
        dict(
            owners=owners,
            master=tile_master,
            x=x,
            cotangent=cotangent.reshape(count, model_width),
            vectors=vectors,
            features=features,
            channels=channels,
            filter_in=filter_in,
            filter_out=filter_out,
            table_hbm=table,
            table_back_hbm=table_back,
        ),
        (seq_devices, row_len, model_width // 2),
    )
    tokens_all = count * lax.axis_size("dp") * seq_devices
    updated = adam_call(
        1.0 / math.sqrt(tokens_all),
        owners,
        reduced,
        late,
        (tile_master, tile_moment, tile_second, tile_average),
        (
            vectors,
            vector_moment,
            vector_second,
            vector_average,
            filter_in,
            in_moment,
            in_second,
            in_average,
            filter_out,
            out_moment,
            out_second,
            out_average,
        ),
    )
    return (output.reshape(tokens.shape), in_grad.reshape(tokens.shape), *updated)


def on_device(*arrays):
    seq_count, dev_rows, row_len, model_width = arrays[0].shape
    seq_devices = lax.axis_size("seq")
    fits = dev_rows == 1 and lax.axis_size("dp") == 4 and seq_devices == 2 * seq_count == 8
    if fits and row_len == 128 and model_width % 256 == 0:
        return on_device_columns(*arrays)
    return on_device_general(*arrays)


def solution(mesh):
    in_specs = (
        P("dp", "seq", None, None),
        P("dp", "seq", None, None),
        P(),
        P("seq", None, None),
        P("seq", None, None),
        P("seq", None, None),
        P("seq", None, None),
        P(),
        P(),
        P(),
        P(),
        P(),
        P(),
        P(),
        P(),
        P(),
        P(),
        P(),
        P(),
    )
    out_specs = (
        P("dp", "seq", None, None),
        P("dp", "seq", None, None),
        P("seq", None, None),
        P("seq", None, None),
        P("seq", None, None),
        P("seq", None, None),
        P(),
        P(),
        P(),
        P(),
        P(),
        P(),
        P(),
        P(),
        P(),
        P(),
        P(),
        P(),
    )
    return jax.shard_map(
        on_device, mesh=mesh, in_specs=in_specs, out_specs=out_specs, check_vma=False
    )
```

```python
import functools
import math

import jax
import jax.numpy as jnp
import ml_dtypes
import numpy as np
from jax import lax
from jax.experimental import pallas as pl
from jax.experimental.pallas import tpu as pltpu
from jax.sharding import PartitionSpec as P

D = 768
FF = 3072
STEP = 10
NTILES = 64


highest = lax.Precision.HIGHEST
beta_one = 0.9
beta_two = 0.999
keep_rate = 0.5
adam_eps = 1e-08
norm_eps = 1e-05
golden = 0.6180339887


def norm_rows(values, gain_vec, bias_vec):
    row_mean = jnp.mean(values, axis=-1, keepdims=True)
    centered = values - row_mean
    spread = jnp.mean(centered * centered, axis=-1, keepdims=True)
    return centered * lax.rsqrt(spread + norm_eps) * gain_vec + bias_vec


def glu_act(gate_value, up_value):
    return jax.nn.gelu(gate_value, approximate=False) * up_value


def filter_taps(filter_in, filter_out, position, length):
    channel = jnp.arange(filter_out.shape[1], dtype=jnp.int32)
    return filter_taps_of(filter_in, filter_out, position, length, channel)


def filter_taps_of(filter_in, filter_out, position, length, channel_index):
    phases = position * (2.0 * math.pi / length)
    features = jnp.stack(
        [
            position / length,
            jnp.cos(phases),
            -jnp.sin(phases),
            jnp.cos(2.0 * phases),
            -jnp.sin(2.0 * phases),
        ],
        axis=1,
    )
    hidden = jnp.sin(jnp.dot(features, filter_in, precision=highest))
    taps_value = jnp.dot(hidden, filter_out, precision=highest)
    channel = channel_index.astype(jnp.float32)
    decay_rates = 0.3 * jnp.exp(math.log(1000.0) * jnp.mod(channel * golden, 1.0))
    decay_rate = jnp.exp(-(position / length)[:, None] * decay_rates[None, :])
    total = jnp.expm1(-2.0 * decay_rates) / jnp.expm1(-2.0 * decay_rates / length)
    norm_scale = lax.rsqrt(total)
    return taps_value * decay_rate * norm_scale


def block_weight(tile_stack, in_tiles, out_tiles):
    tile_side = tile_stack.shape[-1]
    tile_grid = tile_stack.reshape(4, in_tiles, out_tiles, tile_side, tile_side).transpose(
        0, 1, 3, 2, 4
    )
    return tile_grid.reshape(4, in_tiles * tile_side, out_tiles * tile_side)


def tile_split(blocks, in_tiles, out_tiles):
    tile_side = blocks.shape[1] // in_tiles
    tile_grid = blocks.reshape(4, in_tiles, tile_side, out_tiles, tile_side).transpose(
        0, 1, 3, 2, 4
    )
    return tile_grid.reshape(4 * in_tiles * out_tiles, tile_side, tile_side)


def block_apply(values, blocks):
    row_view = values.reshape(values.shape[0], 4, -1)
    return jnp.einsum("nbi,bio->nbo", row_view, blocks, preferred_element_type=jnp.float32).reshape(
        values.shape[0], -1
    )


def block_back(gradient, blocks):
    row_view = gradient.reshape(gradient.shape[0], 4, -1)
    return jnp.einsum("nbo,bio->nbi", row_view, blocks, preferred_element_type=jnp.float32).reshape(
        gradient.shape[0], -1
    )


def block_grad(values, gradient, in_tiles, out_tiles):
    left_rows = values.reshape(values.shape[0], 4, -1)
    right_rows = gradient.reshape(gradient.shape[0], 4, -1)
    blocks = jnp.einsum("nbi,nbo->bio", left_rows, right_rows, preferred_element_type=jnp.float32)
    return tile_split(blocks, in_tiles, out_tiles)


def slot_maps(owners, owner_cap, slot_total):
    tile_count = owners.shape[0]
    tile_index = jnp.arange(tile_count, dtype=jnp.int32)
    earlier = (owners[:, None] == owners[None, :]) & (tile_index[None, :] < tile_index[:, None])
    owner_rank = jnp.sum(earlier.astype(jnp.int32), axis=1)
    slot_of_tile = owners * owner_cap + owner_rank
    slot_hits = slot_of_tile[None, :] == jnp.arange(slot_total, dtype=jnp.int32)[:, None]
    tile_of_slot = jnp.sum(slot_hits.astype(jnp.int32) * tile_index[None, :], axis=1)
    slot_used = jnp.any(slot_hits, axis=1)
    return (slot_of_tile, tile_of_slot, slot_used)


def adam_step(weight, moment, second, average, gradient, step_rate, decay_rate):
    moment = beta_one * moment + (1.0 - beta_one) * gradient
    second = beta_two * second + (1.0 - beta_two) * gradient * gradient
    fixed_moment = moment / (1.0 - beta_one**STEP)
    fixed_second = second / (1.0 - beta_two**STEP)
    weight = weight - step_rate * (
        fixed_moment / (jnp.sqrt(fixed_second) + adam_eps) + decay_rate * weight
    )
    average = keep_rate * average + (1.0 - keep_rate) * weight
    return (second, weight, average)


def wave_table(period, index_one, index_two):
    turn_count = jnp.mod(index_one[:, None] * index_two[None, :], period).astype(jnp.float32)
    angles = turn_count * (2.0 * math.pi / period)
    return (jnp.cos(angles), jnp.sin(angles))


def col_dot(field_in, table_in):
    return jnp.einsum("srcd,ck->srkd", field_in, table_in, precision=highest)


def row_dot(field_in, table_in):
    return jnp.einsum("srkd,rq->sqkd", field_in, table_in, precision=highest)


def cols_forward(field_in, tables):
    col_cos, col_sin, turn_cos, turn_sin, row_cos, row_sin = tables
    real_part = col_dot(field_in, col_cos)
    imag_part = -col_dot(field_in, col_sin)
    real_turn = real_part * turn_cos + imag_part * turn_sin
    imag_turn = imag_part * turn_cos - real_part * turn_sin
    return (real_turn, imag_turn)


def rows_forward(part_real, part_imag, tables):
    row_cos, row_sin = (tables[4], tables[5])
    freq_real = row_dot(part_real, row_cos) + row_dot(part_imag, row_sin)
    freq_imag = row_dot(part_imag, row_cos) - row_dot(part_real, row_sin)
    return (freq_real, freq_imag)


def rows_inverse(prod_real, prod_imag, tables):
    row_cos, row_sin = (tables[4], tables[5])
    back_real = row_dot(prod_real, row_cos) - row_dot(prod_imag, row_sin)
    back_imag = row_dot(prod_real, row_sin) + row_dot(prod_imag, row_cos)
    return (back_real, back_imag)


def cols_inverse(rows_real, rows_imag, tables, length):
    col_cos, col_sin, turn_cos, turn_sin, row_cos, row_sin = tables
    cell_real = rows_real * turn_cos - rows_imag * turn_sin
    cell_imag = rows_real * turn_sin + rows_imag * turn_cos
    return (
        jnp.einsum("srkd,ck->srcd", cell_real, col_cos, precision=highest)
        - jnp.einsum("srkd,ck->srcd", cell_imag, col_sin, precision=highest)
    ) / length


def convolve(field_in, spectrum, tables, conjugate, length):
    spec_real, spec_imag = spectrum
    sign_flip = -1.0 if conjugate else 1.0
    real_turn, imag_turn = cols_forward(field_in, tables)
    part_real = lax.all_to_all(real_turn, "seq", split_axis=2, concat_axis=1, tiled=True)
    part_imag = lax.all_to_all(imag_turn, "seq", split_axis=2, concat_axis=1, tiled=True)
    freq_real, freq_imag = rows_forward(part_real, part_imag, tables)
    prod_real = freq_real * spec_real - sign_flip * freq_imag * spec_imag
    prod_imag = sign_flip * freq_real * spec_imag + freq_imag * spec_real
    back_real, back_imag = rows_inverse(prod_real, prod_imag, tables)
    rows_real = lax.all_to_all(back_real, "seq", split_axis=1, concat_axis=2, tiled=True)
    rows_imag = lax.all_to_all(back_imag, "seq", split_axis=1, concat_axis=2, tiled=True)
    rows_real, rows_imag, freq_real, freq_imag = (rows_real, rows_imag, freq_real, freq_imag)
    field_out = cols_inverse(rows_real, rows_imag, tables, length)
    return (field_out, freq_real, freq_imag)


def real_table(grid_rows, row_len):
    length = grid_rows * row_len
    position = (np.arange(grid_rows)[:, None] + grid_rows * np.arange(row_len)[None, :]).reshape(-1)
    turns = np.mod(np.arange(length // 2)[:, None] * position[None, :], length)
    angles = turns * (2.0 * np.pi / length)
    sines = -np.sin(angles)
    sines[0] = np.cos(np.pi * position)
    return np.concatenate([np.cos(angles), sines]).astype(ml_dtypes.bfloat16)


def on_device_general(
    tokens,
    cotangent,
    owners,
    tile_master,
    tile_moment,
    tile_second,
    tile_average,
    vectors,
    vector_moment,
    vector_second,
    vector_average,
    filter_in,
    in_moment,
    in_second,
    in_average,
    filter_out,
    out_moment,
    out_second,
    out_average,
):
    seq_count, dev_rows, row_len, model_width = tokens.shape
    owner_cap = tile_master.shape[0]
    seq_devices = lax.axis_size("seq")
    grid_rows = dev_rows * seq_devices
    length = grid_rows * row_len
    seq_index = lax.axis_index("seq")
    hidden_ratio = FF // D
    quarter_hidden = FF // 4
    slot_of_tile, tile_of_slot, slot_used = slot_maps(owners, owner_cap, owner_cap * seq_devices)
    gathered = lax.all_gather(tile_master.astype(jnp.bfloat16), "seq", axis=0, tiled=True)
    weights = jnp.take(gathered, slot_of_tile, axis=0)
    w_in = block_weight(weights[0:12], 1, 3)
    w_out = block_weight(weights[12:16], 1, 1)
    w_gate = block_weight(weights[16 : 16 + 4 * hidden_ratio], 1, hidden_ratio)
    w_up = block_weight(weights[16 + 4 * hidden_ratio : 16 + 8 * hidden_ratio], 1, hidden_ratio)
    w_down = block_weight(weights[16 + 8 * hidden_ratio : 16 + 12 * hidden_ratio], hidden_ratio, 1)
    w_gate_up = jnp.concatenate([w_gate, w_up], axis=2)
    col_index = jnp.arange(row_len, dtype=jnp.int32)
    row_index = jnp.arange(grid_rows, dtype=jnp.int32)
    local_rows = seq_index * dev_rows + jnp.arange(dev_rows, dtype=jnp.int32)
    col_cos, col_sin = wave_table(row_len, col_index, col_index)
    row_cos, row_sin = wave_table(grid_rows, row_index, row_index)
    turn_cos, turn_sin = wave_table(length, local_rows, col_index)
    tables = (
        col_cos,
        col_sin,
        turn_cos[None, :, :, None],
        turn_sin[None, :, :, None],
        row_cos,
        row_sin,
    )
    own_position = (
        (local_rows[:, None] + grid_rows * col_index[None, :]).reshape(-1).astype(jnp.float32)
    )
    flat_tokens = tokens.reshape(-1, model_width)
    qkv_all = block_apply(flat_tokens, w_in)
    query_part = qkv_all[:, :model_width]
    key_part = qkv_all[:, model_width : 2 * model_width]
    value_part = qkv_all[:, 2 * model_width :]
    kv_product = key_part * value_part

    def own_taps(weight_one, weight_two):
        return filter_taps(weight_one, weight_two, own_position, length)

    taps_own, filter_pull = jax.vjp(own_taps, filter_in, filter_out)
    taps_real, taps_imag = cols_forward(taps_own.reshape(1, dev_rows, row_len, model_width), tables)
    taps_real, taps_imag = (
        lax.all_to_all(taps_real, "seq", split_axis=2, concat_axis=1, tiled=True),
        lax.all_to_all(taps_imag, "seq", split_axis=2, concat_axis=1, tiled=True),
    )
    spec_real, spec_imag = rows_forward(taps_real, taps_imag, tables)
    taps_spec = (spec_real[0], spec_imag[0])
    conv_out, kv_real, kv_imag = convolve(
        kv_product.reshape(seq_count, dev_rows, row_len, model_width),
        taps_spec,
        tables,
        False,
        length,
    )
    skip_gain = vectors[4]
    inner_sum = conv_out.reshape(-1, model_width) + skip_gain * kv_product
    gated_out = (query_part * inner_sum).astype(jnp.bfloat16)
    branch = block_apply(gated_out, w_out)
    normed, first_pull = jax.vjp(
        norm_rows, flat_tokens.astype(jnp.float32) + branch, vectors[0], vectors[1]
    )
    normed_low = normed.astype(jnp.bfloat16)
    gate_up = block_apply(normed_low, w_gate_up).reshape(-1, 4, 2, quarter_hidden)
    gate_value = gate_up[:, :, 0].reshape(-1, FF)
    up_value = gate_up[:, :, 1].reshape(-1, FF)
    active, active_pull = jax.vjp(glu_act, gate_value, up_value)
    active_low = active.astype(jnp.bfloat16)
    down_value = block_apply(active_low, w_down)
    result, second_pull = jax.vjp(
        norm_rows, normed_low.astype(jnp.float32) + down_value, vectors[2], vectors[3]
    )
    output = result.astype(jnp.bfloat16).reshape(tokens.shape)
    d_second, d_gain_two, d_bias_two = second_pull(
        cotangent.reshape(-1, model_width).astype(jnp.float32)
    )
    d_down = d_second.astype(jnp.bfloat16)
    g_down = block_grad(active_low, d_down, hidden_ratio, 1)
    d_gate, d_up = active_pull(block_back(d_down, w_down))
    d_gate_up = jnp.stack(
        [d_gate.reshape(-1, 4, quarter_hidden), d_up.reshape(-1, 4, quarter_hidden)], axis=2
    )
    d_gate_up = d_gate_up.reshape(-1, 2 * FF).astype(jnp.bfloat16)
    gate_up_tiles = block_grad(normed_low, d_gate_up, 1, 2 * hidden_ratio).reshape(
        4, 2, hidden_ratio, weights.shape[1], weights.shape[2]
    )
    g_gate = gate_up_tiles[:, 0].reshape(-1, weights.shape[1], weights.shape[2])
    g_up = gate_up_tiles[:, 1].reshape(-1, weights.shape[1], weights.shape[2])
    d_normed = d_second + block_back(d_gate_up, w_gate_up)
    d_first, d_gain_one, d_bias_one = first_pull(d_normed)
    d_branch = d_first.astype(jnp.bfloat16)
    g_out = block_grad(gated_out, d_branch, 1, 1)
    d_gated = block_back(d_branch, w_out)
    d_query = d_gated * inner_sum
    d_inner = d_gated * query_part
    d_skip = jnp.sum(d_inner * kv_product, axis=0)
    d_conv, back_real, back_imag = convolve(
        d_inner.reshape(seq_count, dev_rows, row_len, model_width), taps_spec, tables, True, length
    )
    d_kv = d_conv.reshape(-1, model_width) + skip_gain * d_inner
    d_qkv = jnp.concatenate([d_query, d_kv * value_part, d_kv * key_part], axis=1).astype(
        jnp.bfloat16
    )
    g_in = block_grad(flat_tokens, d_qkv, 1, 3)
    in_grad = (d_first + block_back(d_qkv, w_in)).reshape(tokens.shape)
    cross_real = jnp.sum(back_real * kv_real + back_imag * kv_imag, axis=0, keepdims=True)
    cross_imag = jnp.sum(back_imag * kv_real - back_real * kv_imag, axis=0, keepdims=True)
    cross_back_real, cross_back_imag = rows_inverse(cross_real, cross_imag, tables)
    cross_rows_real, cross_rows_imag = (
        lax.all_to_all(
            cross_back_real.astype(jnp.bfloat16), "seq", split_axis=1, concat_axis=2, tiled=True
        ).astype(cross_back_real.dtype),
        lax.all_to_all(
            cross_back_imag.astype(jnp.bfloat16), "seq", split_axis=1, concat_axis=2, tiled=True
        ).astype(cross_back_imag.dtype),
    )
    d_taps = cols_inverse(cross_rows_real, cross_rows_imag, tables, length).reshape(-1, model_width)
    g_filter_in, g_filter_out = filter_pull(d_taps)
    tile_grads = jnp.concatenate([g_in, g_out, g_gate, g_up, g_down], axis=0)
    slot_mask = slot_used.astype(jnp.float32)[:, None, None]
    summed = lax.psum(tile_grads.astype(jnp.bfloat16), "dp").astype(jnp.float32)
    owned = lax.psum_scatter(
        jnp.take(summed, tile_of_slot, axis=0) * slot_mask, "seq", scatter_dimension=0, tiled=True
    )
    tokens_all = seq_count * dev_rows * row_len * lax.axis_size("dp") * seq_devices
    grad_scale = 1.0 / math.sqrt(tokens_all)
    mine_mask = lax.dynamic_slice_in_dim(slot_mask, seq_index * owner_cap, owner_cap, 0)
    tile_grad = owned * grad_scale
    tile_new = adam_step(tile_master, tile_moment, tile_second, tile_average, tile_grad, 0.1, 0.01)
    vector_part = jnp.stack([d_gain_one, d_bias_one, d_gain_two, d_bias_two, d_skip])
    vector_sum, in_sum, out_sum = lax.psum((vector_part, g_filter_in, g_filter_out), ("dp", "seq"))
    vector_grad = vector_sum * grad_scale
    in_grad_filter = in_sum * grad_scale
    out_grad_filter = out_sum * grad_scale
    vector_new = adam_step(
        vectors, vector_moment, vector_second, vector_average, vector_grad, 0.4, 0.0
    )
    in_new = adam_step(filter_in, in_moment, in_second, in_average, in_grad_filter, 0.4, 0.01)
    out_new = adam_step(filter_out, out_moment, out_second, out_average, out_grad_filter, 0.1, 0.01)
    return (
        output,
        in_grad,
        tile_grad,
        tile_new[0] * mine_mask,
        tile_new[1] * mine_mask,
        tile_new[2] * mine_mask,
        vector_grad,
        vector_new[0],
        vector_new[1],
        vector_new[2],
        in_grad_filter,
        in_new[0],
        in_new[1],
        in_new[2],
        out_grad_filter,
        out_new[0],
        out_new[1],
        out_new[2],
    )


MESH = pl.DeviceIdType.MESH
VMEM_LIMIT = 56 * 2**20
STEP_VMEM = 62 * 2**20


def flip(index, bits):
    at = 1
    result = index
    while at <= bits:
        if bits & at:
            result = result + at - 2 * at * lax.rem(lax.div(index, at), 2)
        at *= 2
    return result


class Links:
    def __init__(self, send_sem, recv_sem):
        self.send_sem, self.recv_sem, self.used = send_sem, recv_sem, 0
        self.dp, self.seq = lax.axis_index("dp"), lax.axis_index("seq")
        self.deep = lax.axis_size("seq") // 2
        self.z, self.core = lax.div(self.seq, 2), lax.rem(self.seq, 2)
        self.partner = (self.dp, self.seq + 1 - 2 * self.core)
        low, high = lax.rem(self.dp, 2), lax.div(self.dp, 2)
        across_x = self.dp + 1 - 2 * low
        across_y = self.dp + 2 - 4 * high
        self.near = across_x + self.core * (across_y - across_x)
        self.far = across_y + self.core * (across_x - across_y)
        self.diagonal = 3 - self.dp
        self.to_near, self.to_far = (self.near, self.seq), (self.far, self.seq)
        self.outer = lax.div(self.z, self.deep // 2)
        self.inner = 1 - self.outer
        self.to_inner = (self.dp, self.seq + 2 - 4 * self.outer)
        self.to_outer = (self.dp, self.seq - 2 + 4 * self.outer)
        self.at_end = (self.z == 0) | (self.z == self.deep - 1)

    def peers(self):
        along = [(self.dp, flip(self.seq, bits)) for bits in range(1, 2 * self.deep)]
        return along + [self.to_near, self.to_far]

    def greet(self):
        for peer in self.peers():
            pl.semaphore_signal(
                pltpu.get_barrier_semaphore(), inc=1, device_id=peer, device_id_type=MESH
            )

    def meet(self):
        pl.semaphore_wait(pltpu.get_barrier_semaphore(), len(self.peers()))

    def copy(self, source, target, device):
        at = self.used
        self.used += 1
        return pltpu.make_async_remote_copy(
            src_ref=source,
            dst_ref=target,
            send_sem=self.send_sem.at[at],
            recv_sem=self.recv_sem.at[at],
            device_id=device,
            device_id_type=MESH,
        )


class Chain:
    def __init__(self, links, base, arrived, leaving, send_sem, recv_sem, chunks):
        self.links, self.base, self.arrived, self.leaving = links, base, arrived, leaving
        self.send_sem, self.recv_sem, self.chunks = send_sem, recv_sem, chunks

    def send(self, k, side, device):
        at = self.chunks[k]
        return pltpu.make_async_remote_copy(
            src_ref=self.leaving.at[side, :, at],
            dst_ref=self.arrived.at[1 - side, :, at],
            send_sem=self.send_sem.at[side, k],
            recv_sem=self.recv_sem.at[1 - side, k],
            device_id=device,
            device_id_type=MESH,
        )

    def receive(self, k, side, device):
        at = self.chunks[k]
        return pltpu.make_async_remote_copy(
            src_ref=self.leaving.at[side, :, at],
            dst_ref=self.arrived.at[side, :, at],
            send_sem=self.send_sem.at[side, k],
            recv_sem=self.recv_sem.at[side, k],
            device_id=device,
            device_id_type=MESH,
        )

    def read(self, ref, k, *side):
        return ref[(*side, slice(None), self.chunks[k])].astype(jnp.float32)

    def begin(self, k):
        links, at = self.links, self.chunks[k]

        @pl.when(links.at_end)
        def _():
            own = self.base[:, at].astype(self.leaving.dtype)
            self.leaving[links.inner, :, at] = own
            self.arrived[links.outer, :, at] = jnp.zeros_like(own)
            self.send(k, links.inner, links.to_inner).start()

    def outward(self, k):
        links, at = self.links, self.chunks[k]

        @pl.when(jnp.logical_not(links.at_end))
        def _():
            self.receive(k, links.outer, links.to_outer).wait_recv()
            total = self.read(self.base, k) + self.read(self.arrived, k, links.outer)
            self.leaving[links.inner, :, at] = total.astype(self.leaving.dtype)
            self.send(k, links.inner, links.to_inner).start()

    def inward(self, k):
        links, at = self.links, self.chunks[k]
        self.receive(k, links.inner, links.to_inner).wait_recv()
        total = self.read(self.base, k) + self.read(self.arrived, k, links.inner)

        @pl.when(jnp.logical_not(links.at_end))
        def _():
            self.leaving[links.outer, :, at] = total.astype(self.leaving.dtype)
            self.send(k, links.outer, links.to_outer).start()

        return total + self.read(self.arrived, k, links.outer)

    def finish(self, k):
        links = self.links
        self.send(k, links.inner, links.to_inner).wait_send()

        @pl.when(jnp.logical_not(links.at_end))
        def _():
            self.send(k, links.outer, links.to_outer).wait_send()


def cut(*edges):
    return tuple(pl.ds(a, b - a) for a, b in zip(edges[:-1], edges[1:]))


def half_tiles(half):
    order = []
    for first, per_block in ((0, 3), (12, 1), (16, 4), (32, 4), (48, 4)):
        order += range(first + 2 * half * per_block, first + 2 * (half + 1) * per_block)
    return order


VMEM = pl.BlockSpec(memory_space=pltpu.VMEM)
SMEM = pl.BlockSpec(memory_space=pltpu.SMEM)
NN = (((1,), (0,)), ((), ()))
NT = (((1,), (1,)), ((), ()))
TN = (((0,), (0,)), ((), ()))


def mul(left, right, dims=NN):
    return lax.dot_general(left, right, dims, preferred_element_type=jnp.float32)


def filter_constants(grid_rows, row_len, width):
    length = grid_rows * row_len
    position = (np.arange(grid_rows)[:, None] + grid_rows * np.arange(row_len)[None, :]).reshape(-1)
    turn = 2.0 * np.pi * position / length
    rows = [position / length, np.cos(turn), -np.sin(turn), np.cos(2 * turn), -np.sin(2 * turn)]
    features = np.zeros((length, 8), np.float32)
    features[:, :5] = np.stack(rows, axis=1)
    rate = 0.3 * 1000.0 ** np.mod(golden * np.arange(width), 1.0)
    total = np.expm1(-2.0 * rate) / np.expm1(-2.0 * rate / length)
    channels = np.stack([rate, 1.0 / np.sqrt(total)]).astype(np.float32)
    return (features, channels)


def phases_of(features, filter_in):
    total = features[:, 0:1] * filter_in[0:1, :]
    for i in range(1, filter_in.shape[0]):
        total += features[:, i : i + 1] * filter_in[i : i + 1, :]
    return total


def first_row(shape):
    return lax.broadcasted_iota(jnp.int32, shape, 0) == 0


def spectrum_product(one_real, one_imag, two_real, two_imag, sign):
    first = first_row(one_real.shape)
    cross = jnp.where(first, 0.0, two_imag) * sign
    diag = jnp.where(first, two_imag, two_real)
    return (one_real * two_real - one_imag * cross, one_real * cross + one_imag * diag)


def decay_of(features, channels, lanes):
    return jnp.exp(-features[:, 0:1] * channels[0:1, lanes]) * channels[1:2, lanes]


def half_lanes(width):
    half = lax.rem(lax.axis_index("seq"), 2)
    return pl.ds(pl.multiple_of(half * width, width), width)


def tile_at(packed, half, first):
    return packed[half, :, first : first + packed.shape[1]]


def normalize(values):
    centered = values - jnp.mean(values, axis=-1, keepdims=True)
    spread = lax.rsqrt(jnp.mean(centered * centered, axis=-1, keepdims=True) + norm_eps)
    return (centered * spread, spread)


def normalize_back(gradient, unit, spread):
    mean = jnp.mean(gradient, axis=-1, keepdims=True)
    along = jnp.mean(gradient * unit, axis=-1, keepdims=True)
    return (gradient - mean - unit * along) * spread


def gelu_parts(v):
    share = 0.5 + 0.5 * lax.erf(v * math.sqrt(0.5))
    density = jnp.exp(-0.5 * v * v) * (1.0 / math.sqrt(2.0 * math.pi))
    return (v * share, share + v * density)


def adam(weight, moment, second, average, gradient, rate, decay):
    moment = beta_one * moment + (1.0 - beta_one) * gradient
    second = beta_two * second + (1.0 - beta_two) * gradient * gradient
    moment = moment * (1.0 / (1.0 - beta_one**STEP))
    root = jnp.sqrt(second * (1.0 / (1.0 - beta_two**STEP)))
    weight = weight - rate * (moment / (root + adam_eps) + decay * weight)
    return (second, weight, keep_rate * average + (1.0 - keep_rate) * weight)


def adam_kernel(scale, owners, reduced, late, *refs):
    tile_in, small_in, tile_out, small_out = refs[:4], refs[4:16], refs[16:20], refs[20:32]
    held, fresh, in_sem, out_sem, tile_of_slot = refs[32:36], refs[36:40], *refs[40:43]
    slots, side, _ = held[0].shape
    per_step = 2

    def load(array, step):
        at = pl.ds(step * per_step, per_step)
        return pltpu.make_async_copy(
            tile_in[array].at[at], held[array].at[at], in_sem.at[array, step]
        )

    def store(array, step):
        at = pl.ds(step * per_step, per_step)
        return pltpu.make_async_copy(
            fresh[array].at[at], tile_out[array].at[at], out_sem.at[array, step]
        )

    steps = slots // per_step
    for step in range(steps):
        for array in range(4):
            load(array, step).start()
    me = lax.axis_index("seq")

    def place(i, rank):
        mine = owners[i] == me

        @pl.when(mine)
        def _():
            tile_of_slot[rank] = i

        return rank + jnp.where(mine, 1, 0)

    owned = lax.fori_loop(0, owners.shape[0], place, jnp.int32(0))
    order, model = small_in[8].shape
    width = model // 2
    count, count_in = small_in[0].shape[0], small_in[4].shape[0]
    sums = late[:, :, late.shape[2] - width :].astype(jnp.float32) * scale
    gradients = (
        jnp.concatenate([sums[h, order : order + count] for h in range(2)], axis=1),
        sums[0, order + 8 : order + 8 + count_in, :order],
        jnp.concatenate([sums[h, :order] for h in range(2)], axis=1),
    )
    rates = ((0.4, 0.0), (0.4, 0.01), (0.1, 0.01))
    for i, (gradient, rate) in enumerate(zip(gradients, rates)):
        small_out[4 * i][...] = gradient
        results = adam(*(ref[...] for ref in small_in[4 * i : 4 * i + 4]), gradient, *rate)
        for ref, values in zip(small_out[4 * i + 1 : 4 * i + 4], results):
            ref[...] = values
    for step in range(steps):
        for array in range(4):
            load(array, step).wait()
        for slot in range(step * per_step, (step + 1) * per_step):
            keep = owned > slot
            tile = jnp.where(keep, tile_of_slot[slot], 0)
            at = jnp.minimum(tile, 11)
            first = pl.multiple_of(lax.div(lax.rem(at, 6), 2) * 2 * side, 2 * side)
            pair = late[lax.div(at, 6), :, pl.ds(first, 2 * side)].astype(jnp.float32)
            from_late = jnp.where(lax.rem(at, 2) == 0, pair[:, :side], pair[:, side:])
            early = reduced[:, slot * side : (slot + 1) * side].astype(jnp.float32)
            gradient = jnp.where(keep, jnp.where(tile < 12, from_late, early) * scale, 0.0)
            fresh[0][slot] = gradient
            results = adam(*(ref[slot] for ref in held), gradient, 0.1, 0.01)
            for ref, values in zip(fresh[1:], results):
                ref[slot] = jnp.where(keep, values, 0.0)
        for array in range(4):
            store(array, step).start()
    for step in range(steps):
        for array in range(4):
            store(array, step).wait()


def adam_call(scale, owners, reduced, late, tile_state, small_state):
    slots = tile_state[0].shape[0]
    state = pltpu.VMEM(tile_state[0].shape, jnp.float32)
    anywhere = pl.BlockSpec(memory_space=pl.ANY)
    shape = jax.ShapeDtypeStruct
    return pl.pallas_call(
        functools.partial(adam_kernel, scale),
        out_shape=tuple(shape(a.shape, a.dtype) for a in tile_state + small_state),
        in_specs=[SMEM] + [VMEM] * 2 + [anywhere] * 4 + [VMEM] * 12,
        out_specs=[anywhere] * 4 + [VMEM] * 12,
        scratch_shapes=[state] * 8
        + [pltpu.SemaphoreType.DMA((4, slots // 2))] * 2
        + [pltpu.SMEM((slots,), jnp.int32)],
        compiler_params=pltpu.CompilerParams(vmem_limit_bytes=VMEM_LIMIT),
        name="adam",
    )(owners, reduced, late, *tile_state, *small_state)


class Exchange:
    def __init__(self, links, cells, columns, send_sem, recv_sem):
        self.links, self.cells, self.columns = links, cells, columns
        self.send_sem, self.recv_sem = send_sem, recv_sem

    def copy(self, bits):
        links = self.links
        peer = flip(links.seq, bits)
        return pltpu.make_async_remote_copy(
            src_ref=self.cells.at[peer],
            dst_ref=self.columns.at[links.seq],
            send_sem=self.send_sem.at[bits],
            recv_sem=self.recv_sem.at[bits],
            device_id=(links.dp, peer),
            device_id_type=MESH,
        )

    def send(self, *bits):
        for b in bits:
            if b == 0:
                me = self.links.seq
                self.columns[me] = self.cells[me]
            else:
                self.copy(b).start()

    def arrived(self, *bits):
        for b in bits:
            if b:
                peer = flip(self.links.seq, b)
                pltpu.make_async_remote_copy(
                    src_ref=self.cells.at[peer],
                    dst_ref=self.columns.at[peer],
                    send_sem=self.send_sem.at[b],
                    recv_sem=self.recv_sem.at[b],
                    device_id=(self.links.dp, peer),
                    device_id_type=MESH,
                ).wait_recv()

    def sent(self):
        for b in range(1, self.cells.shape[0]):
            self.copy(b).wait_send()


def columns_of_chip(columns, chip):
    pair = columns[pl.ds(2 * chip, 2)]
    return pair.reshape(2 * pair.shape[1], pair.shape[2])


def transform_arrivals(exchange, table, spec):
    for near in range(exchange.links.deep):
        transform_pair(exchange, table, spec, near)


def transform_pair(exchange, table, spec, near):
    step = 2 * exchange.columns.shape[1]
    exchange.arrived(2 * near, 2 * near + 1)
    chip = flip(exchange.links.z, near)
    lanes = pl.ds(pl.multiple_of(chip * step, step), step)
    part = mul(table[:, lanes], columns_of_chip(exchange.columns, chip))
    if near:
        spec[...] += part
    else:
        spec[...] = part


def send_inverse(exchange, table_back, filtered):
    row_len = exchange.cells.shape[1]
    for near in reversed(range(exchange.links.deep)):
        chip = flip(exchange.links.z, near)
        rows = pl.ds(pl.multiple_of(chip * 2 * row_len, 2 * row_len), 2 * row_len)
        part = mul(table_back[rows, :], filtered[...]).astype(exchange.cells.dtype)
        exchange.cells[pl.ds(2 * chip, 2)] = part.reshape(2, row_len, part.shape[1])
        exchange.send(2 * near, 2 * near + 1)


class Reducer:
    def __init__(self, links, grads, scratch, chunks):
        (
            self.got,
            self.near_in,
            self.far_in,
            self.far_out,
            self.base,
            arrived,
            leaving,
            chain_send,
            chain_recv,
        ) = scratch
        self.links, self.grads, self.chunks = links, grads, chunks
        self.count = len(chunks)
        self.quarter = self.base.shape[0]
        self.chain = Chain(links, self.base, arrived, leaving, chain_send, chain_recv, chunks)
        self.swaps, self.nears, self.diagonals, self.fars = [], [], [], []
        for at in chunks:
            self.swaps.append(
                links.copy(grads.at[1 - links.core, :, at], self.got.at[:, at], links.partner)
            )
            self.nears.append(
                links.copy(
                    grads.at[links.core, self.rows_of(links.near), at],
                    self.near_in.at[0, :, at],
                    links.to_near,
                )
            )
            self.diagonals.append(
                links.copy(
                    grads.at[links.core, self.rows_of(links.diagonal), at],
                    self.near_in.at[1, :, at],
                    links.to_near,
                )
            )
            self.fars.append(links.copy(self.far_out.at[:, at], self.far_in.at[:, at], links.to_far))

    def rows_of(self, index):
        return pl.ds(pl.multiple_of(index * self.quarter, self.quarter), self.quarter)

    def swap(self, k):
        self.swaps[k].start()

    def swap_half(self, k, half):
        @pl.when(self.links.core != half)
        def _():
            self.swaps[k].start()

    def merge_cores(self, k):
        at, wide = self.chunks[k], jnp.float32
        self.swaps[k].wait_recv()
        core = self.links.core
        self.grads[core, :, at] = (
            self.grads[core, :, at].astype(wide) + self.got[:, at].astype(wide)
        ).astype(self.grads.dtype)
        self.diagonals[k].start()
        self.nears[k].start()

    def go_far(self, k):
        at, wide = self.chunks[k], jnp.float32
        self.diagonals[k].wait_recv()
        self.far_out[:, at] = (
            self.grads[self.links.core, self.rows_of(self.links.far), at].astype(wide)
            + self.near_in[1, :, at].astype(wide)
        ).astype(self.far_out.dtype)
        self.fars[k].start()

    def collect(self, k):
        at, wide = self.chunks[k], jnp.float32
        self.nears[k].wait_recv()
        self.fars[k].wait_recv()
        self.base[:, at] = (
            self.grads[self.links.core, self.rows_of(self.links.dp), at].astype(wide)
            + self.near_in[0, :, at].astype(wide)
            + self.far_in[:, at].astype(wide)
        )
        self.chain.begin(k)

    def outward(self, k):
        self.chain.outward(k)

    def finish(self, k):
        self.swaps[k].wait_send()
        self.nears[k].wait_send()
        self.diagonals[k].wait_send()
        self.fars[k].wait_send()
        self.chain.finish(k)


class Refs:
    def __init__(self, names, refs):
        self.__dict__.update(zip(names, refs, strict=True))


def places(owners, seq):
    rank, place = jnp.int32(0), []
    for i in range(owners.shape[0]):
        mine = owners[i] == seq
        place.append((rank, mine))
        rank = rank + jnp.where(mine, 1, 0)
    return (place, rank)


def tiles_of_slots(place, slots):
    tiles = [jnp.int32(0)] * slots
    for i, (rank, mine) in enumerate(place):
        at = jnp.where(mine, rank, -1)
        tiles = [jnp.where(at == slot, i, tile) for slot, tile in enumerate(tiles)]
    return tiles


def assemble(place, held, own):
    side = held.shape[2]
    place = [(jnp.minimum(rank, held.shape[0] - 1), mine) for rank, mine in place]
    for half in range(2):
        order = half_tiles(half)
        for j in range(0, len(order), 2):
            pair = [jnp.where(place[i][1], held[place[i][0]], 0.0) for i in order[j : j + 2]]
            own[half, :, j * side : (j + 2) * side] = jnp.concatenate(pair, axis=1).astype(own.dtype)


def plane_copies(links, array, at):
    quarter = array.shape[1] // 4

    def rows_of(index):
        return pl.ds(pl.multiple_of(index * quarter, quarter), quarter)

    mine = array.at[links.core, rows_of(links.dp), at]
    other = array.at[links.core, rows_of(links.near), at]
    both = array.at[links.core, :, at]
    return (
        links.copy(mine, mine, links.to_near),
        links.copy(mine, mine, links.to_far),
        links.copy(other, other, links.to_far),
        links.copy(both, both, links.partner),
    )


def step_kernel(names, chunks, first_chunks, early_chunks, late_chunks, *refs):
    r = Refs(names, refs)
    low, wide = jnp.bfloat16, jnp.float32
    links = Links(r.send_sem, r.recv_sem)
    _, side, _ = r.full.shape
    quarter_rows = side // 4
    my_rows = pl.ds(pl.multiple_of(links.dp * quarter_rows, quarter_rows), quarter_rows)
    near_rows = pl.ds(pl.multiple_of(links.near * quarter_rows, quarter_rows), quarter_rows)
    devices, row_len, width = r.kv.shape
    seqs = devices // 2
    length = devices * row_len
    half_length = length // 2
    model = 2 * width
    lanes = half_lanes(width)
    pair_seqs = seqs // 2
    pair_rows = pair_seqs * row_len
    loads = (
        pltpu.make_async_copy(r.master.at[:, my_rows, :], r.held, r.load_sem.at[0]),
        pltpu.make_async_copy(r.table_hbm, r.table, r.load_sem.at[1]),
        pltpu.make_async_copy(r.table_back_hbm, r.table_back, r.load_sem.at[2]),
    )
    for load in loads:
        load.start()
    links.greet()
    loads[0].wait()
    place, owned = places(r.owners, links.seq)
    assemble(place, r.held, r.own)
    links.meet()

    swaps, planes = [], []
    for at in chunks:
        swaps.append(links.copy(r.own.at[1 - links.core, :, at], r.got.at[:, at], links.partner))
        swaps[-1].start()
        planes.append(plane_copies(links, r.full, at))
    chain = Chain(links, r.base, r.arrived, r.leaving, r.chain_send, r.chain_recv, chunks)
    count = len(chunks)

    def hidden_step():
        r.hidden[...] = jnp.sin(phases_of(r.features[...], r.filter_in[...])).astype(low)

    def taps_step(part):
        span = slice(part * length // 4, (part + 1) * length // 4)
        values = mul(r.hidden[span, :], r.filter_out[:, lanes].astype(low))
        decay = jnp.exp(-r.features[span, 0:1] * r.channels[0:1, lanes]) * r.channels[1:2, lanes]
        r.filtered[span, :] = (values * decay).astype(low)

    def spectrum_step(part):
        span = slice(part * length // 4, (part + 1) * length // 4)
        scale = 2.0 / length
        if part % 2 == 0:
            scale = jnp.where(first_row((length // 4, 1)), 1.0 / length, 2.0 / length)
        r.taps_spec[span, :] = mul(r.table[span, :], r.filtered[...]) * scale

    fill = [hidden_step]
    fill += [functools.partial(taps_step, i) for i in range(4)]
    fill += [loads[1].wait]
    fill += [functools.partial(spectrum_step, i) for i in range(4)]
    fill.reverse()

    def fill_in(steps):
        for _ in range(min(steps, len(fill))):
            fill.pop()()

    def collect(k):
        at = chunks[k]
        swaps[k].wait()
        r.base[:, at] = r.own[links.core, :, at] + r.got[:, at]
        chain.begin(k)

    def pass_on(k):
        r.full[links.core, my_rows, chunks[k]] = chain.inward(k).astype(low)
        planes[k][0].start()
        planes[k][1].start()

    def relay(k):
        planes[k][0].wait_recv()
        planes[k][2].start()

    def share(k):
        planes[k][1].wait_recv()
        planes[k][2].wait_recv()
        planes[k][3].start()

    fill_in(1)
    for k in range(count):
        collect(k)
    tiles = tiles_of_slots(place, r.held.shape[0])
    stages = ((chain.outward, 0), (pass_on, 1), (relay, 2), (share, 4))
    after = [
        [(stage, k - late) for stage, late in stages if 0 <= k - late < count]
        for k in range(count + 4)
    ]

    def go_on(steps=1):
        for _ in range(min(steps, len(after))):
            for stage, k in after.pop(0):
                stage(k)

    for _ in range(count):
        fill_in(2)
        go_on()
    for k in range(first_chunks):
        planes[k][3].wait_recv()
    fill_in(len(fill))

    outbound = Exchange(links, r.kv, r.columns, r.field_send, r.field_recv)

    def project(pair, tiles_here):
        span = pl.ds(pl.multiple_of(pair * pair_rows, pair_rows), pair_rows)
        for i in tiles_here:
            block = i // 3
            weight = tile_at(r.full, i // 6, (i % 6) * side)
            part = mul(r.x[span, block * side : (block + 1) * side], weight)
            target = (r.query, r.key, r.value)[i // 4]
            at = (i % 4) * side
            target[span, at : at + side] = part.astype(low)

    def multiply(pair):
        for s in range(pair_seqs):
            seq = pair * pair_seqs + s
            line = pl.ds(pl.multiple_of(seq * row_len, row_len), row_len)
            for h in range(2):
                part = slice(h * width, (h + 1) * width)
                both = r.key[line, part].astype(wide) * r.value[line, part].astype(wide)
                r.kv[2 * seq + h] = both.astype(low)

    for pair, bits in ((links.inner, (6, 7, 4, 5)), (links.outer, (2, 3, 1, 0))):
        project(pair, range(4, 12))
        multiply(pair)
        outbound.send(*bits)
        go_on()
    for pair in (links.outer, links.inner):
        project(pair, range(4))
    for near in range(links.deep):
        transform_pair(outbound, r.table, r.kv_spec, near)
        go_on()
    go_on(len(after))

    def filter_with(ref, other, sign, scale=None):
        real, imag = spectrum_product(
            ref[:half_length], ref[half_length:], other[:half_length], other[half_length:], sign
        )
        if scale is not None:
            real, imag = real * scale, imag * scale
        r.filtered[:half_length] = real.astype(low)
        r.filtered[half_length:] = imag.astype(low)

    filter_with(r.kv_spec, r.taps_spec, 1.0)
    loads[2].wait()
    inbound = Exchange(links, r.cells_back, r.conv, r.back_send, r.back_recv)
    send_inverse(inbound, r.table_back, r.filtered)
    for k in range(first_chunks, count):
        planes[k][3].wait_recv()

    out_at, gate_at, up_at, down_at = 6 * side, 8 * side, 16 * side, 24 * side
    quarter = 4 * side
    for b in range(4):
        for i in range(4):
            r.down_weights[b, i * side : (i + 1) * side, :] = tile_at(
                r.full, b // 2, down_at + (4 * (b % 2) + i) * side
            )
    r.sums[...] = jnp.zeros_like(r.sums)
    gain_one, bias_one = r.vectors[0:1], r.vectors[1:2]
    gain_two, bias_two = r.vectors[2:3], r.vectors[3:4]
    skip = r.vectors[4:5]

    def cells(ref, seq, seqs_here):
        parts = ref[pl.ds(2 * seq, 2 * seqs_here)].astype(wide)
        lines = [
            jnp.concatenate([parts[2 * s], parts[2 * s + 1]], axis=1) for s in range(seqs_here)
        ]
        return jnp.concatenate(lines, axis=0)

    def block(values, b):
        return values[:, b * side : (b + 1) * side]

    def weight_of(first, b, count):
        at = first + (b % 2) * count
        return r.full[b // 2, :, at : at + count]

    def add_sum(row, values):
        r.sums[row : row + 1, :] += jnp.sum(values, axis=0, keepdims=True)

    def layer(seq, seqs_here, first):
        rows = pl.ds(pl.multiple_of(seq * row_len, row_len), seqs_here * row_len)
        held = slice(first * row_len, (first + seqs_here) * row_len)
        kv_here = cells(r.kv, seq, seqs_here)
        inner = cells(r.conv, seq, seqs_here) + skip * kv_here
        query_here = r.query[rows, :].astype(wide)
        gated = (query_here * inner).astype(low)
        r.gated[held, :] = gated
        branch = [mul(block(gated, b), weight_of(out_at, b, side)) for b in range(4)]
        unit_one, spread_one = normalize(
            r.x[rows, :].astype(wide) + jnp.concatenate(branch, axis=1)
        )
        normed = (unit_one * gain_one + bias_one).astype(low)
        r.normed[held, :] = normed
        down = []
        for b in range(4):
            span = slice(b * quarter, (b + 1) * quarter)
            here = block(normed, b)
            gate = mul(here, weight_of(gate_at, b, quarter))
            up = mul(here, weight_of(up_at, b, quarter))
            curved, slope = gelu_parts(gate)
            active = (curved * up).astype(low)
            r.active[held, span] = active
            r.d_gate[held, span] = (slope * up).astype(low)
            r.d_up[held, span] = curved.astype(low)
            down.append(mul(active, r.down_weights[b]))
        unit_two, spread_two = normalize(normed.astype(wide) + jnp.concatenate(down, axis=1))
        r.output[rows, :] = (unit_two * gain_two + bias_two).astype(low)
        cot = r.cotangent[rows, :].astype(wide)
        add_sum(2, cot * unit_two)
        add_sum(3, cot)
        d_second = normalize_back(cot * gain_two, unit_two, spread_two)
        d_down = d_second.astype(low)
        r.d_down[held, :] = d_down
        d_normed = []
        for b in range(4):
            span = slice(b * quarter, (b + 1) * quarter)
            d_active = mul(block(d_down, b), r.down_weights[b], NT)
            d_gate = (d_active * r.d_gate[held, span].astype(wide)).astype(low)
            d_up = (d_active * r.d_up[held, span].astype(wide)).astype(low)
            r.d_gate[held, span] = d_gate
            r.d_up[held, span] = d_up
            d_normed.append(
                mul(d_gate, weight_of(gate_at, b, quarter), NT)
                + mul(d_up, weight_of(up_at, b, quarter), NT)
            )
        d_normed = d_second + jnp.concatenate(d_normed, axis=1)
        add_sum(0, d_normed * unit_one)
        add_sum(1, d_normed)
        d_first = normalize_back(d_normed * gain_one, unit_one, spread_one)
        r.in_grad[rows, :] = d_first
        d_branch = d_first.astype(low)
        r.d_branch[held, :] = d_branch
        d_gated = [mul(block(d_branch, b), weight_of(out_at, b, side), NT) for b in range(4)]
        d_gated = jnp.concatenate(d_gated, axis=1)
        r.query[rows, :] = (d_gated * inner).astype(low)
        d_inner = d_gated * query_here
        add_sum(4, d_inner * kv_here)
        d_inner = d_inner.astype(low)
        for s in range(seqs_here):
            for h in range(2):
                r.d_inner[2 * (seq + s) + h] = d_inner[
                    s * row_len : (s + 1) * row_len, h * width : (h + 1) * width
                ]

    def layer_grads(rows, more):
        for b in range(4):
            span = slice(b * quarter, (b + 1) * quarter)
            mine = slice(b * side, (b + 1) * side)
            at = (b % 2) * quarter

            def put(first, values):
                target = slice(first - out_at, first - out_at + values.shape[1])
                if more:
                    values += r.grads[b // 2, :, target].astype(wide)
                r.grads[b // 2, :, target] = values.astype(low)

            put(out_at + (b % 2) * side, mul(r.gated[rows, mine], r.d_branch[rows, mine], TN))
            put(gate_at + at, mul(r.normed[rows, mine], r.d_gate[rows, span], TN))
            put(up_at + at, mul(r.normed[rows, mine], r.d_up[rows, span], TN))
            tall = mul(r.active[rows, span], r.d_down[rows, mine], TN)
            for i in range(4):
                put(down_at + at + i * side, tall[i * side : (i + 1) * side, :])

    back_out = Exchange(links, r.d_inner, r.columns, r.field_send_two, r.field_recv_two)
    inbound.arrived(1, 2, 3)
    layer(links.outer * pair_seqs, pair_seqs, 0)
    back_out.send(2, 3, 1, 0)
    inbound.arrived(6, 7)
    layer(flip(links.z, 3), 1, 2)
    back_out.send(6, 7)
    layer_grads(slice(0, 2 * row_len), False)
    inbound.arrived(4, 5)
    layer(flip(links.z, 2), 1, 1)
    back_out.send(4, 5)
    layer_grads(slice(row_len, 3 * row_len), True)

    early_wide = r.grads.shape[2]
    early = Reducer(
        links,
        r.grads,
        (
            r.early_got,
            r.own.at[:, :, pl.ds(0, early_wide)],
            r.got.at[:, pl.ds(0, early_wide)],
            r.base.at[:, pl.ds(0, early_wide)],
            r.early_base,
            r.arrived.at[:, :, pl.ds(0, early_wide)],
            r.leaving.at[:, :, pl.ds(0, early_wide)],
            r.early_send,
            r.early_recv,
        ),
        early_chunks,
    )
    tail = Reducer(
        links,
        r.late,
        (
            r.late_got,
            r.late_near,
            r.late_far_in,
            r.late_far_out,
            r.late_base,
            r.late_arrived,
            r.late_leaving,
            r.late_send,
            r.late_recv,
        ),
        late_chunks,
    )
    for k in range(count):
        chain.finish(k)
        for copy in planes[k]:
            copy.wait_send()
    for k in range(early.count):
        early.swap(k)
    r.late[...] = jnp.zeros_like(r.late)
    for k in range(early.count):
        early.merge_cores(k)
    per_pair = -(-early.count // links.deep)
    for near in range(links.deep):
        transform_pair(back_out, r.table, r.spec, near)
        for k in range(near * per_pair, min((near + 1) * per_pair, early.count)):
            early.go_far(k)
    filter_with(r.spec, r.taps_spec, -1.0)
    inbound.sent()
    back_in = Exchange(links, r.cells_back, r.conv, r.back_send_two, r.back_recv_two)
    send_inverse(back_in, r.table_back, r.filtered)

    totals = []
    for at in early_chunks:
        part = r.total.at[links.core, :, at]
        totals.append(links.copy(part, part, links.partner))

    def early_total(k):
        r.total[links.core, :, early_chunks[k]] = early.chain.inward(k).astype(low)
        totals[k].start()

    for k in range(early.count):
        early.collect(k)
    scale = jnp.where(first_row((half_length, 1)), 1.0 / length, 2.0 / length)
    filter_with(r.spec, r.kv_spec, -1.0, scale)
    scaled = mul(r.table_back[...], r.filtered[...]) * decay_of(r.features, r.channels, lanes)
    scaled = scaled.astype(low)
    phases = phases_of(r.features[...], r.filter_in[...])
    order = r.filter_in.shape[1]
    first_late = 6 * side
    r.late[links.core, 0:order, first_late:] = mul(r.hidden[...], scaled, TN).astype(low)
    d_hidden = mul(scaled, r.filter_out[:, lanes].astype(low), NT) * jnp.cos(phases)
    lines = [
        jnp.sum(r.features[:, i : i + 1] * d_hidden, axis=0, keepdims=True)
        for i in range(r.filter_in.shape[0])
    ]
    lines.append(jnp.zeros((8 - len(lines), order), wide))
    in_lines = jnp.concatenate(lines, axis=0)
    for half in range(2):
        other = jnp.zeros((8, width), wide)
        if half == 0:
            other = jnp.concatenate([in_lines, jnp.zeros((8, width - order), wide)], axis=1)
        both = jnp.concatenate([r.sums[:, half * width : (half + 1) * width], other], axis=0)
        r.late[half, order : order + 16, first_late:] = both.astype(low)

    per_block = 3 * side
    pairs = ((links.outer, r.d_gate), (links.inner, r.d_up))

    def span_of(pair):
        return pl.ds(pl.multiple_of(pair * pair_rows, pair_rows), pair_rows)

    def fill_rows(pair, d_qkv):
        d_qkv[:pair_rows, :model] = r.query[span_of(pair), :]
        for s in range(pair_seqs):
            seq = pair * pair_seqs + s
            line = pl.ds(pl.multiple_of(seq * row_len, row_len), row_len)
            here = slice(s * row_len, (s + 1) * row_len)
            for h in range(2):
                part = slice(h * width, (h + 1) * width)
                cell = 2 * seq + h
                d_kv = r.conv[cell].astype(wide) + skip[:, part] * r.d_inner[cell].astype(wide)
                d_qkv[here, model + h * width : model + (h + 1) * width] = (
                    d_kv * r.value[line, part].astype(wide)
                ).astype(low)
                d_qkv[here, 2 * model + h * width : 2 * model + (h + 1) * width] = (
                    d_kv * r.key[line, part].astype(wide)
                ).astype(low)

    def first_map_grad(b, pair, d_qkv, more):
        mine = slice(b * side, (b + 1) * side)
        at = (b % 2) * per_block
        target = slice(at, at + per_block)
        values = mul(
            r.x[span_of(pair), mine], d_qkv[:pair_rows, b * per_block : (b + 1) * per_block], TN
        )
        if more:
            values += r.late[b // 2, :, target].astype(wide)
        r.late[b // 2, :, target] = values.astype(low)
        if more and b % 2:
            for k in range(tail.count):
                tail.swap_half(k, b // 2)

    def input_gradient(b):
        mine = slice(b * side, (b + 1) * side)
        span = slice(b * per_block, (b + 1) * per_block)
        for pair, d_qkv in pairs:
            r.in_grad[span_of(pair), mine] += mul(
                d_qkv[:pair_rows, span], weight_of(0, b, per_block), NT
            )

    back_in.arrived(1, 2, 3)
    fill_rows(*pairs[0])
    for b in range(4):
        first_map_grad(b, *pairs[0], False)
    early.outward(0)
    back_in.arrived(4, 5, 6, 7)
    fill_rows(*pairs[1])
    first_map_grad(0, *pairs[1], True)
    early.outward(1)
    first_map_grad(1, *pairs[1], True)
    early_total(0)
    early.outward(2)
    first_map_grad(2, *pairs[1], True)
    early_total(1)
    first_map_grad(3, *pairs[1], True)
    early.outward(3)
    early_total(2)
    for k in range(tail.count):
        tail.merge_cores(k)
    early.outward(4)
    early_total(3)
    for k in range(tail.count):
        tail.go_far(k)
    input_gradient(0)
    early_total(4)
    for k in range(tail.count):
        tail.collect(k)
    input_gradient(1)
    for copy in totals:
        copy.wait()
    for half in range(2):
        for j, i in enumerate(half_tiles(half)):
            if i >= 12:
                at = (j - 6) * side
                r.by_tile[i - 12] = r.total[half, :, at : at + side]
    for s in range(0, len(tiles), 2):
        pair = []
        for k in (s, s + 1):
            values = r.by_tile[jnp.maximum(tiles[k] - 12, 0)].astype(wide)
            pair.append(jnp.where(owned > k, values, 0.0))
        r.spread[my_rows, s * side : (s + 2) * side] = jnp.concatenate(pair, axis=1).astype(low)
    at_home, other = r.spread.at[my_rows, :], r.spread.at[near_rows, :]
    slot_copies = (
        links.copy(at_home, at_home, links.to_near),
        links.copy(at_home, at_home, links.to_far),
        links.copy(other, other, links.to_far),
    )
    late_planes = [plane_copies(links, r.late_full, at) for at in late_chunks]
    slot_copies[0].start()
    slot_copies[1].start()
    for k in range(tail.count):
        tail.outward(k)
    input_gradient(2)
    slot_copies[0].wait_recv()
    slot_copies[2].start()
    for k in range(tail.count):
        r.late_full[links.core, my_rows, late_chunks[k]] = tail.chain.inward(k).astype(low)
        late_planes[k][0].start()
        late_planes[k][1].start()
    for copies in late_planes:
        copies[0].wait_recv()
        copies[2].start()
    input_gradient(3)
    for copies in late_planes:
        copies[1].wait_recv()
        copies[2].wait_recv()
        copies[3].start()
    slot_copies[1].wait_recv()
    slot_copies[2].wait_recv()
    for copies in late_planes:
        for copy in copies[:3]:
            copy.wait_send()
        copies[3].wait()
    for copy in slot_copies:
        copy.wait_send()
    outbound.sent()
    back_out.sent()
    back_in.sent()
    for reducer in (early, tail):
        for k in range(reducer.count):
            reducer.finish(k)


def step_call(arrays, cells):
    slots, side, _ = arrays["master"].shape
    tokens, model = arrays["x"].shape
    order = arrays["filter_in"].shape[1]
    devices, row_len, columns = cells
    length = devices * row_len
    width = arrays["owners"].shape[0] // 2 * side
    early_width = width - 6 * side
    late_width = 6 * side + columns
    chunks = cut(0, 1152, 1920, 2816, 3584, 4480, 5248, width)
    early_chunks = cut(0, 1152, 2176, 3200, 4096, early_width)
    late_chunks = cut(0, 512, 1024, late_width)
    low, wide = jnp.bfloat16, jnp.float32
    quarter, held_tokens = side // 4, 3 * row_len
    shape = jax.ShapeDtypeStruct
    count, early_count, late_count = len(chunks), len(early_chunks), len(late_chunks)
    copies = 5 * (count + early_count) + 8 * late_count + 3
    dma = pltpu.SemaphoreType.DMA
    outputs = dict(
        output=shape((tokens, model), low),
        in_grad=shape((tokens, model), wide),
        spread=shape((side, slots * side), low),
        late_full=shape((2, side, late_width), low),
    )
    scratch = dict(
        held=pltpu.VMEM((slots, quarter, side), wide),
        full=pltpu.VMEM((2, side, width), low),
        own=pltpu.VMEM((2, quarter, width), low),
        got=pltpu.VMEM((quarter, width), low),
        base=pltpu.VMEM((quarter, width), low),
        arrived=pltpu.VMEM((2, quarter, width), low),
        leaving=pltpu.VMEM((2, quarter, width), low),
        table=pltpu.VMEM((length, length), low),
        table_back=pltpu.VMEM((length, length), low),
        hidden=pltpu.VMEM((length, order), low),
        filtered=pltpu.VMEM((length, columns), low),
        taps_spec=pltpu.VMEM((length, columns), wide),
        kv_spec=pltpu.VMEM((length, columns), wide),
        spec=pltpu.VMEM((length, columns), wide),
        query=pltpu.VMEM((tokens, model), low),
        key=pltpu.VMEM((tokens, model), low),
        value=pltpu.VMEM((tokens, model), low),
        gated=pltpu.VMEM((held_tokens, model), low),
        normed=pltpu.VMEM((held_tokens, model), low),
        d_branch=pltpu.VMEM((held_tokens, model), low),
        d_down=pltpu.VMEM((held_tokens, model), low),
        active=pltpu.VMEM((held_tokens, 16 * side), low),
        d_gate=pltpu.VMEM((held_tokens, 16 * side), low),
        d_up=pltpu.VMEM((held_tokens, 16 * side), low),
        down_weights=pltpu.VMEM((4, 4 * side, side), low),
        sums=pltpu.VMEM((8, model), wide),
        grads=pltpu.VMEM((2, side, early_width), low),
        early_got=pltpu.VMEM((side, early_width), low),
        early_base=pltpu.VMEM((quarter, early_width), wide),
        total=pltpu.VMEM((2, quarter, early_width), low),
        by_tile=pltpu.VMEM((NTILES - 12, quarter, side), low),
        late=pltpu.VMEM((2, side, late_width), low),
        late_got=pltpu.VMEM((side, late_width), low),
        late_near=pltpu.VMEM((2, quarter, late_width), low),
        late_far_in=pltpu.VMEM((quarter, late_width), low),
        late_far_out=pltpu.VMEM((quarter, late_width), low),
        late_base=pltpu.VMEM((quarter, late_width), wide),
        late_arrived=pltpu.VMEM((2, quarter, late_width), low),
        late_leaving=pltpu.VMEM((2, quarter, late_width), low),
        load_sem=dma((3,)),
        send_sem=dma((copies,)),
        recv_sem=dma((copies,)),
        chain_send=dma((2, count)),
        chain_recv=dma((2, count)),
        early_send=dma((2, early_count)),
        early_recv=dma((2, early_count)),
        late_send=dma((2, late_count)),
        late_recv=dma((2, late_count)),
    )
    for name in ("kv", "columns", "cells_back", "conv", "d_inner"):
        scratch[name] = pltpu.VMEM(cells, low)
    for name in ("field", "back"):
        for end in ("send", "recv", "send_two", "recv_two"):
            scratch[name + "_" + end] = dma((devices,))
    anywhere = pl.BlockSpec(memory_space=pl.ANY)
    spaces = dict(owners=SMEM, master=anywhere)
    spaces |= dict(table_hbm=anywhere, table_back_hbm=anywhere)
    names = (*arrays, *outputs, *scratch)
    return pl.pallas_call(
        functools.partial(step_kernel, names, chunks, 1, early_chunks, late_chunks),
        out_shape=tuple(outputs.values()),
        in_specs=[spaces.get(name, VMEM) for name in arrays],
        out_specs=(VMEM,) * len(outputs),
        scratch_shapes=list(scratch.values()),
        compiler_params=pltpu.CompilerParams(
            collective_id=0, has_side_effects=True, vmem_limit_bytes=STEP_VMEM
        ),
        name="step",
    )(*arrays.values())


def on_device_columns(
    tokens,
    cotangent,
    owners,
    tile_master,
    tile_moment,
    tile_second,
    tile_average,
    vectors,
    vector_moment,
    vector_second,
    vector_average,
    filter_in,
    in_moment,
    in_second,
    in_average,
    filter_out,
    out_moment,
    out_second,
    out_average,
):
    seq_count, dev_rows, row_len, model_width = tokens.shape
    seq_devices = lax.axis_size("seq")
    grid_rows = dev_rows * seq_devices
    count = seq_count * row_len
    table_host = real_table(grid_rows, row_len)
    table, table_back = jnp.asarray(table_host), jnp.asarray(np.ascontiguousarray(table_host.T))
    features, channels = (
        jnp.asarray(a) for a in filter_constants(grid_rows, row_len, model_width)
    )
    x = tokens.reshape(count, model_width)

    output, in_grad, reduced, late = step_call(
        dict(
            owners=owners,
            master=tile_master,
            x=x,
            cotangent=cotangent.reshape(count, model_width),
            vectors=vectors,
            features=features,
            channels=channels,
            filter_in=filter_in,
            filter_out=filter_out,
            table_hbm=table,
            table_back_hbm=table_back,
        ),
        (seq_devices, row_len, model_width // 2),
    )
    tokens_all = count * lax.axis_size("dp") * seq_devices
    updated = adam_call(
        1.0 / math.sqrt(tokens_all),
        owners,
        reduced,
        late,
        (tile_master, tile_moment, tile_second, tile_average),
        (
            vectors,
            vector_moment,
            vector_second,
            vector_average,
            filter_in,
            in_moment,
            in_second,
            in_average,
            filter_out,
            out_moment,
            out_second,
            out_average,
        ),
    )
    return (output.reshape(tokens.shape), in_grad.reshape(tokens.shape), *updated)


def on_device(*arrays):
    seq_count, dev_rows, row_len, model_width = arrays[0].shape
    seq_devices = lax.axis_size("seq")
    fits = dev_rows == 1 and lax.axis_size("dp") == 4 and seq_devices == 2 * seq_count == 8
    if fits and row_len == 128 and model_width % 256 == 0:
        return on_device_columns(*arrays)
    return on_device_general(*arrays)


def solution(mesh):
    in_specs = (
        P("dp", "seq", None, None),
        P("dp", "seq", None, None),
        P(),
        P("seq", None, None),
        P("seq", None, None),
        P("seq", None, None),
        P("seq", None, None),
        P(),
        P(),
        P(),
        P(),
        P(),
        P(),
        P(),
        P(),
        P(),
        P(),
        P(),
        P(),
    )
    out_specs = (
        P("dp", "seq", None, None),
        P("dp", "seq", None, None),
        P("seq", None, None),
        P("seq", None, None),
        P("seq", None, None),
        P("seq", None, None),
        P(),
        P(),
        P(),
        P(),
        P(),
        P(),
        P(),
        P(),
        P(),
        P(),
        P(),
        P(),
    )
    return jax.shard_map(
        on_device, mesh=mesh, in_specs=in_specs, out_specs=out_specs, check_vma=False
    )
```
